32 devices in a mesh: dp: 4 (over y, x), blk: 4 (over z), head: 2 (over core).
Axes of the slice: x: 2, y: 2, z: 4, core: 2. Of those that a mesh axis runs over, the one named last changes fastest.
Arguments:
- tokens: bfloat16 [4, 2048, 768], P('dp', ('blk', 'head')), may hold values from -6 to 6
- segment: int32 [4, 2048], P('dp'), may hold values from 0 to 7, as said below
- w_qkv: bfloat16 [768, 2304], P(('dp', 'blk', 'head')), may hold values from -0.21875 to 0.21875
- bias_query: bfloat16 [768], P(('dp', 'blk', 'head')), may hold values from -3 to 3
- bias_value: bfloat16 [768], P(('dp', 'blk', 'head')), may hold values from -3 to 3
- w_out: bfloat16 [768, 768], P(('dp', 'blk', 'head')), may hold values from -1.75 to 1.75
- bias_out: bfloat16 [768], P(('dp', 'blk', 'head')), may hold values from -3 to 3
- gain_attn: bfloat16 [768], P(('dp', 'blk', 'head')), may hold values from 0.099609375 to 1.8984375
- shift_attn: bfloat16 [768], P(('dp', 'blk', 'head')), may hold values from -3 to 3
- w_in: bfloat16 [768, 3072], P(('dp', 'blk', 'head')), may hold values from -0.21875 to 0.21875
- bias_in: bfloat16 [3072], P(('dp', 'blk', 'head')), may hold values from -3 to 3
- w_down: bfloat16 [3072, 768], P(('dp', 'blk', 'head')), may hold values from -0.109375 to 0.109375
- bias_down: bfloat16 [768], P(('dp', 'blk', 'head')), may hold values from -3 to 3
- gain_ffn: bfloat16 [768], P(('dp', 'blk', 'head')), may hold values from 0.099609375 to 1.8984375
- shift_ffn: bfloat16 [768], P(('dp', 'blk', 'head')), may hold values from -3 to 3
- cotangent: bfloat16 [4, 2048, 768], P('dp', ('blk', 'head')), may hold values from -6 to 6
Outputs:
- output: bfloat16 [4, 2048, 768], P('dp', ('blk', 'head'))
- grad_tokens: float32 [4, 2048, 768], P('dp', ('blk', 'head'))
- grad_w_qkv: float32 [768, 2304], P(('dp', 'blk', 'head'))
- grad_bias_query: float32 [768], P(('dp', 'blk', 'head'))
- grad_bias_value: float32 [768], P(('dp', 'blk', 'head'))
- grad_w_out: float32 [768, 768], P(('dp', 'blk', 'head'))
- grad_bias_out: float32 [768], P(('dp', 'blk', 'head'))
- grad_gain_attn: float32 [768], P(('dp', 'blk', 'head'))
- grad_shift_attn: float32 [768], P(('dp', 'blk', 'head'))
- grad_w_in: float32 [768, 3072], P(('dp', 'blk', 'head'))
- grad_bias_in: float32 [3072], P(('dp', 'blk', 'head'))
- grad_w_down: float32 [3072, 768], P(('dp', 'blk', 'head'))
- grad_bias_down: float32 [768], P(('dp', 'blk', 'head'))
- grad_gain_ffn: float32 [768], P(('dp', 'blk', 'head'))
- grad_shift_ffn: float32 [768], P(('dp', 'blk', 'head'))
The draws below stay inside these ranges and needn't reach their ends.
Inputs may be any that keep to these rules, and one draw needn't show every extreme that they name: `segment`: document ids of the tokens of each sequence; ids never fall along a sequence (each document is one contiguous run of tokens), and every id of 0 to 7 occurs in every sequence. Among the 1 sequence of each index of dp, one (drawn from the seed) holds a document that covers tokens of the first and of the last of its 4 token blocks.
All inputs are finite; a program needn't handle non-finite values.
Results may differ from the reference program's by a relative error of at most 0.023.
Values may be sent and summed in bfloat16 or wider, within the bound.
A program may use at most 192 MiB of HBM per device.

```python
import jax
import jax.numpy as jnp
from jax import lax

D = 768
HEADS = 12
HEAD_DIM = 64
FF = 3072
SEQS = 1
DOCS = 8
SEQ_LEN = 2048
SEQUENCES = 4
N_DP = 4
N_BLK = 4


def ids_from_lengths(lengths):
    bounds = jnp.cumsum(lengths)[:DOCS - 1].astype(jnp.int32)
    position = jnp.arange(SEQ_LEN, dtype=jnp.int32)
    return jnp.sum((position[:, None] >= bounds[None, :]).astype(jnp.int32), axis=1).astype(jnp.int32)


def ragged_ids(seq_key):
    doc_weights = jax.random.randint(seq_key, (DOCS,), 4, 12).astype(jnp.int32)
    spare = SEQ_LEN - DOCS
    lengths = 1 + doc_weights * spare // jnp.sum(doc_weights)
    lengths = lengths.at[DOCS - 1].add(SEQ_LEN - jnp.sum(lengths))
    return ids_from_lengths(lengths.astype(jnp.int32))


def spanning_ids(seq_key):
    block_len = SEQ_LEN // N_BLK
    doc_index = jnp.arange(DOCS, dtype=jnp.int32)
    middle = jax.random.randint(jax.random.fold_in(seq_key, 5), (), 0, DOCS).astype(jnp.int32)
    raw = jax.random.randint(jax.random.fold_in(seq_key, 3), (DOCS,), 1, 5).astype(jnp.int32)
    count_before = middle
    count_after = DOCS - 1 - middle
    slack_before = block_len - 1 - count_before
    slack_after = block_len - 1 - count_after
    len_before = 1 + (raw - 1) * slack_before // (3 * jnp.maximum(count_before, 1))
    len_after = 1 + (raw - 1) * slack_after // (3 * jnp.maximum(count_after, 1))
    shorts = jnp.where(doc_index < middle, len_before, jnp.where(doc_index > middle, len_after, 0))
    lengths = shorts + jnp.where(doc_index == middle, SEQ_LEN - jnp.sum(shorts), 0)
    return ids_from_lengths(lengths.astype(jnp.int32))


def draw_segment(key, part):
    base = jax.random.fold_in(key, 7)
    seq_keys = jax.random.split(base, SEQUENCES)
    ragged = jax.vmap(ragged_ids)(seq_keys)
    spanning = jax.vmap(spanning_ids)(seq_keys)
    picks = jax.random.randint(jax.random.fold_in(base, 11), (N_DP,), 0, SEQS).astype(jnp.int32)
    seq_index = jnp.arange(SEQUENCES, dtype=jnp.int32)
    chosen = seq_index % SEQS == jnp.repeat(picks, SEQS)
    return jnp.where(chosen[:, None], spanning, ragged).astype(jnp.int32)


def raised(array, rng, source, target, blocks, factor):
    def block_of(dim):
        return (jnp.arange(array.shape[dim]) // (array.shape[dim] // blocks)).reshape((-1,) + (1,) * (array.ndim - 1 - dim))

    one_side = jax.random.permutation(rng, blocks)[block_of(target)]
    far = (block_of(target) + blocks // 2) % blocks
    return jnp.where((block_of(source) == one_side) | (block_of(source) == far), factor * array, array)


def block_scale(key, extent, cuts, least, largest):
    loudness, own = 1.0, jax.random.fold_in(key, 6)
    for axis_at, shards_of in cuts:
        draws = jnp.exp(jax.random.uniform(jax.random.fold_in(own, axis_at), (shards_of,), jnp.float32, least / len(cuts), largest / len(cuts)))
        loudness = loudness * jnp.repeat(draws, extent[axis_at] // shards_of).reshape([-1 if axis == axis_at else 1 for axis in range(len(extent))])
    return loudness


def centred(own_key, shape, spread, reach, cuts=(), kind=jnp.bfloat16):
    level = block_scale(own_key, shape, cuts, -0.22, 0.18) if cuts else 1.0
    values = jax.random.normal(own_key, shape, jnp.float32) * spread * level
    return jnp.minimum(jnp.maximum(values, -reach), reach).astype(kind)


def bell_draw_with(key, dims, spread, limit, shards, heavy, kind=jnp.bfloat16):
    values = spread * jax.random.normal(key, dims, jnp.float32)
    if shards:
        values = values * block_scale(key, dims, shards, -0.22, 0.18)
    return jnp.clip(raised(values, jax.random.fold_in(key, 3), *heavy), -limit, limit).astype(kind)


def setup_inputs(seed: int = 0) -> dict:
    seeds = jax.random.split(jax.random.key(seed), 17)
    tokens = centred(seeds[0], (SEQUENCES, SEQ_LEN, D), 1.0, 6.0, ((0, 4), (1, 8)))
    segment = draw_segment(jax.random.fold_in(seeds[16], 71), 0)
    w_qkv = centred(seeds[2], (D, 3 * D), D ** -0.5, 0.21875, ((0, 32),))
    bias_query = centred(seeds[3], (D,), 0.5, 3.0, ((0, 32),))
    bias_value = centred(seeds[4], (D,), 0.5, 3.0, ((0, 32),))
    w_out = centred(seeds[5], (D, D), (D // 64) ** -0.5, 1.75, ((0, 32),))
    bias_out = centred(seeds[6], (D,), 0.5, 3.0, ((0, 32),))
    gain_attn = jnp.clip(1.0 + 0.18 * jax.random.normal(seeds[7], (D,), jnp.float32), 0.099609375, 1.8984375).astype(jnp.bfloat16)
    shift_attn = centred(seeds[8], (D,), 0.5, 3.0, ((0, 32),))
    w_in = centred(seeds[9], (D, FF), D ** -0.5, 0.21875, ((0, 32),))
    bias_in = centred(seeds[10], (FF,), 0.5, 3.0, ((0, 32),))
    w_down = centred(seeds[11], (FF, D), FF ** -0.5, 0.109375, ((0, 32),))
    bias_down = centred(seeds[12], (D,), 0.5, 3.0, ((0, 32),))
    gain_ffn = jnp.clip(1.0 + 0.18 * jax.random.normal(seeds[13], (D,), jnp.float32), 0.099609375, 1.8984375).astype(jnp.bfloat16)
    shift_ffn = centred(seeds[14], (D,), 0.5, 3.0, ((0, 32),))
    cotangent = bell_draw_with(seeds[15], (SEQUENCES, SEQ_LEN, D), 1.0, 6.0, ((0, 4), (1, 8)), (1, 2, 8, 2.0))
    return {"tokens": tokens, "segment": segment, "w_qkv": w_qkv, "bias_query": bias_query, "bias_value": bias_value, "w_out": w_out, "bias_out": bias_out, "gain_attn": gain_attn, "shift_attn": shift_attn, "w_in": w_in, "bias_in": bias_in, "w_down": w_down, "bias_down": bias_down, "gain_ffn": gain_ffn, "shift_ffn": shift_ffn, "cotangent": cotangent}


@jax.custom_vjp
def low(v):
    return lax.optimization_barrier(v.astype(jnp.bfloat16)).astype(jnp.float32)

@jax.custom_vjp
def low_back(v):
    return v

def low_keep(v):
    return (low(v), None)

def low_pass(kept, grad):
    return (grad,)

def back_keep(v):
    return (v, None)

def back_low(kept, grad):
    return (low(grad),)
low.defvjp(low_keep, low_pass)
low_back.defvjp(back_keep, back_low)
HIGHEST = lax.Precision.HIGHEST
NEG_FILL = -1e+30

def layer_norm(hidden, gain, shift):
    centered = hidden - lax.optimization_barrier(jnp.mean(hidden, axis=-1, keepdims=True))
    variance = lax.optimization_barrier(jnp.mean(centered * centered, axis=-1, keepdims=True))
    return centered * lax.rsqrt(variance + 1e-12) * gain + shift

def gelu_exact(values):
    return jax.nn.gelu(values, approximate=False)

def attend(queries, keys_all, values_all, query_seg, key_seg):
    scores = jnp.einsum('qhd,khd->hqk', queries, keys_all, precision=HIGHEST) * HEAD_DIM ** (-0.5)
    scores = low_back(scores)
    scores = jnp.where(query_seg[None, :, None] == key_seg[None, None, :], scores, NEG_FILL)
    probs = jax.nn.softmax(scores, axis=-1)
    return jnp.einsum('hqk,khd->qhd', low(probs), values_all, precision=HIGHEST)

def one_sequence(inputs, seg_row, params):
    w_qkv, bias_query, bias_value, w_out, bias_out, gain_attn, shift_attn, w_in, bias_in, w_down, bias_down, gain_ffn, shift_ffn = params
    qkv_bias = jnp.concatenate([bias_query, jnp.zeros_like(bias_query), bias_value])
    projected = low(low_back(jnp.dot(inputs, w_qkv, precision=HIGHEST) + qkv_bias))
    queries = projected[:, :D].reshape(SEQ_LEN, HEADS, HEAD_DIM)
    keys_all = projected[:, D:2 * D].reshape(SEQ_LEN, HEADS, HEAD_DIM)
    values_all = projected[:, 2 * D:].reshape(SEQ_LEN, HEADS, HEAD_DIM)
    block_rows = SEQ_LEN // N_BLK
    query_blocks = queries.reshape(N_BLK, block_rows, HEADS, HEAD_DIM)
    seg_blocks = seg_row.reshape(N_BLK, block_rows)
    attend_saved = jax.checkpoint(attend)
    context = lax.map(lambda block_pair: attend_saved(block_pair[0], keys_all, values_all, block_pair[1], seg_row), (query_blocks, seg_blocks))
    context = low(low_back(context.reshape(SEQ_LEN, D)))
    attn_out = low_back(jnp.dot(context, w_out, precision=HIGHEST) + bias_out)
    normed_one = layer_norm(inputs + attn_out, gain_attn, shift_attn)
    pre_act = low_back(jnp.dot(low(normed_one), w_in, precision=HIGHEST) + bias_in)
    activated = low(gelu_exact(pre_act))
    ffn_out = low_back(jnp.dot(activated, w_down, precision=HIGHEST) + bias_down)
    return layer_norm(normed_one + ffn_out, gain_ffn, shift_ffn)

def reference(tokens, segment, w_qkv, bias_query, bias_value, w_out, bias_out, gain_attn, shift_attn, w_in, bias_in, w_down, bias_down, gain_ffn, shift_ffn, cotangent):
    floats = [array_in.astype(jnp.float32) for array_in in (tokens, w_qkv, bias_query, bias_value, w_out, bias_out, gain_attn, shift_attn, w_in, bias_in, w_down, bias_down, gain_ffn, shift_ffn)]
    layer_saved = jax.checkpoint(one_sequence)

    def forward(inputs, *params):
        return lax.map(lambda seq_item: layer_saved(seq_item[0], seq_item[1], params), (inputs, segment))
    result, pull_back = jax.vjp(forward, *floats)
    gradients = pull_back(cotangent.astype(jnp.float32))
    return (result.astype(jnp.bfloat16), gradients[0], gradients[1], gradients[2], gradients[3], gradients[4], gradients[5], gradients[6], gradients[7], gradients[8], gradients[9], gradients[10], gradients[11], gradients[12], gradients[13])
```

```python
import functools

import jax
import jax.numpy as jnp
from jax import lax
from jax.experimental import pallas as pl
from jax.experimental.pallas import tpu as pltpu
from jax.sharding import PartitionSpec as P

MESH = pl.DeviceIdType.MESH
F32, BF16 = jnp.float32, jnp.bfloat16
HD = 64
HEADS = 12
BIG = 2.0**30

class Net:
    def __init__(self, nd, nb, nc):
        self.nd, self.nb, self.nc = nd, nb, nc
        self.levels = nd.bit_length() - 1
        self.d, self.b, self.c = (lax.axis_index(a) for a in ("dp", "blk", "head"))
        top = self.levels - 1
        self.stride = [(1 - self.c) * 2**k + self.c * 2 ** (top - k) for k in range(self.levels)]
        self.sibling = (self.d, self.b, self.nc - 1 - self.c)

    def flip(self, d, k):
        s = self.stride[k]
        return d + s * (1 - 2 * ((d // s) % 2))

    def flips(self, mask):
        d = self.d
        for k in range(self.levels):
            if (mask >> k) & 1:
                d = self.flip(d, k)
        return d

    def across(self, k):
        return (self.flip(self.d, k), self.b, self.c)

    def near(self, e):
        order = [sorted(range(self.nb), key=lambda j: (abs(j - i), -j)) for i in range(self.nb)]
        got = order[0][e]
        for i in range(1, self.nb):
            got = jnp.where(self.b == i, order[i][e], got)
        return got

    def slot(self, mask, blk):
        return (self.flips(mask) * self.nb + blk) * self.nc + self.c

    def peers(self):
        out = [(self.d, (self.b + u) % self.nb, self.c) for u in range(1, self.nb)]
        out += [self.across(k) for k in range(self.levels)]
        return out + [self.sibling]

    def barrier(self):
        bar = pltpu.get_barrier_semaphore()
        ps = self.peers()
        for p in ps:
            pl.semaphore_signal(bar, inc=1, device_id=p, device_id_type=MESH)
        pl.semaphore_wait(bar, len(ps))


def remote(src, dst, send, recv, dev):
    return pltpu.make_async_remote_copy(src_ref=src, dst_ref=dst, send_sem=send, recv_sem=recv, device_id=dev, device_id_type=MESH)


class Gather:
    def __init__(self, net, mine, full, sems, narrow=False):
        self.net, self.mine, self.full, self.narrow = net, mine, full, narrow
        self.zsend, self.xsend, self.ssend, self.srecv, self.recv = sems

    def at(self, mask, blk):
        n = self.net
        if self.narrow:
            return self.full.at[blk * n.nc + n.c]
        return self.full.at[n.slot(mask, blk)]

    def rsem(self, mask, blk):
        return self.recv.at[mask * self.net.nb + blk]

    def spread(self, mask, blk, src, dst):
        n = self.net
        if not self.narrow:
            for k in range(n.levels):
                if mask < (1 << k):
                    remote(src, dst, self.xsend, self.rsem(mask + (1 << k), blk), n.across(k)).start()
        remote(src, dst, self.ssend, self.srecv, n.sibling).start()

    def z(self, e):
        n = self.net
        blk = n.near(e)
        dst = self.at(0, blk)
        src = self.mine if e == 0 else dst
        sem = self.rsem(0, blk)
        if e:
            pltpu.make_async_copy(dst, dst, sem).wait()
        right = (n.d, n.b + 1, n.c)
        left = (n.d, n.b - 1, n.c)

        @pl.when((n.b < n.nb - 1) & (blk <= n.b))
        def _():
            remote(src, dst, self.zsend, sem, right).start()

        @pl.when((n.b > 0) & (blk >= n.b))
        def _():
            remote(src, dst, self.zsend, sem, left).start()

        self.spread(0, blk, src, dst)

    def x(self, mask, e):
        n = self.net
        blk = n.near(e)
        dst = self.at(mask, blk)
        pltpu.make_async_copy(dst, dst, self.rsem(mask, blk)).wait()
        self.spread(mask, blk, dst, dst)

    def own(self, sem):
        n = self.net
        return pltpu.make_async_copy(self.mine, self.at(0, n.b), sem)

    def wait_sibling(self):
        n = self.net
        half = self.full.at[pl.ds(0, n.nb if self.narrow else n.nd * n.nb)]
        pltpu.make_async_copy(half, half, self.srecv).wait()

    def drain(self):
        n = self.net
        half = self.full.at[pl.ds(0, n.nb if self.narrow else n.nd * n.nb)]
        pltpu.make_async_copy(half, half, self.ssend).wait()
        if not self.narrow:
            part = self.full.at[pl.ds(0, (n.nd - 1) * n.nb)]
            pltpu.make_async_copy(part, part, self.xsend).wait()
        edge = (n.b == 0) | (n.b == n.nb - 1)

        @pl.when(edge)
        def _():
            one = self.full.at[pl.ds(0, 1)]
            pltpu.make_async_copy(one, one, self.zsend).wait()

        @pl.when(jnp.logical_not(edge))
        def _():
            many = self.full.at[pl.ds(0, n.nb + 1)]
            pltpu.make_async_copy(many, many, self.zsend).wait()


def gather_sems(n_pieces, nd, nb):
    return [pltpu.SemaphoreType.DMA((n_pieces, 4)), pltpu.SemaphoreType.DMA((n_pieces, nd * nb)), pltpu.SemaphoreType.DMA]


class Scatter:
    def __init__(self, net, full, sib, xrecv, zrecv, out, sems, narrow=False, joined=False):
        self.net, self.full, self.sib, self.xbuf, self.zbuf, self.out = net, full, sib, xrecv, zrecv, out
        self.sib_send, self.x_send, self.z_send, self.sib_sem, self.x_sem, self.z_sem = sems
        self.narrow, self.joined = narrow, joined
        self.nd = 1 if narrow else net.nd
        self.levels = 0 if narrow else net.levels

    def home(self, mask):
        return 0 if self.narrow else self.net.flips(mask)

    def start(self):
        n = self.net
        for mask in range(self.nd - 1, -1, -1):
            mirrored = sum(1 << (self.levels - 1 - k) for k in range(self.levels) if (mask >> k) & 1)
            d = self.home(mirrored)
            rows = pl.ds(d * n.nb, n.nb)
            if self.joined:
                remote(self.sib.at[rows], self.full.at[rows, n.c], self.sib_send, self.sib_sem.at[mask], n.sibling).start()
            else:
                for blk in range(n.nb):
                    at = d * n.nb + blk
                    remote(
                        self.full.at[at * n.nc + n.nc - 1 - n.c], self.sib.at[at], self.sib_send, self.sib_sem.at[mask], n.sibling
                    ).start()

    def wait_sibling(self, mask):
        n = self.net
        some = self.sib.at[pl.ds(0, n.nb)]
        pltpu.make_async_copy(some, some, self.sib_sem.at[mask]).wait()

    def x_at(self, k, mask, blk):
        return ((1 << k) - 1 + mask) * self.net.nb + blk

    def reduce(self, mask, e):
        n = self.net
        if e == n.nb - 1:
            self.wait_sibling(mask)
        blk = n.near(e)
        at = self.home(mask) * n.nb + blk
        place = self.full.at[at] if self.joined else self.full.at[at * n.nc + n.c]
        terms = [place] if self.joined else [place, self.sib.at[at]]
        for k in range(self.levels - 1, -1, -1):
            if mask < (1 << k):
                i = self.x_at(k, mask, blk)
                got = self.xbuf.at[i]
                pltpu.make_async_copy(got, got, self.x_sem.at[i]).wait()
                terms.append(got)
        if mask:
            k = mask.bit_length() - 1
            add_up(terms, place)
            i = self.x_at(k, mask - (1 << k), blk)
            remote(place, self.xbuf.at[i], self.x_send, self.x_sem.at[i], n.across(k)).start()
            return

        def arrived(side, there):
            i = self.z_at(side, blk, n.b)
            got = self.zbuf.at[i]

            @pl.when(there)
            def _():
                pltpu.make_async_copy(got, got, self.z_sem.at[i]).wait()

            terms.append(got)

        if e == 0:
            arrived(0, n.b > 0)
            arrived(1, n.b < n.nb - 1)
            add_up(terms, self.out)
            return
        side = jnp.where(blk > n.b, 0, 1)
        arrived(side, jnp.where(blk > n.b, n.b, n.nb - 1 - n.b) > 0)
        add_up(terms, place)
        to = n.b + 1 - 2 * side
        i = self.z_at(side, blk, to)
        remote(place, self.zbuf.at[i], self.z_send, self.z_sem.at[i], (n.d, to, n.c)).start()

    def z_at(self, side, blk, owner):
        return blk + side * jnp.where(blk == owner, self.net.nb - blk, 0)

    def clear_edges(self):
        n = self.net

        def clear(i, carry):
            self.zbuf[i] = jnp.zeros(self.zbuf.shape[1:], self.zbuf.dtype)
            return carry

        @pl.when(n.b == 0)
        def _():
            lax.fori_loop(0, n.nb, clear, 0)

        @pl.when(n.b == n.nb - 1)
        def _():
            lax.fori_loop(0, n.nb - 1, clear, 0)
            clear(n.nb, 0)

    def drain(self):
        n = self.net
        some = self.sib.at[pl.ds(0, self.nd * n.nb)]
        pltpu.make_async_copy(some, some, self.sib_send).wait()
        if not self.narrow:
            some = self.xbuf.at[pl.ds(0, (n.nd - 1) * n.nb)]
            pltpu.make_async_copy(some, some, self.x_send).wait()
        some = self.zbuf.at[pl.ds(0, n.nb - 1)]
        pltpu.make_async_copy(some, some, self.z_send).wait()


def add_up(terms, to):
    shape = to.shape
    rows = shape[-2]
    step = rows
    while step % 2 == 0 and step > 32:
        step //= 2
    lead = [()] if len(shape) == 2 else [(g,) for g in range(shape[0])]
    for g in lead:
        for r in range(0, rows, step):
            at = g + (slice(r, r + step),)
            total = terms[0][at].astype(F32)
            for t in terms[1:]:
                total = total + t[at].astype(F32)
            to[at] = total.astype(to.dtype)


class AllSum:
    def __init__(self, net, value, got, send, recv):
        self.net, self.value, self.got, self.send, self.recv = net, value, got, send, recv

    def copy(self, stage, dev, src, slot):
        return remote(self.value.at[src], self.got.at[slot], self.send.at[slot], self.recv.at[slot], dev)

    def stages(self):
        n = self.net
        devs = [n.sibling] + [n.across(k) for k in range(n.levels)]
        steps = []
        for i, dev in enumerate(devs):
            steps.append(functools.partial(self.one, i, dev))
        steps.append(self.line_start)
        steps.append(self.line_end)
        return [lambda: self.copy(0, devs[0], 0, 0).start()] + steps

    def one(self, i, dev):
        n = self.net
        self.copy(i, dev, i, i).wait()
        self.value[i + 1] = self.value[i] + self.got[i]
        if i + 1 <= n.levels:
            self.copy(i + 1, n.across(i), i + 1, i + 1).start()

    def line_copy(self, u):
        n = self.net
        return self.copy(None, (n.d, (n.b + u) % n.nb, n.c), n.levels + 1, n.levels + u)

    def line_start(self):
        for u in range(1, self.net.nb):
            self.line_copy(u).start()

    def line_end(self):
        n = self.net
        for u in range(1, n.nb):
            self.line_copy(u).wait()
        total = self.value[n.levels + 1]
        for u in range(1, n.nb):
            total = total + self.got[n.levels + u]
        self.value[0] = total


def scatter_sems(n_pieces, nd, nb):
    return [
        pltpu.SemaphoreType.DMA((n_pieces, 3)),
        pltpu.SemaphoreType.DMA((n_pieces, nd)),
        pltpu.SemaphoreType.DMA((n_pieces, (nd - 1) * nb)),
        pltpu.SemaphoreType.DMA((n_pieces, nb + 1)),
    ]


def dot(a, b, dims=((1,), (0,))):
    return lax.dot_general(a, b, (dims, ((), ())), preferred_element_type=F32)


def mask_lanes(seg_row, count):
    lanes = lax.broadcasted_iota(jnp.int32, (128, count), 0)
    return jnp.transpose(jnp.where(lanes == seg_row, -1.0, 0.0).astype(F32), (1, 0))


def project(tok, w, bias, seg, qaug, kaug, v_scr, q_scr, blk, c, qlen, width):
    total = tok.shape[0]
    pairs = width // 128
    step = min(512, total)
    d_model = tok.shape[1]

    def cols(part):
        return w[:, pl.ds(pl.multiple_of((part * 2 + c) * width, 128), width)]

    wk, wv = cols(1), cols(2)
    bias_v = bias[1:2, :]

    def rows(i, carry):
        at = pl.ds(pl.multiple_of(i * step, step), step)
        piece = tok[at, :]
        keys = dot(piece, wk).astype(BF16)
        vals = (dot(piece, wv) + bias_v).astype(BF16)
        seg_row = seg[:, at]
        lanes = mask_lanes(seg_row, step).astype(BF16)
        for p in range(pairs):
            kaug[p, at, 0:128] = keys[:, p * 128:(p + 1) * 128]
            kaug[p, at, 128:256] = lanes
            v_scr[p, at, :] = vals[:, p * 128:(p + 1) * 128]
        return carry

    lax.fori_loop(0, total // step, rows, 0)
    mine = pl.ds(pl.multiple_of(blk * qlen, qlen), qlen)
    query = (dot(tok[mine, :], cols(0)) + bias[0:1, :]).astype(BF16)
    q_scr[...] = query
    seg_q = seg[:, mine]
    lane = lax.broadcasted_iota(jnp.int32, (qlen, 128), 1)
    feat = jnp.where(lane < 8, BIG * (1.0 + mask_lanes(seg_q, qlen)), 0.0).astype(BF16)
    for p in range(pairs):
        q_pair = query[:, p * 128:(p + 1) * 128].astype(F32) * HD**-0.5
        for half in range(2):
            keep = (lane >= 64) if half else (lane < 64)
            qaug[2 * p + half, :, 0:128] = jnp.where(keep, q_pair, 0.0).astype(BF16)
            qaug[2 * p + half, :, 128:256] = feat


def attend_chunk(i, qaug, kaug, v_scr, o_scr, lse_scr, chunk, per_head):
    h = i // per_head
    at = pl.ds(pl.multiple_of((i % per_head) * chunk, chunk), chunk)
    s = dot(qaug[h, at, :], kaug[h // 2], ((1,), (1,)))
    top = jnp.max(s, axis=-1, keepdims=True)
    p = jnp.exp(s - top)
    total = jnp.sum(p, axis=-1, keepdims=True)
    o = dot(p.astype(BF16), v_scr[h // 2])
    o_scr[h, at, :] = o / total
    lse_scr[h, at, :] = jnp.broadcast_to(top + jnp.log(total), (chunk, 128))


def join_heads(o_scr, p):
    lane = lax.broadcasted_iota(jnp.int32, o_scr.shape[1:], 1)
    return jnp.where(lane < 64, o_scr[2 * p], o_scr[2 * p + 1])


def fwd_kernel(tok, w, bias, seg, ctx, q_out, kaug, v_scr, qaug, lse_scr, o_scr, chunk=256):
    blk, c = lax.axis_index("blk"), lax.axis_index("head")
    qlen, width = ctx.shape
    project(tok, w, bias, seg, qaug, kaug, v_scr, q_out, blk, c, qlen, width)
    per_head = qlen // chunk

    def step(i, carry):
        attend_chunk(i, qaug, kaug, v_scr, o_scr, lse_scr, chunk, per_head)
        return carry

    lax.fori_loop(0, (width // HD) * per_head, step, 0)
    for p in range(width // 128):
        ctx[:, p * 128:(p + 1) * 128] = join_heads(o_scr, p).astype(BF16)


def split3(x):
    hi = x.astype(BF16)
    mid = (x - hi.astype(F32)).astype(BF16)
    low = (x - hi.astype(F32) - mid.astype(F32)).astype(BF16)
    return hi, mid, low


def bwd_head(h, pair, qaug, kaug, v_scr, do_m, lse_row, p_scr, dp_scr, dk_scr, dv_scr, dq_scr, kc, qc, nq):
    total = kaug.shape[1]
    for j in range(nq):
        at = pl.ds(j * qc, qc)
        lse = lse_row[h, 0:1, at]
        q_part = qaug[h, at, :]
        do_part = do_m[h, at, :]

        def first(i, delta):
            rows = pl.ds(pl.multiple_of(i * kc, kc), kc)
            s = dot(kaug[pair, rows, :], q_part, ((1,), (1,)))
            p = jnp.exp(s - lse)
            dp = dot(v_scr[pair, rows, :], do_part, ((1,), (1,)))
            p_scr[rows, :] = p
            dp_scr[rows, :] = dp
            dv = dot(p.astype(BF16), do_part)
            if j:
                dv = dv + dv_scr[h, rows, :].astype(F32)
            dv_scr[h, rows, :] = dv.astype(dv_scr.dtype)
            return delta + jnp.sum((p * dp).reshape(kc // 8, 8, qc), axis=0)

        delta = lax.fori_loop(0, total // kc, first, jnp.zeros((8, qc), F32))
        delta = jnp.sum(delta, axis=0, keepdims=True)
        q_low = q_part[:, 0:128]

        def second(i, dq):
            rows = pl.ds(pl.multiple_of(i * kc, kc), kc)
            ds = (p_scr[rows, :] * (dp_scr[rows, :] - delta)).astype(BF16)
            dk = dot(ds, q_low)
            if j:
                dk = dk + dk_scr[h, rows, :].astype(F32)
            dk_scr[h, rows, :] = dk.astype(dk_scr.dtype)
            return dq + dot(kaug[pair, rows, 0:128], ds, ((0,), (0,)))

        dq = lax.fori_loop(0, total // kc, second, jnp.zeros((128, qc), F32))
        dq_scr[h, at, :] = jnp.transpose(dq, (1, 0))


VMEM = pl.BlockSpec(memory_space=pltpu.VMEM)
HBM = pl.BlockSpec(memory_space=pl.ANY)


def params(limit, collective=None):
    more = {} if collective is None else dict(collective_id=collective, has_side_effects=True)
    return pltpu.CompilerParams(vmem_limit_bytes=limit << 20, **more)


def gather_order(keys, narrow, nd, nb):
    events = []
    for p, (begin, dz, dx) in enumerate(keys):
        for e in range(nb):
            events.append((begin + e * dz, ("z", p, e)))
            if not narrow[p]:
                for mask in range(1, nd):
                    events.append((begin + e * dz + dx * mask.bit_length(), ("x", p, mask, e)))
    events.sort(key=lambda q: q[0])
    return [ev for _, ev in events]


def gather_all(shards, narrow, keys, nd, nb, nc):
    count = len(shards)

    def kernel(*refs):
        mine, full = refs[:count], refs[count:2 * count]
        four, recv, own_sem = refs[2 * count:]
        net = Net(nd, nb, nc)
        pieces = [
            Gather(net, mine[p], full[p], [four.at[p, i] for i in range(4)] + [recv.at[p]], narrow[p]) for p in range(count)
        ]
        net.barrier()
        for ev in gather_order(keys, narrow, nd, nb):
            if ev[0] == "z":
                pieces[ev[1]].z(ev[2])
            else:
                pieces[ev[1]].x(ev[2], ev[3])
        for piece in pieces:
            own = piece.own(own_sem)
            own.start()
            own.wait()
        for piece in pieces:
            piece.wait_sibling()
        for piece in pieces:
            piece.drain()

    outs = [
        jax.ShapeDtypeStruct(((nb * nc if thin else nd * nb * nc),) + s.shape, s.dtype) for s, thin in zip(shards, narrow)
    ]
    return pl.pallas_call(
        kernel,
        out_shape=outs,
        in_specs=[VMEM] * count,
        out_specs=[HBM] * count,
        scratch_shapes=gather_sems(count, nd, nb),
        compiler_params=params(56, 0),
    )(*shards)


def attend_forward(tok, w, bias, seg, qlen, width):
    total = tok.shape[0]
    heads = width // HD
    chunk = min(256, qlen)
    return pl.pallas_call(
        functools.partial(fwd_kernel, chunk=chunk),
        out_shape=[
            jax.ShapeDtypeStruct((qlen, width), BF16),
            jax.ShapeDtypeStruct((qlen, width), BF16),
            jax.ShapeDtypeStruct((width // 128, total, 256), BF16),
            jax.ShapeDtypeStruct((width // 128, total, 128), BF16),
            jax.ShapeDtypeStruct((heads, qlen, 256), BF16),
            jax.ShapeDtypeStruct((heads, qlen, 128), F32),
        ],
        in_specs=[VMEM] * 4,
        out_specs=[VMEM] * 6,
        scratch_shapes=[pltpu.VMEM((heads, qlen, 128), F32)],
        compiler_params=params(56),
    )(tok, w, bias, seg)


def pair_bwd_kernel(qaug, kaug, v_scr, lse_b, gctx, dk, dv, dq, p_scr, dp_scr, do_m, lse_row, dk_scr, dv_scr, dq_scr, kc, qc):
    qlen = qaug.shape[1]
    lane = lax.broadcasted_iota(jnp.int32, (qlen, 128), 1)
    for h in range(2):
        keep = (lane >= 64) if h else (lane < 64)
        piece = gctx[...]
        do_m[h] = jnp.where(keep, piece, jnp.zeros_like(piece))
        lse_row[h] = jnp.transpose(lse_b[h], (1, 0))[0:8, :]

    def head(h, carry):
        bwd_head(h, 0, qaug, kaug, v_scr, do_m, lse_row, p_scr, dp_scr, dk_scr, dv_scr, dq_scr, kc, qc, qlen // qc)
        return carry

    lax.fori_loop(0, 2, head, 0)
    dk[...] = pair_of(dk_scr).astype(BF16)
    dv[...] = pair_of(dv_scr).astype(BF16)
    dq[...] = (pair_of(dq_scr) * HD**-0.5).astype(BF16)


def pair_of(scr):
    first, second = scr[0], scr[1]
    lane = lax.broadcasted_iota(jnp.int32, first.shape, 1)
    return jnp.where(lane < 64, first, second)


def finish_kernel(tok, dk, dv, tok_mine, dq, w, dtok, dw, dbias, own):
    i, c = pl.program_id(0), lax.axis_index("head")
    blk = lax.axis_index("blk")
    step, width = dk.shape
    qlen = dq.shape[0]

    def cols(part):
        return w[:, pl.ds(pl.multiple_of((part * 2 + c) * width, 128), width)]

    piece, grad_k, grad_v = tok[...], dk[...], dv[...]

    @pl.when(i == 0)
    def _():
        dw[:, 0:width] = dot(tok_mine[...], dq[...], ((0,), (0,)))
        dw[:, width:3 * width] = jnp.zeros((dw.shape[0], 2 * width), F32)
        dbias[0:1, :] = jnp.sum(dq[...].astype(F32), axis=0, keepdims=True)
        dbias[1:2, :] = jnp.zeros((1, width), F32)
        own[...] = dot(dq[...], cols(0), ((1,), (1,)))

    dw[:, width:2 * width] += dot(piece, grad_k, ((0,), (0,)))
    dw[:, 2 * width:3 * width] += dot(piece, grad_v, ((0,), (0,)))
    dbias[1:2, :] += jnp.sum(grad_v.astype(F32), axis=0, keepdims=True)
    grad = dot(grad_k, cols(1), ((1,), (1,))) + dot(grad_v, cols(2), ((1,), (1,)))
    per = qlen // step
    mine = i // per == blk
    at = pl.ds(pl.multiple_of((i % per) * step, step), step)
    dtok[...] = (grad + jnp.where(mine, own[at, :], 0.0)).astype(BF16)


def attend_backward(tok, tok_mine, w, qaug, kaug, v_scr, lse_b, gctx):
    heads, qlen, _ = qaug.shape
    total, d_model = tok.shape
    width = heads * HD
    qc = qlen
    while total * qc > 2048 * 512:
        qc //= 2
    kc = min(512, total)
    pair3 = lambda p: (p, 0, 0)
    lanes = lambda p: (0, p)
    dk, dv, dq = pl.pallas_call(
        functools.partial(pair_bwd_kernel, kc=kc, qc=qc),
        grid=(heads // 2,),
        out_shape=[
            jax.ShapeDtypeStruct((total, width), BF16),
            jax.ShapeDtypeStruct((total, width), BF16),
            jax.ShapeDtypeStruct((qlen, width), BF16),
        ],
        in_specs=[
            pl.BlockSpec((2, qlen, 256), pair3),
            pl.BlockSpec((1, total, 256), pair3),
            pl.BlockSpec((1, total, 128), pair3),
            pl.BlockSpec((2, qlen, 128), pair3),
            pl.BlockSpec((qlen, 128), lanes),
        ],
        out_specs=[pl.BlockSpec((total, 128), lanes)] * 2 + [pl.BlockSpec((qlen, 128), lanes)],
        scratch_shapes=[
            pltpu.VMEM((total, qc), F32),
            pltpu.VMEM((total, qc), F32),
            pltpu.VMEM((2, qlen, 128), BF16),
            pltpu.VMEM((2, 8, qlen), F32),
            pltpu.VMEM((2, total, 128), BF16),
            pltpu.VMEM((2, total, 128), BF16),
            pltpu.VMEM((2, qlen, 128), F32),
        ],
        compiler_params=params(56),
    )(qaug, kaug, v_scr, lse_b, gctx)
    step = min(512, qlen)
    whole = lambda i: (0, 0)
    rows = lambda i: (i, 0)
    return pl.pallas_call(
        finish_kernel,
        grid=(total // step,),
        out_shape=[
            jax.ShapeDtypeStruct((total, d_model), BF16),
            jax.ShapeDtypeStruct((d_model, 3 * width), F32),
            jax.ShapeDtypeStruct((2, width), F32),
        ],
        in_specs=[
            pl.BlockSpec((step, d_model), rows),
            pl.BlockSpec((step, width), rows),
            pl.BlockSpec((step, width), rows),
            pl.BlockSpec((qlen, d_model), whole),
            pl.BlockSpec((qlen, width), whole),
            pl.BlockSpec((d_model, w.shape[1]), whole),
        ],
        out_specs=[
            pl.BlockSpec((step, d_model), rows),
            pl.BlockSpec((d_model, 3 * width), whole),
            pl.BlockSpec((2, width), whole),
        ],
        scratch_shapes=[pltpu.VMEM((qlen, d_model), F32)],
        compiler_params=params(56),
    )(tok, dk, dv, tok_mine, dq, w)


def scatter_all(arrays, narrow, joined, small, nd, nb, nc):
    count = len(arrays)
    flat = []
    for a, j in zip(arrays, joined):
        flat += list(a) if j else [a]
    n_in = len(flat) + 1

    def kernel(*refs):
        ins, small_in = list(refs[:n_in - 1]), refs[n_in - 1]
        outs, small_out = refs[n_in:n_in + count], refs[n_in + count]
        rest = list(refs[n_in + count + 1:])
        net = Net(nd, nb, nc)
        s3, sib_sem, x_sem, z_sem, sum_send, sum_recv = rest[-6:]
        value, got = rest[-8:-6]
        bufs = rest[:-8]
        pieces = []
        for p in range(count):
            first = ins.pop(0)
            sib = ins.pop(0) if joined[p] else bufs.pop(0)
            xbuf = None if narrow[p] else bufs.pop(0)
            zbuf = bufs.pop(0)
            sems = [s3.at[p, i] for i in range(3)] + [sib_sem.at[p], x_sem.at[p], z_sem.at[p]]
            pieces.append(Scatter(net, first, sib, xbuf, zbuf, outs[p], sems, narrow[p], joined[p]))
        sums = AllSum(net, value, got, sum_send, sum_recv)
        for piece in pieces:
            piece.clear_edges()
        value[0] = small_in[...]
        net.barrier()
        events = [(0.0, s) for s in [pieces[0].start]]
        for p, piece in enumerate(pieces):
            t = 0.5 * p
            events.append((t - 0.4, piece.start) if p else (t - 1, lambda: None))
            for mask in range(piece.nd - 1, -1, -1):
                for e in range(nb - 1, -1, -1):
                    when = t + (piece.levels - mask.bit_length()) + 0.01 * (nb - 1 - e)
                    events.append((when, functools.partial(piece.reduce, mask, e)))
        for i, s in enumerate(sums.stages()):
            events.append((0.3 * i, s))
        events.sort(key=lambda q: q[0])
        for _, ev in events:
            ev()
        small_out[...] = value[0]
        for piece in pieces:
            piece.drain()

    outs, scratch = [], []
    for a, thin, j in zip(arrays, narrow, joined):
        full = a[0] if j else a
        block = full.shape[1:]
        outs.append(jax.ShapeDtypeStruct(block, F32))
        n_dp = 1 if thin else nd
        if not j:
            scratch.append(pltpu.VMEM((n_dp * nb,) + block, BF16))
        if not thin:
            scratch.append(pltpu.VMEM(((nd - 1) * nb,) + block, BF16))
        scratch.append(pltpu.VMEM((nb + 1,) + block, BF16))
    levels = nd.bit_length() - 1
    scratch += [pltpu.VMEM((levels + 2,) + small.shape, F32), pltpu.VMEM((levels + nb,) + small.shape, F32)]
    scratch += scatter_sems(count, nd, nb)
    scratch += [pltpu.SemaphoreType.DMA((levels + nb,))] * 2
    outs.append(jax.ShapeDtypeStruct(small.shape, F32))
    return pl.pallas_call(
        kernel,
        out_shape=outs,
        in_specs=[VMEM] * n_in,
        out_specs=[VMEM] * (count + 1),
        scratch_shapes=scratch,
        compiler_params=params(60, 1),
    )(*flat, small)


def layer_norm(hidden, gain, shift):
    centered = hidden - jnp.mean(hidden, axis=-1, keepdims=True)
    variance = jnp.mean(centered * centered, axis=-1, keepdims=True)
    return centered * lax.rsqrt(variance + 1e-12) * gain + shift


def gelu_exact(values):
    return jax.nn.gelu(values, approximate=False)


def matmul(left, right):
    return jnp.dot(left, right, preferred_element_type=F32)


def matmul_left_t(left, right):
    return dot(left, right, ((0,), (0,)))


def matmul_right_t(left, right):
    return dot(left, right, ((1,), (1,)))


def body(
    tokens,
    segment,
    w_qkv,
    bias_query,
    bias_value,
    w_out,
    bias_out,
    gain_attn,
    shift_attn,
    w_in,
    bias_in,
    w_down,
    bias_down,
    gain_ffn,
    shift_ffn,
    cotangent,
):
    nd, nb, nc = lax.axis_size("dp"), lax.axis_size("blk"), lax.axis_size("head")
    n_dev = nd * nb * nc
    d_idx, b_idx, c_idx = lax.axis_index("dp"), lax.axis_index("blk"), lax.axis_index("head")
    me = (d_idx * nb + b_idx) * nc + c_idx
    seqs, rows, width = tokens.shape
    ff = w_in.shape[1]
    half_w = width // nc
    qlen = nc * rows
    r = w_qkv.shape[0]
    r_ff = w_down.shape[0]
    vectors = [bias_query, bias_value, bias_out, gain_attn, shift_attn, bias_down, gain_ffn, shift_ffn]
    packed = jnp.concatenate(vectors + [bias_in])
    used = packed.shape[0]
    lanes = -(-used // 128) * 128
    packed = jnp.broadcast_to(jnp.pad(packed, (0, lanes - used))[None], (8, lanes))
    flat_in = tokens.reshape(rows, width)
    n4 = 4
    parts = [flat_in[i * (rows // n4):(i + 1) * (rows // n4)] for i in range(n4)]
    shards = [packed, w_qkv] + parts + [w_out, w_in, w_down]
    narrow = [False, False] + [True] * n4 + [False] * 3
    keys = [(-1, 3, 3), (0, 3, 3), (7, 9, 0), (10, 9, 0), (13, 9, 0), (16, 9, 0), (2, 4, 4), (9, 6, 5), (22, 6, 5)]
    small, g_qkv, t0, t1, t2, t3, g_out, g_in, g_down = gather_all(shards, narrow, keys, nd, nb, nc)
    full_small = small[:, 0, :used]
    vecs = full_small[:, :8 * r].reshape(n_dev, 8, r).transpose(1, 0, 2).reshape(8, width).astype(F32)
    full_bin = full_small[:, 8 * r:].reshape(ff).astype(F32)
    bq, bv, bout, gain_one, shift_one, bdown, gain_two, shift_two = (vecs[i] for i in range(8))
    full_qkv = g_qkv.reshape(width, 3 * width)
    full_wout = g_out.reshape(width, width)
    full_win = g_in.reshape(width, ff)
    full_wdown = g_down.reshape(ff, width)
    tok_all = jnp.stack([t0, t1, t2, t3], axis=1).reshape(nb * qlen, width)
    my_bias = lax.dynamic_slice(vecs, (0, c_idx * half_w), (2, half_w))
    ctx, _, kaug, v_scr, qaug, lse_b = attend_forward(tok_all, full_qkv, my_bias, segment, qlen, half_w)
    context_low = ctx.reshape(seqs, qlen, 1, half_w)
    back_tokens = lax.all_to_all(context_low, "head", split_axis=1, concat_axis=2, tiled=True)
    context_flat = back_tokens.reshape(rows, width)
    attn_out = matmul(context_flat, full_wout) + bout
    resid_one = flat_in.astype(F32) + attn_out
    normed_one, norm_one_pull = jax.vjp(layer_norm, resid_one, gain_one, shift_one)
    normed_low = normed_one.astype(BF16)
    pre_act = matmul(normed_low, full_win) + full_bin
    activated, gelu_pull = jax.vjp(gelu_exact, pre_act)
    act_low = activated.astype(BF16)
    ffn_out = matmul(act_low, full_wdown) + bdown
    resid_two = normed_one + ffn_out
    result, norm_two_pull = jax.vjp(layer_norm, resid_two, gain_two, shift_two)
    output = result.astype(BF16).reshape(seqs, rows, width)
    grad_result = cotangent.reshape(rows, width).astype(F32)
    grad_resid_two, grad_gain_two, grad_shift_two = norm_two_pull(grad_result)
    grad_ffn = grad_resid_two.astype(BF16)
    grad_bias_down = jnp.sum(grad_ffn.astype(F32), axis=0)
    grad_w_down = matmul_left_t(act_low, grad_ffn)
    grad_act = matmul_right_t(grad_ffn, full_wdown)
    (grad_pre,) = gelu_pull(grad_act)
    grad_pre_low = grad_pre.astype(BF16)
    grad_bias_in = jnp.sum(grad_pre_low.astype(F32), axis=0)
    grad_w_in = matmul_left_t(normed_low, grad_pre_low)
    grad_normed = grad_resid_two + matmul_right_t(grad_pre_low, full_win)
    grad_resid_one, grad_gain_one, grad_shift_one = norm_one_pull(grad_normed)
    grad_attn = grad_resid_one.astype(BF16)
    grad_bias_out = jnp.sum(grad_attn.astype(F32), axis=0)
    grad_w_out = matmul_left_t(context_flat, grad_attn)
    grad_context = matmul_right_t(grad_attn, full_wout).astype(BF16)
    grad_headed = lax.all_to_all(
        grad_context.reshape(seqs, rows, nc, half_w), "head", split_axis=2, concat_axis=1, tiled=True
    )
    gctx = grad_headed.reshape(qlen, half_w)
    tok_mine = lax.dynamic_slice(tok_all, (b_idx * qlen, 0), (qlen, width))
    dtok, dw, dbias = attend_backward(tok_all, tok_mine, full_qkv, qaug, kaug, v_scr, lse_b, gctx)
    dw = dw.astype(BF16).reshape(nd * nb, nc, r, 3 * half_w)
    ours = lax.dynamic_index_in_dim(dw, c_idx, 1, keepdims=False)
    theirs = lax.dynamic_index_in_dim(dw, 1 - c_idx, 1, keepdims=False)
    joined_full = jnp.stack([ours, ours], axis=1)
    my_rows = lax.dynamic_update_slice(jnp.zeros((2, width), F32), dbias, (0, c_idx * half_w))
    sums = jnp.concatenate(
        [
            my_rows,
            jnp.stack([grad_bias_out, grad_gain_one, grad_shift_one, grad_bias_down, grad_gain_two, grad_shift_two]),
            grad_bias_in.reshape(ff // width, width),
        ]
    )
    sums = jnp.pad(sums, ((0, -sums.shape[0] % 8), (0, 0)))
    o_down, o_in, o_out, o_tok, o_qkv, total = scatter_all(
        [
            grad_w_down.astype(BF16).reshape(n_dev, r_ff, width),
            grad_w_in.astype(BF16).reshape(n_dev, r, ff),
            grad_w_out.astype(BF16).reshape(n_dev, r, width),
            dtok.reshape(nb * nc, rows, width),
            (joined_full, theirs),
        ],
        [False, False, False, True, False],
        [False, False, False, False, True],
        sums,
        nd,
        nb,
        nc,
    )
    grad_tokens = (grad_resid_one + o_tok).reshape(seqs, rows, width)
    o_qkv = o_qkv.reshape(2, r, 3, half_w).transpose(1, 2, 0, 3).reshape(r, 3 * width)
    mine = lax.dynamic_slice(total, (0, me * r), (8, r))
    mine_in = lax.dynamic_slice(total[8:8 + ff // width].reshape(ff), (me * r_ff,), (r_ff,))
    g_bq, g_bv, g_bo, g_g1, g_s1, g_bd, g_g2, g_s2 = (mine[i] for i in range(8))
    return (
        output,
        grad_tokens,
        o_qkv,
        g_bq,
        g_bv,
        o_out,
        g_bo,
        g_g1,
        g_s1,
        o_in,
        mine_in,
        o_down,
        g_bd,
        g_g2,
        g_s2,
    )


def solution(mesh):
    weight, vector = P(("dp", "blk", "head"), None), P(("dp", "blk", "head"))
    token = P("dp", ("blk", "head"), None)
    return jax.shard_map(
        body,
        mesh=mesh,
        in_specs=(
            token,
            P("dp", None),
            weight,
            vector,
            vector,
            weight,
            vector,
            vector,
            vector,
            weight,
            vector,
            weight,
            vector,
            vector,
            vector,
            token,
        ),
        out_specs=(
            token,
            token,
            weight,
            vector,
            vector,
            weight,
            vector,
            vector,
            vector,
            weight,
            vector,
            weight,
            vector,
            vector,
            vector,
        ),
        check_vma=False,
    )
```

```python
import functools

import jax
import jax.numpy as jnp
from jax import lax
from jax.experimental import pallas as pl
from jax.experimental.pallas import tpu as pltpu
from jax.sharding import PartitionSpec as P

MESH = pl.DeviceIdType.MESH
F32, BF16 = jnp.float32, jnp.bfloat16
HD = 64
HEADS = 12
BIG = 2.0**30

class Net:
    def __init__(self, nd, nb, nc):
        self.nd, self.nb, self.nc = nd, nb, nc
        self.levels = nd.bit_length() - 1
        self.d, self.b, self.c = (lax.axis_index(a) for a in ("dp", "blk", "head"))
        top = self.levels - 1
        self.stride = [(1 - self.c) * 2**k + self.c * 2 ** (top - k) for k in range(self.levels)]
        self.sibling = (self.d, self.b, self.nc - 1 - self.c)

    def flip(self, d, k):
        s = self.stride[k]
        return d + s * (1 - 2 * ((d // s) % 2))

    def flips(self, mask):
        d = self.d
        for k in range(self.levels):
            if (mask >> k) & 1:
                d = self.flip(d, k)
        return d

    def across(self, k):
        return (self.flip(self.d, k), self.b, self.c)

    def near(self, e):
        order = [sorted(range(self.nb), key=lambda j: (abs(j - i), -j)) for i in range(self.nb)]
        got = order[0][e]
        for i in range(1, self.nb):
            got = jnp.where(self.b == i, order[i][e], got)
        return got

    def near_at(self, e):
        got = self.near(0)
        for i in range(1, self.nb):
            got = jnp.where(e == i, self.near(i), got)
        return got

    def slot(self, mask, blk):
        return (self.flips(mask) * self.nb + blk) * self.nc + self.c

    def peers(self):
        out = [(self.d, (self.b + u) % self.nb, self.c) for u in range(1, self.nb)]
        out += [self.across(k) for k in range(self.levels)]
        return out + [self.sibling]

    def barrier(self):
        bar = pltpu.get_barrier_semaphore()
        ps = self.peers()
        for p in ps:
            pl.semaphore_signal(bar, inc=1, device_id=p, device_id_type=MESH)
        pl.semaphore_wait(bar, len(ps))


def remote(src, dst, send, recv, dev):
    return pltpu.make_async_remote_copy(src_ref=src, dst_ref=dst, send_sem=send, recv_sem=recv, device_id=dev, device_id_type=MESH)


def blocks_of(full):
    return (lambda i: full.at[i]), (lambda k: full.at[pl.ds(0, k)])


def rows_of(full, rows, offset=0, stride=None):
    every = rows if stride is None else stride

    def place(i):
        return full.at[pl.ds(pl.multiple_of(i * every + offset, 8), rows)]

    return place, (lambda k: full.at[pl.ds(0, k * rows)])


class Gather:
    def __init__(self, net, mine, place, span, sems, narrow=False):
        self.net, self.mine, self.place, self.span, self.narrow = net, mine, place, span, narrow
        self.zsend, self.xsend, self.ssend, self.srecv, self.recv = sems

    def at(self, mask, blk):
        n = self.net
        if self.narrow:
            return self.place(blk * n.nc + n.c)
        return self.place(n.slot(mask, blk))

    def rsem(self, mask, blk):
        return self.recv.at[mask * self.net.nb + blk]

    def spread(self, mask, blk, src, dst):
        n = self.net
        if not self.narrow:
            for k in range(n.levels):
                if mask < (1 << k):
                    remote(src, dst, self.xsend, self.rsem(mask + (1 << k), blk), n.across(k)).start()
        remote(src, dst, self.ssend, self.srecv, n.sibling).start()

    def along(self, blk, src, dst):
        n = self.net
        sem = self.rsem(0, blk)

        @pl.when((n.b < n.nb - 1) & (blk <= n.b))
        def _():
            remote(src, dst, self.zsend, sem, (n.d, n.b + 1, n.c)).start()

        @pl.when((n.b > 0) & (blk >= n.b))
        def _():
            remote(src, dst, self.zsend, sem, (n.d, n.b - 1, n.c)).start()

    def own_line(self):
        self.along(self.net.b, self.mine, self.at(0, self.net.b))

    def own_spread(self):
        self.spread(0, self.net.b, self.mine, self.at(0, self.net.b))

    def z(self, e):
        blk = self.net.near(e)
        dst = self.at(0, blk)
        pltpu.make_async_copy(dst, dst, self.rsem(0, blk)).wait()
        self.along(blk, dst, dst)
        self.spread(0, blk, dst, dst)

    def x(self, mask, e):
        n = self.net
        blk = n.near(e)
        dst = self.at(mask, blk)
        pltpu.make_async_copy(dst, dst, self.rsem(mask, blk)).wait()
        self.spread(mask, blk, dst, dst)

    def own(self, sem):
        n = self.net
        return pltpu.make_async_copy(self.mine, self.at(0, n.b), sem)

    def wait_sibling(self):
        n = self.net
        half = self.span(n.nb if self.narrow else n.nd * n.nb)
        pltpu.make_async_copy(half, half, self.srecv).wait()

    def drain(self):
        n = self.net
        half = self.span(n.nb if self.narrow else n.nd * n.nb)
        pltpu.make_async_copy(half, half, self.ssend).wait()
        if not self.narrow:
            part = self.span((n.nd - 1) * n.nb)
            pltpu.make_async_copy(part, part, self.xsend).wait()
        edge = (n.b == 0) | (n.b == n.nb - 1)

        @pl.when(edge)
        def _():
            one = self.span(1)
            pltpu.make_async_copy(one, one, self.zsend).wait()

        @pl.when(jnp.logical_not(edge))
        def _():
            many = self.span(n.nb + 1)
            pltpu.make_async_copy(many, many, self.zsend).wait()


def gather_sems(n_pieces, nd, nb):
    return [pltpu.SemaphoreType.DMA((n_pieces, 4)), pltpu.SemaphoreType.DMA((n_pieces, nd * nb)), pltpu.SemaphoreType.DMA]


class Scatter:
    def __init__(self, net, parts, place, theirs, landing, span, xrecv, zrecv, out, sems, narrow=False, extra=()):
        self.net, self.parts, self.place, self.theirs, self.landing = net, parts, place, theirs, landing
        self.span, self.xbuf, self.zbuf, self.out, self.extra = span, xrecv, zrecv, out, extra
        self.sib_send, self.x_send, self.z_send, self.sib_sem, self.x_sem, self.z_sem = sems
        self.narrow, self.seen = narrow, set()
        self.nd = 1 if narrow else net.nd
        self.levels = 0 if narrow else net.levels

    def home(self, mask):
        return 0 if self.narrow else self.net.flips(mask)

    def start(self):
        for mask in range(self.nd - 1, -1, -1):
            mirrored = sum(1 << (self.levels - 1 - k) for k in range(self.levels) if (mask >> k) & 1)
            for blk in range(self.net.nb):
                self.send(self.home(mirrored) * self.net.nb + blk, mask)

    def send(self, at, sem):
        remote(self.theirs(at), self.landing(at), self.sib_send, self.sib_sem.at[sem], self.net.sibling).start()

    def arrived(self, sem, count):
        some = self.span(count)
        pltpu.make_async_copy(some, some, self.sib_sem.at[sem]).wait()

    def x_at(self, k, mask, blk):
        return ((1 << k) - 1 + mask) * self.net.nb + blk

    def z_at(self, side, blk, owner):
        return blk + side * jnp.where(blk == owner, self.net.nb - blk, 0)

    def add(self, at, more, to, extra=()):
        for pick, places in self.parts(at):
            def chosen(ref):
                return ref if pick is None else ref.at[pick]

            add_up(places + [chosen(m) for m in more] + list(extra), chosen(to))

    def reduce(self, mask, e):
        n = self.net
        blk = n.near(e)
        if self.narrow:
            self.arrived(blk, 1)
        elif mask not in self.seen:
            self.seen.add(mask)
            self.arrived(mask, n.nb)
        at = self.home(mask) * n.nb + blk
        place = self.place(at)
        more = []
        for k in range(self.levels - 1, -1, -1):
            if mask < (1 << k):
                i = self.x_at(k, mask, blk)
                got = self.xbuf.at[i]
                pltpu.make_async_copy(got, got, self.x_sem.at[i]).wait()
                more.append(got)
        if mask:
            k = mask.bit_length() - 1
            self.add(at, more, place)
            i = self.x_at(k, mask - (1 << k), blk)
            remote(place, self.xbuf.at[i], self.x_send, self.x_sem.at[i], n.across(k)).start()
            return

        def line(side, there):
            i = self.z_at(side, blk, n.b)
            got = self.zbuf.at[i]

            @pl.when(there)
            def _():
                pltpu.make_async_copy(got, got, self.z_sem.at[i]).wait()

            more.append(got)

        if e == 0:
            line(0, n.b > 0)
            line(1, n.b < n.nb - 1)
            self.add(at, more, self.out, self.extra)
            return
        side = jnp.where(blk > n.b, 0, 1)
        line(side, jnp.where(blk > n.b, n.b, n.nb - 1 - n.b) > 0)
        self.add(at, more, place)
        to = n.b + 1 - 2 * side
        i = self.z_at(side, blk, to)
        remote(place, self.zbuf.at[i], self.z_send, self.z_sem.at[i], (n.d, to, n.c)).start()

    def clear_edges(self):
        n = self.net

        def clear(i, carry):
            self.zbuf[i] = jnp.zeros(self.zbuf.shape[1:], self.zbuf.dtype)
            return carry

        @pl.when(n.b == 0)
        def _():
            lax.fori_loop(0, n.nb, clear, 0)

        @pl.when(n.b == n.nb - 1)
        def _():
            lax.fori_loop(0, n.nb - 1, clear, 0)
            clear(n.nb, 0)

    def drain(self):
        n = self.net
        some = self.span(self.nd * n.nb)
        pltpu.make_async_copy(some, some, self.sib_send).wait()
        if not self.narrow:
            some = self.xbuf.at[pl.ds(0, (n.nd - 1) * n.nb)]
            pltpu.make_async_copy(some, some, self.x_send).wait()
        some = self.zbuf.at[pl.ds(0, n.nb - 1)]
        pltpu.make_async_copy(some, some, self.z_send).wait()


def add_up(terms, to):
    shape = to.shape
    rows = shape[-2]
    step = rows
    while step % 2 == 0 and step > 32:
        step //= 2
    lead = [()] if len(shape) == 2 else [(g,) for g in range(shape[0])]
    for g in lead:
        for r in range(0, rows, step):
            at = g + (slice(r, r + step),)
            total = terms[0][at].astype(F32)
            for t in terms[1:]:
                total = total + t[at].astype(F32)
            to[at] = total.astype(to.dtype)


class AllSum:
    def __init__(self, net, value, got, send, recv):
        self.net, self.value, self.got, self.send, self.recv = net, value, got, send, recv

    def copy(self, stage, dev, src, slot):
        return remote(self.value.at[src], self.got.at[slot], self.send.at[slot], self.recv.at[slot], dev)

    def stages(self):
        n = self.net
        devs = [n.sibling] + [n.across(k) for k in range(n.levels)]
        steps = []
        for i, dev in enumerate(devs):
            steps.append(functools.partial(self.one, i, dev))
        steps.append(self.line_start)
        steps.append(self.line_end)
        return [lambda: self.copy(0, devs[0], 0, 0).start()] + steps

    def one(self, i, dev):
        n = self.net
        self.copy(i, dev, i, i).wait()
        self.value[i + 1] = self.value[i] + self.got[i]
        if i + 1 <= n.levels:
            self.copy(i + 1, n.across(i), i + 1, i + 1).start()

    def line_copy(self, u):
        n = self.net
        return self.copy(None, (n.d, (n.b + u) % n.nb, n.c), n.levels + 1, n.levels + u)

    def line_start(self):
        for u in range(1, self.net.nb):
            self.line_copy(u).start()

    def line_end(self):
        n = self.net
        for u in range(1, n.nb):
            self.line_copy(u).wait()
        total = self.value[n.levels + 1]
        for u in range(1, n.nb):
            total = total + self.got[n.levels + u]
        self.value[0] = total


def scatter_sems(n_pieces, nd, nb):
    return [
        pltpu.SemaphoreType.DMA((n_pieces, 3)),
        pltpu.SemaphoreType.DMA((n_pieces, max(nd, nb))),
        pltpu.SemaphoreType.DMA((n_pieces, (nd - 1) * nb)),
        pltpu.SemaphoreType.DMA((n_pieces, nb + 1)),
    ]


def dot(a, b, dims=((1,), (0,))):
    return lax.dot_general(a, b, (dims, ((), ())), preferred_element_type=F32)


def mask_lanes(seg_row, count):
    lanes = lax.broadcasted_iota(jnp.int32, (128, count), 0)
    return jnp.transpose(jnp.where(lanes == seg_row, -1.0, 0.0).astype(F32), (1, 0))


def project_keys(i, step, tok, wk, wv, bias_v, seg, kaug, v_scr):
    at = pl.ds(pl.multiple_of(i * step, step), step)
    piece = tok[at, :]
    keys = dot(piece, wk).astype(BF16)
    vals = (dot(piece, wv) + bias_v).astype(BF16)
    lanes = mask_lanes(seg[:, at], step).astype(BF16)
    for p in range(kaug.shape[0]):
        kaug[p, at, 0:128] = keys[:, p * 128:(p + 1) * 128]
        kaug[p, at, 128:256] = lanes
        v_scr[p, at, :] = vals[:, p * 128:(p + 1) * 128]


def project_queries(tok, wq, bias_q, seg, qaug, blk, qlen):
    mine = pl.ds(pl.multiple_of(blk * qlen, qlen), qlen)
    query = (dot(tok[mine, :], wq) + bias_q).astype(BF16)
    lane = lax.broadcasted_iota(jnp.int32, (qlen, 128), 1)
    feat = jnp.where(lane < 8, BIG * (1.0 + mask_lanes(seg[:, mine], qlen)), 0.0).astype(BF16)
    for p in range(qaug.shape[0] // 2):
        q_pair = query[:, p * 128:(p + 1) * 128].astype(F32) * HD**-0.5
        for half in range(2):
            keep = (lane >= 64) if half else (lane < 64)
            qaug[2 * p + half, :, 0:128] = jnp.where(keep, q_pair, 0.0).astype(BF16)
            qaug[2 * p + half, :, 128:256] = feat


def attend_chunk(i, qaug, kaug, v_scr, o_scr, exact_scr, lse_scr, chunk, per_head):
    h = i // per_head
    at = pl.ds(pl.multiple_of((i % per_head) * chunk, chunk), chunk)
    s = dot(qaug[h, at, :], kaug[h // 2], ((1,), (1,)))
    top = jnp.max(s, axis=-1, keepdims=True)
    p = jnp.exp(s - top)
    total = jnp.sum(p, axis=-1, keepdims=True)
    low = p.astype(BF16)
    rest = (p - low.astype(F32)).astype(BF16)
    value = v_scr[h // 2]
    o = dot(low, value)
    inverse = 1.0 / total
    o_scr[h, at, :] = o * inverse
    exact_scr[h, at, :] = (o + dot(rest, value)) * inverse
    lse_scr[h, at, :] = jnp.broadcast_to(top + jnp.log(total), (chunk, 128))


def join_heads(scr, p, at=slice(None)):
    first, second = scr[2 * p, at, :], scr[2 * p + 1, at, :]
    lane = lax.broadcasted_iota(jnp.int32, first.shape, 1)
    return jnp.where(lane < 64, first, second)


def head_columns(w, part, c, width):
    return w[:, pl.ds(pl.multiple_of((part * 2 + c) * width, 128), width)]


def fwd_kernel(tok, w, bias, seg, ctx, kaug, v_scr, qaug, lse_out, exact, lse_scr, o_scr, exact_scr, chunk=256):
    blk, c = lax.axis_index("blk"), lax.axis_index("head")
    qlen, width = ctx.shape
    total = tok.shape[0]
    step = min(512, total)
    wk, wv = head_columns(w, 1, c, width), head_columns(w, 2, c, width)

    def rows(i, carry):
        project_keys(i, step, tok, wk, wv, bias[1:2, :], seg, kaug, v_scr)
        return carry

    lax.fori_loop(0, total // step, rows, 0)
    project_queries(tok, head_columns(w, 0, c, width), bias[0:1, :], seg, qaug, blk, qlen)
    per_head = qlen // chunk

    def go(i, carry):
        attend_chunk(i, qaug, kaug, v_scr, o_scr, exact_scr, lse_scr, chunk, per_head)
        return carry

    lax.fori_loop(0, (width // HD) * per_head, go, 0)
    finish_forward(o_scr, exact_scr, lse_scr, lambda p, v: store_lanes(ctx, p, v), lse_out, exact)


def store_lanes(ref, p, value):
    ref[:, p * 128:(p + 1) * 128] = value


def finish_forward(o_scr, exact_scr, lse_scr, put, lse_out, exact):
    for p in range(o_scr.shape[0] // 2):
        put(p, join_heads(o_scr, p).astype(BF16))
        exact[p] = join_heads(exact_scr, p)
    for h in range(o_scr.shape[0]):
        lse_out[h] = jnp.transpose(lse_scr[h], (1, 0))[0:8, :]


def prepare_backward(gctx_of, exact, do_m, delta_row):
    pairs, qlen, _ = exact.shape
    lane = lax.broadcasted_iota(jnp.int32, (qlen, 128), 1)
    for p in range(pairs):
        grad = gctx_of(p)
        product = grad.astype(F32) * exact[p]
        for half in range(2):
            keep = (lane >= 64) if half else (lane < 64)
            do_m[2 * p + half] = jnp.where(keep, grad, jnp.zeros_like(grad))
            across = jnp.transpose(jnp.where(keep, product, 0.0), (1, 0))
            delta_row[2 * p + half] = jnp.broadcast_to(jnp.sum(across, axis=0, keepdims=True), (8, qlen))


def bwd_pair(pair, qaug, k_part, v_part, do_m, lse_row, delta_row, dq_scr, put, first, qs=slice(None)):
    dk = dv = None
    for half in range(2):
        h = 2 * pair + half
        q_part, do_part = qaug[h, qs, :], do_m[h, qs, :]
        s = dot(k_part, q_part, ((1,), (1,)))
        p = jnp.exp(s - lse_row[h, 0:1, qs])
        dp = dot(v_part, do_part, ((1,), (1,)))
        ds = (p * (dp - delta_row[h, 0:1, qs])).astype(BF16)
        v_term = dot(p.astype(BF16), do_part)
        k_term = dot(ds, q_part[:, 0:128])
        dv = v_term if dv is None else dv + v_term
        dk = k_term if dk is None else dk + k_term
        dq = dot(k_part[:, 0:128], ds, ((0,), (0,)))
        if first is None:
            dq_scr[h, :, qs] += dq
        else:
            dq_scr[h, :, qs] = jnp.where(first, dq, dq_scr[h, :, qs] + dq)
    put(dk, dv)


def join_dq(dq_scr, p):
    qlen = dq_scr.shape[2]
    lane = lax.broadcasted_iota(jnp.int32, (qlen, 128), 1)
    first, second = jnp.transpose(dq_scr[2 * p], (1, 0)), jnp.transpose(dq_scr[2 * p + 1], (1, 0))
    return (jnp.where(lane < 64, first, second) * HD**-0.5).astype(BF16)


VMEM = pl.BlockSpec(memory_space=pltpu.VMEM)
HBM = pl.BlockSpec(memory_space=pl.ANY)


def params(limit, collective=None):
    more = {} if collective is None else dict(collective_id=collective, has_side_effects=True)
    return pltpu.CompilerParams(vmem_limit_bytes=limit << 20, **more)


def lane_mean(x):
    return jnp.mean(x, axis=-1, keepdims=True)


def norm_parts(hidden):
    centered = hidden - lane_mean(hidden)
    scale = lax.rsqrt(lane_mean(centered * centered) + 1e-12)
    return centered * scale, scale


def norm_back(grad, unit, scale, gain):
    scaled = grad * gain
    return scale * (scaled - lane_mean(scaled) - unit * lane_mean(scaled * unit))


def gelu_and_slope(pre):
    cdf = 0.5 * (1.0 + lax.erf(pre * 0.7071067811865476))
    return pre * cdf, cdf + pre * (0.3989422804014327 * jnp.exp(-0.5 * pre * pre))


def column_sum(x):
    return jnp.sum(x, axis=0, keepdims=True)


def ffn_kernel(
    ctx, tok, cot, vecs, bias_in, w_out_h, w_in_h, w_down_h,
    out, resid_grad, gctx, dw_down_h, dw_in_h, dw_out_h, sums,
    w_out, w_in, w_down, act, slope, dw_a, dw_b, dw_c, in_sem, out_sem,
):
    groups, rows, half = ctx.shape
    width, ff = w_in.shape
    step = width
    loads = [
        pltpu.make_async_copy(src, dst, in_sem.at[i])
        for i, (src, dst) in enumerate([(w_out_h, w_out), (w_in_h, w_in), (w_down_h, w_down)])
    ]
    for load in loads:
        load.start()
    bias_out, gain_one, shift_one = vecs[2:3, :], vecs[3:4, :], vecs[4:5, :]
    bias_down, gain_two, shift_two = vecs[5:6, :], vecs[6:7, :], vecs[7:8, :]
    context = jnp.concatenate([ctx[g] for g in range(groups)], axis=1)
    loads[0].wait()
    resid_one = tok[...].astype(F32) + (dot(context, w_out[...]) + bias_out)
    unit_one, scale_one = norm_parts(resid_one)
    normed = unit_one * gain_one + shift_one
    normed_low = normed.astype(BF16)
    loads[1].wait()
    chunks = [slice(i, i + step) for i in range(0, ff, step)]
    for at in chunks:
        pre = dot(normed_low, w_in[:, at]) + bias_in[0:1, at]
        value, grad = gelu_and_slope(pre)
        act[:, at] = value.astype(BF16)
        slope[:, at] = grad
    loads[2].wait()
    resid_two = normed + (dot(act[...], w_down[...]) + bias_down)
    unit_two, scale_two = norm_parts(resid_two)
    out[...] = (unit_two * gain_two + shift_two).astype(BF16)
    grad_out = cot[...].astype(F32)
    grad_two = norm_back(grad_out, unit_two, scale_two, gain_two)
    grad_ffn = grad_two.astype(BF16)
    sums[0:2, :] = jnp.zeros((2, width), F32)
    sums[5:6, :] = column_sum(grad_ffn.astype(F32))
    sums[6:7, :] = column_sum(grad_out * unit_two)
    sums[7:8, :] = column_sum(grad_out)
    stores = []

    def store(src, dst):
        copy = pltpu.make_async_copy(src, dst, out_sem.at[len(stores)])
        copy.start()
        stores.append(copy)

    for at in chunks:
        dw_a[at, :] = dot(act[:, at], grad_ffn, ((0,), (0,))).astype(BF16)
        store(dw_a.at[at], dw_down_h.at[at])
    grad_normed = grad_two
    for i, at in enumerate(chunks):
        grad_act = dot(grad_ffn, w_down[at, :], ((1,), (1,)))
        grad_pre = (grad_act * slope[:, at]).astype(BF16)
        sums[8 + i:9 + i, :] = column_sum(grad_pre.astype(F32))
        dw_b[:, at] = dot(normed_low, grad_pre, ((0,), (0,))).astype(BF16)
        grad_normed = grad_normed + dot(grad_pre, w_in[:, at], ((1,), (1,)))
    store(dw_b, dw_in_h)
    sums[8 + len(chunks):, :] = jnp.zeros((sums.shape[0] - 8 - len(chunks), width), F32)
    sums[3:4, :] = column_sum(grad_normed * unit_one)
    sums[4:5, :] = column_sum(grad_normed)
    grad_one = norm_back(grad_normed, unit_one, scale_one, gain_one)
    resid_grad[...] = grad_one
    grad_attn = grad_one.astype(BF16)
    sums[2:3, :] = column_sum(grad_attn.astype(F32))
    dw_c[...] = dot(context, grad_attn, ((0,), (0,))).astype(BF16)
    store(dw_c, dw_out_h)
    grad_context = dot(grad_attn, w_out[...], ((1,), (1,))).astype(BF16)
    for g in range(groups):
        gctx[g] = grad_context[:, g * half:(g + 1) * half]
    for copy in stores:
        copy.wait()


def feed_forward(ctx, tok, cot, vecs, bias_in, w_out, w_in, w_down):
    groups, rows, half = ctx.shape
    width, ff = w_in.shape
    n_sums = 8 + -(-(ff // width) // 8) * 8
    return pl.pallas_call(
        ffn_kernel,
        out_shape=[
            jax.ShapeDtypeStruct((rows, width), BF16),
            jax.ShapeDtypeStruct((rows, width), F32),
            jax.ShapeDtypeStruct((groups, rows, half), BF16),
            jax.ShapeDtypeStruct((ff, width), BF16),
            jax.ShapeDtypeStruct((width, ff), BF16),
            jax.ShapeDtypeStruct((width, width), BF16),
            jax.ShapeDtypeStruct((n_sums, width), F32),
        ],
        in_specs=[VMEM] * 5 + [HBM] * 3,
        out_specs=[VMEM] * 3 + [HBM] * 3 + [VMEM],
        scratch_shapes=[
            pltpu.VMEM((width, width), BF16),
            pltpu.VMEM((width, ff), BF16),
            pltpu.VMEM((ff, width), BF16),
            pltpu.VMEM((rows, ff), BF16),
            pltpu.VMEM((rows, ff), F32),
            pltpu.VMEM((ff, width), BF16),
            pltpu.VMEM((width, ff), BF16),
            pltpu.VMEM((width, width), BF16),
            pltpu.SemaphoreType.DMA((3,)),
            pltpu.SemaphoreType.DMA((ff // width + 2,)),
        ],
        compiler_params=params(56),
    )(ctx, tok, cot, vecs, bias_in, w_out, w_in, w_down)


def gather_order(keys, narrow, nd, nb):
    events = []
    for p, (begin, dz, dx) in enumerate(keys):
        for e in range(nb):
            events.append((begin + e * dz, ("z", p, e)))
            if not narrow[p]:
                for mask in range(1, nd):
                    events.append((begin + e * dz + dx * mask.bit_length(), ("x", p, mask, e)))
    events.sort(key=lambda q: q[0])
    return [ev for _, ev in events]


def gather_all(shards, narrow, keys, nd, nb, nc):
    count = len(shards)

    def kernel(*refs):
        mine, full = refs[:count], refs[count:2 * count]
        four, recv, own_sem = refs[2 * count:]
        net = Net(nd, nb, nc)
        pieces = [
            Gather(net, mine[p], *blocks_of(full[p]), [four.at[p, i] for i in range(4)] + [recv.at[p]], narrow[p]) for p in range(count)
        ]
        net.barrier()
        for ev in gather_order(keys, narrow, nd, nb):
            if ev[0] == "z" and ev[2] == 0:
                pieces[ev[1]].own_line()
                pieces[ev[1]].own_spread()
            elif ev[0] == "z":
                pieces[ev[1]].z(ev[2])
            else:
                pieces[ev[1]].x(ev[2], ev[3])
        for piece in pieces:
            own = piece.own(own_sem)
            own.start()
            own.wait()
        for piece in pieces:
            piece.wait_sibling()
        for piece in pieces:
            piece.drain()

    outs = [
        jax.ShapeDtypeStruct(((nb * nc if thin else nd * nb * nc),) + s.shape, s.dtype) for s, thin in zip(shards, narrow)
    ]
    return pl.pallas_call(
        kernel,
        out_shape=outs,
        in_specs=[VMEM] * count,
        out_specs=[HBM] * count,
        scratch_shapes=gather_sems(count, nd, nb),
        compiler_params=params(56, 0),
    )(*shards)


def attend_forward(tok, w, bias, seg, qlen, width):
    total = tok.shape[0]
    heads = width // HD
    chunk = min(256, qlen)
    while chunk * total > 256 * 4096:
        chunk //= 2
    return pl.pallas_call(
        functools.partial(fwd_kernel, chunk=chunk),
        out_shape=[
            jax.ShapeDtypeStruct((qlen, width), BF16),
            jax.ShapeDtypeStruct((width // 128, total, 256), BF16),
            jax.ShapeDtypeStruct((width // 128, total, 128), BF16),
            jax.ShapeDtypeStruct((heads, qlen, 256), BF16),
            jax.ShapeDtypeStruct((heads, 8, qlen), F32),
            jax.ShapeDtypeStruct((heads // 2, qlen, 128), F32),
        ],
        in_specs=[VMEM] * 4,
        out_specs=[VMEM] * 6,
        scratch_shapes=[pltpu.VMEM((heads, qlen, 128), F32)] * 3,
        compiler_params=params(58),
    )(tok, w, bias, seg)


def pair_bwd_kernel(qaug, kaug, v_scr, lse, exact, gctx, dk, dv, dq, do_m, delta_row, dq_scr):
    step = pl.program_id(1)

    @pl.when(step == 0)
    def _():
        prepare_backward(lambda p: gctx[...], exact, do_m, delta_row)

    def put(k_term, v_term):
        dk[...] = k_term.astype(BF16)
        dv[...] = v_term.astype(BF16)

    bwd_pair(0, qaug, kaug[0], v_scr[0], do_m, lse, delta_row, dq_scr, put, step == 0)

    @pl.when(step == pl.num_programs(1) - 1)
    def _():
        dq[...] = join_dq(dq_scr, 0)


def finish_kernel(tok, dk, dv, tok_mine, dq, w, dtok, dw, dbias, own):
    i, c = pl.program_id(0), lax.axis_index("head")
    blk = lax.axis_index("blk")
    step, width = dk.shape
    qlen = dq.shape[0]

    def cols(part):
        return w[:, pl.ds(pl.multiple_of((part * 2 + c) * width, 128), width)]

    piece, grad_k, grad_v = tok[...], dk[...], dv[...]

    @pl.when(i == 0)
    def _():
        dw[:, 0:width] = dot(tok_mine[...], dq[...], ((0,), (0,)))
        dw[:, width:3 * width] = jnp.zeros((dw.shape[0], 2 * width), F32)
        dbias[0:1, :] = jnp.sum(dq[...].astype(F32), axis=0, keepdims=True)
        dbias[1:2, :] = jnp.zeros((1, width), F32)
        own[...] = dot(dq[...], cols(0), ((1,), (1,)))

    dw[:, width:2 * width] += dot(piece, grad_k, ((0,), (0,)))
    dw[:, 2 * width:3 * width] += dot(piece, grad_v, ((0,), (0,)))
    dbias[1:2, :] += jnp.sum(grad_v.astype(F32), axis=0, keepdims=True)
    grad = dot(grad_k, cols(1), ((1,), (1,))) + dot(grad_v, cols(2), ((1,), (1,)))
    per = qlen // step
    mine = i // per == blk
    at = pl.ds(pl.multiple_of((i % per) * step, step), step)
    dtok[...] = (grad + jnp.where(mine, own[at, :], 0.0)).astype(BF16)


def attend_backward(tok, tok_mine, w, qaug, kaug, v_scr, lse, exact, gctx):
    heads, qlen, _ = qaug.shape
    total, d_model = tok.shape
    width = heads * HD
    kc = min(512, total)
    dk, dv, dq = pl.pallas_call(
        pair_bwd_kernel,
        grid=(heads // 2, total // kc),
        out_shape=[
            jax.ShapeDtypeStruct((total, width), BF16),
            jax.ShapeDtypeStruct((total, width), BF16),
            jax.ShapeDtypeStruct((qlen, width), BF16),
        ],
        in_specs=[
            pl.BlockSpec((2, qlen, 256), lambda p, j: (p, 0, 0)),
            pl.BlockSpec((1, kc, 256), lambda p, j: (p, j, 0)),
            pl.BlockSpec((1, kc, 128), lambda p, j: (p, j, 0)),
            pl.BlockSpec((2, 8, qlen), lambda p, j: (p, 0, 0)),
            pl.BlockSpec((1, qlen, 128), lambda p, j: (p, 0, 0)),
            pl.BlockSpec((qlen, 128), lambda p, j: (0, p)),
        ],
        out_specs=[pl.BlockSpec((kc, 128), lambda p, j: (j, p))] * 2 + [pl.BlockSpec((qlen, 128), lambda p, j: (0, p))],
        scratch_shapes=[
            pltpu.VMEM((2, qlen, 128), BF16),
            pltpu.VMEM((2, 8, qlen), F32),
            pltpu.VMEM((2, 128, qlen), F32),
        ],
        compiler_params=params(56),
    )(qaug, kaug, v_scr, lse, exact, gctx)
    step = min(512, qlen)
    whole = lambda i: (0, 0)
    rows = lambda i: (i, 0)
    return pl.pallas_call(
        finish_kernel,
        grid=(total // step,),
        out_shape=[
            jax.ShapeDtypeStruct((total, d_model), BF16),
            jax.ShapeDtypeStruct((d_model, 3 * width), F32),
            jax.ShapeDtypeStruct((2, width), F32),
        ],
        in_specs=[
            pl.BlockSpec((step, d_model), rows),
            pl.BlockSpec((step, width), rows),
            pl.BlockSpec((step, width), rows),
            pl.BlockSpec((qlen, d_model), whole),
            pl.BlockSpec((qlen, width), whole),
            pl.BlockSpec((d_model, w.shape[1]), whole),
        ],
        out_specs=[
            pl.BlockSpec((step, d_model), rows),
            pl.BlockSpec((d_model, 3 * width), whole),
            pl.BlockSpec((2, width), whole),
        ],
        scratch_shapes=[pltpu.VMEM((qlen, d_model), F32)],
        compiler_params=params(56),
    )(tok, dk, dv, tok_mine, dq, w)


SPACE = (0.25, 1.0, 0.2)


def send_blocks(piece, nb):
    for blk in range(nb):
        piece.send(blk, blk)


def scatter_all(arrays, narrow, joined, small, nd, nb, nc):
    count = len(arrays)
    flat = []
    for a, j in zip(arrays, joined):
        flat += list(a) if j else [a]
    n_in = len(flat) + 1

    def kernel(*refs):
        ins, small_in = list(refs[:n_in - 1]), refs[n_in - 1]
        outs, small_out = refs[n_in:n_in + count], refs[n_in + count]
        rest = list(refs[n_in + count + 1:])
        net = Net(nd, nb, nc)
        s3, sib_sem, x_sem, z_sem, sum_send, sum_recv = rest[-6:]
        value, got = rest[-8:-6]
        bufs = rest[:-8]
        pieces = []
        for p in range(count):
            first = ins.pop(0)
            sib = ins.pop(0) if joined[p] else bufs.pop(0)
            xbuf = None if narrow[p] else bufs.pop(0)
            zbuf = bufs.pop(0)
            sems = [s3.at[p, i] for i in range(3)] + [sib_sem.at[p], x_sem.at[p], z_sem.at[p]]
            if joined[p]:
                parts = lambda at, first=first: [(None, [first.at[at]])]
                place = lambda at, first=first: first.at[at]
                theirs = lambda at, sib=sib: sib.at[at]
                landing = lambda at, first=first: first.at[at, net.c]
            else:
                place = lambda at, first=first: first.at[at * nc + net.c]
                parts = lambda at, place=place, sib=sib: [(None, [place(at), sib.at[at]])]
                theirs = lambda at, first=first: first.at[at * nc + nc - 1 - net.c]
                landing = lambda at, sib=sib: sib.at[at]
            span = lambda k, sib=sib: sib.at[pl.ds(0, k)]
            pieces.append(Scatter(net, parts, place, theirs, landing, span, xbuf, zbuf, outs[p], sems, narrow[p]))
        sums = AllSum(net, value, got, sum_send, sum_recv)
        for piece in pieces:
            piece.clear_edges()
        value[0] = small_in[...]
        net.barrier()
        events = []
        for p, piece in enumerate(pieces):
            t = SPACE[0] * p
            begin = functools.partial(send_blocks, piece, nb) if narrow[p] else piece.start
            events.append((t - 0.4, begin))
            for mask in range(piece.nd - 1, -1, -1):
                for e in range(nb - 1, -1, -1):
                    when = t + SPACE[1] * (piece.levels - mask.bit_length()) + SPACE[2] * (nb - 1 - e)
                    events.append((when, functools.partial(piece.reduce, mask, e)))
        for i, s in enumerate(sums.stages()):
            events.append((0.3 * i, s))
        events.sort(key=lambda q: q[0])
        for _, ev in events:
            ev()
        small_out[...] = value[0]
        for piece in pieces:
            piece.drain()

    outs, scratch = [], []
    for a, thin, j in zip(arrays, narrow, joined):
        full = a[0] if j else a
        block = full.shape[1:]
        outs.append(jax.ShapeDtypeStruct(block, F32))
        n_dp = 1 if thin else nd
        if not j:
            scratch.append(pltpu.VMEM((n_dp * nb,) + block, BF16))
        if not thin:
            scratch.append(pltpu.VMEM(((nd - 1) * nb,) + block, BF16))
        scratch.append(pltpu.VMEM((nb + 1,) + block, BF16))
    levels = nd.bit_length() - 1
    scratch += [pltpu.VMEM((levels + 2,) + small.shape, F32), pltpu.VMEM((levels + nb,) + small.shape, F32)]
    scratch += scatter_sems(count, nd, nb)
    scratch += [pltpu.SemaphoreType.DMA((levels + nb,))] * 2
    outs.append(jax.ShapeDtypeStruct(small.shape, F32))
    return pl.pallas_call(
        kernel,
        out_shape=outs,
        in_specs=[VMEM] * n_in,
        out_specs=[VMEM] * (count + 1),
        scratch_shapes=scratch,
        compiler_params=params(60, 1),
    )(*flat, small)


def unpack_vectors(small, vecs, bias_in, r, r_ff):
    n = small.shape[0]
    width, ff = vecs.shape[1], bias_in.shape[1]

    def gathered(rows, per, count):
        lane = lax.broadcasted_iota(jnp.int32, (8, 128), 1)
        tiles = [jnp.zeros((8, 128), F32) for _ in range(count // 128)]
        for i in range(n):
            piece = small[i, rows, :].astype(F32)
            shift, tile = per * i % 128, per * i // 128
            if shift:
                piece = pltpu.roll(piece, shift, 1)
            if shift + per <= 128:
                tiles[tile] = tiles[tile] + piece
            else:
                tiles[tile] = tiles[tile] + jnp.where(lane >= shift, piece, 0.0)
                tiles[tile + 1] = tiles[tile + 1] + jnp.where(lane < shift, piece, 0.0)
        return tiles

    for t, tile in enumerate(gathered(slice(0, 8), r, width)):
        vecs[:, t * 128:(t + 1) * 128] = tile
    for t, tile in enumerate(gathered(slice(8, 16), r_ff, ff)):
        bias_in[:, t * 128:(t + 1) * 128] = tile[0:1, :]


def pack_vectors(vectors, bias_in):
    row = lax.broadcasted_iota(jnp.int32, (16, 128), 0)
    packed = jnp.zeros((16, 128), F32)
    for i, v in enumerate(list(vectors) + [bias_in]):
        line = jnp.pad(v.astype(F32), (0, 128 - v.shape[0]))
        packed = jnp.where(row == i, line[None, :], packed)
    return packed.astype(BF16)


FRONT = {
    "small": (21, 16, ((21, 29, 32, 39), (34, 55, 60, 63), (35, 54, 59, 64), (58, 73, 75, 76))),
    "q": (2, 0, ((2, 8, 10, 20), (6, 17, 23, 42), (7, 19, 25, 43), (14, 37, 49, 68))),
    "t0": (3, 4, ((3, 9, 15, 27),)),
    "t1": (26, 1, ((26, 41, 48, 52),)),
    "t2": (44, 40, ((44, 53, 67, 77),)),
    "t3": (45, 31, ((45, 65, 71, 80),)),
    "o": (11, 22, ((11, 18, 24, 30), (46, 36, 50, 57), (47, 38, 51, 56), (69, 66, 72, 74))),
    "i": (91, 33, ((91, 101, 104, 107), (61, 110, 113, 118), (62, 109, 114, 119), (78, 121, 122, 124))),
    "d": (70, 5, ((70, 81, 83, 89), (12, 85, 94, 99), (13, 86, 93, 100), (28, 96, 103, 111))),
    "work": (79, 82, 84, 87, 88, 90, 92, 95, 97, 98, 102, 105, 106, 108, 112, 115, 116, 117, 120, 123),
}


def front_time(nd, nb, kind, what, e=0):
    if (nd, nb) == (4, 4) and (kind != "work" or e == len(FRONT["work"])):
        row = FRONT[kind]
        if kind == "work":
            return row[what]
        if what == "line":
            return row[0]
        if what == "spread":
            return row[1]
        return row[2][what][e]
    first = ["small", "q", "t0", "t1", "t2", "t3", "o", "i", "d"].index(kind) * 10 if kind != "work" else 0
    if kind == "work":
        return (40 if what == 0 else 200) + what
    if what in ("line", "spread"):
        return first
    return first + 3 * e + (4 * what.bit_length() if what else 0)


def front(small, w_qkv, tok, w_out, w_in, w_down, seg, nd, nb, nc):
    n = nd * nb * nc
    rows, width = tok.shape
    half, qlen, total = width // nc, nc * rows, nb * nc * rows
    heads = half // HD
    pairs = heads // 2
    r, r_ff, ff = w_qkv.shape[0], w_down.shape[0], w_in.shape[1]
    quarters = 4
    part = rows // quarters
    chunk = min(256, qlen)
    per_head = qlen // chunk
    step = min(512, total)

    def kernel(
        small_in, q_in, tok_in, o_in, i_in, d_in, seg_in,
        ctx2, vecs, bias_in, lse_out, exact, q_h, tok_h, o_h, i_h, d_h, kaug_h, v_h, qaug_h,
        small_all, w_v, tok_v, kaug, v_scr, qaug, o_scr, exact_scr, lse_scr, ctx_loc,
        four, recv, own_sem, load_sem, save_sem, swap_sem,
    ):
        net = Net(nd, nb, nc)
        c = net.c
        specs = [("small", small_in, blocks_of(small_all), False), ("q", q_in, rows_of(q_h, r), False)]
        for i in range(quarters):
            mine = tok_in.at[pl.ds(i * part, part)]
            specs.append((("t", i), mine, rows_of(tok_h, part, i * part, rows), True))
        specs += [("o", o_in, rows_of(o_h, r), False), ("i", i_in, rows_of(i_h, r), False), ("d", d_in, rows_of(d_h, r_ff), False)]
        piece, own = {}, {}
        for p, (name, mine, (place, span), narrow) in enumerate(specs):
            sems = [four.at[p, i] for i in range(4)] + [recv.at[p]]
            piece[name] = Gather(net, mine, place, span, sems, narrow)
            own[name] = piece[name].own(own_sem.at[p])
        tokens = [("t", i) for i in range(quarters)]
        for name in piece:
            own[name].start()
        net.barrier()

        def unpack():
            piece["small"].wait_sibling()
            own["small"].wait()
            unpack_vectors(small_all, vecs, bias_in, r, r_ff)

        def load():
            copies = []
            for name in ["q"] + tokens:
                piece[name].wait_sibling()
                own[name].wait()
            for k in range(3):
                lanes = pl.ds(pl.multiple_of((k * nc + c) * half, 128), half)
                copies.append(pltpu.make_async_copy(q_h.at[:, lanes], w_v.at[:, pl.ds(k * half, half)], load_sem.at[k]))
            copies.append(pltpu.make_async_copy(tok_h, tok_v, load_sem.at[3]))
            for copy in copies:
                copy.start()
            for copy in copies:
                copy.wait()

        lanes = pl.ds(pl.multiple_of(c * half, 128), half)

        def keys(i):
            project_keys(i, step, tok_v, w_v[:, half:2 * half], w_v[:, 2 * half:3 * half], vecs[1:2, lanes], seg_in, kaug, v_scr)

        saves = [
            pltpu.make_async_copy(src, dst, save_sem.at[i])
            for i, (src, dst) in enumerate([(kaug, kaug_h), (v_scr, v_h), (qaug, qaug_h)])
        ]

        def queries():
            project_queries(tok_v, w_v[:, 0:half], vecs[0:1, lanes], seg_in, qaug, net.b, qlen)
            for save in saves:
                save.start()

        swap = remote(ctx_loc.at[nc - 1 - c], ctx2.at[c], swap_sem.at[0], swap_sem.at[1], net.sibling)

        def finish():
            def put(p, value):
                for g in range(nc):
                    ctx_loc[g, :, p * 128:(p + 1) * 128] = value[g * rows:(g + 1) * rows]

            finish_forward(o_scr, exact_scr, lse_scr, put, lse_out, exact)
            swap.start()
            ctx2[c] = ctx_loc[c]

        steps = heads * per_head
        order = []
        for name in piece:
            kind = "t" + str(name[1]) if name in tokens else name
            order.append((front_time(nd, nb, kind, "line"), piece[name].own_line, None))
            order.append((front_time(nd, nb, kind, "spread"), piece[name].own_spread, None))
            for e in range(1, nb):
                order.append((front_time(nd, nb, kind, 0, e), functools.partial(piece[name].z, e), None))
            for mask in range(1, 1 if name in tokens else nd):
                for e in range(nb):
                    order.append((front_time(nd, nb, kind, mask, e), functools.partial(piece[name].x, mask, e), None))
        work = [unpack, load] + [functools.partial(keys, i) for i in range(total // step)] + [queries]
        work += [None] * steps + [finish]
        for i, act in enumerate(work):
            index = i - (len(work) - steps - 1) if act is None else None
            order.append((front_time(nd, nb, "work", i, len(work)), act, index))
        order.sort(key=lambda q: q[0])
        begin = next(i for i, q in enumerate(order) if q[2] == 0)
        end = next(i for i, q in enumerate(order) if q[2] == steps - 1)
        for _, act, _ in order[:begin]:
            act()
        beside = {}
        for _, act, i in order[begin:end + 1]:
            if act is None:
                at_step = i
            else:
                beside.setdefault(at_step, []).append(act)

        def attention(i, carry):
            attend_chunk(i, qaug, kaug, v_scr, o_scr, exact_scr, lse_scr, chunk, per_head)
            for g, acts in beside.items():

                @pl.when(i == g)
                def _(acts=acts):
                    for act in acts:
                        act()

            return carry

        lax.fori_loop(0, steps, attention, 0)
        for _, act, _ in order[end + 1:]:
            act()
        for name in ("o", "i", "d"):
            piece[name].wait_sibling()
            own[name].wait()
        for name in piece:
            piece[name].drain()
        for save in saves:
            save.wait()
        swap.wait()

    count = 5 + quarters
    return pl.pallas_call(
        kernel,
        out_shape=[
            jax.ShapeDtypeStruct((nc, rows, half), BF16),
            jax.ShapeDtypeStruct((8, width), F32),
            jax.ShapeDtypeStruct((1, ff), F32),
            jax.ShapeDtypeStruct((heads, 8, qlen), F32),
            jax.ShapeDtypeStruct((pairs, qlen, 128), F32),
            jax.ShapeDtypeStruct((n * r, 3 * width), BF16),
            jax.ShapeDtypeStruct((total, width), BF16),
            jax.ShapeDtypeStruct((n * r, width), BF16),
            jax.ShapeDtypeStruct((n * r, ff), BF16),
            jax.ShapeDtypeStruct((n * r_ff, width), BF16),
            jax.ShapeDtypeStruct((pairs, total, 256), BF16),
            jax.ShapeDtypeStruct((pairs, total, 128), BF16),
            jax.ShapeDtypeStruct((heads, qlen, 256), BF16),
        ],
        in_specs=[VMEM] * 7,
        out_specs=[VMEM] * 5 + [HBM] * 8,
        scratch_shapes=[
            pltpu.VMEM((n, 16, 128), BF16),
            pltpu.VMEM((width, 3 * half), BF16),
            pltpu.VMEM((total, width), BF16),
            pltpu.VMEM((pairs, total, 256), BF16),
            pltpu.VMEM((pairs, total, 128), BF16),
            pltpu.VMEM((heads, qlen, 256), BF16),
            pltpu.VMEM((heads, qlen, 128), F32),
            pltpu.VMEM((heads, qlen, 128), F32),
            pltpu.VMEM((heads, qlen, 128), F32),
            pltpu.VMEM((nc, rows, half), BF16),
            pltpu.SemaphoreType.DMA((count, 4)),
            pltpu.SemaphoreType.DMA((count, nd * nb)),
            pltpu.SemaphoreType.DMA((count,)),
            pltpu.SemaphoreType.DMA((4,)),
            pltpu.SemaphoreType.DMA((3,)),
            pltpu.SemaphoreType.DMA((2,)),
        ],
        compiler_params=params(56, 2),
    )(small, w_qkv, tok, w_out, w_in, w_down, seg)


BACK = {
    "d": (0, ((77, 67, 62, 57), (15, 16, 26, 27), (2, 3, 4, 5), (6, 7, 8, 9))),
    "i": (13, ((85, 75, 74, 73), (33, 34, 37, 39), (19, 21, 23, 25), (18, 20, 22, 24))),
    "o": (42, ((88, 82, 81, 79), (56, 58, 59, 61), (44, 45, 46, 47), (48, 49, 50, 51))),
    "q": (53, ((91, 90, 89, 86), (76, 78, 80, 83), (60, 64, 65, 66), (63, 69, 70, 71))),
    "t": (0, ((68, 40, 35, 28),)),
    "work": (1, 10, 11, 12, 14, 17, 29, 30, 31, 32, 36, 38, 41, 43, 53, 54, 52, 52.1, 55, 72, 84, 84.1, 87),
}


def back_time(nd, nb, kind, what, e=0):
    if (nd, nb) == (4, 4) and (kind != "work" or e == len(BACK["work"])):
        row = BACK[kind]
        if kind == "work":
            return row[what]
        return row[0] if what == "start" else row[1][what][e]
    if kind == "work":
        return 20 + 10 * what + (100 if what > e - 10 else 0)
    first = {"d": 0, "i": 10, "o": 20, "t": 300, "q": 400}[kind]
    if what == "start":
        return first
    return first + 30 - 5 * what.bit_length() + (nb - 1 - e)


def back(dw_down, dw_in, dw_out, tok, w_qkv, kaug_in, v_in, qaug_in, lse, exact_in, gctx, resid_grad, sums, nd, nb, nc):
    owners = nd * nb
    n = owners * nc
    rows, width = resid_grad.shape
    total = tok.shape[0]
    half, qlen = width // nc, nc * rows
    heads = half // HD
    pairs = heads // 2
    r, ff = dw_in.shape[2], dw_in.shape[3]
    r_ff = dw_down.shape[2]
    levels = nd.bit_length() - 1
    names = ["d", "i", "o", "t", "q"]

    def kernel(
        d_h, i_h, o_h, tok_h, w_h, kaug_h, v_h, qaug_h, lse_row, exact, gctx_in, resid, sums_in,
        g_tok, g_qkv, g_out, g_in, g_down, g_small,
        d_own, i_own, o_own, d_sib, i_sib, o_sib, t_sib, q_sib, d_x, i_x, o_x, q_x, d_z, i_z, o_z, t_z, q_z,
        t_part, q_part, q_full, q_out, tok_v, tok_t, w_v, kaug, v_scr, qaug, gctx_all, do_m, delta_row, dq_scr, dkv, grad_q,
        value, got,
        own_sem, load_sem, swap_sem, s3, sib_sem, x_sem, z_sem, sum_send, sum_recv,
    ):
        net = Net(nd, nb, nc)
        c, other = net.c, nc - 1 - net.c
        copies = {}
        for i, (name, src, dst) in enumerate([("d", d_h, d_own), ("i", i_h, i_own), ("o", o_h, o_own)]):
            copies[name] = pltpu.make_async_copy(src.at[:, c], dst, own_sem.at[i])
        loads = [(kaug_h, kaug), (v_h, v_scr), (qaug_h, qaug), (tok_h, tok_v)]
        for k in range(3):
            lanes = pl.ds(pl.multiple_of((k * nc + c) * half, 128), half)
            loads.append((w_h.at[:, lanes], w_v.at[:, pl.ds(k * half, half)]))
        loads = [pltpu.make_async_copy(src, dst, load_sem.at[i]) for i, (src, dst) in enumerate(loads)]
        for copy in list(copies.values()) + loads:
            copy.start()
        piece = {}
        for p, (name, src, own, sib, xbuf, zbuf, out) in enumerate(
            [
                ("d", d_h, d_own, d_sib, d_x, d_z, g_down),
                ("i", i_h, i_own, i_sib, i_x, i_z, g_in),
                ("o", o_h, o_own, o_sib, o_x, o_z, g_out),
                ("t", None, None, t_sib, None, t_z, g_tok),
                ("q", None, None, q_sib, q_x, q_z, q_out),
            ]
        ):
            sems = [s3.at[p, i] for i in range(3)] + [sib_sem.at[p], x_sem.at[p], z_sem.at[p]]
            landing = lambda at, sib=sib: sib.at[at]
            span = lambda k, sib=sib: sib.at[pl.ds(0, k)]
            extra = ()
            if name == "t":
                place = lambda at: t_part.at[at, c]
                parts = lambda at: [(None, [t_part.at[at, c], t_sib.at[at]])]
                theirs = lambda at: t_part.at[at, other]
                extra = (resid,)
            elif name == "q":
                place = lambda at: q_full.at[at]
                parts = lambda at: [(c, [q_part.at[at, c]]), (other, [q_sib.at[at]])]
                theirs = lambda at: q_part.at[at, other]
            else:
                place = lambda at, own=own: own.at[at]
                parts = lambda at, own=own, sib=sib: [(None, [own.at[at], sib.at[at]])]
                theirs = lambda at, src=src: src.at[at, other]
            piece[name] = Scatter(net, parts, place, theirs, landing, span, xbuf, zbuf, out, sems, name == "t", extra)
            piece[name].clear_edges()
        whole = AllSum(net, value, got, sum_send, sum_recv)
        swap = remote(gctx_in.at[other], gctx_all.at[c], swap_sem.at[0], swap_sem.at[1], net.sibling)
        net.barrier()
        swap.start()
        gctx_all[c] = gctx_in[c]

        def begin(name):
            piece[name].start()
            copies[name].wait()

        def prepare():
            for copy in loads:
                copy.wait()
            swap.wait()
            tok_t[...] = jnp.transpose(tok_v[...], (1, 0))
            lane = lambda p: slice(p * 128, (p + 1) * 128)
            prepare_backward(
                lambda p: jnp.concatenate([gctx_all[g, :, lane(p)] for g in range(nc)], axis=0), exact, do_m, delta_row
            )

        def token_grad(blk):
            at = pl.ds(pl.multiple_of(blk * qlen, qlen), qlen)
            return dot(dkv[at, :], w_v[:, half:3 * half], ((1,), (1,)))

        def put_tokens(blk, grad):
            for g in range(nc):
                t_part[blk, g] = grad[g * rows:(g + 1) * rows].astype(BF16)
            piece["t"].send(blk, blk)

        def weights():
            grad_q[...] = jnp.concatenate([join_dq(dq_scr, p) for p in range(pairs)], axis=1)
            mine = pl.ds(pl.multiple_of(net.b * qlen, qlen), qlen)
            for k in range(3):
                if k:
                    grad = dot(tok_t[...], dkv[:, (k - 1) * half:k * half])
                else:
                    grad = dot(tok_t[:, mine], grad_q[...])
                for at in range(owners):
                    for g in range(nc):
                        i = at * nc + g
                        q_part[at, g, :, k * half:(k + 1) * half] = grad[i * r:(i + 1) * r].astype(BF16)

        def own_tokens():
            put_tokens(net.b, token_grad(net.b) + dot(grad_q[...], w_v[:, 0:half], ((1,), (1,))))

        def small_sums():
            lanes = pl.ds(pl.multiple_of(c * half, 128), half)
            value[0] = sums_in[...]
            value[0, 0:1, lanes] = column_sum(grad_q[...].astype(F32))
            value[0, 1:2, lanes] = column_sum(dkv[:, half:2 * half].astype(F32))

        order = []
        for name in names:
            p = piece[name]
            if name in copies:
                order.append((back_time(nd, nb, name, "start"), functools.partial(begin, name), None))
            for mask in range(p.nd):
                for e in range(nb):
                    order.append((back_time(nd, nb, name, mask, e), functools.partial(p.reduce, mask, e), None))
        steps = nb * pairs
        work = [prepare] + [None] * steps + [weights, piece["q"].start, own_tokens, small_sums] + whole.stages()
        for i, act in enumerate(work):
            order.append((back_time(nd, nb, "work", i, len(work)), act, i - 1 if act is None else None))
        order.sort(key=lambda q: q[0])
        first = next(i for i, q in enumerate(order) if q[2] == 0)
        last = next(i for i, q in enumerate(order) if q[2] == steps - 1)
        for _, act, _ in order[:first]:
            act()
        beside = {}
        for _, act, i in order[first:last + 1]:
            if act is None:
                at_step = i
            else:
                beside.setdefault(at_step, []).append(act)

        def attention(i, carry):
            pair = i % pairs
            blk = net.near_at(nb - 1 - i // pairs)
            at = pl.ds(pl.multiple_of(blk * qlen, qlen), qlen)

            def put(dk, dv):
                dkv[at, pl.ds(pl.multiple_of(pair * 128, 128), 128)] = dk.astype(BF16)
                dkv[at, pl.ds(pl.multiple_of(half + pair * 128, 128), 128)] = dv.astype(BF16)

            bwd_pair(pair, qaug, kaug[pair, at, :], v_scr[pair, at, :], do_m, lse_row, delta_row, dq_scr, put, i < pairs)

            @pl.when((pair == pairs - 1) & (i < steps - 1))
            def _():
                put_tokens(blk, token_grad(blk))

            for g, acts in beside.items():

                @pl.when(i == g)
                def _(acts=acts):
                    for act in acts:
                        act()

            return carry

        lax.fori_loop(0, steps, attention, 0)
        for _, act, _ in order[last + 1:]:
            act()
        for k in range(3):
            for g in range(nc):
                lanes = slice((k * nc + g) * half, (k * nc + g + 1) * half)
                g_qkv[:, lanes] = q_out[g, :, k * half:(k + 1) * half]
        me = (net.d * nb + net.b) * nc + c
        feature = lax.broadcasted_iota(jnp.int32, (width, 128), 0)
        lane = lax.broadcasted_iota(jnp.int32, (width, 128), 1)
        pick = jnp.where((feature == me * r + lane) & (lane < r), 1.0, 0.0).astype(F32)
        in_row, in_lane = (me * r_ff) // width, (me * r_ff) % width
        pick_in = jnp.where((feature == in_lane + lane) & (lane < r_ff), 1.0, 0.0).astype(F32)
        exactly = dict(precision=lax.Precision.HIGHEST, preferred_element_type=F32)
        g_small[0:8, :] = jnp.dot(value[0, 0:8, :], pick, **exactly)
        found = jnp.dot(value[0, 8:16, :], pick_in, **exactly)
        row = lax.broadcasted_iota(jnp.int32, found.shape, 0)
        g_small[8:16, :] = jnp.broadcast_to(column_sum(jnp.where(row == in_row, found, 0.0)), (8, 128))
        for name in names:
            piece[name].drain()

    block = {"d": (r_ff, width), "i": (r, ff), "o": (r, width), "t": (rows, width)}
    joined = (nc, r, 3 * half)
    vmem = lambda shape, kind=BF16: pltpu.VMEM(shape, kind)
    scratch = [vmem((owners,) + block[k]) for k in "dio"] + [vmem((owners,) + block[k]) for k in "dio"]
    scratch += [vmem((nb,) + block["t"]), vmem((owners, r, 3 * half))]
    scratch += [vmem(((nd - 1) * nb,) + block[k]) for k in "dio"] + [vmem(((nd - 1) * nb,) + joined)]
    scratch += [vmem((nb + 1,) + block[k]) for k in "diot"] + [vmem((nb + 1,) + joined)]
    scratch += [
        vmem((nb, nc, rows, width)),
        vmem((owners,) + joined),
        vmem((owners,) + joined),
        vmem(joined, F32),
        vmem((total, width)),
        vmem((width, total)),
        vmem((width, 3 * half)),
        vmem((pairs, total, 256)),
        vmem((pairs, total, 128)),
        vmem((heads, qlen, 256)),
        vmem((nc, rows, half)),
        vmem((heads, qlen, 128)),
        vmem((heads, 8, qlen), F32),
        vmem((heads, 128, qlen), F32),
        vmem((total, 2 * half)),
        vmem((qlen, half)),
        vmem((levels + 2,) + sums.shape, F32),
        vmem((levels + nb,) + sums.shape, F32),
        pltpu.SemaphoreType.DMA((3,)),
        pltpu.SemaphoreType.DMA((7,)),
        pltpu.SemaphoreType.DMA((2,)),
    ]
    scratch += scatter_sems(5, nd, nb) + [pltpu.SemaphoreType.DMA((levels + nb,))] * 2
    return pl.pallas_call(
        kernel,
        out_shape=[
            jax.ShapeDtypeStruct((rows, width), F32),
            jax.ShapeDtypeStruct((r, 3 * width), F32),
            jax.ShapeDtypeStruct((r, width), F32),
            jax.ShapeDtypeStruct((r, ff), F32),
            jax.ShapeDtypeStruct((r_ff, width), F32),
            jax.ShapeDtypeStruct((16, 128), F32),
        ],
        in_specs=[HBM] * 8 + [VMEM] * 5,
        out_specs=[VMEM] * 6,
        scratch_shapes=scratch,
        compiler_params=params(62, 3),
    )(dw_down, dw_in, dw_out, tok, w_qkv, kaug_in, v_in, qaug_in, lse, exact_in, gctx, resid_grad, sums)


def body(
    tokens,
    segment,
    w_qkv,
    bias_query,
    bias_value,
    w_out,
    bias_out,
    gain_attn,
    shift_attn,
    w_in,
    bias_in,
    w_down,
    bias_down,
    gain_ffn,
    shift_ffn,
    cotangent,
):
    nd, nb, nc = lax.axis_size("dp"), lax.axis_size("blk"), lax.axis_size("head")
    n_dev = nd * nb * nc
    d_idx, b_idx, c_idx = lax.axis_index("dp"), lax.axis_index("blk"), lax.axis_index("head")
    me = (d_idx * nb + b_idx) * nc + c_idx
    seqs, rows, width = tokens.shape
    ff = w_in.shape[1]
    half_w = width // nc
    qlen = nc * rows
    r = w_qkv.shape[0]
    r_ff = w_down.shape[0]
    flat_in = tokens.reshape(rows, width)
    cot = cotangent.reshape(rows, width)
    vectors = [bias_query, bias_value, bias_out, gain_attn, shift_attn, bias_down, gain_ffn, shift_ffn]
    if nb * qlen <= 2048 and r % 8 == 0 and ff // width <= 8:
        small = pack_vectors(vectors, bias_in)
        ctx2, vecs, full_bin, lse, exact, f_qkv, tok_all, f_out, f_in, f_down, kaug, v_all, qaug = front(
            small, w_qkv, flat_in, w_out, w_in, w_down, segment, nd, nb, nc
        )
        out, resid_grad, gctx2, dw_down, dw_in, dw_out, sums = feed_forward(
            ctx2, flat_in, cot, vecs, full_bin, f_out, f_in, f_down
        )
        g_tok, o_qkv, o_out, o_in, o_down, g_small = back(
            dw_down.reshape(nd * nb, nc, r_ff, width),
            dw_in.reshape(nd * nb, nc, r, ff),
            dw_out.reshape(nd * nb, nc, r, width),
            tok_all, f_qkv, kaug, v_all, qaug, lse, exact, gctx2, resid_grad, sums, nd, nb, nc,
        )
        g_bq, g_bv, g_bo, g_g1, g_s1, g_bd, g_g2, g_s2 = (g_small[i, :r] for i in range(8))
        return (
            out.reshape(seqs, rows, width), g_tok.reshape(seqs, rows, width),
            o_qkv, g_bq, g_bv, o_out, g_bo, g_g1, g_s1, o_in, g_small[8, :r_ff], o_down, g_bd, g_g2, g_s2,
        )
    packed = jnp.concatenate(vectors + [bias_in])
    used = packed.shape[0]
    lanes = -(-used // 128) * 128
    packed = jnp.broadcast_to(jnp.pad(packed, (0, lanes - used))[None], (8, lanes))
    n4 = 4
    parts = [flat_in[i * (rows // n4):(i + 1) * (rows // n4)] for i in range(n4)]
    shards = [packed, w_qkv] + parts + [w_out, w_in, w_down]
    narrow = [False, False] + [True] * n4 + [False] * 3
    keys = [(-1, 3, 3), (0, 3, 3), (7, 9, 0), (10, 9, 0), (13, 9, 0), (16, 9, 0), (2, 4, 4), (9, 6, 5), (22, 6, 5)]
    small, g_qkv, t0, t1, t2, t3, g_out, g_in, g_down = gather_all(shards, narrow, keys, nd, nb, nc)
    full_small = small[:, 0, :used]
    vecs = full_small[:, :8 * r].reshape(n_dev, 8, r).transpose(1, 0, 2).reshape(8, width).astype(F32)
    full_bin = full_small[:, 8 * r:].reshape(ff).astype(F32)
    bq, bv, bout, gain_one, shift_one, bdown, gain_two, shift_two = (vecs[i] for i in range(8))
    full_qkv = g_qkv.reshape(width, 3 * width)
    full_wout = g_out.reshape(width, width)
    full_win = g_in.reshape(width, ff)
    full_wdown = g_down.reshape(ff, width)
    tok_all = jnp.stack([t0, t1, t2, t3], axis=1).reshape(nb * qlen, width)
    my_bias = lax.dynamic_slice(vecs, (0, c_idx * half_w), (2, half_w))
    ctx, kaug, v_scr, qaug, lse, exact = attend_forward(tok_all, full_qkv, my_bias, segment, qlen, half_w)
    context_low = ctx.reshape(seqs, qlen, 1, half_w)
    back_tokens = lax.all_to_all(context_low, "head", split_axis=1, concat_axis=2, tiled=True)
    ctx2 = back_tokens.reshape(rows, nc, half_w).transpose(1, 0, 2)
    out, grad_resid_one, gctx2, dw_down, dw_in, dw_out, sums = feed_forward(
        ctx2, flat_in, cot, vecs, full_bin.reshape(1, ff), full_wout, full_win, full_wdown
    )
    output = out.reshape(seqs, rows, width)
    grad_context = gctx2.transpose(1, 0, 2)
    grad_headed = lax.all_to_all(
        grad_context.reshape(seqs, rows, nc, half_w), "head", split_axis=2, concat_axis=1, tiled=True
    )
    gctx = grad_headed.reshape(qlen, half_w)
    tok_mine = lax.dynamic_slice(tok_all, (b_idx * qlen, 0), (qlen, width))
    dtok, dw, dbias = attend_backward(tok_all, tok_mine, full_qkv, qaug, kaug, v_scr, lse, exact, gctx)
    dw = dw.astype(BF16).reshape(nd * nb, nc, r, 3 * half_w)
    ours = lax.dynamic_index_in_dim(dw, c_idx, 1, keepdims=False)
    theirs = lax.dynamic_index_in_dim(dw, 1 - c_idx, 1, keepdims=False)
    joined_full = jnp.stack([ours, ours], axis=1)
    sums = lax.dynamic_update_slice(sums, dbias, (0, c_idx * half_w))
    o_down, o_in, o_out, o_tok, o_qkv, total = scatter_all(
        [
            dw_down.reshape(n_dev, r_ff, width),
            dw_in.reshape(n_dev, r, ff),
            dw_out.reshape(n_dev, r, width),
            dtok.reshape(nb * nc, rows, width),
            (joined_full, theirs),
        ],
        [False, False, False, True, False],
        [False, False, False, False, True],
        sums,
        nd,
        nb,
        nc,
    )
    grad_tokens = (grad_resid_one + o_tok).reshape(seqs, rows, width)
    o_qkv = o_qkv.reshape(2, r, 3, half_w).transpose(1, 2, 0, 3).reshape(r, 3 * width)
    mine = lax.dynamic_slice(total, (0, me * r), (8, r))
    mine_in = lax.dynamic_slice(total[8:8 + ff // width].reshape(ff), (me * r_ff,), (r_ff,))
    g_bq, g_bv, g_bo, g_g1, g_s1, g_bd, g_g2, g_s2 = (mine[i] for i in range(8))
    return (
        output,
        grad_tokens,
        o_qkv,
        g_bq,
        g_bv,
        o_out,
        g_bo,
        g_g1,
        g_s1,
        o_in,
        mine_in,
        o_down,
        g_bd,
        g_g2,
        g_s2,
    )


def solution(mesh):
    weight, vector = P(("dp", "blk", "head"), None), P(("dp", "blk", "head"))
    token = P("dp", ("blk", "head"), None)
    return jax.shard_map(
        body,
        mesh=mesh,
        in_specs=(
            token,
            P("dp", None),
            weight,
            vector,
            vector,
            weight,
            vector,
            vector,
            vector,
            weight,
            vector,
            weight,
            vector,
            vector,
            vector,
            token,
        ),
        out_specs=(
            token,
            token,
            weight,
            vector,
            vector,
            weight,
            vector,
            vector,
            vector,
            weight,
            vector,
            weight,
            vector,
            vector,
            vector,
        ),
        check_vma=False,
    )
```

```python
import functools

import jax
import jax.numpy as jnp
from jax import lax
from jax.experimental import pallas as pl
from jax.experimental.pallas import tpu as pltpu
from jax.sharding import PartitionSpec as P

MESH = pl.DeviceIdType.MESH
F32, BF16 = jnp.float32, jnp.bfloat16
HD = 64
HEADS = 12
BIG = 2.0**30

class Net:
    def __init__(self, nd, nb, nc):
        self.nd, self.nb, self.nc = nd, nb, nc
        self.levels = nd.bit_length() - 1
        self.d, self.b, self.c = (lax.axis_index(a) for a in ("dp", "blk", "head"))
        top = self.levels - 1
        self.stride = [(1 - self.c) * 2**k + self.c * 2 ** (top - k) for k in range(self.levels)]
        self.sibling = (self.d, self.b, self.nc - 1 - self.c)
        steps = [s * (1 - 2 * ((self.d // s) % 2)) for s in self.stride]
        self.flipped = [self.d]
        for step in steps:
            self.flipped += [d + step for d in self.flipped]
        self.nearest = [self.find_near(e) for e in range(self.nb)]

    def flips(self, mask):
        return self.flipped[mask]

    def across(self, k):
        return (self.flipped[1 << k], self.b, self.c)

    def near(self, e):
        return self.nearest[e]

    def find_near(self, e):
        order = [sorted(range(self.nb), key=lambda j: (abs(j - i), -j)) for i in range(self.nb)]
        got = order[0][e]
        for i in range(1, self.nb):
            got = jnp.where(self.b == i, order[i][e], got)
        return got

    def near_at(self, e):
        got = self.near(0)
        for i in range(1, self.nb):
            got = jnp.where(e == i, self.near(i), got)
        return got

    def slot(self, mask, blk):
        return (self.flips(mask) * self.nb + blk) * self.nc + self.c

    def peers(self):
        out = [(self.d, (self.b + u) % self.nb, self.c) for u in range(1, self.nb)]
        out += [self.across(k) for k in range(self.levels)]
        return out + [self.sibling]

    def barrier(self):
        bar = pltpu.get_barrier_semaphore()
        ps = self.peers()
        for p in ps:
            pl.semaphore_signal(bar, inc=1, device_id=p, device_id_type=MESH)
        pl.semaphore_wait(bar, len(ps))


def remote(src, dst, send, recv, dev):
    return pltpu.make_async_remote_copy(src_ref=src, dst_ref=dst, send_sem=send, recv_sem=recv, device_id=dev, device_id_type=MESH)


def blocks_of(full):
    return (lambda i: full.at[i]), (lambda k: full.at[pl.ds(0, k)])


def rows_of(full, rows, offset=0, stride=None):
    every = rows if stride is None else stride

    def place(i):
        return full.at[pl.ds(pl.multiple_of(i * every + offset, 8), rows)]

    return place, (lambda k: full.at[pl.ds(0, k * rows)])


class Gather:
    def __init__(self, net, mine, place, span, sems, narrow=False):
        self.net, self.mine, self.place, self.span, self.narrow = net, mine, place, span, narrow
        self.zsend, self.xsend, self.ssend, self.srecv, self.recv = sems

    def at(self, mask, blk):
        n = self.net
        if self.narrow:
            return self.place(blk * n.nc + n.c)
        return self.place(n.slot(mask, blk))

    def rsem(self, mask, blk):
        return self.recv.at[mask * self.net.nb + blk]

    def spread(self, mask, blk, src, dst):
        n = self.net
        if not self.narrow:
            for k in range(n.levels):
                if mask < (1 << k):
                    remote(src, dst, self.xsend, self.rsem(mask + (1 << k), blk), n.across(k)).start()
        remote(src, dst, self.ssend, self.srecv, n.sibling).start()

    def along(self, blk, src, dst):
        n = self.net
        sem = self.rsem(0, blk)

        @pl.when((n.b < n.nb - 1) & (blk <= n.b))
        def _():
            remote(src, dst, self.zsend, sem, (n.d, n.b + 1, n.c)).start()

        @pl.when((n.b > 0) & (blk >= n.b))
        def _():
            remote(src, dst, self.zsend, sem, (n.d, n.b - 1, n.c)).start()

    def own_line(self):
        self.along(self.net.b, self.mine, self.at(0, self.net.b))

    def own_spread(self):
        self.spread(0, self.net.b, self.mine, self.at(0, self.net.b))

    def z(self, e):
        blk = self.net.near(e)
        dst = self.at(0, blk)
        pltpu.make_async_copy(dst, dst, self.rsem(0, blk)).wait()
        self.along(blk, dst, dst)
        self.spread(0, blk, dst, dst)

    def x(self, mask, e):
        n = self.net
        blk = n.near(e)
        dst = self.at(mask, blk)
        pltpu.make_async_copy(dst, dst, self.rsem(mask, blk)).wait()
        self.spread(mask, blk, dst, dst)

    def own(self, sem):
        n = self.net
        return pltpu.make_async_copy(self.mine, self.at(0, n.b), sem)

    def wait_sibling(self):
        n = self.net
        half = self.span(n.nb if self.narrow else n.nd * n.nb)
        pltpu.make_async_copy(half, half, self.srecv).wait()

    def drain(self):
        n = self.net
        half = self.span(n.nb if self.narrow else n.nd * n.nb)
        pltpu.make_async_copy(half, half, self.ssend).wait()
        if not self.narrow:
            part = self.span((n.nd - 1) * n.nb)
            pltpu.make_async_copy(part, part, self.xsend).wait()
        edge = (n.b == 0) | (n.b == n.nb - 1)

        @pl.when(edge)
        def _():
            one = self.span(1)
            pltpu.make_async_copy(one, one, self.zsend).wait()

        @pl.when(jnp.logical_not(edge))
        def _():
            many = self.span(n.nb + 1)
            pltpu.make_async_copy(many, many, self.zsend).wait()


def gather_sems(n_pieces, nd, nb):
    return [pltpu.SemaphoreType.DMA((n_pieces, 4)), pltpu.SemaphoreType.DMA((n_pieces, nd * nb)), pltpu.SemaphoreType.DMA]


class Scatter:
    def __init__(self, net, parts, place, theirs, landing, span, xrecv, zrecv, out, sems, narrow=False, extra=(), early=False):
        self.net, self.parts, self.place, self.theirs, self.landing = net, parts, place, theirs, landing
        self.span, self.xbuf, self.zbuf, self.out, self.extra = span, xrecv, zrecv, out, extra
        self.sib_send, self.x_send, self.z_send, self.sib_sem, self.x_sem, self.z_sem = sems
        self.narrow, self.seen, self.early = narrow, set(), early
        self.nd = 1 if narrow else net.nd
        self.levels = 0 if narrow else net.levels

    def home(self, mask):
        return 0 if self.narrow else self.net.flips(mask)

    def start(self):
        for mask in range(self.nd - 1, -1, -1):
            self.start_home(self.home(mask))

    def start_home(self, d):
        for blk in range(self.net.nb):
            self.send(d * self.net.nb + blk, d)

    def send(self, at, sem):
        remote(self.theirs(at), self.landing(at), self.sib_send, self.sib_sem.at[sem], self.net.sibling).start()

    def arrived(self, sem, count):
        some = self.span(count)
        pltpu.make_async_copy(some, some, self.sib_sem.at[sem]).wait()

    def sent(self):
        some = self.span(self.nd * self.net.nb)
        pltpu.make_async_copy(some, some, self.sib_send).wait()

    def x_at(self, k, mask, blk):
        return ((1 << k) - 1 + mask) * self.net.nb + blk

    def z_at(self, side, blk, owner):
        return blk + side * jnp.where(blk == owner, self.net.nb - blk, 0)

    def add(self, at, more, to, extra=()):
        for pick, places in self.parts(at):
            def chosen(ref):
                return ref if pick is None else ref.at[pick]

            add_up(places + [chosen(m) for m in more] + list(extra), chosen(to))

    def reduce(self, mask, e):
        n = self.net
        blk = n.near(e)
        if self.narrow:
            self.arrived(blk, 1)
        elif mask not in self.seen:
            self.seen.add(mask)
            self.arrived(self.home(mask), n.nb)
        at = self.home(mask) * n.nb + blk
        place = self.place(at)
        more = []
        for k in range(self.levels - 1, -1, -1):
            if mask < (1 << k):
                i = self.x_at(k, mask, blk)
                got = self.xbuf.at[i]
                pltpu.make_async_copy(got, got, self.x_sem.at[i]).wait()
                more.append(got)
        if mask:
            k = mask.bit_length() - 1
            self.add(at, more, place)
            i = self.x_at(k, mask - (1 << k), blk)
            remote(place, self.xbuf.at[i], self.x_send, self.x_sem.at[i], n.across(k)).start()
            return

        def line(side, there):
            i = self.z_at(side, blk, n.b)
            got = self.zbuf.at[i]

            @pl.when(there)
            def _():
                pltpu.make_async_copy(got, got, self.z_sem.at[i]).wait()

            more.append(got)

        if e == 0:
            line(0, n.b > 0)
            line(1, n.b < n.nb - 1)
            self.add(at, more, self.out, self.extra)
            return
        side = jnp.where(blk > n.b, 0, 1)
        line(side, jnp.where(blk > n.b, n.b, n.nb - 1 - n.b) > 0)
        self.add(at, more, place)
        to = n.b + 1 - 2 * side
        i = self.z_at(side, blk, to)
        remote(place, self.zbuf.at[i], self.z_send, self.z_sem.at[i], (n.d, to, n.c)).start()

    def clear_edges(self):
        n = self.net

        def clear(i, carry):
            self.zbuf[i] = jnp.zeros(self.zbuf.shape[1:], self.zbuf.dtype)
            return carry

        @pl.when(n.b == 0)
        def _():
            lax.fori_loop(0, n.nb, clear, 0)

        @pl.when(n.b == n.nb - 1)
        def _():
            lax.fori_loop(0, n.nb - 1, clear, 0)
            clear(n.nb, 0)

    def drain(self):
        n = self.net
        if not self.early:
            self.sent()
        if not self.narrow:
            some = self.xbuf.at[pl.ds(0, (n.nd - 1) * n.nb)]
            pltpu.make_async_copy(some, some, self.x_send).wait()
        some = self.zbuf.at[pl.ds(0, n.nb - 1)]
        pltpu.make_async_copy(some, some, self.z_send).wait()


def add_up(terms, to):
    shape = to.shape
    rows = shape[-2]
    step = rows
    while step % 2 == 0 and step > 32:
        step //= 2
    lead = [()] if len(shape) == 2 else [(g,) for g in range(shape[0])]
    for g in lead:
        for r in range(0, rows, step):
            at = g + (slice(r, r + step),)
            total = terms[0][at].astype(F32)
            for t in terms[1:]:
                total = total + t[at].astype(F32)
            to[at] = total.astype(to.dtype)


class AllSum:
    def __init__(self, net, value, got, send, recv):
        self.net, self.value, self.got, self.send, self.recv = net, value, got, send, recv

    def copy(self, stage, dev, src, slot):
        return remote(self.value.at[src], self.got.at[slot], self.send.at[slot], self.recv.at[slot], dev)

    def stages(self):
        n = self.net
        devs = [n.sibling] + [n.across(k) for k in range(n.levels)]
        steps = []
        for i, dev in enumerate(devs):
            steps.append(functools.partial(self.one, i, dev))
        steps.append(self.line_start)
        steps.append(self.line_end)
        return [lambda: self.copy(0, devs[0], 0, 0).start()] + steps

    def one(self, i, dev):
        n = self.net
        self.copy(i, dev, i, i).wait()
        self.value[i + 1] = self.value[i] + self.got[i]
        if i + 1 <= n.levels:
            self.copy(i + 1, n.across(i), i + 1, i + 1).start()

    def line_copy(self, u):
        n = self.net
        return self.copy(None, (n.d, (n.b + u) % n.nb, n.c), n.levels + 1, n.levels + u)

    def line_start(self):
        for u in range(1, self.net.nb):
            self.line_copy(u).start()

    def line_end(self):
        n = self.net
        for u in range(1, n.nb):
            self.line_copy(u).wait()
        total = self.value[n.levels + 1]
        for u in range(1, n.nb):
            total = total + self.got[n.levels + u]
        self.value[0] = total


def scatter_sems(n_pieces, nd, nb):
    return [
        pltpu.SemaphoreType.DMA((n_pieces, 3)),
        pltpu.SemaphoreType.DMA((n_pieces, max(nd, nb))),
        pltpu.SemaphoreType.DMA((n_pieces, (nd - 1) * nb)),
        pltpu.SemaphoreType.DMA((n_pieces, nb + 1)),
    ]


def dot(a, b, dims=((1,), (0,))):
    return lax.dot_general(a, b, (dims, ((), ())), preferred_element_type=F32)


def mask_lanes(seg_row, count):
    lanes = lax.broadcasted_iota(jnp.int32, (128, count), 0)
    return jnp.transpose(jnp.where(lanes == seg_row, -1.0, 0.0).astype(F32), (1, 0))


def project_keys(i, step, tok, wk, wv, bias_v, seg, kaug, v_scr):
    at = pl.ds(pl.multiple_of(i * step, step), step)
    piece = tok[at, :]
    keys = dot(piece, wk).astype(BF16)
    vals = (dot(piece, wv) + bias_v).astype(BF16)
    lanes = mask_lanes(seg[:, at], step).astype(BF16)
    for p in range(kaug.shape[0]):
        kaug[p, at, 0:128] = keys[:, p * 128:(p + 1) * 128]
        kaug[p, at, 128:256] = lanes
        v_scr[p, at, :] = vals[:, p * 128:(p + 1) * 128]


def project_queries(tok, wq, bias_q, seg, qaug, blk, qlen):
    mine = pl.ds(pl.multiple_of(blk * qlen, qlen), qlen)
    query = (dot(tok[mine, :], wq) + bias_q).astype(BF16)
    lane = lax.broadcasted_iota(jnp.int32, (qlen, 128), 1)
    feat = jnp.where(lane < 8, BIG * (1.0 + mask_lanes(seg[:, mine], qlen)), 0.0).astype(BF16)
    for p in range(qaug.shape[0] // 2):
        q_pair = query[:, p * 128:(p + 1) * 128].astype(F32) * HD**-0.5
        for half in range(2):
            keep = (lane >= 64) if half else (lane < 64)
            qaug[2 * p + half, :, 0:128] = jnp.where(keep, q_pair, 0.0).astype(BF16)
            qaug[2 * p + half, :, 128:256] = feat


def attend_chunk(i, qaug, kaug, v_scr, o_scr, exact_scr, lse_scr, chunk, per_head):
    h = i // per_head
    at = pl.ds(pl.multiple_of((i % per_head) * chunk, chunk), chunk)
    s = dot(qaug[h, at, :], kaug[h // 2], ((1,), (1,)))
    top = jnp.max(s, axis=-1, keepdims=True)
    p = jnp.exp(s - top)
    total = jnp.sum(p, axis=-1, keepdims=True)
    low = p.astype(BF16)
    rest = (p - low.astype(F32)).astype(BF16)
    value = v_scr[h // 2]
    o = dot(low, value)
    inverse = 1.0 / total
    o_scr[h, at, :] = o * inverse
    exact_scr[h, at, :] = (o + dot(rest, value)) * inverse
    lse_scr[h, at, :] = jnp.broadcast_to(top + jnp.log(total), (chunk, 128))


def join_heads(scr, p, at=slice(None)):
    first, second = scr[2 * p, at, :], scr[2 * p + 1, at, :]
    lane = lax.broadcasted_iota(jnp.int32, first.shape, 1)
    return jnp.where(lane < 64, first, second)


def head_columns(w, part, c, width):
    return w[:, pl.ds(pl.multiple_of((part * 2 + c) * width, 128), width)]


def fwd_kernel(tok, w, bias, seg, ctx, kaug, v_scr, qaug, lse_out, exact, lse_scr, o_scr, exact_scr, chunk=256):
    blk, c = lax.axis_index("blk"), lax.axis_index("head")
    qlen, width = ctx.shape
    total = tok.shape[0]
    step = min(512, total)
    wk, wv = head_columns(w, 1, c, width), head_columns(w, 2, c, width)

    def rows(i, carry):
        project_keys(i, step, tok, wk, wv, bias[1:2, :], seg, kaug, v_scr)
        return carry

    lax.fori_loop(0, total // step, rows, 0)
    project_queries(tok, head_columns(w, 0, c, width), bias[0:1, :], seg, qaug, blk, qlen)
    per_head = qlen // chunk

    def go(i, carry):
        attend_chunk(i, qaug, kaug, v_scr, o_scr, exact_scr, lse_scr, chunk, per_head)
        return carry

    lax.fori_loop(0, (width // HD) * per_head, go, 0)
    finish_forward(o_scr, exact_scr, lse_scr, lambda p, v: store_lanes(ctx, p, v), lse_out, exact)


def store_lanes(ref, p, value):
    ref[:, p * 128:(p + 1) * 128] = value


def finish_forward(o_scr, exact_scr, lse_scr, put, lse_out, exact):
    for p in range(o_scr.shape[0] // 2):
        put(p, join_heads(o_scr, p).astype(BF16))
        exact[p] = join_heads(exact_scr, p)
    for h in range(o_scr.shape[0]):
        lse_out[h] = jnp.transpose(lse_scr[h], (1, 0))[0:8, :]


def prepare_backward(gctx_of, exact, do_m, delta_row):
    pairs, qlen, _ = exact.shape
    lane = lax.broadcasted_iota(jnp.int32, (qlen, 128), 1)
    for p in range(pairs):
        grad = gctx_of(p)
        product = grad.astype(F32) * exact[p]
        for half in range(2):
            keep = (lane >= 64) if half else (lane < 64)
            do_m[2 * p + half] = jnp.where(keep, grad, jnp.zeros_like(grad))
            across = jnp.transpose(jnp.where(keep, product, 0.0), (1, 0))
            delta_row[2 * p + half] = jnp.broadcast_to(jnp.sum(across, axis=0, keepdims=True), (8, qlen))


def bwd_pair(pair, qaug, k_part, v_part, do_m, lse_row, delta_row, dq_scr, put, first, qs=slice(None)):
    dk = dv = None
    for half in range(2):
        h = 2 * pair + half
        q_part, do_part = qaug[h, qs, :], do_m[h, qs, :]
        s = dot(k_part, q_part, ((1,), (1,)))
        p = jnp.exp(s - lse_row[h, 0:1, qs])
        dp = dot(v_part, do_part, ((1,), (1,)))
        ds = (p * (dp - delta_row[h, 0:1, qs])).astype(BF16)
        v_term = dot(p.astype(BF16), do_part)
        k_term = dot(ds, q_part[:, 0:128])
        dv = v_term if dv is None else dv + v_term
        dk = k_term if dk is None else dk + k_term
        dq = dot(k_part[:, 0:128], ds, ((0,), (0,)))
        if first is None:
            dq_scr[h, :, qs] += dq
        else:
            dq_scr[h, :, qs] = jnp.where(first, dq, dq_scr[h, :, qs] + dq)
    put(dk, dv)


def join_dq(dq_scr, p):
    qlen = dq_scr.shape[2]
    lane = lax.broadcasted_iota(jnp.int32, (qlen, 128), 1)
    first, second = jnp.transpose(dq_scr[2 * p], (1, 0)), jnp.transpose(dq_scr[2 * p + 1], (1, 0))
    return (jnp.where(lane < 64, first, second) * HD**-0.5).astype(BF16)


VMEM = pl.BlockSpec(memory_space=pltpu.VMEM)
HBM = pl.BlockSpec(memory_space=pltpu.HBM)


def params(limit, collective=None):
    more = {} if collective is None else dict(collective_id=collective, has_side_effects=True)
    return pltpu.CompilerParams(vmem_limit_bytes=limit << 20, **more)


def lane_mean(x):
    return jnp.mean(x, axis=-1, keepdims=True)


def norm_parts(hidden):
    centered = hidden - lane_mean(hidden)
    scale = lax.rsqrt(lane_mean(centered * centered) + 1e-12)
    return centered * scale, scale


def norm_back(grad, unit, scale, gain):
    scaled = grad * gain
    return scale * (scaled - lane_mean(scaled) - unit * lane_mean(scaled * unit))


def gelu_and_slope(pre):
    cdf = 0.5 * (1.0 + lax.erf(pre * 0.7071067811865476))
    return pre * cdf, cdf + pre * (0.3989422804014327 * jnp.exp(-0.5 * pre * pre))


def column_sum(x):
    return jnp.sum(x, axis=0, keepdims=True)


def ffn_kernel(
    ctx, tok, cot, vecs, bias_in, w_out_h, w_in_h, w_down_h,
    out, resid_grad, gctx, dw_down_h, dw_in_h, dw_out_h, sums,
    w_out, w_in, w_down, act, slope, dw_a, dw_b, dw_c, in_sem, out_sem,
):
    groups, rows, half = ctx.shape
    width, ff = w_in.shape
    step = width
    loads = [
        pltpu.make_async_copy(src, dst, in_sem.at[i])
        for i, (src, dst) in enumerate([(w_out_h, w_out), (w_in_h, w_in), (w_down_h, w_down)])
    ]
    for load in loads:
        load.start()
    bias_out, gain_one, shift_one = vecs[2:3, :], vecs[3:4, :], vecs[4:5, :]
    bias_down, gain_two, shift_two = vecs[5:6, :], vecs[6:7, :], vecs[7:8, :]
    context = jnp.concatenate([ctx[g] for g in range(groups)], axis=1)
    loads[0].wait()
    resid_one = tok[...].astype(F32) + (dot(context, w_out[...]) + bias_out)
    unit_one, scale_one = norm_parts(resid_one)
    normed = unit_one * gain_one + shift_one
    normed_low = normed.astype(BF16)
    loads[1].wait()
    chunks = [slice(i, i + step) for i in range(0, ff, step)]
    for at in chunks:
        pre = dot(normed_low, w_in[:, at]) + bias_in[0:1, at]
        value, grad = gelu_and_slope(pre)
        act[:, at] = value.astype(BF16)
        slope[:, at] = grad
    loads[2].wait()
    resid_two = normed + (dot(act[...], w_down[...]) + bias_down)
    unit_two, scale_two = norm_parts(resid_two)
    out[...] = (unit_two * gain_two + shift_two).astype(BF16)
    grad_out = cot[...].astype(F32)
    grad_two = norm_back(grad_out, unit_two, scale_two, gain_two)
    grad_ffn = grad_two.astype(BF16)
    sums[0:2, :] = jnp.zeros((2, width), F32)
    sums[5:6, :] = column_sum(grad_ffn.astype(F32))
    sums[6:7, :] = column_sum(grad_out * unit_two)
    sums[7:8, :] = column_sum(grad_out)
    stores = []

    def store(src, dst):
        copy = pltpu.make_async_copy(src, dst, out_sem.at[len(stores)])
        copy.start()
        stores.append(copy)

    for at in chunks:
        dw_a[at, :] = dot(act[:, at], grad_ffn, ((0,), (0,))).astype(BF16)
        store(dw_a.at[at], dw_down_h.at[at])
    grad_normed = grad_two
    for i, at in enumerate(chunks):
        grad_act = dot(grad_ffn, w_down[at, :], ((1,), (1,)))
        grad_pre = (grad_act * slope[:, at]).astype(BF16)
        sums[8 + i:9 + i, :] = column_sum(grad_pre.astype(F32))
        dw_b[:, at] = dot(normed_low, grad_pre, ((0,), (0,))).astype(BF16)
        grad_normed = grad_normed + dot(grad_pre, w_in[:, at], ((1,), (1,)))
    store(dw_b, dw_in_h)
    sums[8 + len(chunks):, :] = jnp.zeros((sums.shape[0] - 8 - len(chunks), width), F32)
    sums[3:4, :] = column_sum(grad_normed * unit_one)
    sums[4:5, :] = column_sum(grad_normed)
    grad_one = norm_back(grad_normed, unit_one, scale_one, gain_one)
    resid_grad[...] = grad_one
    grad_attn = grad_one.astype(BF16)
    sums[2:3, :] = column_sum(grad_attn.astype(F32))
    dw_c[...] = dot(context, grad_attn, ((0,), (0,))).astype(BF16)
    store(dw_c, dw_out_h)
    grad_context = dot(grad_attn, w_out[...], ((1,), (1,))).astype(BF16)
    for g in range(groups):
        gctx[g] = grad_context[:, g * half:(g + 1) * half]
    for copy in stores:
        copy.wait()


def feed_forward(ctx, tok, cot, vecs, bias_in, w_out, w_in, w_down):
    groups, rows, half = ctx.shape
    width, ff = w_in.shape
    n_sums = 8 + -(-(ff // width) // 8) * 8
    return pl.pallas_call(
        ffn_kernel,
        out_shape=[
            jax.ShapeDtypeStruct((rows, width), BF16),
            jax.ShapeDtypeStruct((rows, width), F32),
            jax.ShapeDtypeStruct((groups, rows, half), BF16),
            jax.ShapeDtypeStruct((ff, width), BF16),
            jax.ShapeDtypeStruct((width, ff), BF16),
            jax.ShapeDtypeStruct((width, width), BF16),
            jax.ShapeDtypeStruct((n_sums, width), F32),
        ],
        in_specs=[VMEM] * 5 + [HBM] * 3,
        out_specs=[VMEM] * 3 + [HBM] * 3 + [VMEM],
        scratch_shapes=[
            pltpu.VMEM((width, width), BF16),
            pltpu.VMEM((width, ff), BF16),
            pltpu.VMEM((ff, width), BF16),
            pltpu.VMEM((rows, ff), BF16),
            pltpu.VMEM((rows, ff), F32),
            pltpu.VMEM((ff, width), BF16),
            pltpu.VMEM((width, ff), BF16),
            pltpu.VMEM((width, width), BF16),
            pltpu.SemaphoreType.DMA((3,)),
            pltpu.SemaphoreType.DMA((ff // width + 2,)),
        ],
        compiler_params=params(56),
    )(ctx, tok, cot, vecs, bias_in, w_out, w_in, w_down)


def gather_order(keys, narrow, nd, nb):
    events = []
    for p, (begin, dz, dx) in enumerate(keys):
        for e in range(nb):
            events.append((begin + e * dz, ("z", p, e)))
            if not narrow[p]:
                for mask in range(1, nd):
                    events.append((begin + e * dz + dx * mask.bit_length(), ("x", p, mask, e)))
    events.sort(key=lambda q: q[0])
    return [ev for _, ev in events]


def gather_all(shards, narrow, keys, nd, nb, nc):
    count = len(shards)

    def kernel(*refs):
        mine, full = refs[:count], refs[count:2 * count]
        four, recv, own_sem = refs[2 * count:]
        net = Net(nd, nb, nc)
        pieces = [
            Gather(net, mine[p], *blocks_of(full[p]), [four.at[p, i] for i in range(4)] + [recv.at[p]], narrow[p]) for p in range(count)
        ]
        net.barrier()
        for ev in gather_order(keys, narrow, nd, nb):
            if ev[0] == "z" and ev[2] == 0:
                pieces[ev[1]].own_line()
                pieces[ev[1]].own_spread()
            elif ev[0] == "z":
                pieces[ev[1]].z(ev[2])
            else:
                pieces[ev[1]].x(ev[2], ev[3])
        for piece in pieces:
            own = piece.own(own_sem)
            own.start()
            own.wait()
        for piece in pieces:
            piece.wait_sibling()
        for piece in pieces:
            piece.drain()

    outs = [
        jax.ShapeDtypeStruct(((nb * nc if thin else nd * nb * nc),) + s.shape, s.dtype) for s, thin in zip(shards, narrow)
    ]
    return pl.pallas_call(
        kernel,
        out_shape=outs,
        in_specs=[VMEM] * count,
        out_specs=[HBM] * count,
        scratch_shapes=gather_sems(count, nd, nb),
        compiler_params=params(56, 0),
    )(*shards)


def attend_forward(tok, w, bias, seg, qlen, width):
    total = tok.shape[0]
    heads = width // HD
    chunk = min(256, qlen)
    while chunk * total > 256 * 4096:
        chunk //= 2
    return pl.pallas_call(
        functools.partial(fwd_kernel, chunk=chunk),
        out_shape=[
            jax.ShapeDtypeStruct((qlen, width), BF16),
            jax.ShapeDtypeStruct((width // 128, total, 256), BF16),
            jax.ShapeDtypeStruct((width // 128, total, 128), BF16),
            jax.ShapeDtypeStruct((heads, qlen, 256), BF16),
            jax.ShapeDtypeStruct((heads, 8, qlen), F32),
            jax.ShapeDtypeStruct((heads // 2, qlen, 128), F32),
        ],
        in_specs=[VMEM] * 4,
        out_specs=[VMEM] * 6,
        scratch_shapes=[pltpu.VMEM((heads, qlen, 128), F32)] * 3,
        compiler_params=params(58),
    )(tok, w, bias, seg)


def pair_bwd_kernel(qaug, kaug, v_scr, lse, exact, gctx, dk, dv, dq, do_m, delta_row, dq_scr):
    step = pl.program_id(1)

    @pl.when(step == 0)
    def _():
        prepare_backward(lambda p: gctx[...], exact, do_m, delta_row)

    def put(k_term, v_term):
        dk[...] = k_term.astype(BF16)
        dv[...] = v_term.astype(BF16)

    bwd_pair(0, qaug, kaug[0], v_scr[0], do_m, lse, delta_row, dq_scr, put, step == 0)

    @pl.when(step == pl.num_programs(1) - 1)
    def _():
        dq[...] = join_dq(dq_scr, 0)


def finish_kernel(tok, dk, dv, tok_mine, dq, w, dtok, dw, dbias, own):
    i, c = pl.program_id(0), lax.axis_index("head")
    blk = lax.axis_index("blk")
    step, width = dk.shape
    qlen = dq.shape[0]

    def cols(part):
        return w[:, pl.ds(pl.multiple_of((part * 2 + c) * width, 128), width)]

    piece, grad_k, grad_v = tok[...], dk[...], dv[...]

    @pl.when(i == 0)
    def _():
        dw[:, 0:width] = dot(tok_mine[...], dq[...], ((0,), (0,)))
        dw[:, width:3 * width] = jnp.zeros((dw.shape[0], 2 * width), F32)
        dbias[0:1, :] = jnp.sum(dq[...].astype(F32), axis=0, keepdims=True)
        dbias[1:2, :] = jnp.zeros((1, width), F32)
        own[...] = dot(dq[...], cols(0), ((1,), (1,)))

    dw[:, width:2 * width] += dot(piece, grad_k, ((0,), (0,)))
    dw[:, 2 * width:3 * width] += dot(piece, grad_v, ((0,), (0,)))
    dbias[1:2, :] += jnp.sum(grad_v.astype(F32), axis=0, keepdims=True)
    grad = dot(grad_k, cols(1), ((1,), (1,))) + dot(grad_v, cols(2), ((1,), (1,)))
    per = qlen // step
    mine = i // per == blk
    at = pl.ds(pl.multiple_of((i % per) * step, step), step)
    dtok[...] = (grad + jnp.where(mine, own[at, :], 0.0)).astype(BF16)


def attend_backward(tok, tok_mine, w, qaug, kaug, v_scr, lse, exact, gctx):
    heads, qlen, _ = qaug.shape
    total, d_model = tok.shape
    width = heads * HD
    kc = min(512, total)
    dk, dv, dq = pl.pallas_call(
        pair_bwd_kernel,
        grid=(heads // 2, total // kc),
        out_shape=[
            jax.ShapeDtypeStruct((total, width), BF16),
            jax.ShapeDtypeStruct((total, width), BF16),
            jax.ShapeDtypeStruct((qlen, width), BF16),
        ],
        in_specs=[
            pl.BlockSpec((2, qlen, 256), lambda p, j: (p, 0, 0)),
            pl.BlockSpec((1, kc, 256), lambda p, j: (p, j, 0)),
            pl.BlockSpec((1, kc, 128), lambda p, j: (p, j, 0)),
            pl.BlockSpec((2, 8, qlen), lambda p, j: (p, 0, 0)),
            pl.BlockSpec((1, qlen, 128), lambda p, j: (p, 0, 0)),
            pl.BlockSpec((qlen, 128), lambda p, j: (0, p)),
        ],
        out_specs=[pl.BlockSpec((kc, 128), lambda p, j: (j, p))] * 2 + [pl.BlockSpec((qlen, 128), lambda p, j: (0, p))],
        scratch_shapes=[
            pltpu.VMEM((2, qlen, 128), BF16),
            pltpu.VMEM((2, 8, qlen), F32),
            pltpu.VMEM((2, 128, qlen), F32),
        ],
        compiler_params=params(56),
    )(qaug, kaug, v_scr, lse, exact, gctx)
    step = min(512, qlen)
    whole = lambda i: (0, 0)
    rows = lambda i: (i, 0)
    return pl.pallas_call(
        finish_kernel,
        grid=(total // step,),
        out_shape=[
            jax.ShapeDtypeStruct((total, d_model), BF16),
            jax.ShapeDtypeStruct((d_model, 3 * width), F32),
            jax.ShapeDtypeStruct((2, width), F32),
        ],
        in_specs=[
            pl.BlockSpec((step, d_model), rows),
            pl.BlockSpec((step, width), rows),
            pl.BlockSpec((step, width), rows),
            pl.BlockSpec((qlen, d_model), whole),
            pl.BlockSpec((qlen, width), whole),
            pl.BlockSpec((d_model, w.shape[1]), whole),
        ],
        out_specs=[
            pl.BlockSpec((step, d_model), rows),
            pl.BlockSpec((d_model, 3 * width), whole),
            pl.BlockSpec((2, width), whole),
        ],
        scratch_shapes=[pltpu.VMEM((qlen, d_model), F32)],
        compiler_params=params(56),
    )(tok, dk, dv, tok_mine, dq, w)


SPACE = (0.25, 1.0, 0.2)


def send_blocks(piece, nb):
    for blk in range(nb):
        piece.send(blk, blk)


def scatter_all(arrays, narrow, joined, small, nd, nb, nc):
    count = len(arrays)
    flat = []
    for a, j in zip(arrays, joined):
        flat += list(a) if j else [a]
    n_in = len(flat) + 1

    def kernel(*refs):
        ins, small_in = list(refs[:n_in - 1]), refs[n_in - 1]
        outs, small_out = refs[n_in:n_in + count], refs[n_in + count]
        rest = list(refs[n_in + count + 1:])
        net = Net(nd, nb, nc)
        s3, sib_sem, x_sem, z_sem, sum_send, sum_recv = rest[-6:]
        value, got = rest[-8:-6]
        bufs = rest[:-8]
        pieces = []
        for p in range(count):
            first = ins.pop(0)
            sib = ins.pop(0) if joined[p] else bufs.pop(0)
            xbuf = None if narrow[p] else bufs.pop(0)
            zbuf = bufs.pop(0)
            sems = [s3.at[p, i] for i in range(3)] + [sib_sem.at[p], x_sem.at[p], z_sem.at[p]]
            if joined[p]:
                parts = lambda at, first=first: [(None, [first.at[at]])]
                place = lambda at, first=first: first.at[at]
                theirs = lambda at, sib=sib: sib.at[at]
                landing = lambda at, first=first: first.at[at, net.c]
            else:
                place = lambda at, first=first: first.at[at * nc + net.c]
                parts = lambda at, place=place, sib=sib: [(None, [place(at), sib.at[at]])]
                theirs = lambda at, first=first: first.at[at * nc + nc - 1 - net.c]
                landing = lambda at, sib=sib: sib.at[at]
            span = lambda k, sib=sib: sib.at[pl.ds(0, k)]
            pieces.append(Scatter(net, parts, place, theirs, landing, span, xbuf, zbuf, outs[p], sems, narrow[p]))
        sums = AllSum(net, value, got, sum_send, sum_recv)
        for piece in pieces:
            piece.clear_edges()
        value[0] = small_in[...]
        net.barrier()
        events = []
        for p, piece in enumerate(pieces):
            t = SPACE[0] * p
            begin = functools.partial(send_blocks, piece, nb) if narrow[p] else piece.start
            events.append((t - 0.4, begin))
            for mask in range(piece.nd - 1, -1, -1):
                for e in range(nb - 1, -1, -1):
                    when = t + SPACE[1] * (piece.levels - mask.bit_length()) + SPACE[2] * (nb - 1 - e)
                    events.append((when, functools.partial(piece.reduce, mask, e)))
        for i, s in enumerate(sums.stages()):
            events.append((0.3 * i, s))
        events.sort(key=lambda q: q[0])
        for _, ev in events:
            ev()
        small_out[...] = value[0]
        for piece in pieces:
            piece.drain()

    outs, scratch = [], []
    for a, thin, j in zip(arrays, narrow, joined):
        full = a[0] if j else a
        block = full.shape[1:]
        outs.append(jax.ShapeDtypeStruct(block, F32))
        n_dp = 1 if thin else nd
        if not j:
            scratch.append(pltpu.VMEM((n_dp * nb,) + block, BF16))
        if not thin:
            scratch.append(pltpu.VMEM(((nd - 1) * nb,) + block, BF16))
        scratch.append(pltpu.VMEM((nb + 1,) + block, BF16))
    levels = nd.bit_length() - 1
    scratch += [pltpu.VMEM((levels + 2,) + small.shape, F32), pltpu.VMEM((levels + nb,) + small.shape, F32)]
    scratch += scatter_sems(count, nd, nb)
    scratch += [pltpu.SemaphoreType.DMA((levels + nb,))] * 2
    outs.append(jax.ShapeDtypeStruct(small.shape, F32))
    return pl.pallas_call(
        kernel,
        out_shape=outs,
        in_specs=[VMEM] * n_in,
        out_specs=[VMEM] * (count + 1),
        scratch_shapes=scratch,
        compiler_params=params(60, 1),
    )(*flat, small)


def hand_out(arrays, small, r, r_ff):
    count = len(arrays)

    def kernel(*refs):
        ins, small_in = refs[:count], refs[count]
        outs, vectors, sems = refs[count + 1:2 * count + 1], refs[2 * count + 1:-1], refs[-1]
        copies = [pltpu.make_async_copy(a, b, sems.at[i]) for i, (a, b) in enumerate(zip(ins, outs))]
        for copy in copies:
            copy.start()
        for i, out in enumerate(vectors):
            out[...] = small_in[i, 0:out.shape[0]]
        for copy in copies:
            copy.wait()

    sizes = [r] * 8 + [r_ff]
    return pl.pallas_call(
        kernel,
        out_shape=[jax.ShapeDtypeStruct(a.shape, a.dtype) for a in arrays] + [jax.ShapeDtypeStruct((s,), F32) for s in sizes],
        in_specs=[VMEM] * (count + 1),
        out_specs=[HBM] * count + [VMEM] * 9,
        scratch_shapes=[pltpu.SemaphoreType.DMA((count,))],
        compiler_params=params(60),
    )(*arrays, small)


def unpack_vectors(small, vecs, bias_in, r, r_ff):
    n = small.shape[0]
    width, ff = vecs.shape[1], bias_in.shape[1]

    def gathered(rows, per, count):
        lane = lax.broadcasted_iota(jnp.int32, (8, 128), 1)
        tiles = [jnp.zeros((8, 128), F32) for _ in range(count // 128)]
        for i in range(n):
            piece = small[i, rows, :].astype(F32)
            shift, tile = per * i % 128, per * i // 128
            if shift:
                piece = pltpu.roll(piece, shift, 1)
            if shift + per <= 128:
                tiles[tile] = tiles[tile] + piece
            else:
                tiles[tile] = tiles[tile] + jnp.where(lane >= shift, piece, 0.0)
                tiles[tile + 1] = tiles[tile + 1] + jnp.where(lane < shift, piece, 0.0)
        return tiles

    for t, tile in enumerate(gathered(slice(0, 8), r, width)):
        vecs[:, t * 128:(t + 1) * 128] = tile
    for t, tile in enumerate(gathered(slice(8, 16), r_ff, ff)):
        bias_in[:, t * 128:(t + 1) * 128] = tile[0:1, :]


def pack_vectors(vectors, bias_in):
    shape = (16,) + vectors[0].shape
    row = lax.broadcasted_iota(jnp.int32, shape, 0)
    few = jnp.zeros(shape, BF16)
    for i, v in enumerate(vectors):
        few = jnp.where(row == i, v[None, :], few)
    return few, jnp.broadcast_to(bias_in[None, :], (16,) + bias_in.shape)


FRONT = {
    "small": (2, 55, ((2, 6, 11, 30), (71, 15, 26, 41), (72, 14, 25, 40), (78, 28, 35, 62))),
    "q": (0, 51, ((0, 5, 9, 22), (67, 13, 21, 36), (68, 12, 20, 37), (77, 27, 32, 52))),
    "t0": (29, 23, ((29, 47, 53, 66),)),
    "t1": (49, 65, ((49, 69, 76, 85),)),
    "t2": (3, 61, ((3, 10, 18, 34),)),
    "t3": (4, 82, ((4, 16, 24, 42),)),
    "o": (17, 33, ((17, 31, 44, 48), (45, 39, 58, 63), (46, 38, 57, 64), (56, 54, 70, 73))),
    "i": (80, 43, ((80, 93, 96, 103), (60, 106, 110, 117), (59, 105, 109, 115), (74, 118, 121, 123))),
    "d": (50, 1, ((50, 75, 79, 88), (8, 84, 86, 101), (7, 83, 89, 100), (19, 91, 98, 113))),
    "work": (81, 87, 90, 92, 94, 95, 97, 99, 102, 104, 107, 108, 111, 112, 114, 116, 119, 120, 122, 124),
}


def front_time(nd, nb, kind, what, e=0):
    if (nd, nb) == (4, 4) and (kind != "work" or e == len(FRONT["work"])):
        row = FRONT[kind]
        if kind == "work":
            return row[what]
        if what == "line":
            return row[0]
        if what == "spread":
            return row[1]
        return row[2][what][e]
    first = ["small", "q", "t0", "t1", "t2", "t3", "o", "i", "d"].index(kind) * 10 if kind != "work" else 0
    if kind == "work":
        return (40 if what == 0 else 200) + what
    if what in ("line", "spread"):
        return first
    return first + 3 * e + (4 * what.bit_length() if what else 0)


def front(few, many, w_qkv, tok, w_out, w_in, w_down, seg, nd, nb, nc):
    n = nd * nb * nc
    rows, width = tok.shape
    half, qlen, total = width // nc, nc * rows, nb * nc * rows
    heads = half // HD
    pairs = heads // 2
    r, r_ff, ff = w_qkv.shape[0], w_down.shape[0], w_in.shape[1]
    quarters = 4
    part = rows // quarters
    chunk = min(256, qlen)
    per_head = qlen // chunk
    step = min(512, total)

    def kernel(
        few_in, many_in, q_in, tok_in, o_in, i_in, d_in, seg_in,
        ctx2, vecs, bias_in, lse_out, exact, q_h, tok_h, o_h, i_h, d_h, kaug_h, v_h, qaug_h, tok_t_h,
        small_in, small_all, w_v, tok_v, tok_t, kaug, v_scr, qaug, o_scr, exact_scr, lse_scr, ctx_loc,
        four, recv, own_sem, load_sem, save_sem, swap_sem,
    ):
        net = Net(nd, nb, nc)
        c = net.c
        small_in[...] = jnp.zeros((16, 128), BF16)
        small_in[:, 0:r] = few_in[...]
        row = lax.broadcasted_iota(jnp.int32, (16, r_ff), 0)
        small_in[:, 0:r_ff] = jnp.where(row == 8, many_in[...], small_in[:, 0:r_ff])
        specs = [("small", small_in, blocks_of(small_all), False), ("q", q_in, rows_of(q_h, r), False)]
        for i in range(quarters):
            mine = tok_in.at[pl.ds(i * part, part)]
            specs.append((("t", i), mine, rows_of(tok_h, part, i * part, rows), True))
        specs += [("o", o_in, rows_of(o_h, r), False), ("i", i_in, rows_of(i_h, r), False), ("d", d_in, rows_of(d_h, r_ff), False)]
        piece, own = {}, {}
        for p, (name, mine, (place, span), narrow) in enumerate(specs):
            sems = [four.at[p, i] for i in range(4)] + [recv.at[p]]
            piece[name] = Gather(net, mine, place, span, sems, narrow)
            own[name] = piece[name].own(own_sem.at[p])
        tokens = [("t", i) for i in range(quarters)]
        for name in piece:
            own[name].start()
        net.barrier()

        def unpack():
            piece["small"].wait_sibling()
            own["small"].wait()
            unpack_vectors(small_all, vecs, bias_in, r, r_ff)

        def load():
            copies = []
            for name in ["q"] + tokens:
                piece[name].wait_sibling()
                own[name].wait()
            for k in range(3):
                lanes = pl.ds(pl.multiple_of((k * nc + c) * half, 128), half)
                copies.append(pltpu.make_async_copy(q_h.at[:, lanes], w_v.at[:, pl.ds(k * half, half)], load_sem.at[k]))
            copies.append(pltpu.make_async_copy(tok_h, tok_v, load_sem.at[3]))
            for copy in copies:
                copy.start()
            for copy in copies:
                copy.wait()

        lanes = pl.ds(pl.multiple_of(c * half, 128), half)

        def keys(i):
            project_keys(i, step, tok_v, w_v[:, half:2 * half], w_v[:, 2 * half:3 * half], vecs[1:2, lanes], seg_in, kaug, v_scr)

        saves = [
            pltpu.make_async_copy(src, dst, save_sem.at[i])
            for i, (src, dst) in enumerate([(kaug, kaug_h), (v_scr, v_h), (qaug, qaug_h), (tok_t, tok_t_h)])
        ]

        def queries():
            project_queries(tok_v, w_v[:, 0:half], vecs[0:1, lanes], seg_in, qaug, net.b, qlen)
            tok_t[...] = jnp.transpose(tok_v[...], (1, 0))
            for save in saves:
                save.start()

        swap = remote(ctx_loc.at[nc - 1 - c], ctx2.at[c], swap_sem.at[0], swap_sem.at[1], net.sibling)

        def finish():
            def put(p, value):
                for g in range(nc):
                    ctx_loc[g, :, p * 128:(p + 1) * 128] = value[g * rows:(g + 1) * rows]

            finish_forward(o_scr, exact_scr, lse_scr, put, lse_out, exact)
            swap.start()
            ctx2[c] = ctx_loc[c]

        steps = heads * per_head
        order = []
        for name in piece:
            kind = "t" + str(name[1]) if name in tokens else name
            order.append((front_time(nd, nb, kind, "line"), piece[name].own_line, None))
            order.append((front_time(nd, nb, kind, "spread"), piece[name].own_spread, None))
            for e in range(1, nb):
                order.append((front_time(nd, nb, kind, 0, e), functools.partial(piece[name].z, e), None))
            for mask in range(1, 1 if name in tokens else nd):
                for e in range(nb):
                    order.append((front_time(nd, nb, kind, mask, e), functools.partial(piece[name].x, mask, e), None))
        work = [unpack, load] + [functools.partial(keys, i) for i in range(total // step)] + [queries]
        work += [None] * steps + [finish]
        for i, act in enumerate(work):
            index = i - (len(work) - steps - 1) if act is None else None
            order.append((front_time(nd, nb, "work", i, len(work)), act, index))
        order.sort(key=lambda q: q[0])
        begin = next(i for i, q in enumerate(order) if q[2] == 0)
        end = next(i for i, q in enumerate(order) if q[2] == steps - 1)
        for _, act, _ in order[:begin]:
            act()
        beside = {}
        for _, act, i in order[begin:end + 1]:
            if act is None:
                at_step = i
            else:
                beside.setdefault(at_step, []).append(act)

        def attention(i, carry):
            attend_chunk(i, qaug, kaug, v_scr, o_scr, exact_scr, lse_scr, chunk, per_head)
            for g, acts in beside.items():

                @pl.when(i == g)
                def _(acts=acts):
                    for act in acts:
                        act()

            return carry

        lax.fori_loop(0, steps, attention, 0)
        for _, act, _ in order[end + 1:]:
            act()
        for name in ("o", "i", "d"):
            piece[name].wait_sibling()
            own[name].wait()
        for name in piece:
            piece[name].drain()
        for save in saves:
            save.wait()
        swap.wait()

    count = 5 + quarters
    return pl.pallas_call(
        kernel,
        out_shape=[
            jax.ShapeDtypeStruct((nc, rows, half), BF16),
            jax.ShapeDtypeStruct((8, width), F32),
            jax.ShapeDtypeStruct((1, ff), F32),
            jax.ShapeDtypeStruct((heads, 8, qlen), F32),
            jax.ShapeDtypeStruct((pairs, qlen, 128), F32),
            jax.ShapeDtypeStruct((n * r, 3 * width), BF16),
            jax.ShapeDtypeStruct((total, width), BF16),
            jax.ShapeDtypeStruct((n * r, width), BF16),
            jax.ShapeDtypeStruct((n * r, ff), BF16),
            jax.ShapeDtypeStruct((n * r_ff, width), BF16),
            jax.ShapeDtypeStruct((pairs, total, 256), BF16),
            jax.ShapeDtypeStruct((pairs, total, 128), BF16),
            jax.ShapeDtypeStruct((heads, qlen, 256), BF16),
            jax.ShapeDtypeStruct((width, total), BF16),
        ],
        in_specs=[VMEM] * 8,
        out_specs=[VMEM] * 5 + [HBM] * 9,
        scratch_shapes=[
            pltpu.VMEM((16, 128), BF16),
            pltpu.VMEM((n, 16, 128), BF16),
            pltpu.VMEM((width, 3 * half), BF16),
            pltpu.VMEM((total, width), BF16),
            pltpu.VMEM((width, total), BF16),
            pltpu.VMEM((pairs, total, 256), BF16),
            pltpu.VMEM((pairs, total, 128), BF16),
            pltpu.VMEM((heads, qlen, 256), BF16),
            pltpu.VMEM((heads, qlen, 128), F32),
            pltpu.VMEM((heads, qlen, 128), F32),
            pltpu.VMEM((heads, qlen, 128), F32),
            pltpu.VMEM((nc, rows, half), BF16),
            pltpu.SemaphoreType.DMA((count, 4)),
            pltpu.SemaphoreType.DMA((count, nd * nb)),
            pltpu.SemaphoreType.DMA((count,)),
            pltpu.SemaphoreType.DMA((4,)),
            pltpu.SemaphoreType.DMA((4,)),
            pltpu.SemaphoreType.DMA((2,)),
        ],
        compiler_params=params(56, 2),
    )(few, many, w_qkv, tok, w_out, w_in, w_down, seg)


BACK = {
    "d": (0, ((63, 50, 41, 35), (49, 38, 27, 19), (32, 22, 16, 15), (33, 23, 12, 11))),
    "i": (0, ((103, 94, 89, 78), (81, 77, 66, 57), (72, 64, 53, 43), (73, 65, 54, 44))),
    "o": (0, ((91, 76, 69, 61), (67, 58, 47, 40), (55, 45, 36, 30), (56, 46, 37, 31))),
    "q": (0, ((108, 107, 106, 102), (104, 99, 97, 95), (100, 92, 87, 86), (101, 93, 88, 85))),
    "t": (0, ((96, 79, 70, 52),)),
    "work": (0, 1, 2, 3, 4, 5, 6, 7, 8, 9, 10, 13, 14, 17, 18, 20, 21, 24, 25, 26, 28, 29, 34, 39, 42, 48, 51, 59, 60, 62, 68, 71, 74, 75, 82, 84, 80, 80.1, 83, 90, 98, 98.1, 105),
}


def back_time(nd, nb, kind, what, e=0):
    if (nd, nb) == (4, 4) and (kind != "work" or e == len(BACK["work"])):
        row = BACK[kind]
        if kind == "work":
            return row[what]
        return row[0] if what == "start" else row[1][what][e]
    if kind == "work":
        return 20 + 10 * what + (100 if what > e - 10 else 0)
    first = {"d": 0, "i": 10, "o": 20, "t": 300, "q": 400}[kind]
    if what == "start":
        return first
    return first + 30 - 5 * what.bit_length() + (nb - 1 - e)


def back(
    ctx, tok, cot, vecs, bias_in, w_out, w_in, w_down,
    tok_t_in, w_qkv, kaug_in, v_in, qaug_in, lse, exact_in, nd, nb, nc,
):
    owners = nd * nb
    rows, width = tok.shape
    total = tok_t_in.shape[1]
    ff = w_in.shape[1]
    half, qlen = width // nc, nc * rows
    heads = half // HD
    pairs = heads // 2
    r, r_ff = width // (owners * nc), ff // (owners * nc)
    levels = nd.bit_length() - 1
    names = ["d", "i", "o", "t", "q"]
    chunks = [slice(i, i + width) for i in range(0, ff, width)]
    n_sums = 8 + -(-len(chunks) // 8) * 8

    def kernel(
        ctx_in, tok_in, cot_in, vecs_in, bias_in, wo_h, wi_h, wd_h, tok_t_h, w_h, kaug_h, v_h, qaug_h, lse_row, exact,
        out, g_tok, g_qkv, g_out, g_in, g_down, g_small,
        d_own, i_own, o_own, d_sib, i_sib, o_sib, t_sib, q_sib, d_x, i_x, o_x, q_x, d_z, i_z, o_z, t_z, q_z,
        q_out, resid, gctx, gctx_all, grad_q, value, got,
        load_sem, swap_sem, s3, sib_sem, x_sem, z_sem, sum_send, sum_recv,
    ):
        net = Net(nd, nb, nc)
        c, other = net.c, nc - 1 - net.c
        piece, held = {}, {}
        for p, (name, own, sib, xbuf, zbuf, result) in enumerate(
            [
                ("d", d_own, d_sib, d_x, d_z, g_down),
                ("i", i_own, i_sib, i_x, i_z, g_in),
                ("o", o_own, o_sib, o_x, o_z, g_out),
                ("t", None, t_sib, None, t_z, g_tok),
                ("q", None, q_sib, q_x, q_z, q_out),
            ]
        ):
            sems = [s3.at[p, i] for i in range(3)] + [sib_sem.at[p], x_sem.at[p], z_sem.at[p]]
            landing = lambda at, sib=sib: sib.at[at]
            span = lambda k, sib=sib: sib.at[pl.ds(0, k)]
            extra = ()
            if name == "t":
                place = lambda at: held["t"].at[at, c]
                parts = lambda at: [(None, [held["t"].at[at, c], t_sib.at[at]])]
                theirs = lambda at: held["t"].at[at, other]
                extra = (resid,)
            elif name == "q":
                place = lambda at: held["q_full"].at[at]
                parts = lambda at: [(c, [held["q"].at[at, c]]), (other, [q_sib.at[at]])]
                theirs = lambda at: held["q"].at[at, other]
            else:
                place = lambda at, own=own: own.at[at]
                parts = lambda at, own=own, sib=sib: [(None, [own.at[at], sib.at[at]])]
                theirs = lambda at, name=name: held[name].at[at]
            piece[name] = Scatter(
                net, parts, place, theirs, landing, span, xbuf, zbuf, result, sems, name == "t", extra, name in "dio"
            )
        whole = AllSum(net, value, got, sum_send, sum_recv)
        swap = remote(gctx.at[other], gctx_all.at[c], swap_sem.at[0], swap_sem.at[1], net.sibling)
        st = {}

        def split(name, at, first, second):
            mine = c == 0
            own = {"d": d_own, "i": i_own, "o": o_own}[name]
            own[at] = jnp.where(mine, first, second).astype(BF16)
            held[name][at] = jnp.where(mine, second, first).astype(BF16)

        def split_rows(name, d, grad, per):
            for a in range(nb):
                at = 2 * a * per
                split(name, d * nb + a, grad[at:at + per], grad[at + per:at + 2 * per])
            piece[name].start_home(d)

        def feed_forward_steps(w_o, w_i, w_d, act, slope, pre_grad, norm_t, ctx_t, d_out, i_out, o_out):
            held.update(d=d_out, i=i_out, o=o_out)
            loads = [
                pltpu.make_async_copy(src, dst, load_sem.at[i])
                for i, (src, dst) in enumerate([(wo_h, w_o), (wi_h, w_i), (wd_h, w_d)])
            ]
            for load in loads:
                load.start()
            bias_out, gain_one, shift_one = vecs_in[2:3, :], vecs_in[3:4, :], vecs_in[4:5, :]
            bias_down, gain_two, shift_two = vecs_in[5:6, :], vecs_in[6:7, :], vecs_in[7:8, :]

            def enter():
                for p in piece.values():
                    p.clear_edges()
                net.barrier()
                context = jnp.concatenate([ctx_in[g] for g in range(nc)], axis=1)
                ctx_t[...] = jnp.transpose(context, (1, 0))
                loads[0].wait()
                resid_one = tok_in[...].astype(F32) + (dot(context, w_o[...]) + bias_out)
                st["unit_one"], st["scale_one"] = norm_parts(resid_one)
                st["normed"] = st["unit_one"] * gain_one + shift_one
                st["low"] = st["normed"].astype(BF16)
                norm_t[...] = jnp.transpose(st["low"], (1, 0))
                loads[1].wait()

            def expand(at):
                pre = dot(st["low"], w_i[:, at]) + bias_in[0:1, at]
                result, grad = gelu_and_slope(pre)
                act[:, at] = result.astype(BF16)
                slope[:, at] = grad

            def turn():
                loads[2].wait()
                unit, scale = norm_parts(st["normed"] + (dot(act[...], w_d[...]) + bias_down))
                out[...] = (unit * gain_two + shift_two).astype(BF16)
                grad_out = cot_in[...].astype(F32)
                st["two"] = norm_back(grad_out, unit, scale, gain_two)
                st["ffn"] = st["two"].astype(BF16)
                value[0] = jnp.zeros((n_sums, width), F32)
                value[0, 5:6, :] = column_sum(st["ffn"].astype(F32))
                value[0, 6:7, :] = column_sum(grad_out * unit)
                value[0, 7:8, :] = column_sum(grad_out)

            def down(mask):
                d = net.flips(mask)
                lanes = pl.ds(pl.multiple_of(d * (ff // nd), 128), ff // nd)
                split_rows("d", d, dot(act[:, lanes], st["ffn"], ((0,), (0,))), r_ff)

            def pre(i, at):
                grad = (dot(st["ffn"], w_d[at, :], ((1,), (1,))) * slope[:, at]).astype(BF16)
                pre_grad[:, at] = grad
                value[0, 8 + i:9 + i, :] = column_sum(grad.astype(F32))
                st["two"] = st["two"] + dot(grad, w_i[:, at], ((1,), (1,)))

            def norm_one():
                grad = st["two"]
                value[0, 3:4, :] = column_sum(grad * st["unit_one"])
                value[0, 4:5, :] = column_sum(grad)
                grad = norm_back(grad, st["unit_one"], st["scale_one"], gain_one)
                resid[...] = grad
                st["attn"] = grad.astype(BF16)
                value[0, 2:3, :] = column_sum(st["attn"].astype(F32))
                grad = dot(st["attn"], w_o[...], ((1,), (1,))).astype(BF16)
                for g in range(nc):
                    gctx[g] = grad[:, g * half:(g + 1) * half]
                swap.start()
                gctx_all[c] = gctx[c]

            def weight_in(mask):
                d = net.flips(mask)
                at = pl.ds(pl.multiple_of(d * (width // nd), 8), width // nd)
                split_rows("i", d, dot(norm_t[at, :], pre_grad[...]), r)

            def weight_out():
                for d in range(nd):
                    at = slice(d * (width // nd), (d + 1) * (width // nd))
                    split_rows("o", d, dot(ctx_t[at, :], st["attn"]), r)

            masks = range(nd - 1, -1, -1)
            acts = [enter] + [functools.partial(expand, at) for at in chunks] + [turn]
            acts += [functools.partial(down, m) for m in masks]
            acts += [functools.partial(pre, i, at) for i, at in enumerate(chunks)] + [norm_one]
            return acts + [functools.partial(weight_in, m) for m in masks] + [weight_out]

        n_ffn = 4 + 2 * len(chunks) + 2 * nd
        steps = nb * pairs
        n_work = n_ffn + 1 + steps + 4 + len(whole.stages())
        order = []
        for name in names:
            p = piece[name]
            for mask in range(p.nd):
                for e in range(nb):
                    order.append((back_time(nd, nb, name, mask, e), functools.partial(p.reduce, mask, e), None))
        for i in range(n_work):
            order.append((back_time(nd, nb, "work", i, n_work), None, i))
        order.sort(key=lambda q: q[0])
        index = [i for i, q in enumerate(order) if q[2] is not None]
        first, last = index[n_ffn + 1], index[n_ffn + steps]

        def run(entries, acts, base):
            for _, act, i in entries:
                (act if i is None else acts[i - base])()

        def feed_forward_scope(*refs):
            run(order[:index[n_ffn - 1] + 1], feed_forward_steps(*refs), 0)
            for name in "dio":
                piece[name].sent()

        def attention_scope(tok_t, w_v, kaug, v_scr, qaug, do_m, delta_row, dq_scr, dkv, t_part, q_part, q_full):
            held.update(t=t_part, q=q_part, q_full=q_full)
            loads = [(qaug_h, qaug)]
            for k in range(3):
                lanes = pl.ds(pl.multiple_of((k * nc + c) * half, 128), half)
                loads.append((w_h.at[:, lanes], w_v.at[:, pl.ds(k * half, half)]))
            loads.append((tok_t_h, tok_t))
            loads = [pltpu.make_async_copy(src, dst, load_sem.at[3 + i]) for i, (src, dst) in enumerate(loads)]

            def block_loads(blk):
                at = pl.ds(pl.multiple_of(blk * qlen, qlen), qlen)
                return [
                    pltpu.make_async_copy(kaug_h.at[:, at], kaug.at[:, at], load_sem.at[8 + blk]),
                    pltpu.make_async_copy(v_h.at[:, at], v_scr.at[:, at], load_sem.at[8 + nb + blk]),
                ]

            loads[0].start()
            for e in range(nb - 1, -1, -1):
                for copy in block_loads(net.near(e)):
                    copy.start()
            for copy in loads[1:]:
                copy.start()

            def prepare():
                swap.wait()
                lane = lambda p: slice(p * 128, (p + 1) * 128)
                prepare_backward(
                    lambda p: jnp.concatenate([gctx_all[g, :, lane(p)] for g in range(nc)], axis=0), exact, do_m, delta_row
                )
                for copy in loads:
                    copy.wait()

            def token_grad(blk):
                at = pl.ds(pl.multiple_of(blk * qlen, qlen), qlen)
                return dot(dkv[at, :], w_v[:, half:3 * half], ((1,), (1,)))

            def put_tokens(blk, grad):
                for g in range(nc):
                    t_part[blk, g] = grad[g * rows:(g + 1) * rows].astype(BF16)
                piece["t"].send(blk, blk)

            def weights():
                grad_q[...] = jnp.concatenate([join_dq(dq_scr, p) for p in range(pairs)], axis=1)
                mine = pl.ds(pl.multiple_of(net.b * qlen, qlen), qlen)
                for k in range(3):
                    if k:
                        grad = dot(tok_t[...], dkv[:, (k - 1) * half:k * half])
                    else:
                        grad = dot(tok_t[:, mine], grad_q[...])
                    for at in range(owners):
                        for g in range(nc):
                            i = at * nc + g
                            q_part[at, g, :, k * half:(k + 1) * half] = grad[i * r:(i + 1) * r].astype(BF16)

            def own_tokens():
                put_tokens(net.b, token_grad(net.b) + dot(grad_q[...], w_v[:, 0:half], ((1,), (1,))))

            def small_sums():
                lanes = pl.ds(pl.multiple_of(c * half, 128), half)
                value[0, 0:1, lanes] = column_sum(grad_q[...].astype(F32))
                value[0, 1:2, lanes] = column_sum(dkv[:, half:2 * half].astype(F32))

            acts = [prepare] + [None] * steps + [weights, piece["q"].start, own_tokens, small_sums] + whole.stages()
            run(order[index[n_ffn - 1] + 1:first], acts, n_ffn)
            beside = {}
            for _, act, i in order[first:last + 1]:
                if i is not None:
                    at_step = i - n_ffn - 1
                else:
                    beside.setdefault(at_step, []).append(act)

            def attention(i, carry):
                pair = i % pairs
                blk = net.near_at(nb - 1 - i // pairs)
                at = pl.ds(pl.multiple_of(blk * qlen, qlen), qlen)

                @pl.when(pair == 0)
                def _():
                    for copy in block_loads(blk):
                        copy.wait()

                def put(dk, dv):
                    dkv[at, pl.ds(pl.multiple_of(pair * 128, 128), 128)] = dk.astype(BF16)
                    dkv[at, pl.ds(pl.multiple_of(half + pair * 128, 128), 128)] = dv.astype(BF16)

                bwd_pair(pair, qaug, kaug[pair, at, :], v_scr[pair, at, :], do_m, lse_row, delta_row, dq_scr, put, i < pairs)

                @pl.when((pair == pairs - 1) & (i < steps - 1))
                def _():
                    put_tokens(blk, token_grad(blk))

                for g, acts in beside.items():

                    @pl.when(i == g)
                    def _(acts=acts):
                        for act in acts:
                            act()

                return carry

            lax.fori_loop(0, steps, attention, 0)
            run(order[last + 1:], acts, n_ffn)
            for k in range(3):
                for g in range(nc):
                    lanes = slice((k * nc + g) * half, (k * nc + g + 1) * half)
                    g_qkv[:, lanes] = q_out[g, :, k * half:(k + 1) * half]
            me = (net.d * nb + net.b) * nc + c
            feature = lax.broadcasted_iota(jnp.int32, (width, 128), 0)
            lane = lax.broadcasted_iota(jnp.int32, (width, 128), 1)
            pick = jnp.where((feature == me * r + lane) & (lane < r), 1.0, 0.0).astype(F32)
            in_row, in_lane = (me * r_ff) // width, (me * r_ff) % width
            pick_in = jnp.where((feature == in_lane + lane) & (lane < r_ff), 1.0, 0.0).astype(F32)
            exactly = dict(precision=lax.Precision.HIGHEST, preferred_element_type=F32)
            g_small[0:8, :] = jnp.dot(value[0, 0:8, :], pick, **exactly)
            found = jnp.dot(value[0, 8:16, :], pick_in, **exactly)
            row = lax.broadcasted_iota(jnp.int32, found.shape, 0)
            g_small[8:16, :] = jnp.broadcast_to(column_sum(jnp.where(row == in_row, found, 0.0)), (8, 128))
            for name in names:
                piece[name].drain()

        pl.run_scoped(feed_forward_scope, *scopes[0])
        pl.run_scoped(attention_scope, *scopes[1])

    block = {"d": (r_ff, width), "i": (r, ff), "o": (r, width), "t": (rows, width)}
    joined = (nc, r, 3 * half)
    vmem = lambda shape, kind=BF16: pltpu.VMEM(shape, kind)
    held_out = [vmem((owners,) + block[k]) for k in "dio"]
    scopes = (
        [
            vmem((width, width)),
            vmem((width, ff)),
            vmem((ff, width)),
            vmem((rows, ff)),
            vmem((rows, ff), F32),
            vmem((rows, ff)),
            vmem((width, rows)),
            vmem((width, rows)),
        ]
        + held_out,
        [
            vmem((width, total)),
            vmem((width, 3 * half)),
            vmem((pairs, total, 256)),
            vmem((pairs, total, 128)),
            vmem((heads, qlen, 256)),
            vmem((heads, qlen, 128)),
            vmem((heads, 8, qlen), F32),
            vmem((heads, 128, qlen), F32),
            vmem((total, 2 * half)),
            vmem((nb, nc, rows, width)),
            vmem((owners,) + joined),
            vmem((owners,) + joined),
        ],
    )
    scratch = [vmem((owners,) + block[k]) for k in "dio"] + [vmem((owners,) + block[k]) for k in "dio"]
    scratch += [vmem((nb,) + block["t"]), vmem((owners, r, 3 * half))]
    scratch += [vmem(((nd - 1) * nb,) + block[k]) for k in "dio"] + [vmem(((nd - 1) * nb,) + joined)]
    scratch += [vmem((nb + 1,) + block[k]) for k in "diot"] + [vmem((nb + 1,) + joined)]
    scratch += [
        vmem(joined, F32),
        vmem((rows, width), F32),
        vmem((nc, rows, half)),
        vmem((nc, rows, half)),
        vmem((qlen, half)),
        vmem((levels + 2, n_sums, width), F32),
        vmem((levels + nb, n_sums, width), F32),
        pltpu.SemaphoreType.DMA((8 + 2 * nb,)),
        pltpu.SemaphoreType.DMA((2,)),
    ]
    scratch += scatter_sems(5, nd, nb) + [pltpu.SemaphoreType.DMA((levels + nb,))] * 2
    return pl.pallas_call(
        kernel,
        out_shape=[
            jax.ShapeDtypeStruct((rows, width), BF16),
            jax.ShapeDtypeStruct((rows, width), F32),
            jax.ShapeDtypeStruct((r, 3 * width), F32),
            jax.ShapeDtypeStruct((r, width), F32),
            jax.ShapeDtypeStruct((r, ff), F32),
            jax.ShapeDtypeStruct((r_ff, width), F32),
            jax.ShapeDtypeStruct((16, 128), F32),
        ],
        in_specs=[VMEM] * 5 + [HBM] * 8 + [VMEM] * 2,
        out_specs=[VMEM] * 7,
        scratch_shapes=scratch,
        compiler_params=params(62, 3),
    )(ctx, tok, cot, vecs, bias_in, w_out, w_in, w_down, tok_t_in, w_qkv, kaug_in, v_in, qaug_in, lse, exact_in)


def body(
    tokens,
    segment,
    w_qkv,
    bias_query,
    bias_value,
    w_out,
    bias_out,
    gain_attn,
    shift_attn,
    w_in,
    bias_in,
    w_down,
    bias_down,
    gain_ffn,
    shift_ffn,
    cotangent,
):
    nd, nb, nc = lax.axis_size("dp"), lax.axis_size("blk"), lax.axis_size("head")
    n_dev = nd * nb * nc
    d_idx, b_idx, c_idx = lax.axis_index("dp"), lax.axis_index("blk"), lax.axis_index("head")
    me = (d_idx * nb + b_idx) * nc + c_idx
    seqs, rows, width = tokens.shape
    ff = w_in.shape[1]
    half_w = width // nc
    qlen = nc * rows
    r = w_qkv.shape[0]
    r_ff = w_down.shape[0]
    flat_in = tokens.reshape(rows, width)
    cot = cotangent.reshape(rows, width)
    vectors = [bias_query, bias_value, bias_out, gain_attn, shift_attn, bias_down, gain_ffn, shift_ffn]
    if nb * qlen <= 2048 and r % 8 == 0 and ff // width <= 8:
        few, many = pack_vectors(vectors, bias_in)
        ctx2, vecs, full_bin, lse, exact, f_qkv, _, f_out, f_in, f_down, kaug, v_all, qaug, tok_t = front(
            few, many, w_qkv, flat_in, w_out, w_in, w_down, segment, nd, nb, nc
        )
        out, g_tok, o_qkv, o_out, o_in, o_down, g_small = back(
            ctx2, flat_in, cot, vecs, full_bin, f_out, f_in, f_down,
            tok_t, f_qkv, kaug, v_all, qaug, lse, exact, nd, nb, nc,
        )
        out, g_tok, o_qkv, o_out, o_in, o_down, g_bq, g_bv, g_bo, g_g1, g_s1, g_bd, g_g2, g_s2, g_bin = hand_out(
            [out, g_tok, o_qkv, o_out, o_in, o_down], g_small, r, r_ff
        )
        return (
            out.reshape(seqs, rows, width), g_tok.reshape(seqs, rows, width),
            o_qkv, g_bq, g_bv, o_out, g_bo, g_g1, g_s1, o_in, g_bin, o_down, g_bd, g_g2, g_s2,
        )
    packed = jnp.concatenate(vectors + [bias_in])
    used = packed.shape[0]
    lanes = -(-used // 128) * 128
    packed = jnp.broadcast_to(jnp.pad(packed, (0, lanes - used))[None], (8, lanes))
    n4 = 4
    parts = [flat_in[i * (rows // n4):(i + 1) * (rows // n4)] for i in range(n4)]
    shards = [packed, w_qkv] + parts + [w_out, w_in, w_down]
    narrow = [False, False] + [True] * n4 + [False] * 3
    keys = [(-1, 3, 3), (0, 3, 3), (7, 9, 0), (10, 9, 0), (13, 9, 0), (16, 9, 0), (2, 4, 4), (9, 6, 5), (22, 6, 5)]
    small, g_qkv, t0, t1, t2, t3, g_out, g_in, g_down = gather_all(shards, narrow, keys, nd, nb, nc)
    full_small = small[:, 0, :used]
    vecs = full_small[:, :8 * r].reshape(n_dev, 8, r).transpose(1, 0, 2).reshape(8, width).astype(F32)
    full_bin = full_small[:, 8 * r:].reshape(ff).astype(F32)
    bq, bv, bout, gain_one, shift_one, bdown, gain_two, shift_two = (vecs[i] for i in range(8))
    full_qkv = g_qkv.reshape(width, 3 * width)
    full_wout = g_out.reshape(width, width)
    full_win = g_in.reshape(width, ff)
    full_wdown = g_down.reshape(ff, width)
    tok_all = jnp.stack([t0, t1, t2, t3], axis=1).reshape(nb * qlen, width)
    my_bias = lax.dynamic_slice(vecs, (0, c_idx * half_w), (2, half_w))
    ctx, kaug, v_scr, qaug, lse, exact = attend_forward(tok_all, full_qkv, my_bias, segment, qlen, half_w)
    context_low = ctx.reshape(seqs, qlen, 1, half_w)
    back_tokens = lax.all_to_all(context_low, "head", split_axis=1, concat_axis=2, tiled=True)
    ctx2 = back_tokens.reshape(rows, nc, half_w).transpose(1, 0, 2)
    out, grad_resid_one, gctx2, dw_down, dw_in, dw_out, sums = feed_forward(
        ctx2, flat_in, cot, vecs, full_bin.reshape(1, ff), full_wout, full_win, full_wdown
    )
    output = out.reshape(seqs, rows, width)
    grad_context = gctx2.transpose(1, 0, 2)
    grad_headed = lax.all_to_all(
        grad_context.reshape(seqs, rows, nc, half_w), "head", split_axis=2, concat_axis=1, tiled=True
    )
    gctx = grad_headed.reshape(qlen, half_w)
    tok_mine = lax.dynamic_slice(tok_all, (b_idx * qlen, 0), (qlen, width))
    dtok, dw, dbias = attend_backward(tok_all, tok_mine, full_qkv, qaug, kaug, v_scr, lse, exact, gctx)
    dw = dw.astype(BF16).reshape(nd * nb, nc, r, 3 * half_w)
    ours = lax.dynamic_index_in_dim(dw, c_idx, 1, keepdims=False)
    theirs = lax.dynamic_index_in_dim(dw, 1 - c_idx, 1, keepdims=False)
    joined_full = jnp.stack([ours, ours], axis=1)
    sums = lax.dynamic_update_slice(sums, dbias, (0, c_idx * half_w))
    o_down, o_in, o_out, o_tok, o_qkv, total = scatter_all(
        [
            dw_down.reshape(n_dev, r_ff, width),
            dw_in.reshape(n_dev, r, ff),
            dw_out.reshape(n_dev, r, width),
            dtok.reshape(nb * nc, rows, width),
            (joined_full, theirs),
        ],
        [False, False, False, True, False],
        [False, False, False, False, True],
        sums,
        nd,
        nb,
        nc,
    )
    grad_tokens = (grad_resid_one + o_tok).reshape(seqs, rows, width)
    o_qkv = o_qkv.reshape(2, r, 3, half_w).transpose(1, 2, 0, 3).reshape(r, 3 * width)
    mine = lax.dynamic_slice(total, (0, me * r), (8, r))
    mine_in = lax.dynamic_slice(total[8:8 + ff // width].reshape(ff), (me * r_ff,), (r_ff,))
    g_bq, g_bv, g_bo, g_g1, g_s1, g_bd, g_g2, g_s2 = (mine[i] for i in range(8))
    return (
        output,
        grad_tokens,
        o_qkv,
        g_bq,
        g_bv,
        o_out,
        g_bo,
        g_g1,
        g_s1,
        o_in,
        mine_in,
        o_down,
        g_bd,
        g_g2,
        g_s2,
    )


def solution(mesh):
    weight, vector = P(("dp", "blk", "head"), None), P(("dp", "blk", "head"))
    token = P("dp", ("blk", "head"), None)
    return jax.shard_map(
        body,
        mesh=mesh,
        in_specs=(
            token,
            P("dp", None),
            weight,
            vector,
            vector,
            weight,
            vector,
            vector,
            vector,
            weight,
            vector,
            weight,
            vector,
            vector,
            vector,
            token,
        ),
        out_specs=(
            token,
            token,
            weight,
            vector,
            vector,
            weight,
            vector,
            vector,
            vector,
            weight,
            vector,
            weight,
            vector,
            vector,
            vector,
        ),
        check_vma=False,
    )
```

```python
import functools

import jax
import jax.numpy as jnp
from jax import lax
from jax.experimental import pallas as pl
from jax.experimental.pallas import tpu as pltpu
from jax.sharding import PartitionSpec as P

MESH = pl.DeviceIdType.MESH
F32, BF16 = jnp.float32, jnp.bfloat16
HD = 64
HEADS = 12
BIG = 2.0**30

class Net:
    def __init__(self, nd, nb, nc):
        self.nd, self.nb, self.nc = nd, nb, nc
        self.levels = nd.bit_length() - 1
        self.d, self.b, self.c = (lax.axis_index(a) for a in ("dp", "blk", "head"))
        top = self.levels - 1
        self.stride = [(1 - self.c) * 2**k + self.c * 2 ** (top - k) for k in range(self.levels)]
        self.sibling = (self.d, self.b, self.nc - 1 - self.c)
        steps = [s * (1 - 2 * ((self.d // s) % 2)) for s in self.stride]
        self.flipped = [self.d]
        for step in steps:
            self.flipped += [d + step for d in self.flipped]
        self.nearest = [self.find_near(e) for e in range(self.nb)]

    def flips(self, mask):
        return self.flipped[mask]

    def across(self, k):
        return (self.flipped[1 << k], self.b, self.c)

    def near(self, e):
        return self.nearest[e]

    def find_near(self, e):
        order = [sorted(range(self.nb), key=lambda j: (abs(j - i), -j)) for i in range(self.nb)]
        got = order[0][e]
        for i in range(1, self.nb):
            got = jnp.where(self.b == i, order[i][e], got)
        return got

    def near_at(self, e):
        got = self.near(0)
        for i in range(1, self.nb):
            got = jnp.where(e == i, self.near(i), got)
        return got

    def slot(self, mask, blk):
        return (self.flips(mask) * self.nb + blk) * self.nc + self.c

    def peers(self):
        out = [(self.d, (self.b + u) % self.nb, self.c) for u in range(1, self.nb)]
        out += [self.across(k) for k in range(self.levels)]
        return out + [self.sibling]

    def barrier(self):
        bar = pltpu.get_barrier_semaphore()
        ps = self.peers()
        for p in ps:
            pl.semaphore_signal(bar, inc=1, device_id=p, device_id_type=MESH)
        pl.semaphore_wait(bar, len(ps))


def remote(src, dst, send, recv, dev):
    return pltpu.make_async_remote_copy(src_ref=src, dst_ref=dst, send_sem=send, recv_sem=recv, device_id=dev, device_id_type=MESH)


def blocks_of(full):
    return (lambda i: full.at[i]), (lambda k: full.at[pl.ds(0, k)])


def rows_of(full, rows, offset=0, stride=None):
    every = rows if stride is None else stride

    def place(i):
        return full.at[pl.ds(pl.multiple_of(i * every + offset, 8), rows)]

    return place, (lambda k: full.at[pl.ds(0, k * rows)])


class Gather:
    def __init__(self, net, mine, place, span, sems, narrow=False, direct=False):
        self.net, self.mine, self.place, self.span, self.narrow, self.direct = net, mine, place, span, narrow, direct
        self.zsend, self.xsend, self.ssend, self.srecv, self.recv = sems

    def at(self, mask, blk):
        n = self.net
        if self.narrow:
            return self.place(blk * n.nc + n.c)
        return self.place(n.slot(mask, blk))

    def rsem(self, mask, blk):
        return self.recv.at[mask * self.net.nb + blk]

    def spread(self, mask, blk, src, dst):
        n = self.net
        if not self.narrow:
            for k in range(n.levels):
                if mask < (1 << k):
                    remote(src, dst, self.xsend, self.rsem(mask + (1 << k), blk), n.across(k)).start()
        arrival = self.srecv.at[blk] if self.narrow else self.srecv
        remote(src, dst, self.ssend, arrival, n.sibling).start()

    def along(self, blk, src, dst):
        n = self.net
        sem = self.rsem(0, blk)

        @pl.when((n.b < n.nb - 1) & (blk <= n.b))
        def _():
            remote(src, dst, self.zsend, sem, (n.d, n.b + 1, n.c)).start()

        @pl.when((n.b > 0) & (blk >= n.b))
        def _():
            remote(src, dst, self.zsend, sem, (n.d, n.b - 1, n.c)).start()

    def own_line(self):
        n = self.net
        dst = self.at(0, n.b)
        if not self.direct:
            self.along(n.b, self.mine, dst)
            return
        for e in range(n.nb - 1, 0, -1):
            remote(self.mine, dst, self.zsend, self.rsem(0, n.b), (n.d, n.near(e), n.c)).start()

    def own_spread(self):
        self.spread(0, self.net.b, self.mine, self.at(0, self.net.b))

    def z(self, e):
        blk = self.net.near(e)
        dst = self.at(0, blk)
        pltpu.make_async_copy(dst, dst, self.rsem(0, blk)).wait()
        if not self.direct:
            self.along(blk, dst, dst)
        self.spread(0, blk, dst, dst)

    def x(self, mask, e):
        n = self.net
        blk = n.near(e)
        dst = self.at(mask, blk)
        pltpu.make_async_copy(dst, dst, self.rsem(mask, blk)).wait()
        self.spread(mask, blk, dst, dst)

    def own(self, sem):
        n = self.net
        return pltpu.make_async_copy(self.mine, self.at(0, n.b), sem)

    def wait_sibling_block(self, blk):
        one = self.span(1)
        pltpu.make_async_copy(one, one, self.srecv.at[blk]).wait()

    def wait_sibling(self):
        n = self.net
        if self.narrow:
            for blk in range(n.nb):
                self.wait_sibling_block(blk)
            return
        half = self.span(n.nd * n.nb)
        pltpu.make_async_copy(half, half, self.srecv).wait()

    def drain(self):
        n = self.net
        half = self.span(n.nb if self.narrow else n.nd * n.nb)
        pltpu.make_async_copy(half, half, self.ssend).wait()
        if not self.narrow:
            part = self.span((n.nd - 1) * n.nb)
            pltpu.make_async_copy(part, part, self.xsend).wait()
        if self.direct:
            sent = self.span(n.nb - 1)
            pltpu.make_async_copy(sent, sent, self.zsend).wait()
            return
        edge = (n.b == 0) | (n.b == n.nb - 1)

        @pl.when(edge)
        def _():
            one = self.span(1)
            pltpu.make_async_copy(one, one, self.zsend).wait()

        @pl.when(jnp.logical_not(edge))
        def _():
            many = self.span(n.nb + 1)
            pltpu.make_async_copy(many, many, self.zsend).wait()


def gather_refs(four, recv, block, p, narrow):
    last = block.at[p] if narrow else four.at[p, 3]
    return [four.at[p, 0], four.at[p, 1], four.at[p, 2], last, recv.at[p]]


def gather_sems(n_pieces, nd, nb):
    return [pltpu.SemaphoreType.DMA((n_pieces, 4)), pltpu.SemaphoreType.DMA((n_pieces, nd * nb)), pltpu.SemaphoreType.DMA]


class Scatter:
    def __init__(self, net, parts, place, theirs, landing, span, xrecv, zrecv, out, sems, narrow=False, extra=(), early=False, direct=False):
        self.net, self.parts, self.place, self.theirs, self.landing = net, parts, place, theirs, landing
        self.span, self.xbuf, self.zbuf, self.out, self.extra = span, xrecv, zrecv, out, extra
        self.sib_send, self.x_send, self.z_send, self.sib_sem, self.x_sem, self.z_sem = sems
        self.narrow, self.seen, self.early, self.direct = narrow, set(), early, direct
        self.nd = 1 if narrow else net.nd
        self.levels = 0 if narrow else net.levels

    def home(self, mask):
        return 0 if self.narrow else self.net.flips(mask)

    def start(self):
        for mask in range(self.nd - 1, -1, -1):
            self.start_home(self.home(mask))

    def start_home(self, d):
        for blk in range(self.net.nb):
            self.send(d * self.net.nb + blk, d)

    def send(self, at, sem):
        remote(self.theirs(at), self.landing(at), self.sib_send, self.sib_sem.at[sem], self.net.sibling).start()

    def arrived(self, sem, count):
        some = self.span(count)
        pltpu.make_async_copy(some, some, self.sib_sem.at[sem]).wait()

    def sent(self):
        some = self.span(self.nd * self.net.nb)
        pltpu.make_async_copy(some, some, self.sib_send).wait()

    def x_at(self, k, mask, blk):
        return ((1 << k) - 1 + mask) * self.net.nb + blk

    def z_at(self, side, blk, owner):
        return blk + side * jnp.where(blk == owner, self.net.nb - blk, 0)

    def add(self, at, more, to, extra=()):
        for pick, places in self.parts(at):
            def chosen(ref):
                return ref if pick is None else ref.at[pick]

            add_up(places + [chosen(m) for m in more] + list(extra), chosen(to))

    def reduce(self, mask, e):
        n = self.net
        blk = n.near(e)
        if self.narrow:
            self.arrived(blk, 1)
        elif mask not in self.seen:
            self.seen.add(mask)
            self.arrived(self.home(mask), n.nb)
        at = self.home(mask) * n.nb + blk
        place = self.place(at)
        more = []
        for k in range(self.levels - 1, -1, -1):
            if mask < (1 << k):
                i = self.x_at(k, mask, blk)
                got = self.xbuf.at[i]
                pltpu.make_async_copy(got, got, self.x_sem.at[i]).wait()
                more.append(got)
        if mask:
            k = mask.bit_length() - 1
            self.add(at, more, place)
            i = self.x_at(k, mask - (1 << k), blk)
            remote(place, self.xbuf.at[i], self.x_send, self.x_sem.at[i], n.across(k)).start()
            return

        if self.direct:
            if e:
                self.add(at, more, place)
                remote(place, self.zbuf.at[n.b], self.z_send, self.z_sem.at[n.b], (n.d, blk, n.c)).start()
                return
            for u in range(1, n.nb):
                got = self.zbuf.at[n.near(u)]
                pltpu.make_async_copy(got, got, self.z_sem.at[n.near(u)]).wait()
                more.append(got)
            self.add(at, more, self.out, self.extra)
            return

        def line(side, there):
            i = self.z_at(side, blk, n.b)
            got = self.zbuf.at[i]

            @pl.when(there)
            def _():
                pltpu.make_async_copy(got, got, self.z_sem.at[i]).wait()

            more.append(got)

        if e == 0:
            line(0, n.b > 0)
            line(1, n.b < n.nb - 1)
            self.add(at, more, self.out, self.extra)
            return
        side = jnp.where(blk > n.b, 0, 1)
        line(side, jnp.where(blk > n.b, n.b, n.nb - 1 - n.b) > 0)
        self.add(at, more, place)
        to = n.b + 1 - 2 * side
        i = self.z_at(side, blk, to)
        remote(place, self.zbuf.at[i], self.z_send, self.z_sem.at[i], (n.d, to, n.c)).start()

    def clear_edges(self):
        n = self.net
        if self.direct:
            return

        def clear(i, carry):
            self.zbuf[i] = jnp.zeros(self.zbuf.shape[1:], self.zbuf.dtype)
            return carry

        @pl.when(n.b == 0)
        def _():
            lax.fori_loop(0, n.nb, clear, 0)

        @pl.when(n.b == n.nb - 1)
        def _():
            lax.fori_loop(0, n.nb - 1, clear, 0)
            clear(n.nb, 0)

    def drain(self):
        n = self.net
        if not self.early:
            self.sent()
        if not self.narrow:
            some = self.xbuf.at[pl.ds(0, (n.nd - 1) * n.nb)]
            pltpu.make_async_copy(some, some, self.x_send).wait()
        some = self.zbuf.at[pl.ds(0, n.nb - 1)]
        pltpu.make_async_copy(some, some, self.z_send).wait()


def add_up(terms, to):
    shape = to.shape
    rows = shape[-2]
    step = rows
    while step % 2 == 0 and step > 32:
        step //= 2
    lead = [()] if len(shape) == 2 else [(g,) for g in range(shape[0])]
    for g in lead:
        for r in range(0, rows, step):
            at = g + (slice(r, r + step),)
            total = terms[0][at].astype(F32)
            for t in terms[1:]:
                total = total + t[at].astype(F32)
            to[at] = total.astype(to.dtype)


class AllSum:
    def __init__(self, net, value, got, send, recv):
        self.net, self.value, self.got, self.send, self.recv = net, value, got, send, recv

    def copy(self, stage, dev, src, slot):
        return remote(self.value.at[src], self.got.at[slot], self.send.at[slot], self.recv.at[slot], dev)

    def stages(self):
        n = self.net
        devs = [n.sibling] + [n.across(k) for k in range(n.levels)]
        steps = []
        for i, dev in enumerate(devs):
            steps.append(functools.partial(self.one, i, dev))
        steps.append(self.line_start)
        steps.append(self.line_end)
        return [lambda: self.copy(0, devs[0], 0, 0).start()] + steps

    def one(self, i, dev):
        n = self.net
        self.copy(i, dev, i, i).wait()
        self.value[i + 1] = self.value[i] + self.got[i]
        if i + 1 <= n.levels:
            self.copy(i + 1, n.across(i), i + 1, i + 1).start()

    def line_copy(self, u):
        n = self.net
        return self.copy(None, (n.d, (n.b + u) % n.nb, n.c), n.levels + 1, n.levels + u)

    def line_start(self):
        for u in range(1, self.net.nb):
            self.line_copy(u).start()

    def line_end(self):
        n = self.net
        for u in range(1, n.nb):
            self.line_copy(u).wait()
        total = self.value[n.levels + 1]
        for u in range(1, n.nb):
            total = total + self.got[n.levels + u]
        self.value[0] = total


def scatter_sems(n_pieces, nd, nb):
    return [
        pltpu.SemaphoreType.DMA((n_pieces, 3)),
        pltpu.SemaphoreType.DMA((n_pieces, max(nd, nb))),
        pltpu.SemaphoreType.DMA((n_pieces, (nd - 1) * nb)),
        pltpu.SemaphoreType.DMA((n_pieces, nb + 1)),
    ]


def dot(a, b, dims=((1,), (0,))):
    return lax.dot_general(a, b, (dims, ((), ())), preferred_element_type=F32)


def mask_lanes(seg_row, count):
    lanes = lax.broadcasted_iota(jnp.int32, (128, count), 0)
    return jnp.transpose(jnp.where(lanes == seg_row, -1.0, 0.0).astype(F32), (1, 0))


def project_keys(i, step, tok, wk, wv, bias_v, seg, kaug, v_scr):
    at = pl.ds(pl.multiple_of(i * step, step), step)
    piece = tok[at, :]
    keys = dot(piece, wk).astype(BF16)
    vals = (dot(piece, wv) + bias_v).astype(BF16)
    lanes = mask_lanes(seg[:, at], step).astype(BF16)
    for p in range(kaug.shape[0]):
        kaug[p, at, 0:128] = keys[:, p * 128:(p + 1) * 128]
        kaug[p, at, 128:256] = lanes
        v_scr[p, at, :] = vals[:, p * 128:(p + 1) * 128]


def project_queries(tok, wq, bias_q, seg, qaug, blk, qlen):
    mine = pl.ds(pl.multiple_of(blk * qlen, qlen), qlen)
    query = (dot(tok[mine, :], wq) + bias_q).astype(BF16)
    lane = lax.broadcasted_iota(jnp.int32, (qlen, 128), 1)
    feat = jnp.where(lane < 8, BIG * (1.0 + mask_lanes(seg[:, mine], qlen)), 0.0).astype(BF16)
    for p in range(qaug.shape[0] // 2):
        q_pair = query[:, p * 128:(p + 1) * 128].astype(F32) * HD**-0.5
        for half in range(2):
            keep = (lane >= 64) if half else (lane < 64)
            qaug[2 * p + half, :, 0:128] = jnp.where(keep, q_pair, 0.0).astype(BF16)
            qaug[2 * p + half, :, 128:256] = feat


def attend_chunk(i, qaug, kaug, v_scr, o_scr, exact_scr, lse_scr, chunk, per_head):
    h = i // per_head
    at = pl.ds(pl.multiple_of((i % per_head) * chunk, chunk), chunk)
    s = dot(qaug[h, at, :], kaug[h // 2], ((1,), (1,)))
    top = jnp.max(s, axis=-1, keepdims=True)
    p = jnp.exp(s - top)
    total = jnp.sum(p, axis=-1, keepdims=True)
    low = p.astype(BF16)
    rest = (p - low.astype(F32)).astype(BF16)
    value = v_scr[h // 2]
    o = dot(low, value)
    inverse = 1.0 / total
    o_scr[h, at, :] = o * inverse
    exact_scr[h, at, :] = (o + dot(rest, value)) * inverse
    lse_scr[h, at, :] = jnp.broadcast_to(top + jnp.log(total), (chunk, 128))


def attend_block(h, at, qaug, kaug, v_scr, top_scr, sum_scr, o_scr, rest_scr):
    s = dot(qaug[h], kaug[h // 2, at, :], ((1,), (1,)))
    before = top_scr[h]
    top = jnp.maximum(before, jnp.broadcast_to(jnp.max(s, axis=-1, keepdims=True), before.shape))
    p = jnp.exp(s - jnp.concatenate([top] * (s.shape[1] // 128), axis=1))
    fade = jnp.exp(before - top)
    low = p.astype(BF16)
    rest = (p - low.astype(F32)).astype(BF16)
    value = v_scr[h // 2, at, :]
    top_scr[h] = top
    sum_scr[h] = sum_scr[h] * fade + jnp.broadcast_to(jnp.sum(p, axis=-1, keepdims=True), before.shape)
    o_scr[h] = o_scr[h] * fade + dot(low, value)
    rest_scr[h] = rest_scr[h] * fade + dot(rest, value)


def close_blocks(top_scr, sum_scr, o_scr, rest_scr):
    for h in range(o_scr.shape[0]):
        total = sum_scr[h]
        inverse = 1.0 / total
        o = o_scr[h]
        rest_scr[h] = (o + rest_scr[h]) * inverse
        o_scr[h] = o * inverse
        top_scr[h] = top_scr[h] + jnp.log(total)


def join_heads(scr, p, at=slice(None)):
    first, second = scr[2 * p, at, :], scr[2 * p + 1, at, :]
    lane = lax.broadcasted_iota(jnp.int32, first.shape, 1)
    return jnp.where(lane < 64, first, second)


def head_columns(w, part, c, width):
    return w[:, pl.ds(pl.multiple_of((part * 2 + c) * width, 128), width)]


def fwd_kernel(tok, w, bias, seg, ctx, kaug, v_scr, qaug, lse_out, exact, lse_scr, o_scr, exact_scr, chunk=256):
    blk, c = lax.axis_index("blk"), lax.axis_index("head")
    qlen, width = ctx.shape
    total = tok.shape[0]
    step = min(512, total)
    wk, wv = head_columns(w, 1, c, width), head_columns(w, 2, c, width)

    def rows(i, carry):
        project_keys(i, step, tok, wk, wv, bias[1:2, :], seg, kaug, v_scr)
        return carry

    lax.fori_loop(0, total // step, rows, 0)
    project_queries(tok, head_columns(w, 0, c, width), bias[0:1, :], seg, qaug, blk, qlen)
    per_head = qlen // chunk

    def go(i, carry):
        attend_chunk(i, qaug, kaug, v_scr, o_scr, exact_scr, lse_scr, chunk, per_head)
        return carry

    lax.fori_loop(0, (width // HD) * per_head, go, 0)
    finish_forward(o_scr, exact_scr, lse_scr, lambda p, v: store_lanes(ctx, p, v), lse_out, exact)


def store_lanes(ref, p, value):
    ref[:, p * 128:(p + 1) * 128] = value


def finish_forward(o_scr, exact_scr, lse_scr, put, lse_out, exact):
    for p in range(o_scr.shape[0] // 2):
        put(p, join_heads(o_scr, p).astype(BF16))
        exact[p] = join_heads(exact_scr, p)
    for h in range(o_scr.shape[0]):
        lse_out[h] = jnp.transpose(lse_scr[h], (1, 0))[0:8, :]


def prepare_backward(gctx_of, exact, do_m, delta_row):
    pairs, qlen, _ = exact.shape
    lane = lax.broadcasted_iota(jnp.int32, (qlen, 128), 1)
    for p in range(pairs):
        grad = gctx_of(p)
        product = grad.astype(F32) * exact[p]
        for half in range(2):
            keep = (lane >= 64) if half else (lane < 64)
            do_m[2 * p + half] = jnp.where(keep, grad, jnp.zeros_like(grad))
            across = jnp.transpose(jnp.where(keep, product, 0.0), (1, 0))
            delta_row[2 * p + half] = jnp.broadcast_to(jnp.sum(across, axis=0, keepdims=True), (8, qlen))


def bwd_pair(pair, qaug, k_part, v_part, do_m, lse_row, delta_row, dq_scr, put, first, qs=slice(None)):
    dk = dv = None
    for half in range(2):
        h = 2 * pair + half
        q_part, do_part = qaug[h, qs, :], do_m[h, qs, :]
        s = dot(k_part, q_part, ((1,), (1,)))
        p = jnp.exp(s - lse_row[h, 0:1, qs])
        dp = dot(v_part, do_part, ((1,), (1,)))
        ds = (p * (dp - delta_row[h, 0:1, qs])).astype(BF16)
        v_term = dot(p.astype(BF16), do_part)
        k_term = dot(ds, q_part[:, 0:128])
        dv = v_term if dv is None else dv + v_term
        dk = k_term if dk is None else dk + k_term
        dq = dot(k_part[:, 0:128], ds, ((0,), (0,)))
        if first is True:
            dq_scr[h, :, qs] = dq
        elif first is None:
            dq_scr[h, :, qs] += dq
        else:
            dq_scr[h, :, qs] = jnp.where(first, dq, dq_scr[h, :, qs] + dq)
    put(dk, dv)


def join_dq(dq_scr, p):
    qlen = dq_scr.shape[2]
    lane = lax.broadcasted_iota(jnp.int32, (qlen, 128), 1)
    first, second = jnp.transpose(dq_scr[2 * p], (1, 0)), jnp.transpose(dq_scr[2 * p + 1], (1, 0))
    return (jnp.where(lane < 64, first, second) * HD**-0.5).astype(BF16)


VMEM = pl.BlockSpec(memory_space=pltpu.VMEM)
HBM = pl.BlockSpec(memory_space=pltpu.HBM)


def params(limit, collective=None):
    more = {} if collective is None else dict(collective_id=collective, has_side_effects=True)
    return pltpu.CompilerParams(vmem_limit_bytes=limit << 20, **more)


def lane_mean(x):
    return jnp.mean(x, axis=-1, keepdims=True)


def norm_parts(hidden):
    centered = hidden - lane_mean(hidden)
    scale = lax.rsqrt(lane_mean(centered * centered) + 1e-12)
    return centered * scale, scale


def norm_back(grad, unit, scale, gain):
    scaled = grad * gain
    return scale * (scaled - lane_mean(scaled) - unit * lane_mean(scaled * unit))


def gelu_and_slope(pre):
    cdf = 0.5 * (1.0 + lax.erf(pre * 0.7071067811865476))
    return pre * cdf, cdf + pre * (0.3989422804014327 * jnp.exp(-0.5 * pre * pre))


def column_sum(x):
    return jnp.sum(x, axis=0, keepdims=True)


def ffn_kernel(
    ctx, tok, cot, vecs, bias_in, w_out_h, w_in_h, w_down_h,
    out, resid_grad, gctx, dw_down_h, dw_in_h, dw_out_h, sums,
    w_out, w_in, w_down, act, slope, dw_a, dw_b, dw_c, in_sem, out_sem,
):
    groups, rows, half = ctx.shape
    width, ff = w_in.shape
    step = width
    loads = [
        pltpu.make_async_copy(src, dst, in_sem.at[i])
        for i, (src, dst) in enumerate([(w_out_h, w_out), (w_in_h, w_in), (w_down_h, w_down)])
    ]
    for load in loads:
        load.start()
    bias_out, gain_one, shift_one = vecs[2:3, :], vecs[3:4, :], vecs[4:5, :]
    bias_down, gain_two, shift_two = vecs[5:6, :], vecs[6:7, :], vecs[7:8, :]
    context = jnp.concatenate([ctx[g] for g in range(groups)], axis=1)
    loads[0].wait()
    resid_one = tok[...].astype(F32) + (dot(context, w_out[...]) + bias_out)
    unit_one, scale_one = norm_parts(resid_one)
    normed = unit_one * gain_one + shift_one
    normed_low = normed.astype(BF16)
    loads[1].wait()
    chunks = [slice(i, i + step) for i in range(0, ff, step)]
    for at in chunks:
        pre = dot(normed_low, w_in[:, at]) + bias_in[0:1, at]
        value, grad = gelu_and_slope(pre)
        act[:, at] = value.astype(BF16)
        slope[:, at] = grad
    loads[2].wait()
    resid_two = normed + (dot(act[...], w_down[...]) + bias_down)
    unit_two, scale_two = norm_parts(resid_two)
    out[...] = (unit_two * gain_two + shift_two).astype(BF16)
    grad_out = cot[...].astype(F32)
    grad_two = norm_back(grad_out, unit_two, scale_two, gain_two)
    grad_ffn = grad_two.astype(BF16)
    sums[0:2, :] = jnp.zeros((2, width), F32)
    sums[5:6, :] = column_sum(grad_ffn.astype(F32))
    sums[6:7, :] = column_sum(grad_out * unit_two)
    sums[7:8, :] = column_sum(grad_out)
    stores = []

    def store(src, dst):
        copy = pltpu.make_async_copy(src, dst, out_sem.at[len(stores)])
        copy.start()
        stores.append(copy)

    for at in chunks:
        dw_a[at, :] = dot(act[:, at], grad_ffn, ((0,), (0,))).astype(BF16)
        store(dw_a.at[at], dw_down_h.at[at])
    grad_normed = grad_two
    for i, at in enumerate(chunks):
        grad_act = dot(grad_ffn, w_down[at, :], ((1,), (1,)))
        grad_pre = (grad_act * slope[:, at]).astype(BF16)
        sums[8 + i:9 + i, :] = column_sum(grad_pre.astype(F32))
        dw_b[:, at] = dot(normed_low, grad_pre, ((0,), (0,))).astype(BF16)
        grad_normed = grad_normed + dot(grad_pre, w_in[:, at], ((1,), (1,)))
    store(dw_b, dw_in_h)
    sums[8 + len(chunks):, :] = jnp.zeros((sums.shape[0] - 8 - len(chunks), width), F32)
    sums[3:4, :] = column_sum(grad_normed * unit_one)
    sums[4:5, :] = column_sum(grad_normed)
    grad_one = norm_back(grad_normed, unit_one, scale_one, gain_one)
    resid_grad[...] = grad_one
    grad_attn = grad_one.astype(BF16)
    sums[2:3, :] = column_sum(grad_attn.astype(F32))
    dw_c[...] = dot(context, grad_attn, ((0,), (0,))).astype(BF16)
    store(dw_c, dw_out_h)
    grad_context = dot(grad_attn, w_out[...], ((1,), (1,))).astype(BF16)
    for g in range(groups):
        gctx[g] = grad_context[:, g * half:(g + 1) * half]
    for copy in stores:
        copy.wait()


def feed_forward(ctx, tok, cot, vecs, bias_in, w_out, w_in, w_down):
    groups, rows, half = ctx.shape
    width, ff = w_in.shape
    n_sums = 8 + -(-(ff // width) // 8) * 8
    return pl.pallas_call(
        ffn_kernel,
        out_shape=[
            jax.ShapeDtypeStruct((rows, width), BF16),
            jax.ShapeDtypeStruct((rows, width), F32),
            jax.ShapeDtypeStruct((groups, rows, half), BF16),
            jax.ShapeDtypeStruct((ff, width), BF16),
            jax.ShapeDtypeStruct((width, ff), BF16),
            jax.ShapeDtypeStruct((width, width), BF16),
            jax.ShapeDtypeStruct((n_sums, width), F32),
        ],
        in_specs=[VMEM] * 5 + [HBM] * 3,
        out_specs=[VMEM] * 3 + [HBM] * 3 + [VMEM],
        scratch_shapes=[
            pltpu.VMEM((width, width), BF16),
            pltpu.VMEM((width, ff), BF16),
            pltpu.VMEM((ff, width), BF16),
            pltpu.VMEM((rows, ff), BF16),
            pltpu.VMEM((rows, ff), F32),
            pltpu.VMEM((ff, width), BF16),
            pltpu.VMEM((width, ff), BF16),
            pltpu.VMEM((width, width), BF16),
            pltpu.SemaphoreType.DMA((3,)),
            pltpu.SemaphoreType.DMA((ff // width + 2,)),
        ],
        compiler_params=params(56),
    )(ctx, tok, cot, vecs, bias_in, w_out, w_in, w_down)


def gather_order(keys, narrow, nd, nb):
    events = []
    for p, (begin, dz, dx) in enumerate(keys):
        for e in range(nb):
            events.append((begin + e * dz, ("z", p, e)))
            if not narrow[p]:
                for mask in range(1, nd):
                    events.append((begin + e * dz + dx * mask.bit_length(), ("x", p, mask, e)))
    events.sort(key=lambda q: q[0])
    return [ev for _, ev in events]


def gather_all(shards, narrow, keys, nd, nb, nc):
    count = len(shards)

    def kernel(*refs):
        mine, full = refs[:count], refs[count:2 * count]
        four, recv, own_sem, block_sem = refs[2 * count:]
        net = Net(nd, nb, nc)
        pieces = [
            Gather(net, mine[p], *blocks_of(full[p]), gather_refs(four, recv, block_sem, p, narrow[p]), narrow[p]) for p in range(count)
        ]
        net.barrier()
        for ev in gather_order(keys, narrow, nd, nb):
            if ev[0] == "z" and ev[2] == 0:
                pieces[ev[1]].own_line()
                pieces[ev[1]].own_spread()
            elif ev[0] == "z":
                pieces[ev[1]].z(ev[2])
            else:
                pieces[ev[1]].x(ev[2], ev[3])
        for piece in pieces:
            own = piece.own(own_sem)
            own.start()
            own.wait()
        for piece in pieces:
            piece.wait_sibling()
        for piece in pieces:
            piece.drain()

    outs = [
        jax.ShapeDtypeStruct(((nb * nc if thin else nd * nb * nc),) + s.shape, s.dtype) for s, thin in zip(shards, narrow)
    ]
    return pl.pallas_call(
        kernel,
        out_shape=outs,
        in_specs=[VMEM] * count,
        out_specs=[HBM] * count,
        scratch_shapes=gather_sems(count, nd, nb) + [pltpu.SemaphoreType.DMA((count, nb))],
        compiler_params=params(56, 0),
    )(*shards)


def attend_forward(tok, w, bias, seg, qlen, width):
    total = tok.shape[0]
    heads = width // HD
    chunk = min(256, qlen)
    while chunk * total > 256 * 4096:
        chunk //= 2
    return pl.pallas_call(
        functools.partial(fwd_kernel, chunk=chunk),
        out_shape=[
            jax.ShapeDtypeStruct((qlen, width), BF16),
            jax.ShapeDtypeStruct((width // 128, total, 256), BF16),
            jax.ShapeDtypeStruct((width // 128, total, 128), BF16),
            jax.ShapeDtypeStruct((heads, qlen, 256), BF16),
            jax.ShapeDtypeStruct((heads, 8, qlen), F32),
            jax.ShapeDtypeStruct((heads // 2, qlen, 128), F32),
        ],
        in_specs=[VMEM] * 4,
        out_specs=[VMEM] * 6,
        scratch_shapes=[pltpu.VMEM((heads, qlen, 128), F32)] * 3,
        compiler_params=params(58),
    )(tok, w, bias, seg)


def pair_bwd_kernel(qaug, kaug, v_scr, lse, exact, gctx, dk, dv, dq, do_m, delta_row, dq_scr):
    step = pl.program_id(1)

    @pl.when(step == 0)
    def _():
        prepare_backward(lambda p: gctx[...], exact, do_m, delta_row)

    def put(k_term, v_term):
        dk[...] = k_term.astype(BF16)
        dv[...] = v_term.astype(BF16)

    bwd_pair(0, qaug, kaug[0], v_scr[0], do_m, lse, delta_row, dq_scr, put, step == 0)

    @pl.when(step == pl.num_programs(1) - 1)
    def _():
        dq[...] = join_dq(dq_scr, 0)


def finish_kernel(tok, dk, dv, tok_mine, dq, w, dtok, dw, dbias, own):
    i, c = pl.program_id(0), lax.axis_index("head")
    blk = lax.axis_index("blk")
    step, width = dk.shape
    qlen = dq.shape[0]

    def cols(part):
        return w[:, pl.ds(pl.multiple_of((part * 2 + c) * width, 128), width)]

    piece, grad_k, grad_v = tok[...], dk[...], dv[...]

    @pl.when(i == 0)
    def _():
        dw[:, 0:width] = dot(tok_mine[...], dq[...], ((0,), (0,)))
        dw[:, width:3 * width] = jnp.zeros((dw.shape[0], 2 * width), F32)
        dbias[0:1, :] = jnp.sum(dq[...].astype(F32), axis=0, keepdims=True)
        dbias[1:2, :] = jnp.zeros((1, width), F32)
        own[...] = dot(dq[...], cols(0), ((1,), (1,)))

    dw[:, width:2 * width] += dot(piece, grad_k, ((0,), (0,)))
    dw[:, 2 * width:3 * width] += dot(piece, grad_v, ((0,), (0,)))
    dbias[1:2, :] += jnp.sum(grad_v.astype(F32), axis=0, keepdims=True)
    grad = dot(grad_k, cols(1), ((1,), (1,))) + dot(grad_v, cols(2), ((1,), (1,)))
    per = qlen // step
    mine = i // per == blk
    at = pl.ds(pl.multiple_of((i % per) * step, step), step)
    dtok[...] = (grad + jnp.where(mine, own[at, :], 0.0)).astype(BF16)


def attend_backward(tok, tok_mine, w, qaug, kaug, v_scr, lse, exact, gctx):
    heads, qlen, _ = qaug.shape
    total, d_model = tok.shape
    width = heads * HD
    kc = min(512, total)
    dk, dv, dq = pl.pallas_call(
        pair_bwd_kernel,
        grid=(heads // 2, total // kc),
        out_shape=[
            jax.ShapeDtypeStruct((total, width), BF16),
            jax.ShapeDtypeStruct((total, width), BF16),
            jax.ShapeDtypeStruct((qlen, width), BF16),
        ],
        in_specs=[
            pl.BlockSpec((2, qlen, 256), lambda p, j: (p, 0, 0)),
            pl.BlockSpec((1, kc, 256), lambda p, j: (p, j, 0)),
            pl.BlockSpec((1, kc, 128), lambda p, j: (p, j, 0)),
            pl.BlockSpec((2, 8, qlen), lambda p, j: (p, 0, 0)),
            pl.BlockSpec((1, qlen, 128), lambda p, j: (p, 0, 0)),
            pl.BlockSpec((qlen, 128), lambda p, j: (0, p)),
        ],
        out_specs=[pl.BlockSpec((kc, 128), lambda p, j: (j, p))] * 2 + [pl.BlockSpec((qlen, 128), lambda p, j: (0, p))],
        scratch_shapes=[
            pltpu.VMEM((2, qlen, 128), BF16),
            pltpu.VMEM((2, 8, qlen), F32),
            pltpu.VMEM((2, 128, qlen), F32),
        ],
        compiler_params=params(56),
    )(qaug, kaug, v_scr, lse, exact, gctx)
    step = min(512, qlen)
    whole = lambda i: (0, 0)
    rows = lambda i: (i, 0)
    return pl.pallas_call(
        finish_kernel,
        grid=(total // step,),
        out_shape=[
            jax.ShapeDtypeStruct((total, d_model), BF16),
            jax.ShapeDtypeStruct((d_model, 3 * width), F32),
            jax.ShapeDtypeStruct((2, width), F32),
        ],
        in_specs=[
            pl.BlockSpec((step, d_model), rows),
            pl.BlockSpec((step, width), rows),
            pl.BlockSpec((step, width), rows),
            pl.BlockSpec((qlen, d_model), whole),
            pl.BlockSpec((qlen, width), whole),
            pl.BlockSpec((d_model, w.shape[1]), whole),
        ],
        out_specs=[
            pl.BlockSpec((step, d_model), rows),
            pl.BlockSpec((d_model, 3 * width), whole),
            pl.BlockSpec((2, width), whole),
        ],
        scratch_shapes=[pltpu.VMEM((qlen, d_model), F32)],
        compiler_params=params(56),
    )(tok, dk, dv, tok_mine, dq, w)


SPACE = (0.25, 1.0, 0.2)


def send_blocks(piece, nb):
    for blk in range(nb):
        piece.send(blk, blk)


def scatter_all(arrays, narrow, joined, small, nd, nb, nc):
    count = len(arrays)
    flat = []
    for a, j in zip(arrays, joined):
        flat += list(a) if j else [a]
    n_in = len(flat) + 1

    def kernel(*refs):
        ins, small_in = list(refs[:n_in - 1]), refs[n_in - 1]
        outs, small_out = refs[n_in:n_in + count], refs[n_in + count]
        rest = list(refs[n_in + count + 1:])
        net = Net(nd, nb, nc)
        s3, sib_sem, x_sem, z_sem, sum_send, sum_recv = rest[-6:]
        value, got = rest[-8:-6]
        bufs = rest[:-8]
        pieces = []
        for p in range(count):
            first = ins.pop(0)
            sib = ins.pop(0) if joined[p] else bufs.pop(0)
            xbuf = None if narrow[p] else bufs.pop(0)
            zbuf = bufs.pop(0)
            sems = [s3.at[p, i] for i in range(3)] + [sib_sem.at[p], x_sem.at[p], z_sem.at[p]]
            if joined[p]:
                parts = lambda at, first=first: [(None, [first.at[at]])]
                place = lambda at, first=first: first.at[at]
                theirs = lambda at, sib=sib: sib.at[at]
                landing = lambda at, first=first: first.at[at, net.c]
            else:
                place = lambda at, first=first: first.at[at * nc + net.c]
                parts = lambda at, place=place, sib=sib: [(None, [place(at), sib.at[at]])]
                theirs = lambda at, first=first: first.at[at * nc + nc - 1 - net.c]
                landing = lambda at, sib=sib: sib.at[at]
            span = lambda k, sib=sib: sib.at[pl.ds(0, k)]
            pieces.append(Scatter(net, parts, place, theirs, landing, span, xbuf, zbuf, outs[p], sems, narrow[p]))
        sums = AllSum(net, value, got, sum_send, sum_recv)
        for piece in pieces:
            piece.clear_edges()
        value[0] = small_in[...]
        net.barrier()
        events = []
        for p, piece in enumerate(pieces):
            t = SPACE[0] * p
            begin = functools.partial(send_blocks, piece, nb) if narrow[p] else piece.start
            events.append((t - 0.4, begin))
            for mask in range(piece.nd - 1, -1, -1):
                for e in range(nb - 1, -1, -1):
                    when = t + SPACE[1] * (piece.levels - mask.bit_length()) + SPACE[2] * (nb - 1 - e)
                    events.append((when, functools.partial(piece.reduce, mask, e)))
        for i, s in enumerate(sums.stages()):
            events.append((0.3 * i, s))
        events.sort(key=lambda q: q[0])
        for _, ev in events:
            ev()
        small_out[...] = value[0]
        for piece in pieces:
            piece.drain()

    outs, scratch = [], []
    for a, thin, j in zip(arrays, narrow, joined):
        full = a[0] if j else a
        block = full.shape[1:]
        outs.append(jax.ShapeDtypeStruct(block, F32))
        n_dp = 1 if thin else nd
        if not j:
            scratch.append(pltpu.VMEM((n_dp * nb,) + block, BF16))
        if not thin:
            scratch.append(pltpu.VMEM(((nd - 1) * nb,) + block, BF16))
        scratch.append(pltpu.VMEM((nb + 1,) + block, BF16))
    levels = nd.bit_length() - 1
    scratch += [pltpu.VMEM((levels + 2,) + small.shape, F32), pltpu.VMEM((levels + nb,) + small.shape, F32)]
    scratch += scatter_sems(count, nd, nb)
    scratch += [pltpu.SemaphoreType.DMA((levels + nb,))] * 2
    outs.append(jax.ShapeDtypeStruct(small.shape, F32))
    return pl.pallas_call(
        kernel,
        out_shape=outs,
        in_specs=[VMEM] * n_in,
        out_specs=[VMEM] * (count + 1),
        scratch_shapes=scratch,
        compiler_params=params(60, 1),
    )(*flat, small)


def hand_out(arrays, small, r, r_ff):
    count = len(arrays)

    def kernel(*refs):
        ins, small_in = refs[:count], refs[count]
        outs, vectors, sems = refs[count + 1:2 * count + 1], refs[2 * count + 1:-1], refs[-1]
        copies = [pltpu.make_async_copy(a, b, sems.at[i]) for i, (a, b) in enumerate(zip(ins, outs))]
        for copy in copies:
            copy.start()
        for i, out in enumerate(vectors):
            out[...] = small_in[i, 0:out.shape[0]]
        for copy in copies:
            copy.wait()

    sizes = [r] * 8 + [r_ff]
    return pl.pallas_call(
        kernel,
        out_shape=[jax.ShapeDtypeStruct(a.shape, a.dtype) for a in arrays] + [jax.ShapeDtypeStruct((s,), F32) for s in sizes],
        in_specs=[VMEM] * (count + 1),
        out_specs=[HBM] * count + [VMEM] * 9,
        scratch_shapes=[pltpu.SemaphoreType.DMA((count,))],
        compiler_params=params(60),
    )(*arrays, small)


def unpack_vectors(small, vecs, bias_in, r, r_ff):
    n = small.shape[0]
    width, ff = vecs.shape[1], bias_in.shape[1]

    def gathered(rows, per, count):
        lane = lax.broadcasted_iota(jnp.int32, (8, 128), 1)
        tiles = [jnp.zeros((8, 128), F32) for _ in range(count // 128)]
        for i in range(n):
            piece = small[i, rows, :].astype(F32)
            shift, tile = per * i % 128, per * i // 128
            if shift:
                piece = pltpu.roll(piece, shift, 1)
            if shift + per <= 128:
                tiles[tile] = tiles[tile] + piece
            else:
                tiles[tile] = tiles[tile] + jnp.where(lane >= shift, piece, 0.0)
                tiles[tile + 1] = tiles[tile + 1] + jnp.where(lane < shift, piece, 0.0)
        return tiles

    for t, tile in enumerate(gathered(slice(0, 8), r, width)):
        vecs[:, t * 128:(t + 1) * 128] = tile
    for t, tile in enumerate(gathered(slice(8, 16), r_ff, ff)):
        bias_in[:, t * 128:(t + 1) * 128] = tile[0:1, :]


def pack_vectors(vectors, bias_in):
    shape = (16,) + vectors[0].shape
    row = lax.broadcasted_iota(jnp.int32, shape, 0)
    few = jnp.zeros(shape, BF16)
    for i, v in enumerate(vectors):
        few = jnp.where(row == i, v[None, :], few)
    return few, jnp.broadcast_to(bias_in[None, :], (16,) + bias_in.shape)


FRONT = {
    "small": (1, 2, ((1, 9, 11, 15), (6, 26, 28, 38), (5, 24, 27, 37), (16, 44, 46, 55))),
    "q": (0, 8, ((0, 7, 10, 14), (21, 19, 25, 34), (20, 18, 23, 35), (41, 42, 45, 54))),
    "t0": (29, 17, ((29, 47, 64, 88),)),
    "t1": (36, 43, ((36, 61, 74, 105),)),
    "o": (3, 31, ((3, 13, 30, 66), (49, 33, 50, 84), (48, 32, 51, 83), (67, 53, 68, 99))),
    "i": (22, 4, ((22, 39, 56, 85), (40, 58, 73, 101), (12, 57, 72, 102), (59, 78, 95, 113))),
    "d": (52, 60, ((52, 77, 96, 108), (79, 93, 110, 120), (76, 92, 111, 121), (97, 107, 122, 125))),
    "work": (62, 63, 65, 69, 70, 71, 75, 80, 81, 82, 86, 87, 89, 90, 91, 94, 98, 100, 103, 104, 106, 109, 112, 114, 115, 116, 117, 118, 119, 123, 124, 126, 127, 128),
}


def front_time(nd, nb, kind, what, e=0):
    if (nd, nb) == (4, 4) and (kind != "work" or e == len(FRONT["work"])):
        row = FRONT[kind]
        if kind == "work":
            return row[what]
        if what == "line":
            return row[0]
        if what == "spread":
            return row[1]
        return row[2][what][e]
    first = ["small", "q", "t0", "t1", "o", "i", "d"].index(kind) * 10 if kind != "work" else 0
    if kind == "work":
        return (40 if what == 0 else 200) + what
    if what in ("line", "spread"):
        return first
    return first + 3 * e + (4 * what.bit_length() if what else 0)


DIRECT = ()


def front(few, many, w_qkv, tok, w_out, w_in, w_down, seg, nd, nb, nc):
    n = nd * nb * nc
    rows, width = tok.shape
    half, qlen, total = width // nc, nc * rows, nb * nc * rows
    heads = half // HD
    pairs = heads // 2
    r, r_ff, ff = w_qkv.shape[0], w_down.shape[0], w_in.shape[1]
    parts = 2
    part = rows // parts
    steps = nb * heads
    chunks = [slice(i, i + width) for i in range(0, ff, width)]

    def kernel(
        few_in, many_in, q_in, tok_in, o_in, i_in, d_in, seg_in,
        ctx2, vecs, lse_out, scale_one,
        q_h, o_h, i_h, d_h, kaug_h, v_h, qaug_h, tok_t_h, act_h, slope_h, exact_h, normed_h, unit_h,
        small_in, small_all, w_v, tok_v, tok_t, kaug, v_scr, qaug, top_scr, sum_scr, o_scr, rest_scr, ctx_loc,
        w_o, w_i, act, slope, bias_in, exact, normed, unit_one,
        four, recv, block_sem, own_sem, load_sem, save_sem, swap_sem,
    ):
        net = Net(nd, nb, nc)
        c = net.c
        small_in[...] = jnp.zeros((16, 128), BF16)
        small_in[:, 0:r] = few_in[...]
        row = lax.broadcasted_iota(jnp.int32, (16, r_ff), 0)
        small_in[:, 0:r_ff] = jnp.where(row == 8, many_in[...], small_in[:, 0:r_ff])
        specs = [("small", small_in, blocks_of(small_all), False), ("q", q_in, rows_of(q_h, r), False)]
        for i in range(parts):
            mine = tok_in.at[pl.ds(i * part, part)]
            specs.append(("t" + str(i), mine, rows_of(tok_v, part, i * part, rows), True))
        specs += [("o", o_in, rows_of(o_h, r), False), ("i", i_in, rows_of(i_h, r), False), ("d", d_in, rows_of(d_h, r_ff), False)]
        piece, own = {}, {}
        for p, (name, mine, (place, span), narrow) in enumerate(specs):
            piece[name] = Gather(net, mine, place, span, gather_refs(four, recv, block_sem, p, narrow), narrow, name in DIRECT)
            own[name] = piece[name].own(own_sem.at[p])
        tokens = ["t" + str(i) for i in range(parts)]
        for name in piece:
            own[name].start()
        net.barrier()
        lanes = pl.ds(pl.multiple_of(c * half, 128), half)

        def whole(name):
            piece[name].wait_sibling()
            own[name].wait()

        def unpack():
            whole("small")
            unpack_vectors(small_all, vecs, bias_in, r, r_ff)

        def load():
            whole("q")
            copies = []
            for k in range(3):
                at = pl.ds(pl.multiple_of((k * nc + c) * half, 128), half)
                copies.append(pltpu.make_async_copy(q_h.at[:, at], w_v.at[:, pl.ds(k * half, half)], load_sem.at[k]))
            for copy in copies:
                copy.start()
            for copy in copies:
                copy.wait()

        def queries():
            for name in tokens:
                own[name].wait()
                piece[name].wait_sibling_block(net.b)
            project_queries(tok_v, w_v[:, 0:half], vecs[0:1, lanes], seg_in, qaug, net.b, qlen)
            for scr, start in ((top_scr, -3e38), (sum_scr, 0.0), (o_scr, 0.0), (rest_scr, 0.0)):
                scr[...] = jnp.full(scr.shape, start, F32)

        saves = [
            pltpu.make_async_copy(src, dst, save_sem.at[i])
            for i, (src, dst) in enumerate(
                [
                    (kaug, kaug_h), (v_scr, v_h), (qaug, qaug_h), (tok_t, tok_t_h),
                    (exact, exact_h), (normed, normed_h), (unit_one, unit_h),
                ]
                + [(a.at[:, at], b.at[:, at]) for a, b in ((act, act_h), (slope, slope_h)) for at in chunks]
            )
        ]

        def turn_tokens():
            tok_t[...] = jnp.transpose(tok_v[...], (1, 0))
            for save in saves[:4]:
                save.start()

        swap = remote(ctx_loc.at[nc - 1 - c], ctx2.at[c], swap_sem.at[0], swap_sem.at[1], net.sibling)
        st = {}

        def finish():
            def put(p, value):
                for g in range(nc):
                    ctx_loc[g, :, p * 128:(p + 1) * 128] = value[g * rows:(g + 1) * rows]

            close_blocks(top_scr, sum_scr, o_scr, rest_scr)
            finish_forward(o_scr, rest_scr, top_scr, put, lse_out, exact)
            swap.start()
            saves[4].start()
            ctx2[c] = ctx_loc[c]

        def fetch(name, src, dst):
            whole(name)
            copy = pltpu.make_async_copy(src, dst, load_sem.at[3])
            copy.start()
            copy.wait()

        def first_norm():
            fetch("o", o_h, w_o)
            swap.wait()
            context = jnp.concatenate([ctx2[g] for g in range(nc)], axis=1)
            resid = tok_in[...].astype(F32) + (dot(context, w_o[...]) + vecs[2:3, :])
            unit, scale = norm_parts(resid)
            value = unit * vecs[3:4, :] + vecs[4:5, :]
            normed[...] = value
            unit_one[...] = unit
            scale_one[...] = jnp.broadcast_to(scale, scale_one.shape)
            saves[5].start()
            saves[6].start()
            st["low"] = value.astype(BF16)

        def expand(i, at):
            if i == 0:
                fetch("i", i_h, w_i)
            pre = dot(st["low"], w_i[:, at]) + bias_in[0:1, at]
            result, grad = gelu_and_slope(pre)
            act[:, at] = result.astype(BF16)
            slope[:, at] = grad
            saves[7 + i].start()
            saves[7 + len(chunks) + i].start()

        order = []
        for name in piece:
            order.append((front_time(nd, nb, name, "line"), piece[name].own_line, None))
            order.append((front_time(nd, nb, name, "spread"), piece[name].own_spread, None))
            for e in range(1, nb):
                order.append((front_time(nd, nb, name, 0, e), functools.partial(piece[name].z, e), None))
            for mask in range(1, 1 if name in tokens else nd):
                for e in range(nb):
                    order.append((front_time(nd, nb, name, mask, e), functools.partial(piece[name].x, mask, e), None))
        work = [unpack, load, queries] + [None] * steps + [turn_tokens, finish, first_norm]
        work += [functools.partial(expand, i, at) for i, at in enumerate(chunks)]
        for i, act_now in enumerate(work):
            order.append((front_time(nd, nb, "work", i, len(work)), act_now, i - 3 if act_now is None else None))
        order.sort(key=lambda q: q[0])
        begin = next(i for i, q in enumerate(order) if q[2] == 0)
        end = next(i for i, q in enumerate(order) if q[2] == steps - 1)
        for _, act_now, _ in order[:begin]:
            act_now()
        beside = {}
        for _, act_now, i in order[begin:end + 1]:
            if act_now is None:
                at_step = i
            else:
                beside.setdefault(at_step, []).append(act_now)

        for e in range(nb):
            blk = net.near(e)
            if e:
                for name in tokens:
                    piece[name].wait_sibling_block(blk)
            project_keys(blk, qlen, tok_v, w_v[:, half:2 * half], w_v[:, 2 * half:3 * half], vecs[1:2, lanes], seg_in, kaug, v_scr)
            at = pl.ds(pl.multiple_of(blk * qlen, qlen), qlen)
            for h in range(heads):
                attend_block(h, at, qaug, kaug, v_scr, top_scr, sum_scr, o_scr, rest_scr)
                for act_now in beside.get(e * heads + h, ()):
                    act_now()
        for _, act_now, _ in order[end + 1:]:
            act_now()
        whole("d")
        for name in piece:
            piece[name].drain()
        for save in saves:
            save.wait()

    count = 5 + parts
    vmem = lambda *shape: pltpu.VMEM(shape, BF16)
    wide = pltpu.VMEM((heads, qlen, 128), F32)
    return pl.pallas_call(
        kernel,
        out_shape=[
            jax.ShapeDtypeStruct((nc, rows, half), BF16),
            jax.ShapeDtypeStruct((8, width), F32),
            jax.ShapeDtypeStruct((heads, 8, qlen), F32),
            jax.ShapeDtypeStruct((rows, 128), F32),
            jax.ShapeDtypeStruct((n * r, 3 * width), BF16),
            jax.ShapeDtypeStruct((n * r, width), BF16),
            jax.ShapeDtypeStruct((n * r, ff), BF16),
            jax.ShapeDtypeStruct((n * r_ff, width), BF16),
            jax.ShapeDtypeStruct((pairs, total, 256), BF16),
            jax.ShapeDtypeStruct((pairs, total, 128), BF16),
            jax.ShapeDtypeStruct((heads, qlen, 256), BF16),
            jax.ShapeDtypeStruct((width, total), BF16),
            jax.ShapeDtypeStruct((rows, ff), BF16),
            jax.ShapeDtypeStruct((rows, ff), F32),
            jax.ShapeDtypeStruct((pairs, qlen, 128), F32),
            jax.ShapeDtypeStruct((rows, width), F32),
            jax.ShapeDtypeStruct((rows, width), F32),
        ],
        in_specs=[VMEM] * 8,
        out_specs=[VMEM] * 4 + [HBM] * 13,
        scratch_shapes=[
            vmem(16, 128),
            vmem(n, 16, 128),
            vmem(width, 3 * half),
            vmem(total, width),
            vmem(width, total),
            vmem(pairs, total, 256),
            vmem(pairs, total, 128),
            vmem(heads, qlen, 256),
            wide,
            wide,
            wide,
            wide,
            vmem(nc, rows, half),
            vmem(width, width),
            vmem(width, ff),
            vmem(rows, ff),
            pltpu.VMEM((rows, ff), F32),
            pltpu.VMEM((1, ff), F32),
            pltpu.VMEM((pairs, qlen, 128), F32),
            pltpu.VMEM((rows, width), F32),
            pltpu.VMEM((rows, width), F32),
            pltpu.SemaphoreType.DMA((count, 4)),
            pltpu.SemaphoreType.DMA((count, nd * nb)),
            pltpu.SemaphoreType.DMA((count, nb)),
            pltpu.SemaphoreType.DMA((count,)),
            pltpu.SemaphoreType.DMA((4,)),
            pltpu.SemaphoreType.DMA((7 + 2 * len(chunks),)),
            pltpu.SemaphoreType.DMA((2,)),
        ],
        compiler_params=params(58, 2),
    )(few, many, w_qkv, tok, w_out, w_in, w_down, seg)


BACK = {
    "d": (0, ((67, 52, 44, 39), (56, 41, 16, 20), (42, 24, 12, 13), (43, 25, 7, 8))),
    "i": (0, ((104, 96, 87, 55), (97, 81, 60, 36), (88, 70, 47, 26), (90, 71, 48, 21))),
    "o": (0, ((99, 69, 64, 61), (68, 63, 58, 53), (37, 30, 28, 32), (38, 31, 29, 33))),
    "q": (0, ((103, 98, 92, 89), (100, 91, 85, 84), (93, 82, 79, 78), (95, 83, 77, 76))),
    "t": (0, ((101, 75, 66, 50),)),
    "work": (0, 1, 2, 3, 4, 5, 6, 9, 10, 11, 14, 15, 17, 18, 19, 22, 23, 27, 34, 35, 40, 45, 46, 49, 51, 54, 57, 59, 62, 65, 72, 74, 73, 73.1, 80, 86, 94, 94.1, 102),
}


def back_time(nd, nb, kind, what, e=0):
    if (nd, nb) == (4, 4) and (kind != "work" or e == len(BACK["work"])):
        row = BACK[kind]
        if kind == "work":
            return row[what]
        return row[0] if what == "start" else row[1][what][e]
    if kind == "work":
        return 20 + 10 * what + (100 if what > e - 10 else 0)
    first = {"d": 0, "i": 10, "o": 20, "t": 300, "q": 400}[kind]
    if what == "start":
        return first
    return first + 30 - 5 * what.bit_length() + (nb - 1 - e)


def back(
    ctx, cot, vecs, lse, scale_one, normed, unit_one, exact_in, w_out, w_in, w_down, act_in, slope_in,
    tok_t_in, w_qkv, kaug_in, v_in, qaug_in, nd, nb, nc,
):
    owners = nd * nb
    rows, width = cot.shape
    total = tok_t_in.shape[1]
    ff = w_in.shape[1]
    half, qlen = width // nc, nc * rows
    heads = half // HD
    pairs = heads // 2
    r, r_ff = width // (owners * nc), ff // (owners * nc)
    levels = nd.bit_length() - 1
    names = ["d", "i", "o", "t", "q"]
    chunks = [slice(i, i + width) for i in range(0, ff, width)]
    n_sums = 8 + -(-len(chunks) // 8) * 8

    def kernel(
        ctx_in, cot_in, vecs_in, lse_row, scale_in, normed_h, unit_h, exact_h, wo_h, wi_h, wd_h, act_h, slope_h, tok_t_h, w_h,
        kaug_h, v_h, qaug_h,
        out, g_tok, g_qkv, g_out, g_in, g_down, g_small,
        d_own, i_own, o_own, d_sib, i_sib, o_sib, t_sib, q_sib, d_x, i_x, o_x, q_x, d_z, i_z, o_z, t_z, q_z,
        q_out, resid, gctx, gctx_all, grad_q, normed_in, unit_in, exact, value, got,
        load_sem, swap_sem, s3, sib_sem, x_sem, z_sem, sum_send, sum_recv,
    ):
        net = Net(nd, nb, nc)
        c, other = net.c, nc - 1 - net.c
        piece, held = {}, {}
        for p, (name, own, sib, xbuf, zbuf, result) in enumerate(
            [
                ("d", d_own, d_sib, d_x, d_z, g_down),
                ("i", i_own, i_sib, i_x, i_z, g_in),
                ("o", o_own, o_sib, o_x, o_z, g_out),
                ("t", None, t_sib, None, t_z, g_tok),
                ("q", None, q_sib, q_x, q_z, q_out),
            ]
        ):
            sems = [s3.at[p, i] for i in range(3)] + [sib_sem.at[p], x_sem.at[p], z_sem.at[p]]
            landing = lambda at, sib=sib: sib.at[at]
            span = lambda k, sib=sib: sib.at[pl.ds(0, k)]
            extra = ()
            if name == "t":
                place = lambda at: held["t"].at[at, c]
                parts = lambda at: [(None, [held["t"].at[at, c], t_sib.at[at]])]
                theirs = lambda at: held["t"].at[at, other]
                extra = (resid,)
            elif name == "q":
                place = lambda at: held["q_full"].at[at]
                parts = lambda at: [(c, [held["q"].at[at, c]]), (other, [q_sib.at[at]])]
                theirs = lambda at: held["q"].at[at, other]
            else:
                place = lambda at, own=own: own.at[at]
                parts = lambda at, own=own, sib=sib: [(None, [own.at[at], sib.at[at]])]
                theirs = lambda at, name=name: held[name].at[at]
            piece[name] = Scatter(
                net, parts, place, theirs, landing, span, xbuf, zbuf, result, sems, name == "t", extra, name in "dio", name in "oq"
            )
        whole = AllSum(net, value, got, sum_send, sum_recv)
        swap = remote(gctx.at[other], gctx_all.at[c], swap_sem.at[0], swap_sem.at[1], net.sibling)
        st = {}

        def split(name, at, first, second):
            mine = c == 0
            own = {"d": d_own, "i": i_own, "o": o_own}[name]
            own[at] = jnp.where(mine, first, second).astype(BF16)
            held[name][at] = jnp.where(mine, second, first).astype(BF16)

        def split_rows(name, d, grad, per):
            for a in range(nb):
                at = 2 * a * per
                split(name, d * nb + a, grad[at:at + per], grad[at + per:at + 2 * per])
            piece[name].start_home(d)

        def feed_forward_steps(w_o, w_i, w_d, act, slope, pre_grad, norm_t, ctx_t, d_out, i_out, o_out):
            held.update(d=d_out, i=i_out, o=o_out)
            loads = [
                pltpu.make_async_copy(src, dst, load_sem.at[i])
                for i, (src, dst) in enumerate(
                    [
                        (act_h, act), (wd_h, w_d), (normed_h, normed_in), (slope_h, slope), (wi_h, w_i), (unit_h, unit_in),
                        (wo_h, w_o), (exact_h, exact),
                    ]
                )
            ]
            for load in loads:
                load.start()
            gain_one, bias_down = vecs_in[3:4, :], vecs_in[5:6, :]
            gain_two, shift_two = vecs_in[6:7, :], vecs_in[7:8, :]

            def enter():
                for p in piece.values():
                    p.clear_edges()
                net.barrier()
                ctx_t[...] = jnp.transpose(jnp.concatenate([ctx_in[g] for g in range(nc)], axis=1), (1, 0))
                for load in loads[:3]:
                    load.wait()
                norm_t[...] = jnp.transpose(normed_in[...].astype(BF16), (1, 0))

            def turn():
                unit, scale = norm_parts(normed_in[...] + (dot(act[...], w_d[...]) + bias_down))
                out[...] = (unit * gain_two + shift_two).astype(BF16)
                grad_out = cot_in[...].astype(F32)
                st["two"] = norm_back(grad_out, unit, scale, gain_two)
                st["ffn"] = st["two"].astype(BF16)
                value[0] = jnp.zeros((n_sums, width), F32)
                value[0, 5:6, :] = column_sum(st["ffn"].astype(F32))
                value[0, 6:7, :] = column_sum(grad_out * unit)
                value[0, 7:8, :] = column_sum(grad_out)

            def down(mask):
                d = net.flips(mask)
                lanes = pl.ds(pl.multiple_of(d * (ff // nd), 128), ff // nd)
                split_rows("d", d, dot(act[:, lanes], st["ffn"], ((0,), (0,))), r_ff)

            def pre(i, at):
                if i == 0:
                    loads[3].wait()
                    loads[4].wait()
                grad = (dot(st["ffn"], w_d[at, :], ((1,), (1,))) * slope[:, at]).astype(BF16)
                pre_grad[:, at] = grad
                value[0, 8 + i:9 + i, :] = column_sum(grad.astype(F32))
                st["two"] = st["two"] + dot(grad, w_i[:, at], ((1,), (1,)))

            def norm_one():
                grad = st["two"]
                for load in loads[5:]:
                    load.wait()
                value[0, 3:4, :] = column_sum(grad * unit_in[...])
                value[0, 4:5, :] = column_sum(grad)
                grad = norm_back(grad, unit_in[...], scale_in[:, 0:1], gain_one)
                resid[...] = grad
                st["attn"] = grad.astype(BF16)
                value[0, 2:3, :] = column_sum(st["attn"].astype(F32))
                grad = dot(st["attn"], w_o[...], ((1,), (1,))).astype(BF16)
                for g in range(nc):
                    gctx[g] = grad[:, g * half:(g + 1) * half]
                swap.start()
                gctx_all[c] = gctx[c]

            def weight_in(mask):
                d = net.flips(mask)
                at = pl.ds(pl.multiple_of(d * (width // nd), 8), width // nd)
                split_rows("i", d, dot(norm_t[at, :], pre_grad[...]), r)

            def weight_out():
                for d in range(nd):
                    at = slice(d * (width // nd), (d + 1) * (width // nd))
                    split_rows("o", d, dot(ctx_t[at, :], st["attn"]), r)

            masks = range(nd - 1, -1, -1)
            acts = [enter, turn]
            acts += [functools.partial(down, m) for m in masks]
            acts += [functools.partial(pre, i, at) for i, at in enumerate(chunks)] + [norm_one]
            return acts + [functools.partial(weight_in, m) for m in masks] + [weight_out]

        n_ffn = 4 + len(chunks) + 2 * nd
        steps = nb * pairs
        n_work = n_ffn + 1 + steps + 4 + len(whole.stages())
        order = []
        for name in names:
            p = piece[name]
            for mask in range(p.nd):
                for e in range(nb):
                    order.append((back_time(nd, nb, name, mask, e), functools.partial(p.reduce, mask, e), None))
        for i in range(n_work):
            order.append((back_time(nd, nb, "work", i, n_work), None, i))
        order.sort(key=lambda q: q[0])
        index = [i for i, q in enumerate(order) if q[2] is not None]
        first, last = index[n_ffn + 1], index[n_ffn + steps]

        def run(entries, acts, base):
            for _, act, i in entries:
                (act if i is None else acts[i - base])()

        def feed_forward_scope(*refs):
            run(order[:index[n_ffn - 1] + 1], feed_forward_steps(*refs), 0)
            for name in "dio":
                piece[name].sent()

        def attention_scope(tok_t, w_v, kaug, v_scr, qaug, do_m, delta_row, dq_scr, dkv, t_part, q_part, q_full):
            held.update(t=t_part, q=q_part, q_full=q_full)
            loads = [(qaug_h, qaug)]
            for k in range(3):
                lanes = pl.ds(pl.multiple_of((k * nc + c) * half, 128), half)
                loads.append((w_h.at[:, lanes], w_v.at[:, pl.ds(k * half, half)]))
            loads.append((tok_t_h, tok_t))
            loads = [pltpu.make_async_copy(src, dst, load_sem.at[8 + i]) for i, (src, dst) in enumerate(loads)]

            def block_loads(blk):
                at = pl.ds(pl.multiple_of(blk * qlen, qlen), qlen)
                return [
                    pltpu.make_async_copy(kaug_h.at[:, at], kaug.at[:, at], load_sem.at[13 + blk]),
                    pltpu.make_async_copy(v_h.at[:, at], v_scr.at[:, at], load_sem.at[13 + nb + blk]),
                ]

            loads[0].start()
            for e in range(nb - 1, -1, -1):
                for copy in block_loads(net.near(e)):
                    copy.start()
            for copy in loads[1:]:
                copy.start()

            def prepare():
                swap.wait()
                lane = lambda p: slice(p * 128, (p + 1) * 128)
                prepare_backward(
                    lambda p: jnp.concatenate([gctx_all[g, :, lane(p)] for g in range(nc)], axis=0), exact, do_m, delta_row
                )
                for copy in loads:
                    copy.wait()

            def token_grad(blk):
                at = pl.ds(pl.multiple_of(blk * qlen, qlen), qlen)
                return dot(dkv[at, :], w_v[:, half:3 * half], ((1,), (1,)))

            def put_tokens(blk, grad):
                for g in range(nc):
                    t_part[blk, g] = grad[g * rows:(g + 1) * rows].astype(BF16)
                piece["t"].send(blk, blk)

            def weights():
                grad_q[...] = jnp.concatenate([join_dq(dq_scr, p) for p in range(pairs)], axis=1)
                mine = pl.ds(pl.multiple_of(net.b * qlen, qlen), qlen)
                for k in range(3):
                    if k:
                        grad = dot(tok_t[...], dkv[:, (k - 1) * half:k * half])
                    else:
                        grad = dot(tok_t[:, mine], grad_q[...])
                    for at in range(owners):
                        for g in range(nc):
                            i = at * nc + g
                            q_part[at, g, :, k * half:(k + 1) * half] = grad[i * r:(i + 1) * r].astype(BF16)

            def own_tokens():
                put_tokens(net.b, token_grad(net.b) + dot(grad_q[...], w_v[:, 0:half], ((1,), (1,))))

            def small_sums():
                lanes = pl.ds(pl.multiple_of(c * half, 128), half)
                value[0, 0:1, lanes] = column_sum(grad_q[...].astype(F32))
                value[0, 1:2, lanes] = column_sum(dkv[:, half:2 * half].astype(F32))

            acts = [prepare] + [None] * steps + [weights, piece["q"].start, own_tokens, small_sums] + whole.stages()
            run(order[index[n_ffn - 1] + 1:first], acts, n_ffn)
            beside = {}
            for _, act, i in order[first:last + 1]:
                if i is not None:
                    at_step = i - n_ffn - 1
                else:
                    beside.setdefault(at_step, []).append(act)

            def put(at, pair, dk, dv):
                dkv[at, pair * 128:(pair + 1) * 128] = dk.astype(BF16)
                dkv[at, half + pair * 128:half + (pair + 1) * 128] = dv.astype(BF16)

            for e in range(nb - 1, -1, -1):
                blk = net.near(e)
                for copy in block_loads(blk):
                    copy.wait()
                at = pl.ds(pl.multiple_of(blk * qlen, qlen), qlen)
                new = True if e == nb - 1 else None
                for pair in range(pairs):
                    bwd_pair(
                        pair, qaug, kaug[pair, at, :], v_scr[pair, at, :], do_m, lse_row, delta_row, dq_scr,
                        functools.partial(put, at, pair), new,
                    )
                    if e and pair == pairs - 1:
                        put_tokens(blk, token_grad(blk))
                    for act in beside.get((nb - 1 - e) * pairs + pair, ()):
                        act()
            run(order[last + 1:], acts, n_ffn)
            for k in range(3):
                for g in range(nc):
                    lanes = slice((k * nc + g) * half, (k * nc + g + 1) * half)
                    g_qkv[:, lanes] = q_out[g, :, k * half:(k + 1) * half]
            me = (net.d * nb + net.b) * nc + c
            feature = lax.broadcasted_iota(jnp.int32, (width, 128), 0)
            lane = lax.broadcasted_iota(jnp.int32, (width, 128), 1)
            pick = jnp.where((feature == me * r + lane) & (lane < r), 1.0, 0.0).astype(F32)
            in_row, in_lane = (me * r_ff) // width, (me * r_ff) % width
            pick_in = jnp.where((feature == in_lane + lane) & (lane < r_ff), 1.0, 0.0).astype(F32)
            exactly = dict(precision=lax.Precision.HIGHEST, preferred_element_type=F32)
            g_small[0:8, :] = jnp.dot(value[0, 0:8, :], pick, **exactly)
            found = jnp.dot(value[0, 8:16, :], pick_in, **exactly)
            row = lax.broadcasted_iota(jnp.int32, found.shape, 0)
            g_small[8:16, :] = jnp.broadcast_to(column_sum(jnp.where(row == in_row, found, 0.0)), (8, 128))
            for name in names:
                piece[name].drain()

        pl.run_scoped(feed_forward_scope, *scopes[0])
        pl.run_scoped(attention_scope, *scopes[1])

    block = {"d": (r_ff, width), "i": (r, ff), "o": (r, width), "t": (rows, width)}
    joined = (nc, r, 3 * half)
    vmem = lambda shape, kind=BF16: pltpu.VMEM(shape, kind)
    held_out = [vmem((owners,) + block[k]) for k in "dio"]
    scopes = (
        [
            vmem((width, width)),
            vmem((width, ff)),
            vmem((ff, width)),
            vmem((rows, ff)),
            vmem((rows, ff), F32),
            vmem((rows, ff)),
            vmem((width, rows)),
            vmem((width, rows)),
        ]
        + held_out,
        [
            vmem((width, total)),
            vmem((width, 3 * half)),
            vmem((pairs, total, 256)),
            vmem((pairs, total, 128)),
            vmem((heads, qlen, 256)),
            vmem((heads, qlen, 128)),
            vmem((heads, 8, qlen), F32),
            vmem((heads, 128, qlen), F32),
            vmem((total, 2 * half)),
            vmem((nb, nc, rows, width)),
            vmem((owners,) + joined),
            vmem((owners,) + joined),
        ],
    )
    scratch = [vmem((owners,) + block[k]) for k in "dio"] + [vmem((owners,) + block[k]) for k in "dio"]
    scratch += [vmem((nb,) + block["t"]), vmem((owners, r, 3 * half))]
    scratch += [vmem(((nd - 1) * nb,) + block[k]) for k in "dio"] + [vmem(((nd - 1) * nb,) + joined)]
    scratch += [vmem((nb + 1,) + block[k]) for k in "diot"] + [vmem((nb + 1,) + joined)]
    scratch += [
        vmem(joined, F32),
        vmem((rows, width), F32),
        vmem((nc, rows, half)),
        vmem((nc, rows, half)),
        vmem((qlen, half)),
        vmem((rows, width), F32),
        vmem((rows, width), F32),
        vmem((pairs, qlen, 128), F32),
        vmem((levels + 2, n_sums, width), F32),
        vmem((levels + nb, n_sums, width), F32),
        pltpu.SemaphoreType.DMA((13 + 2 * nb,)),
        pltpu.SemaphoreType.DMA((2,)),
    ]
    scratch += scatter_sems(5, nd, nb) + [pltpu.SemaphoreType.DMA((levels + nb,))] * 2
    return pl.pallas_call(
        kernel,
        out_shape=[
            jax.ShapeDtypeStruct((rows, width), BF16),
            jax.ShapeDtypeStruct((rows, width), F32),
            jax.ShapeDtypeStruct((r, 3 * width), F32),
            jax.ShapeDtypeStruct((r, width), F32),
            jax.ShapeDtypeStruct((r, ff), F32),
            jax.ShapeDtypeStruct((r_ff, width), F32),
            jax.ShapeDtypeStruct((16, 128), F32),
        ],
        in_specs=[VMEM] * 5 + [HBM] * 13,
        out_specs=[VMEM] * 7,
        scratch_shapes=scratch,
        compiler_params=params(62, 3),
    )(
        ctx, cot, vecs, lse, scale_one, normed, unit_one, exact_in, w_out, w_in, w_down, act_in, slope_in,
        tok_t_in, w_qkv, kaug_in, v_in, qaug_in,
    )


def body(
    tokens,
    segment,
    w_qkv,
    bias_query,
    bias_value,
    w_out,
    bias_out,
    gain_attn,
    shift_attn,
    w_in,
    bias_in,
    w_down,
    bias_down,
    gain_ffn,
    shift_ffn,
    cotangent,
):
    nd, nb, nc = lax.axis_size("dp"), lax.axis_size("blk"), lax.axis_size("head")
    n_dev = nd * nb * nc
    d_idx, b_idx, c_idx = lax.axis_index("dp"), lax.axis_index("blk"), lax.axis_index("head")
    me = (d_idx * nb + b_idx) * nc + c_idx
    seqs, rows, width = tokens.shape
    ff = w_in.shape[1]
    half_w = width // nc
    qlen = nc * rows
    r = w_qkv.shape[0]
    r_ff = w_down.shape[0]
    flat_in = tokens.reshape(rows, width)
    cot = cotangent.reshape(rows, width)
    vectors = [bias_query, bias_value, bias_out, gain_attn, shift_attn, bias_down, gain_ffn, shift_ffn]
    if nb * qlen <= 2048 and r % 8 == 0 and ff // width <= 8:
        few, many = pack_vectors(vectors, bias_in)
        (
            ctx2, vecs, lse, scale_one,
            f_qkv, f_out, f_in, f_down, kaug, v_all, qaug, tok_t, act, slope, exact, normed, unit_one,
        ) = front(few, many, w_qkv, flat_in, w_out, w_in, w_down, segment, nd, nb, nc)
        out, g_tok, o_qkv, o_out, o_in, o_down, g_small = back(
            ctx2, cot, vecs, lse, scale_one, normed, unit_one, exact, f_out, f_in, f_down, act, slope,
            tok_t, f_qkv, kaug, v_all, qaug, nd, nb, nc,
        )
        out, g_tok, o_qkv, o_out, o_in, o_down, g_bq, g_bv, g_bo, g_g1, g_s1, g_bd, g_g2, g_s2, g_bin = hand_out(
            [out, g_tok, o_qkv, o_out, o_in, o_down], g_small, r, r_ff
        )
        return (
            out.reshape(seqs, rows, width), g_tok.reshape(seqs, rows, width),
            o_qkv, g_bq, g_bv, o_out, g_bo, g_g1, g_s1, o_in, g_bin, o_down, g_bd, g_g2, g_s2,
        )
    packed = jnp.concatenate(vectors + [bias_in])
    used = packed.shape[0]
    lanes = -(-used // 128) * 128
    packed = jnp.broadcast_to(jnp.pad(packed, (0, lanes - used))[None], (8, lanes))
    n4 = 4
    parts = [flat_in[i * (rows // n4):(i + 1) * (rows // n4)] for i in range(n4)]
    shards = [packed, w_qkv] + parts + [w_out, w_in, w_down]
    narrow = [False, False] + [True] * n4 + [False] * 3
    keys = [(-1, 3, 3), (0, 3, 3), (7, 9, 0), (10, 9, 0), (13, 9, 0), (16, 9, 0), (2, 4, 4), (9, 6, 5), (22, 6, 5)]
    small, g_qkv, t0, t1, t2, t3, g_out, g_in, g_down = gather_all(shards, narrow, keys, nd, nb, nc)
    full_small = small[:, 0, :used]
    vecs = full_small[:, :8 * r].reshape(n_dev, 8, r).transpose(1, 0, 2).reshape(8, width).astype(F32)
    full_bin = full_small[:, 8 * r:].reshape(ff).astype(F32)
    bq, bv, bout, gain_one, shift_one, bdown, gain_two, shift_two = (vecs[i] for i in range(8))
    full_qkv = g_qkv.reshape(width, 3 * width)
    full_wout = g_out.reshape(width, width)
    full_win = g_in.reshape(width, ff)
    full_wdown = g_down.reshape(ff, width)
    tok_all = jnp.stack([t0, t1, t2, t3], axis=1).reshape(nb * qlen, width)
    my_bias = lax.dynamic_slice(vecs, (0, c_idx * half_w), (2, half_w))
    ctx, kaug, v_scr, qaug, lse, exact = attend_forward(tok_all, full_qkv, my_bias, segment, qlen, half_w)
    context_low = ctx.reshape(seqs, qlen, 1, half_w)
    back_tokens = lax.all_to_all(context_low, "head", split_axis=1, concat_axis=2, tiled=True)
    ctx2 = back_tokens.reshape(rows, nc, half_w).transpose(1, 0, 2)
    out, grad_resid_one, gctx2, dw_down, dw_in, dw_out, sums = feed_forward(
        ctx2, flat_in, cot, vecs, full_bin.reshape(1, ff), full_wout, full_win, full_wdown
    )
    output = out.reshape(seqs, rows, width)
    grad_context = gctx2.transpose(1, 0, 2)
    grad_headed = lax.all_to_all(
        grad_context.reshape(seqs, rows, nc, half_w), "head", split_axis=2, concat_axis=1, tiled=True
    )
    gctx = grad_headed.reshape(qlen, half_w)
    tok_mine = lax.dynamic_slice(tok_all, (b_idx * qlen, 0), (qlen, width))
    dtok, dw, dbias = attend_backward(tok_all, tok_mine, full_qkv, qaug, kaug, v_scr, lse, exact, gctx)
    dw = dw.astype(BF16).reshape(nd * nb, nc, r, 3 * half_w)
    ours = lax.dynamic_index_in_dim(dw, c_idx, 1, keepdims=False)
    theirs = lax.dynamic_index_in_dim(dw, 1 - c_idx, 1, keepdims=False)
    joined_full = jnp.stack([ours, ours], axis=1)
    sums = lax.dynamic_update_slice(sums, dbias, (0, c_idx * half_w))
    o_down, o_in, o_out, o_tok, o_qkv, total = scatter_all(
        [
            dw_down.reshape(n_dev, r_ff, width),
            dw_in.reshape(n_dev, r, ff),
            dw_out.reshape(n_dev, r, width),
            dtok.reshape(nb * nc, rows, width),
            (joined_full, theirs),
        ],
        [False, False, False, True, False],
        [False, False, False, False, True],
        sums,
        nd,
        nb,
        nc,
    )
    grad_tokens = (grad_resid_one + o_tok).reshape(seqs, rows, width)
    o_qkv = o_qkv.reshape(2, r, 3, half_w).transpose(1, 2, 0, 3).reshape(r, 3 * width)
    mine = lax.dynamic_slice(total, (0, me * r), (8, r))
    mine_in = lax.dynamic_slice(total[8:8 + ff // width].reshape(ff), (me * r_ff,), (r_ff,))
    g_bq, g_bv, g_bo, g_g1, g_s1, g_bd, g_g2, g_s2 = (mine[i] for i in range(8))
    return (
        output,
        grad_tokens,
        o_qkv,
        g_bq,
        g_bv,
        o_out,
        g_bo,
        g_g1,
        g_s1,
        o_in,
        mine_in,
        o_down,
        g_bd,
        g_g2,
        g_s2,
    )


def solution(mesh):
    weight, vector = P(("dp", "blk", "head"), None), P(("dp", "blk", "head"))
    token = P("dp", ("blk", "head"), None)
    return jax.shard_map(
        body,
        mesh=mesh,
        in_specs=(
            token,
            P("dp", None),
            weight,
            vector,
            vector,
            weight,
            vector,
            vector,
            vector,
            weight,
            vector,
            weight,
            vector,
            vector,
            vector,
            token,
        ),
        out_specs=(
            token,
            token,
            weight,
            vector,
            vector,
            weight,
            vector,
            vector,
            vector,
            weight,
            vector,
            weight,
            vector,
            vector,
            vector,
        ),
        check_vma=False,
    )
```

```python
import functools

import jax
import jax.numpy as jnp
from jax import lax
from jax.experimental import pallas as pl
from jax.experimental.pallas import tpu as pltpu
from jax.sharding import PartitionSpec as P

MESH = pl.DeviceIdType.MESH
F32, BF16 = jnp.float32, jnp.bfloat16
HD = 64
HEADS = 12
BIG = 2.0**30

class Net:
    def __init__(self, nd, nb, nc):
        self.nd, self.nb, self.nc = nd, nb, nc
        self.levels = nd.bit_length() - 1
        self.d, self.b, self.c = (lax.axis_index(a) for a in ("dp", "blk", "head"))
        top = self.levels - 1
        self.stride = [(1 - self.c) * 2**k + self.c * 2 ** (top - k) for k in range(self.levels)]
        self.sibling = (self.d, self.b, self.nc - 1 - self.c)
        steps = [s * (1 - 2 * ((self.d // s) % 2)) for s in self.stride]
        self.flipped = [self.d]
        for step in steps:
            self.flipped += [d + step for d in self.flipped]
        self.nearest = [self.find_near(e) for e in range(self.nb)]

    def flips(self, mask):
        return self.flipped[mask]

    def across(self, k):
        return (self.flipped[1 << k], self.b, self.c)

    def near(self, e):
        return self.nearest[e]

    def find_near(self, e):
        order = [sorted(range(self.nb), key=lambda j: (abs(j - i), -j)) for i in range(self.nb)]
        got = order[0][e]
        for i in range(1, self.nb):
            got = jnp.where(self.b == i, order[i][e], got)
        return got

    def near_at(self, e):
        got = self.near(0)
        for i in range(1, self.nb):
            got = jnp.where(e == i, self.near(i), got)
        return got

    def slot(self, mask, blk):
        return (self.flips(mask) * self.nb + blk) * self.nc + self.c

    def peers(self):
        out = [(self.d, (self.b + u) % self.nb, self.c) for u in range(1, self.nb)]
        out += [self.across(k) for k in range(self.levels)]
        return out + [self.sibling]

    def barrier(self):
        bar = pltpu.get_barrier_semaphore()
        ps = self.peers()
        for p in ps:
            pl.semaphore_signal(bar, inc=1, device_id=p, device_id_type=MESH)
        pl.semaphore_wait(bar, len(ps))


def remote(src, dst, send, recv, dev):
    return pltpu.make_async_remote_copy(src_ref=src, dst_ref=dst, send_sem=send, recv_sem=recv, device_id=dev, device_id_type=MESH)


def blocks_of(full):
    return (lambda i: full.at[i]), (lambda k: full.at[pl.ds(0, k)])


def rows_of(full, rows, offset=0, stride=None):
    every = rows if stride is None else stride

    def place(i):
        return full.at[pl.ds(pl.multiple_of(i * every + offset, 8), rows)]

    return place, (lambda k: full.at[pl.ds(0, k * rows)])


class Gather:
    def __init__(self, net, mine, place, span, sems, narrow=False, direct=False):
        self.net, self.mine, self.place, self.span, self.narrow, self.direct = net, mine, place, span, narrow, direct
        self.zsend, self.xsend, self.ssend, self.srecv, self.recv = sems

    def at(self, mask, blk):
        n = self.net
        if self.narrow:
            return self.place(blk * n.nc + n.c)
        return self.place(n.slot(mask, blk))

    def rsem(self, mask, blk):
        return self.recv.at[mask * self.net.nb + blk]

    def spread(self, mask, blk, src, dst):
        n = self.net
        if not self.narrow:
            for k in range(n.levels):
                if mask < (1 << k):
                    remote(src, dst, self.xsend, self.rsem(mask + (1 << k), blk), n.across(k)).start()
        arrival = self.srecv.at[blk] if self.narrow else self.srecv
        remote(src, dst, self.ssend, arrival, n.sibling).start()

    def along(self, blk, src, dst):
        n = self.net
        sem = self.rsem(0, blk)

        @pl.when((n.b < n.nb - 1) & (blk <= n.b))
        def _():
            remote(src, dst, self.zsend, sem, (n.d, n.b + 1, n.c)).start()

        @pl.when((n.b > 0) & (blk >= n.b))
        def _():
            remote(src, dst, self.zsend, sem, (n.d, n.b - 1, n.c)).start()

    def own_line(self):
        n = self.net
        dst = self.at(0, n.b)
        if not self.direct:
            self.along(n.b, self.mine, dst)
            return
        for e in range(n.nb - 1, 0, -1):
            remote(self.mine, dst, self.zsend, self.rsem(0, n.b), (n.d, n.near(e), n.c)).start()

    def own_spread(self):
        self.spread(0, self.net.b, self.mine, self.at(0, self.net.b))

    def z(self, e):
        blk = self.net.near(e)
        dst = self.at(0, blk)
        pltpu.make_async_copy(dst, dst, self.rsem(0, blk)).wait()
        if not self.direct:
            self.along(blk, dst, dst)
        self.spread(0, blk, dst, dst)

    def x(self, mask, e):
        n = self.net
        blk = n.near(e)
        dst = self.at(mask, blk)
        pltpu.make_async_copy(dst, dst, self.rsem(mask, blk)).wait()
        self.spread(mask, blk, dst, dst)

    def own(self, sem):
        n = self.net
        return pltpu.make_async_copy(self.mine, self.at(0, n.b), sem)

    def wait_sibling_block(self, blk):
        one = self.span(1)
        pltpu.make_async_copy(one, one, self.srecv.at[blk]).wait()

    def wait_sibling(self):
        n = self.net
        if self.narrow:
            for blk in range(n.nb):
                self.wait_sibling_block(blk)
            return
        half = self.span(n.nd * n.nb)
        pltpu.make_async_copy(half, half, self.srecv).wait()

    def drain(self):
        n = self.net
        half = self.span(n.nb if self.narrow else n.nd * n.nb)
        pltpu.make_async_copy(half, half, self.ssend).wait()
        if not self.narrow:
            part = self.span((n.nd - 1) * n.nb)
            pltpu.make_async_copy(part, part, self.xsend).wait()
        if self.direct:
            sent = self.span(n.nb - 1)
            pltpu.make_async_copy(sent, sent, self.zsend).wait()
            return
        edge = (n.b == 0) | (n.b == n.nb - 1)

        @pl.when(edge)
        def _():
            one = self.span(1)
            pltpu.make_async_copy(one, one, self.zsend).wait()

        @pl.when(jnp.logical_not(edge))
        def _():
            many = self.span(n.nb + 1)
            pltpu.make_async_copy(many, many, self.zsend).wait()


def gather_refs(four, recv, block, p, narrow):
    last = block.at[p] if narrow else four.at[p, 3]
    return [four.at[p, 0], four.at[p, 1], four.at[p, 2], last, recv.at[p]]


def gather_sems(n_pieces, nd, nb):
    return [pltpu.SemaphoreType.DMA((n_pieces, 4)), pltpu.SemaphoreType.DMA((n_pieces, nd * nb)), pltpu.SemaphoreType.DMA]


class Scatter:
    def __init__(self, net, parts, place, theirs, landing, span, xrecv, zrecv, out, sems, narrow=False, extra=(), early=False, direct=False):
        self.net, self.parts, self.place, self.theirs, self.landing = net, parts, place, theirs, landing
        self.span, self.xbuf, self.zbuf, self.out, self.extra = span, xrecv, zrecv, out, extra
        self.sib_send, self.x_send, self.z_send, self.sib_sem, self.x_sem, self.z_sem = sems
        self.narrow, self.seen, self.early, self.direct = narrow, set(), early, direct
        self.nd = 1 if narrow else net.nd
        self.levels = 0 if narrow else net.levels

    def home(self, mask):
        return 0 if self.narrow else self.net.flips(mask)

    def start(self):
        for mask in range(self.nd - 1, -1, -1):
            self.start_home(self.home(mask))

    def start_home(self, d):
        for blk in range(self.net.nb):
            self.send(d * self.net.nb + blk, d)

    def send(self, at, sem):
        remote(self.theirs(at), self.landing(at), self.sib_send, self.sib_sem.at[sem], self.net.sibling).start()

    def arrived(self, sem, count):
        some = self.span(count)
        pltpu.make_async_copy(some, some, self.sib_sem.at[sem]).wait()

    def sent(self):
        some = self.span(self.nd * self.net.nb)
        pltpu.make_async_copy(some, some, self.sib_send).wait()

    def x_at(self, k, mask, blk):
        return ((1 << k) - 1 + mask) * self.net.nb + blk

    def z_at(self, side, blk, owner):
        return blk + side * jnp.where(blk == owner, self.net.nb - blk, 0)

    def add(self, at, more, to, extra=()):
        for pick, places in self.parts(at):
            def chosen(ref):
                return ref if pick is None else ref.at[pick]

            add_up(places + [chosen(m) for m in more] + list(extra), chosen(to))

    def reduce(self, mask, e):
        n = self.net
        blk = n.near(e)
        if self.narrow:
            self.arrived(blk, 1)
        elif mask not in self.seen:
            self.seen.add(mask)
            self.arrived(self.home(mask), n.nb)
        at = self.home(mask) * n.nb + blk
        place = self.place(at)
        more = []
        for k in range(self.levels - 1, -1, -1):
            if mask < (1 << k):
                i = self.x_at(k, mask, blk)
                got = self.xbuf.at[i]
                pltpu.make_async_copy(got, got, self.x_sem.at[i]).wait()
                more.append(got)
        if mask:
            k = mask.bit_length() - 1
            self.add(at, more, place)
            i = self.x_at(k, mask - (1 << k), blk)
            remote(place, self.xbuf.at[i], self.x_send, self.x_sem.at[i], n.across(k)).start()
            return

        if self.direct:
            if e:
                self.add(at, more, place)
                remote(place, self.zbuf.at[n.b], self.z_send, self.z_sem.at[n.b], (n.d, blk, n.c)).start()
                return
            for u in range(1, n.nb):
                got = self.zbuf.at[n.near(u)]
                pltpu.make_async_copy(got, got, self.z_sem.at[n.near(u)]).wait()
                more.append(got)
            self.add(at, more, self.out, self.extra)
            return

        def line(side, there):
            i = self.z_at(side, blk, n.b)
            got = self.zbuf.at[i]

            @pl.when(there)
            def _():
                pltpu.make_async_copy(got, got, self.z_sem.at[i]).wait()

            more.append(got)

        if e == 0:
            line(0, n.b > 0)
            line(1, n.b < n.nb - 1)
            self.add(at, more, self.out, self.extra)
            return
        side = jnp.where(blk > n.b, 0, 1)
        line(side, jnp.where(blk > n.b, n.b, n.nb - 1 - n.b) > 0)
        self.add(at, more, place)
        to = n.b + 1 - 2 * side
        i = self.z_at(side, blk, to)
        remote(place, self.zbuf.at[i], self.z_send, self.z_sem.at[i], (n.d, to, n.c)).start()

    def clear_edges(self):
        n = self.net
        if self.direct:
            return

        def clear(i, carry):
            self.zbuf[i] = jnp.zeros(self.zbuf.shape[1:], self.zbuf.dtype)
            return carry

        @pl.when(n.b == 0)
        def _():
            lax.fori_loop(0, n.nb, clear, 0)

        @pl.when(n.b == n.nb - 1)
        def _():
            lax.fori_loop(0, n.nb - 1, clear, 0)
            clear(n.nb, 0)

    def drain(self):
        n = self.net
        if not self.early:
            self.sent()
        if not self.narrow:
            some = self.xbuf.at[pl.ds(0, (n.nd - 1) * n.nb)]
            pltpu.make_async_copy(some, some, self.x_send).wait()
        some = self.zbuf.at[pl.ds(0, n.nb - 1)]
        pltpu.make_async_copy(some, some, self.z_send).wait()


def add_up(terms, to):
    shape = to.shape
    rows = shape[-2]
    step = rows
    while step % 2 == 0 and step > 32:
        step //= 2
    lead = [()] if len(shape) == 2 else [(g,) for g in range(shape[0])]
    for g in lead:
        for r in range(0, rows, step):
            at = g + (slice(r, r + step),)
            total = terms[0][at].astype(F32)
            for t in terms[1:]:
                total = total + t[at].astype(F32)
            to[at] = total.astype(to.dtype)


class AllSum:
    def __init__(self, net, value, got, send, recv):
        self.net, self.value, self.got, self.send, self.recv = net, value, got, send, recv

    def copy(self, stage, dev, src, slot):
        return remote(self.value.at[src], self.got.at[slot], self.send.at[slot], self.recv.at[slot], dev)

    def stages(self):
        n = self.net
        devs = [n.sibling] + [n.across(k) for k in range(n.levels)]
        steps = []
        for i, dev in enumerate(devs):
            steps.append(functools.partial(self.one, i, dev))
        steps.append(self.line_start)
        steps.append(self.line_end)
        return [lambda: self.copy(0, devs[0], 0, 0).start()] + steps

    def one(self, i, dev):
        n = self.net
        self.copy(i, dev, i, i).wait()
        self.value[i + 1] = self.value[i] + self.got[i]
        if i + 1 <= n.levels:
            self.copy(i + 1, n.across(i), i + 1, i + 1).start()

    def line_copy(self, u):
        n = self.net
        return self.copy(None, (n.d, (n.b + u) % n.nb, n.c), n.levels + 1, n.levels + u)

    def line_start(self):
        for u in range(1, self.net.nb):
            self.line_copy(u).start()

    def line_end(self):
        n = self.net
        for u in range(1, n.nb):
            self.line_copy(u).wait()
        total = self.value[n.levels + 1]
        for u in range(1, n.nb):
            total = total + self.got[n.levels + u]
        self.value[0] = total


def scatter_sems(n_pieces, nd, nb):
    return [
        pltpu.SemaphoreType.DMA((n_pieces, 3)),
        pltpu.SemaphoreType.DMA((n_pieces, max(nd, nb))),
        pltpu.SemaphoreType.DMA((n_pieces, (nd - 1) * nb)),
        pltpu.SemaphoreType.DMA((n_pieces, nb + 1)),
    ]


def dot(a, b, dims=((1,), (0,))):
    return lax.dot_general(a, b, (dims, ((), ())), preferred_element_type=F32)


def mask_lanes(seg_row, count):
    lanes = lax.broadcasted_iota(jnp.int32, (128, count), 0)
    return jnp.transpose(jnp.where(lanes == seg_row, -1.0, 0.0).astype(F32), (1, 0))


def project_keys(i, step, tok, wk, wv, bias_v, seg, kaug, v_scr):
    at = pl.ds(pl.multiple_of(i * step, step), step)
    piece = tok[at, :]
    keys = dot(piece, wk).astype(BF16)
    vals = (dot(piece, wv) + bias_v).astype(BF16)
    lanes = mask_lanes(seg[:, at], step).astype(BF16)
    for p in range(kaug.shape[0]):
        kaug[p, at, 0:128] = keys[:, p * 128:(p + 1) * 128]
        kaug[p, at, 128:256] = lanes
        v_scr[p, at, :] = vals[:, p * 128:(p + 1) * 128]


def project_queries(tok, wq, bias_q, seg, qaug, blk, qlen):
    mine = pl.ds(pl.multiple_of(blk * qlen, qlen), qlen)
    query = (dot(tok[mine, :], wq) + bias_q).astype(BF16)
    lane = lax.broadcasted_iota(jnp.int32, (qlen, 128), 1)
    feat = jnp.where(lane < 8, BIG * (1.0 + mask_lanes(seg[:, mine], qlen)), 0.0).astype(BF16)
    for p in range(qaug.shape[0] // 2):
        q_pair = query[:, p * 128:(p + 1) * 128].astype(F32) * HD**-0.5
        for half in range(2):
            keep = (lane >= 64) if half else (lane < 64)
            qaug[2 * p + half, :, 0:128] = jnp.where(keep, q_pair, 0.0).astype(BF16)
            qaug[2 * p + half, :, 128:256] = feat


def attend_chunk(i, qaug, kaug, v_scr, o_scr, exact_scr, lse_scr, chunk, per_head):
    h = i // per_head
    at = pl.ds(pl.multiple_of((i % per_head) * chunk, chunk), chunk)
    s = dot(qaug[h, at, :], kaug[h // 2], ((1,), (1,)))
    top = jnp.max(s, axis=-1, keepdims=True)
    p = jnp.exp(s - top)
    total = jnp.sum(p, axis=-1, keepdims=True)
    low = p.astype(BF16)
    rest = (p - low.astype(F32)).astype(BF16)
    value = v_scr[h // 2]
    o = dot(low, value)
    inverse = 1.0 / total
    o_scr[h, at, :] = o * inverse
    exact_scr[h, at, :] = (o + dot(rest, value)) * inverse
    lse_scr[h, at, :] = jnp.broadcast_to(top + jnp.log(total), (chunk, 128))


def attend_block(h, at, qaug, kaug, v_scr, top_scr, sum_scr, o_scr, rest_scr):
    s = dot(qaug[h], kaug[h // 2, at, :], ((1,), (1,)))
    before = top_scr[h]
    top = jnp.maximum(before, jnp.broadcast_to(jnp.max(s, axis=-1, keepdims=True), before.shape))
    p = jnp.exp(s - jnp.concatenate([top] * (s.shape[1] // 128), axis=1))
    fade = jnp.exp(before - top)
    low = p.astype(BF16)
    rest = (p - low.astype(F32)).astype(BF16)
    value = v_scr[h // 2, at, :]
    top_scr[h] = top
    sum_scr[h] = sum_scr[h] * fade + jnp.broadcast_to(jnp.sum(p, axis=-1, keepdims=True), before.shape)
    o_scr[h] = o_scr[h] * fade + dot(low, value)
    rest_scr[h] = rest_scr[h] * fade + dot(rest, value)


def close_blocks(top_scr, sum_scr, o_scr, rest_scr):
    for h in range(o_scr.shape[0]):
        total = sum_scr[h]
        inverse = 1.0 / total
        o = o_scr[h]
        rest_scr[h] = (o + rest_scr[h]) * inverse
        o_scr[h] = o * inverse
        top_scr[h] = top_scr[h] + jnp.log(total)


def join_heads(scr, p, at=slice(None)):
    first, second = scr[2 * p, at, :], scr[2 * p + 1, at, :]
    lane = lax.broadcasted_iota(jnp.int32, first.shape, 1)
    return jnp.where(lane < 64, first, second)


def head_columns(w, part, c, width):
    return w[:, pl.ds(pl.multiple_of((part * 2 + c) * width, 128), width)]


def fwd_kernel(tok, w, bias, seg, ctx, kaug, v_scr, qaug, lse_out, exact, lse_scr, o_scr, exact_scr, chunk=256):
    blk, c = lax.axis_index("blk"), lax.axis_index("head")
    qlen, width = ctx.shape
    total = tok.shape[0]
    step = min(512, total)
    wk, wv = head_columns(w, 1, c, width), head_columns(w, 2, c, width)

    def rows(i, carry):
        project_keys(i, step, tok, wk, wv, bias[1:2, :], seg, kaug, v_scr)
        return carry

    lax.fori_loop(0, total // step, rows, 0)
    project_queries(tok, head_columns(w, 0, c, width), bias[0:1, :], seg, qaug, blk, qlen)
    per_head = qlen // chunk

    def go(i, carry):
        attend_chunk(i, qaug, kaug, v_scr, o_scr, exact_scr, lse_scr, chunk, per_head)
        return carry

    lax.fori_loop(0, (width // HD) * per_head, go, 0)
    finish_forward(o_scr, exact_scr, lse_scr, lambda p, v: store_lanes(ctx, p, v), lse_out, exact)


def store_lanes(ref, p, value):
    ref[:, p * 128:(p + 1) * 128] = value


def finish_forward(o_scr, exact_scr, lse_scr, put, lse_out, exact):
    for p in range(o_scr.shape[0] // 2):
        put(p, join_heads(o_scr, p).astype(BF16))
        exact[p] = join_heads(exact_scr, p)
    for h in range(o_scr.shape[0]):
        lse_out[h] = jnp.transpose(lse_scr[h], (1, 0))[0:8, :]


def prepare_backward(gctx_of, exact, do_m, delta_row):
    pairs, qlen, _ = exact.shape
    lane = lax.broadcasted_iota(jnp.int32, (qlen, 128), 1)
    for p in range(pairs):
        grad = gctx_of(p)
        product = grad.astype(F32) * exact[p]
        for half in range(2):
            keep = (lane >= 64) if half else (lane < 64)
            do_m[2 * p + half] = jnp.where(keep, grad, jnp.zeros_like(grad))
            across = jnp.transpose(jnp.where(keep, product, 0.0), (1, 0))
            delta_row[2 * p + half] = jnp.broadcast_to(jnp.sum(across, axis=0, keepdims=True), (8, qlen))


def bwd_pair(pair, qaug, k_part, v_part, do_m, lse_row, delta_row, dq_scr, put, first, qs=slice(None)):
    dk = dv = None
    for half in range(2):
        h = 2 * pair + half
        q_part, do_part = qaug[h, qs, :], do_m[h, qs, :]
        s = dot(k_part, q_part, ((1,), (1,)))
        p = jnp.exp(s - lse_row[h, 0:1, qs])
        dp = dot(v_part, do_part, ((1,), (1,)))
        ds = (p * (dp - delta_row[h, 0:1, qs])).astype(BF16)
        v_term = dot(p.astype(BF16), do_part)
        k_term = dot(ds, q_part[:, 0:128])
        dv = v_term if dv is None else dv + v_term
        dk = k_term if dk is None else dk + k_term
        dq = dot(k_part[:, 0:128], ds, ((0,), (0,)))
        if first is True:
            dq_scr[h, :, qs] = dq
        elif first is None:
            dq_scr[h, :, qs] += dq
        else:
            dq_scr[h, :, qs] = jnp.where(first, dq, dq_scr[h, :, qs] + dq)
    put(dk, dv)


def join_dq(dq_scr, p):
    qlen = dq_scr.shape[2]
    lane = lax.broadcasted_iota(jnp.int32, (qlen, 128), 1)
    first, second = jnp.transpose(dq_scr[2 * p], (1, 0)), jnp.transpose(dq_scr[2 * p + 1], (1, 0))
    return (jnp.where(lane < 64, first, second) * HD**-0.5).astype(BF16)


VMEM = pl.BlockSpec(memory_space=pltpu.VMEM)
HBM = pl.BlockSpec(memory_space=pltpu.HBM)


def params(limit, collective=None):
    more = {} if collective is None else dict(collective_id=collective, has_side_effects=True)
    return pltpu.CompilerParams(vmem_limit_bytes=limit << 20, **more)


def lane_mean(x):
    return jnp.mean(x, axis=-1, keepdims=True)


def norm_parts(hidden):
    centered = hidden - lane_mean(hidden)
    scale = lax.rsqrt(lane_mean(centered * centered) + 1e-12)
    return centered * scale, scale


def norm_back(grad, unit, scale, gain):
    scaled = grad * gain
    return scale * (scaled - lane_mean(scaled) - unit * lane_mean(scaled * unit))


def gelu_and_slope(pre):
    cdf = 0.5 * (1.0 + lax.erf(pre * 0.7071067811865476))
    return pre * cdf, cdf + pre * (0.3989422804014327 * jnp.exp(-0.5 * pre * pre))


def column_sum(x):
    return jnp.sum(x, axis=0, keepdims=True)


def ffn_kernel(
    ctx, tok, cot, vecs, bias_in, w_out_h, w_in_h, w_down_h,
    out, resid_grad, gctx, dw_down_h, dw_in_h, dw_out_h, sums,
    w_out, w_in, w_down, act, slope, dw_a, dw_b, dw_c, in_sem, out_sem,
):
    groups, rows, half = ctx.shape
    width, ff = w_in.shape
    step = width
    loads = [
        pltpu.make_async_copy(src, dst, in_sem.at[i])
        for i, (src, dst) in enumerate([(w_out_h, w_out), (w_in_h, w_in), (w_down_h, w_down)])
    ]
    for load in loads:
        load.start()
    bias_out, gain_one, shift_one = vecs[2:3, :], vecs[3:4, :], vecs[4:5, :]
    bias_down, gain_two, shift_two = vecs[5:6, :], vecs[6:7, :], vecs[7:8, :]
    context = jnp.concatenate([ctx[g] for g in range(groups)], axis=1)
    loads[0].wait()
    resid_one = tok[...].astype(F32) + (dot(context, w_out[...]) + bias_out)
    unit_one, scale_one = norm_parts(resid_one)
    normed = unit_one * gain_one + shift_one
    normed_low = normed.astype(BF16)
    loads[1].wait()
    chunks = [slice(i, i + step) for i in range(0, ff, step)]
    for at in chunks:
        pre = dot(normed_low, w_in[:, at]) + bias_in[0:1, at]
        value, grad = gelu_and_slope(pre)
        act[:, at] = value.astype(BF16)
        slope[:, at] = grad
    loads[2].wait()
    resid_two = normed + (dot(act[...], w_down[...]) + bias_down)
    unit_two, scale_two = norm_parts(resid_two)
    out[...] = (unit_two * gain_two + shift_two).astype(BF16)
    grad_out = cot[...].astype(F32)
    grad_two = norm_back(grad_out, unit_two, scale_two, gain_two)
    grad_ffn = grad_two.astype(BF16)
    sums[0:2, :] = jnp.zeros((2, width), F32)
    sums[5:6, :] = column_sum(grad_ffn.astype(F32))
    sums[6:7, :] = column_sum(grad_out * unit_two)
    sums[7:8, :] = column_sum(grad_out)
    stores = []

    def store(src, dst):
        copy = pltpu.make_async_copy(src, dst, out_sem.at[len(stores)])
        copy.start()
        stores.append(copy)

    for at in chunks:
        dw_a[at, :] = dot(act[:, at], grad_ffn, ((0,), (0,))).astype(BF16)
        store(dw_a.at[at], dw_down_h.at[at])
    grad_normed = grad_two
    for i, at in enumerate(chunks):
        grad_act = dot(grad_ffn, w_down[at, :], ((1,), (1,)))
        grad_pre = (grad_act * slope[:, at]).astype(BF16)
        sums[8 + i:9 + i, :] = column_sum(grad_pre.astype(F32))
        dw_b[:, at] = dot(normed_low, grad_pre, ((0,), (0,))).astype(BF16)
        grad_normed = grad_normed + dot(grad_pre, w_in[:, at], ((1,), (1,)))
    store(dw_b, dw_in_h)
    sums[8 + len(chunks):, :] = jnp.zeros((sums.shape[0] - 8 - len(chunks), width), F32)
    sums[3:4, :] = column_sum(grad_normed * unit_one)
    sums[4:5, :] = column_sum(grad_normed)
    grad_one = norm_back(grad_normed, unit_one, scale_one, gain_one)
    resid_grad[...] = grad_one
    grad_attn = grad_one.astype(BF16)
    sums[2:3, :] = column_sum(grad_attn.astype(F32))
    dw_c[...] = dot(context, grad_attn, ((0,), (0,))).astype(BF16)
    store(dw_c, dw_out_h)
    grad_context = dot(grad_attn, w_out[...], ((1,), (1,))).astype(BF16)
    for g in range(groups):
        gctx[g] = grad_context[:, g * half:(g + 1) * half]
    for copy in stores:
        copy.wait()


def feed_forward(ctx, tok, cot, vecs, bias_in, w_out, w_in, w_down):
    groups, rows, half = ctx.shape
    width, ff = w_in.shape
    n_sums = 8 + -(-(ff // width) // 8) * 8
    return pl.pallas_call(
        ffn_kernel,
        out_shape=[
            jax.ShapeDtypeStruct((rows, width), BF16),
            jax.ShapeDtypeStruct((rows, width), F32),
            jax.ShapeDtypeStruct((groups, rows, half), BF16),
            jax.ShapeDtypeStruct((ff, width), BF16),
            jax.ShapeDtypeStruct((width, ff), BF16),
            jax.ShapeDtypeStruct((width, width), BF16),
            jax.ShapeDtypeStruct((n_sums, width), F32),
        ],
        in_specs=[VMEM] * 5 + [HBM] * 3,
        out_specs=[VMEM] * 3 + [HBM] * 3 + [VMEM],
        scratch_shapes=[
            pltpu.VMEM((width, width), BF16),
            pltpu.VMEM((width, ff), BF16),
            pltpu.VMEM((ff, width), BF16),
            pltpu.VMEM((rows, ff), BF16),
            pltpu.VMEM((rows, ff), F32),
            pltpu.VMEM((ff, width), BF16),
            pltpu.VMEM((width, ff), BF16),
            pltpu.VMEM((width, width), BF16),
            pltpu.SemaphoreType.DMA((3,)),
            pltpu.SemaphoreType.DMA((ff // width + 2,)),
        ],
        compiler_params=params(56),
    )(ctx, tok, cot, vecs, bias_in, w_out, w_in, w_down)


def gather_order(keys, narrow, nd, nb):
    events = []
    for p, (begin, dz, dx) in enumerate(keys):
        for e in range(nb):
            events.append((begin + e * dz, ("z", p, e)))
            if not narrow[p]:
                for mask in range(1, nd):
                    events.append((begin + e * dz + dx * mask.bit_length(), ("x", p, mask, e)))
    events.sort(key=lambda q: q[0])
    return [ev for _, ev in events]


def gather_all(shards, narrow, keys, nd, nb, nc):
    count = len(shards)

    def kernel(*refs):
        mine, full = refs[:count], refs[count:2 * count]
        four, recv, own_sem, block_sem = refs[2 * count:]
        net = Net(nd, nb, nc)
        pieces = [
            Gather(net, mine[p], *blocks_of(full[p]), gather_refs(four, recv, block_sem, p, narrow[p]), narrow[p]) for p in range(count)
        ]
        net.barrier()
        for ev in gather_order(keys, narrow, nd, nb):
            if ev[0] == "z" and ev[2] == 0:
                pieces[ev[1]].own_line()
                pieces[ev[1]].own_spread()
            elif ev[0] == "z":
                pieces[ev[1]].z(ev[2])
            else:
                pieces[ev[1]].x(ev[2], ev[3])
        for piece in pieces:
            own = piece.own(own_sem)
            own.start()
            own.wait()
        for piece in pieces:
            piece.wait_sibling()
        for piece in pieces:
            piece.drain()

    outs = [
        jax.ShapeDtypeStruct(((nb * nc if thin else nd * nb * nc),) + s.shape, s.dtype) for s, thin in zip(shards, narrow)
    ]
    return pl.pallas_call(
        kernel,
        out_shape=outs,
        in_specs=[VMEM] * count,
        out_specs=[HBM] * count,
        scratch_shapes=gather_sems(count, nd, nb) + [pltpu.SemaphoreType.DMA((count, nb))],
        compiler_params=params(56, 0),
    )(*shards)


def attend_forward(tok, w, bias, seg, qlen, width):
    total = tok.shape[0]
    heads = width // HD
    chunk = min(256, qlen)
    while chunk * total > 256 * 4096:
        chunk //= 2
    return pl.pallas_call(
        functools.partial(fwd_kernel, chunk=chunk),
        out_shape=[
            jax.ShapeDtypeStruct((qlen, width), BF16),
            jax.ShapeDtypeStruct((width // 128, total, 256), BF16),
            jax.ShapeDtypeStruct((width // 128, total, 128), BF16),
            jax.ShapeDtypeStruct((heads, qlen, 256), BF16),
            jax.ShapeDtypeStruct((heads, 8, qlen), F32),
            jax.ShapeDtypeStruct((heads // 2, qlen, 128), F32),
        ],
        in_specs=[VMEM] * 4,
        out_specs=[VMEM] * 6,
        scratch_shapes=[pltpu.VMEM((heads, qlen, 128), F32)] * 3,
        compiler_params=params(58),
    )(tok, w, bias, seg)


def pair_bwd_kernel(qaug, kaug, v_scr, lse, exact, gctx, dk, dv, dq, do_m, delta_row, dq_scr):
    step = pl.program_id(1)

    @pl.when(step == 0)
    def _():
        prepare_backward(lambda p: gctx[...], exact, do_m, delta_row)

    def put(k_term, v_term):
        dk[...] = k_term.astype(BF16)
        dv[...] = v_term.astype(BF16)

    bwd_pair(0, qaug, kaug[0], v_scr[0], do_m, lse, delta_row, dq_scr, put, step == 0)

    @pl.when(step == pl.num_programs(1) - 1)
    def _():
        dq[...] = join_dq(dq_scr, 0)


def finish_kernel(tok, dk, dv, tok_mine, dq, w, dtok, dw, dbias, own):
    i, c = pl.program_id(0), lax.axis_index("head")
    blk = lax.axis_index("blk")
    step, width = dk.shape
    qlen = dq.shape[0]

    def cols(part):
        return w[:, pl.ds(pl.multiple_of((part * 2 + c) * width, 128), width)]

    piece, grad_k, grad_v = tok[...], dk[...], dv[...]

    @pl.when(i == 0)
    def _():
        dw[:, 0:width] = dot(tok_mine[...], dq[...], ((0,), (0,)))
        dw[:, width:3 * width] = jnp.zeros((dw.shape[0], 2 * width), F32)
        dbias[0:1, :] = jnp.sum(dq[...].astype(F32), axis=0, keepdims=True)
        dbias[1:2, :] = jnp.zeros((1, width), F32)
        own[...] = dot(dq[...], cols(0), ((1,), (1,)))

    dw[:, width:2 * width] += dot(piece, grad_k, ((0,), (0,)))
    dw[:, 2 * width:3 * width] += dot(piece, grad_v, ((0,), (0,)))
    dbias[1:2, :] += jnp.sum(grad_v.astype(F32), axis=0, keepdims=True)
    grad = dot(grad_k, cols(1), ((1,), (1,))) + dot(grad_v, cols(2), ((1,), (1,)))
    per = qlen // step
    mine = i // per == blk
    at = pl.ds(pl.multiple_of((i % per) * step, step), step)
    dtok[...] = (grad + jnp.where(mine, own[at, :], 0.0)).astype(BF16)


def attend_backward(tok, tok_mine, w, qaug, kaug, v_scr, lse, exact, gctx):
    heads, qlen, _ = qaug.shape
    total, d_model = tok.shape
    width = heads * HD
    kc = min(512, total)
    dk, dv, dq = pl.pallas_call(
        pair_bwd_kernel,
        grid=(heads // 2, total // kc),
        out_shape=[
            jax.ShapeDtypeStruct((total, width), BF16),
            jax.ShapeDtypeStruct((total, width), BF16),
            jax.ShapeDtypeStruct((qlen, width), BF16),
        ],
        in_specs=[
            pl.BlockSpec((2, qlen, 256), lambda p, j: (p, 0, 0)),
            pl.BlockSpec((1, kc, 256), lambda p, j: (p, j, 0)),
            pl.BlockSpec((1, kc, 128), lambda p, j: (p, j, 0)),
            pl.BlockSpec((2, 8, qlen), lambda p, j: (p, 0, 0)),
            pl.BlockSpec((1, qlen, 128), lambda p, j: (p, 0, 0)),
            pl.BlockSpec((qlen, 128), lambda p, j: (0, p)),
        ],
        out_specs=[pl.BlockSpec((kc, 128), lambda p, j: (j, p))] * 2 + [pl.BlockSpec((qlen, 128), lambda p, j: (0, p))],
        scratch_shapes=[
            pltpu.VMEM((2, qlen, 128), BF16),
            pltpu.VMEM((2, 8, qlen), F32),
            pltpu.VMEM((2, 128, qlen), F32),
        ],
        compiler_params=params(56),
    )(qaug, kaug, v_scr, lse, exact, gctx)
    step = min(512, qlen)
    whole = lambda i: (0, 0)
    rows = lambda i: (i, 0)
    return pl.pallas_call(
        finish_kernel,
        grid=(total // step,),
        out_shape=[
            jax.ShapeDtypeStruct((total, d_model), BF16),
            jax.ShapeDtypeStruct((d_model, 3 * width), F32),
            jax.ShapeDtypeStruct((2, width), F32),
        ],
        in_specs=[
            pl.BlockSpec((step, d_model), rows),
            pl.BlockSpec((step, width), rows),
            pl.BlockSpec((step, width), rows),
            pl.BlockSpec((qlen, d_model), whole),
            pl.BlockSpec((qlen, width), whole),
            pl.BlockSpec((d_model, w.shape[1]), whole),
        ],
        out_specs=[
            pl.BlockSpec((step, d_model), rows),
            pl.BlockSpec((d_model, 3 * width), whole),
            pl.BlockSpec((2, width), whole),
        ],
        scratch_shapes=[pltpu.VMEM((qlen, d_model), F32)],
        compiler_params=params(56),
    )(tok, dk, dv, tok_mine, dq, w)


SPACE = (0.25, 1.0, 0.2)


def send_blocks(piece, nb):
    for blk in range(nb):
        piece.send(blk, blk)


def scatter_all(arrays, narrow, joined, small, nd, nb, nc):
    count = len(arrays)
    flat = []
    for a, j in zip(arrays, joined):
        flat += list(a) if j else [a]
    n_in = len(flat) + 1

    def kernel(*refs):
        ins, small_in = list(refs[:n_in - 1]), refs[n_in - 1]
        outs, small_out = refs[n_in:n_in + count], refs[n_in + count]
        rest = list(refs[n_in + count + 1:])
        net = Net(nd, nb, nc)
        s3, sib_sem, x_sem, z_sem, sum_send, sum_recv = rest[-6:]
        value, got = rest[-8:-6]
        bufs = rest[:-8]
        pieces = []
        for p in range(count):
            first = ins.pop(0)
            sib = ins.pop(0) if joined[p] else bufs.pop(0)
            xbuf = None if narrow[p] else bufs.pop(0)
            zbuf = bufs.pop(0)
            sems = [s3.at[p, i] for i in range(3)] + [sib_sem.at[p], x_sem.at[p], z_sem.at[p]]
            if joined[p]:
                parts = lambda at, first=first: [(None, [first.at[at]])]
                place = lambda at, first=first: first.at[at]
                theirs = lambda at, sib=sib: sib.at[at]
                landing = lambda at, first=first: first.at[at, net.c]
            else:
                place = lambda at, first=first: first.at[at * nc + net.c]
                parts = lambda at, place=place, sib=sib: [(None, [place(at), sib.at[at]])]
                theirs = lambda at, first=first: first.at[at * nc + nc - 1 - net.c]
                landing = lambda at, sib=sib: sib.at[at]
            span = lambda k, sib=sib: sib.at[pl.ds(0, k)]
            pieces.append(Scatter(net, parts, place, theirs, landing, span, xbuf, zbuf, outs[p], sems, narrow[p]))
        sums = AllSum(net, value, got, sum_send, sum_recv)
        for piece in pieces:
            piece.clear_edges()
        value[0] = small_in[...]
        net.barrier()
        events = []
        for p, piece in enumerate(pieces):
            t = SPACE[0] * p
            begin = functools.partial(send_blocks, piece, nb) if narrow[p] else piece.start
            events.append((t - 0.4, begin))
            for mask in range(piece.nd - 1, -1, -1):
                for e in range(nb - 1, -1, -1):
                    when = t + SPACE[1] * (piece.levels - mask.bit_length()) + SPACE[2] * (nb - 1 - e)
                    events.append((when, functools.partial(piece.reduce, mask, e)))
        for i, s in enumerate(sums.stages()):
            events.append((0.3 * i, s))
        events.sort(key=lambda q: q[0])
        for _, ev in events:
            ev()
        small_out[...] = value[0]
        for piece in pieces:
            piece.drain()

    outs, scratch = [], []
    for a, thin, j in zip(arrays, narrow, joined):
        full = a[0] if j else a
        block = full.shape[1:]
        outs.append(jax.ShapeDtypeStruct(block, F32))
        n_dp = 1 if thin else nd
        if not j:
            scratch.append(pltpu.VMEM((n_dp * nb,) + block, BF16))
        if not thin:
            scratch.append(pltpu.VMEM(((nd - 1) * nb,) + block, BF16))
        scratch.append(pltpu.VMEM((nb + 1,) + block, BF16))
    levels = nd.bit_length() - 1
    scratch += [pltpu.VMEM((levels + 2,) + small.shape, F32), pltpu.VMEM((levels + nb,) + small.shape, F32)]
    scratch += scatter_sems(count, nd, nb)
    scratch += [pltpu.SemaphoreType.DMA((levels + nb,))] * 2
    outs.append(jax.ShapeDtypeStruct(small.shape, F32))
    return pl.pallas_call(
        kernel,
        out_shape=outs,
        in_specs=[VMEM] * n_in,
        out_specs=[VMEM] * (count + 1),
        scratch_shapes=scratch,
        compiler_params=params(60, 1),
    )(*flat, small)


def hand_out(arrays, small, r, r_ff):
    count = len(arrays)

    def kernel(*refs):
        ins, small_in = refs[:count], refs[count]
        outs, vectors, sems = refs[count + 1:2 * count + 1], refs[2 * count + 1:-1], refs[-1]
        copies = [pltpu.make_async_copy(a, b, sems.at[i]) for i, (a, b) in enumerate(zip(ins, outs))]
        for copy in copies:
            copy.start()
        for i, out in enumerate(vectors):
            out[...] = small_in[i, 0:out.shape[0]]
        for copy in copies:
            copy.wait()

    sizes = [r] * 8 + [r_ff]
    return pl.pallas_call(
        kernel,
        out_shape=[jax.ShapeDtypeStruct(a.shape, a.dtype) for a in arrays] + [jax.ShapeDtypeStruct((s,), F32) for s in sizes],
        in_specs=[VMEM] * (count + 1),
        out_specs=[HBM] * count + [VMEM] * 9,
        scratch_shapes=[pltpu.SemaphoreType.DMA((count,))],
        compiler_params=params(60),
    )(*arrays, small)


def unpack_vectors(small, vecs, bias_in, r, r_ff):
    n = small.shape[0]
    width, ff = vecs.shape[1], bias_in.shape[1]

    def gathered(rows, per, count):
        lane = lax.broadcasted_iota(jnp.int32, (8, 128), 1)
        tiles = [jnp.zeros((8, 128), F32) for _ in range(count // 128)]
        for i in range(n):
            piece = small[i, rows, :].astype(F32)
            shift, tile = per * i % 128, per * i // 128
            if shift:
                piece = pltpu.roll(piece, shift, 1)
            if shift + per <= 128:
                tiles[tile] = tiles[tile] + piece
            else:
                tiles[tile] = tiles[tile] + jnp.where(lane >= shift, piece, 0.0)
                tiles[tile + 1] = tiles[tile + 1] + jnp.where(lane < shift, piece, 0.0)
        return tiles

    for t, tile in enumerate(gathered(slice(0, 8), r, width)):
        vecs[:, t * 128:(t + 1) * 128] = tile
    for t, tile in enumerate(gathered(slice(8, 16), r_ff, ff)):
        bias_in[:, t * 128:(t + 1) * 128] = tile[0:1, :]


def pack_vectors(vectors, bias_in):
    shape = (16,) + vectors[0].shape
    row = lax.broadcasted_iota(jnp.int32, shape, 0)
    few = jnp.zeros(shape, BF16)
    for i, v in enumerate(vectors):
        few = jnp.where(row == i, v[None, :], few)
    return few, jnp.broadcast_to(bias_in[None, :], (16,) + bias_in.shape)


FRONT = {
    "small": (2, 21, ((2, 6, 15, 23), (37, 13, 29, 40), (38, 12, 30, 39), (46, 22, 45, 49))),
    "q": (3, 18, ((3, 10, 14, 25), (32, 17, 26, 41), (31, 19, 28, 43), (44, 33, 42, 51))),
    "t0": (27, 35, ((27, 48, 71, 99),)),
    "t1": (5, 7, ((5, 24, 50, 79),)),
    "o": (0, 83, ((0, 4, 20, 47), (102, 59, 60, 64), (101, 11, 36, 56), (113, 76, 77, 81))),
    "i": (34, 57, ((34, 53, 66, 86), (70, 63, 88, 105), (69, 62, 85, 103), (90, 80, 104, 120))),
    "d": (52, 1, ((52, 73, 94, 107), (9, 93, 112, 121), (8, 92, 111, 119), (16, 108, 122, 125))),
    "work": (54, 55, 58, 61, 65, 67, 68, 72, 74, 75, 78, 82, 84, 87, 89, 91, 95, 96, 97, 98, 100, 106, 109, 110, 114, 115, 116, 117, 118, 123, 124, 126, 127, 128),
}


def front_time(nd, nb, kind, what, e=0):
    if (nd, nb) == (4, 4) and (kind != "work" or e == len(FRONT["work"])):
        row = FRONT[kind]
        if kind == "work":
            return row[what]
        if what == "line":
            return row[0]
        if what == "spread":
            return row[1]
        return row[2][what][e]
    first = ["small", "q", "t0", "t1", "o", "i", "d"].index(kind) * 10 if kind != "work" else 0
    if kind == "work":
        return (40 if what == 0 else 200) + what
    if what in ("line", "spread"):
        return first
    return first + 3 * e + (4 * what.bit_length() if what else 0)


DIRECT = ()


def front(few, many, w_qkv, tok, w_out, w_in, w_down, seg, nd, nb, nc):
    n = nd * nb * nc
    rows, width = tok.shape
    half, qlen, total = width // nc, nc * rows, nb * nc * rows
    heads = half // HD
    pairs = heads // 2
    r, r_ff, ff = w_qkv.shape[0], w_down.shape[0], w_in.shape[1]
    parts = 2
    part = rows // parts
    steps = nb * heads
    chunks = [slice(i, i + width) for i in range(0, ff, width)]

    def kernel(
        few_in, many_in, q_in, tok_in, o_in, i_in, d_in, seg_in,
        ctx2, vecs, lse_out, scale_one,
        q_h, o_h, i_h, d_h, kaug_h, v_h, qaug_h, tok_t_h, act_h, slope_h, exact_h, normed_h, unit_h,
        small_in, small_all, w_v, tok_v, tok_t, kaug, v_scr, qaug, top_scr, sum_scr, o_scr, rest_scr, ctx_loc,
        w_o, w_i, act, slope, bias_in, exact, normed, unit_one,
        four, recv, block_sem, own_sem, load_sem, save_sem, swap_sem,
    ):
        net = Net(nd, nb, nc)
        c = net.c
        small_in[...] = jnp.zeros((16, 128), BF16)
        small_in[:, 0:r] = few_in[...]
        row = lax.broadcasted_iota(jnp.int32, (16, r_ff), 0)
        small_in[:, 0:r_ff] = jnp.where(row == 8, many_in[...], small_in[:, 0:r_ff])
        specs = [("small", small_in, blocks_of(small_all), False), ("q", q_in, rows_of(q_h, r), False)]
        for i in range(parts):
            mine = tok_in.at[pl.ds(i * part, part)]
            specs.append(("t" + str(i), mine, rows_of(tok_v, part, i * part, rows), True))
        specs += [("o", o_in, rows_of(o_h, r), False), ("i", i_in, rows_of(i_h, r), False), ("d", d_in, rows_of(d_h, r_ff), False)]
        piece, own = {}, {}
        for p, (name, mine, (place, span), narrow) in enumerate(specs):
            piece[name] = Gather(net, mine, place, span, gather_refs(four, recv, block_sem, p, narrow), narrow, name in DIRECT)
            own[name] = piece[name].own(own_sem.at[p])
        tokens = ["t" + str(i) for i in range(parts)]
        for name in piece:
            own[name].start()
        net.barrier()
        lanes = pl.ds(pl.multiple_of(c * half, 128), half)

        def whole(name):
            piece[name].wait_sibling()
            own[name].wait()

        def unpack():
            whole("small")
            unpack_vectors(small_all, vecs, bias_in, r, r_ff)

        def load():
            whole("q")
            copies = []
            for k in range(3):
                at = pl.ds(pl.multiple_of((k * nc + c) * half, 128), half)
                copies.append(pltpu.make_async_copy(q_h.at[:, at], w_v.at[:, pl.ds(k * half, half)], load_sem.at[k]))
            for copy in copies:
                copy.start()
            for copy in copies:
                copy.wait()

        def queries():
            for name in tokens:
                own[name].wait()
                piece[name].wait_sibling_block(net.b)
            project_queries(tok_v, w_v[:, 0:half], vecs[0:1, lanes], seg_in, qaug, net.b, qlen)
            for scr, start in ((top_scr, -3e38), (sum_scr, 0.0), (o_scr, 0.0), (rest_scr, 0.0)):
                scr[...] = jnp.full(scr.shape, start, F32)

        saves = [
            pltpu.make_async_copy(src, dst, save_sem.at[i])
            for i, (src, dst) in enumerate(
                [
                    (kaug, kaug_h), (v_scr, v_h), (qaug, qaug_h), (tok_t, tok_t_h),
                    (exact, exact_h), (normed, normed_h), (unit_one, unit_h),
                ]
                + [(a.at[:, at], b.at[:, at]) for a, b in ((act, act_h), (slope, slope_h)) for at in chunks]
            )
        ]

        def turn_tokens():
            tok_t[...] = jnp.transpose(tok_v[...], (1, 0))
            for save in saves[:4]:
                save.start()

        swap = remote(ctx_loc.at[nc - 1 - c], ctx2.at[c], swap_sem.at[0], swap_sem.at[1], net.sibling)
        st = {}

        def finish():
            def put(p, value):
                for g in range(nc):
                    ctx_loc[g, :, p * 128:(p + 1) * 128] = value[g * rows:(g + 1) * rows]

            close_blocks(top_scr, sum_scr, o_scr, rest_scr)
            finish_forward(o_scr, rest_scr, top_scr, put, lse_out, exact)
            swap.start()
            saves[4].start()
            ctx2[c] = ctx_loc[c]

        def fetch(name, src, dst):
            whole(name)
            copy = pltpu.make_async_copy(src, dst, load_sem.at[3])
            copy.start()
            copy.wait()

        def first_norm():
            fetch("o", o_h, w_o)
            swap.wait()
            context = jnp.concatenate([ctx2[g] for g in range(nc)], axis=1)
            resid = tok_in[...].astype(F32) + (dot(context, w_o[...]) + vecs[2:3, :])
            unit, scale = norm_parts(resid)
            value = unit * vecs[3:4, :] + vecs[4:5, :]
            normed[...] = value
            unit_one[...] = unit
            scale_one[...] = jnp.broadcast_to(scale, scale_one.shape)
            saves[5].start()
            saves[6].start()
            st["low"] = value.astype(BF16)

        def expand(i, at):
            if i == 0:
                fetch("i", i_h, w_i)
            pre = dot(st["low"], w_i[:, at]) + bias_in[0:1, at]
            result, grad = gelu_and_slope(pre)
            act[:, at] = result.astype(BF16)
            slope[:, at] = grad
            saves[7 + i].start()
            saves[7 + len(chunks) + i].start()

        order = []
        for name in piece:
            order.append((front_time(nd, nb, name, "line"), piece[name].own_line, None))
            order.append((front_time(nd, nb, name, "spread"), piece[name].own_spread, None))
            for e in range(1, nb):
                order.append((front_time(nd, nb, name, 0, e), functools.partial(piece[name].z, e), None))
            for mask in range(1, 1 if name in tokens else nd):
                for e in range(nb):
                    order.append((front_time(nd, nb, name, mask, e), functools.partial(piece[name].x, mask, e), None))
        work = [unpack, load, queries] + [None] * steps + [turn_tokens, finish, first_norm]
        work += [functools.partial(expand, i, at) for i, at in enumerate(chunks)]
        for i, act_now in enumerate(work):
            order.append((front_time(nd, nb, "work", i, len(work)), act_now, i - 3 if act_now is None else None))
        order.sort(key=lambda q: q[0])
        begin = next(i for i, q in enumerate(order) if q[2] == 0)
        end = next(i for i, q in enumerate(order) if q[2] == steps - 1)
        for _, act_now, _ in order[:begin]:
            act_now()
        beside = {}
        for _, act_now, i in order[begin:end + 1]:
            if act_now is None:
                at_step = i
            else:
                beside.setdefault(at_step, []).append(act_now)

        def attention(e, h, carry):
            blk = net.near(e)
            at = pl.ds(pl.multiple_of(blk * qlen, qlen), qlen)
            attend_block(h, at, qaug, kaug, v_scr, top_scr, sum_scr, o_scr, rest_scr)
            for g in range(heads):
                acts = beside.get(e * heads + g, ())
                if acts:

                    @pl.when(h == g)
                    def _(acts=acts):
                        for act_now in acts:
                            act_now()

            return carry

        for e in range(nb):
            blk = net.near(e)
            if e:
                for name in tokens:
                    piece[name].wait_sibling_block(blk)
            project_keys(blk, qlen, tok_v, w_v[:, half:2 * half], w_v[:, 2 * half:3 * half], vecs[1:2, lanes], seg_in, kaug, v_scr)
            lax.fori_loop(0, heads, functools.partial(attention, e), 0)
        for _, act_now, _ in order[end + 1:]:
            act_now()
        whole("d")
        for name in piece:
            piece[name].drain()
        for save in saves:
            save.wait()

    count = 5 + parts
    vmem = lambda *shape: pltpu.VMEM(shape, BF16)
    wide = pltpu.VMEM((heads, qlen, 128), F32)
    return pl.pallas_call(
        kernel,
        out_shape=[
            jax.ShapeDtypeStruct((nc, rows, half), BF16),
            jax.ShapeDtypeStruct((8, width), F32),
            jax.ShapeDtypeStruct((heads, 8, qlen), F32),
            jax.ShapeDtypeStruct((rows, 128), F32),
            jax.ShapeDtypeStruct((n * r, 3 * width), BF16),
            jax.ShapeDtypeStruct((n * r, width), BF16),
            jax.ShapeDtypeStruct((n * r, ff), BF16),
            jax.ShapeDtypeStruct((n * r_ff, width), BF16),
            jax.ShapeDtypeStruct((pairs, total, 256), BF16),
            jax.ShapeDtypeStruct((pairs, total, 128), BF16),
            jax.ShapeDtypeStruct((heads, qlen, 256), BF16),
            jax.ShapeDtypeStruct((width, total), BF16),
            jax.ShapeDtypeStruct((rows, ff), BF16),
            jax.ShapeDtypeStruct((rows, ff), F32),
            jax.ShapeDtypeStruct((pairs, qlen, 128), F32),
            jax.ShapeDtypeStruct((rows, width), F32),
            jax.ShapeDtypeStruct((rows, width), F32),
        ],
        in_specs=[VMEM] * 8,
        out_specs=[VMEM] * 4 + [HBM] * 13,
        scratch_shapes=[
            vmem(16, 128),
            vmem(n, 16, 128),
            vmem(width, 3 * half),
            vmem(total, width),
            vmem(width, total),
            vmem(pairs, total, 256),
            vmem(pairs, total, 128),
            vmem(heads, qlen, 256),
            wide,
            wide,
            wide,
            wide,
            vmem(nc, rows, half),
            vmem(width, width),
            vmem(width, ff),
            vmem(rows, ff),
            pltpu.VMEM((rows, ff), F32),
            pltpu.VMEM((1, ff), F32),
            pltpu.VMEM((pairs, qlen, 128), F32),
            pltpu.VMEM((rows, width), F32),
            pltpu.VMEM((rows, width), F32),
            pltpu.SemaphoreType.DMA((count, 4)),
            pltpu.SemaphoreType.DMA((count, nd * nb)),
            pltpu.SemaphoreType.DMA((count, nb)),
            pltpu.SemaphoreType.DMA((count,)),
            pltpu.SemaphoreType.DMA((4,)),
            pltpu.SemaphoreType.DMA((7 + 2 * len(chunks),)),
            pltpu.SemaphoreType.DMA((2,)),
        ],
        compiler_params=params(58, 2),
    )(few, many, w_qkv, tok, w_out, w_in, w_down, seg)


BACK = {
    "d": (0, ((64, 49, 47, 42), (50, 25, 21, 18), (26, 15, 14, 13), (27, 11, 8, 7))),
    "i": (0, ((104, 97, 90, 72), (79, 76, 62, 45), (68, 54, 41, 29), (69, 55, 43, 24))),
    "o": (0, ((100, 73, 67, 66), (59, 58, 53, 52), (37, 35, 33, 31), (38, 36, 34, 32))),
    "q": (0, ((103, 99, 95, 94), (98, 93, 88, 85), (91, 86, 82, 81), (92, 87, 83, 80))),
    "t": (0, ((101, 77, 70, 57),)),
    "work": (0, 1, 2, 3, 4, 5, 6, 9, 10, 12, 16, 17, 19, 20, 22, 23, 28, 30, 39, 40, 44, 46, 48, 51, 56, 60, 61, 63, 65, 71, 74, 78, 75, 75.1, 84, 89, 96, 96.1, 102),
}


def back_time(nd, nb, kind, what, e=0):
    if (nd, nb) == (4, 4) and (kind != "work" or e == len(BACK["work"])):
        row = BACK[kind]
        if kind == "work":
            return row[what]
        return row[0] if what == "start" else row[1][what][e]
    if kind == "work":
        return 20 + 10 * what + (100 if what > e - 10 else 0)
    first = {"d": 0, "i": 10, "o": 20, "t": 300, "q": 400}[kind]
    if what == "start":
        return first
    return first + 30 - 5 * what.bit_length() + (nb - 1 - e)


def back(
    ctx, cot, vecs, lse, scale_one, normed, unit_one, exact_in, w_out, w_in, w_down, act_in, slope_in,
    tok_t_in, w_qkv, kaug_in, v_in, qaug_in, nd, nb, nc,
):
    owners = nd * nb
    rows, width = cot.shape
    total = tok_t_in.shape[1]
    ff = w_in.shape[1]
    half, qlen = width // nc, nc * rows
    heads = half // HD
    pairs = heads // 2
    r, r_ff = width // (owners * nc), ff // (owners * nc)
    levels = nd.bit_length() - 1
    names = ["d", "i", "o", "t", "q"]
    chunks = [slice(i, i + width) for i in range(0, ff, width)]
    n_sums = 8 + -(-len(chunks) // 8) * 8

    def kernel(
        ctx_in, cot_in, vecs_in, lse_row, scale_in, normed_h, unit_h, exact_h, wo_h, wi_h, wd_h, act_h, slope_h, tok_t_h, w_h,
        kaug_h, v_h, qaug_h,
        out, g_tok, g_qkv, g_out, g_in, g_down, g_small,
        d_own, i_own, o_own, d_sib, i_sib, o_sib, t_sib, q_sib, d_x, i_x, o_x, q_x, d_z, i_z, o_z, t_z, q_z,
        q_out, resid, gctx, gctx_all, grad_q, normed_in, unit_in, exact, value, got,
        load_sem, swap_sem, s3, sib_sem, x_sem, z_sem, sum_send, sum_recv,
    ):
        net = Net(nd, nb, nc)
        c, other = net.c, nc - 1 - net.c
        piece, held = {}, {}
        for p, (name, own, sib, xbuf, zbuf, result) in enumerate(
            [
                ("d", d_own, d_sib, d_x, d_z, g_down),
                ("i", i_own, i_sib, i_x, i_z, g_in),
                ("o", o_own, o_sib, o_x, o_z, g_out),
                ("t", None, t_sib, None, t_z, g_tok),
                ("q", None, q_sib, q_x, q_z, q_out),
            ]
        ):
            sems = [s3.at[p, i] for i in range(3)] + [sib_sem.at[p], x_sem.at[p], z_sem.at[p]]
            landing = lambda at, sib=sib: sib.at[at]
            span = lambda k, sib=sib: sib.at[pl.ds(0, k)]
            extra = ()
            if name == "t":
                place = lambda at: held["t"].at[at, c]
                parts = lambda at: [(None, [held["t"].at[at, c], t_sib.at[at]])]
                theirs = lambda at: held["t"].at[at, other]
                extra = (resid,)
            elif name == "q":
                place = lambda at: held["q_full"].at[at]
                parts = lambda at: [(c, [held["q"].at[at, c]]), (other, [q_sib.at[at]])]
                theirs = lambda at: held["q"].at[at, other]
            else:
                place = lambda at, own=own: own.at[at]
                parts = lambda at, own=own, sib=sib: [(None, [own.at[at], sib.at[at]])]
                theirs = lambda at, name=name: held[name].at[at]
            piece[name] = Scatter(
                net, parts, place, theirs, landing, span, xbuf, zbuf, result, sems, name == "t", extra, name in "dio", name in "oq"
            )
        whole = AllSum(net, value, got, sum_send, sum_recv)
        swap = remote(gctx.at[other], gctx_all.at[c], swap_sem.at[0], swap_sem.at[1], net.sibling)
        st = {}

        def split(name, at, first, second):
            mine = c == 0
            own = {"d": d_own, "i": i_own, "o": o_own}[name]
            own[at] = jnp.where(mine, first, second).astype(BF16)
            held[name][at] = jnp.where(mine, second, first).astype(BF16)

        def split_rows(name, d, grad, per):
            for a in range(nb):
                at = 2 * a * per
                split(name, d * nb + a, grad[at:at + per], grad[at + per:at + 2 * per])
            piece[name].start_home(d)

        def feed_forward_steps(w_o, w_i, w_d, act, slope, pre_grad, norm_t, ctx_t, d_out, i_out, o_out):
            held.update(d=d_out, i=i_out, o=o_out)
            loads = [
                pltpu.make_async_copy(src, dst, load_sem.at[i])
                for i, (src, dst) in enumerate(
                    [
                        (act_h, act), (wd_h, w_d), (normed_h, normed_in), (slope_h, slope), (wi_h, w_i), (unit_h, unit_in),
                        (wo_h, w_o), (exact_h, exact),
                    ]
                )
            ]
            for load in loads:
                load.start()
            gain_one, bias_down = vecs_in[3:4, :], vecs_in[5:6, :]
            gain_two, shift_two = vecs_in[6:7, :], vecs_in[7:8, :]

            def enter():
                for p in piece.values():
                    p.clear_edges()
                net.barrier()
                ctx_t[...] = jnp.transpose(jnp.concatenate([ctx_in[g] for g in range(nc)], axis=1), (1, 0))
                for load in loads[:3]:
                    load.wait()
                norm_t[...] = jnp.transpose(normed_in[...].astype(BF16), (1, 0))

            def turn():
                unit, scale = norm_parts(normed_in[...] + (dot(act[...], w_d[...]) + bias_down))
                out[...] = (unit * gain_two + shift_two).astype(BF16)
                grad_out = cot_in[...].astype(F32)
                st["two"] = norm_back(grad_out, unit, scale, gain_two)
                st["ffn"] = st["two"].astype(BF16)
                value[0] = jnp.zeros((n_sums, width), F32)
                value[0, 5:6, :] = column_sum(st["ffn"].astype(F32))
                value[0, 6:7, :] = column_sum(grad_out * unit)
                value[0, 7:8, :] = column_sum(grad_out)

            def down(mask):
                d = net.flips(mask)
                lanes = pl.ds(pl.multiple_of(d * (ff // nd), 128), ff // nd)
                split_rows("d", d, dot(act[:, lanes], st["ffn"], ((0,), (0,))), r_ff)

            def pre(i, at):
                if i == 0:
                    loads[3].wait()
                    loads[4].wait()
                grad = (dot(st["ffn"], w_d[at, :], ((1,), (1,))) * slope[:, at]).astype(BF16)
                pre_grad[:, at] = grad
                value[0, 8 + i:9 + i, :] = column_sum(grad.astype(F32))
                st["two"] = st["two"] + dot(grad, w_i[:, at], ((1,), (1,)))

            def norm_one():
                grad = st["two"]
                for load in loads[5:]:
                    load.wait()
                value[0, 3:4, :] = column_sum(grad * unit_in[...])
                value[0, 4:5, :] = column_sum(grad)
                grad = norm_back(grad, unit_in[...], scale_in[:, 0:1], gain_one)
                resid[...] = grad
                st["attn"] = grad.astype(BF16)
                value[0, 2:3, :] = column_sum(st["attn"].astype(F32))
                grad = dot(st["attn"], w_o[...], ((1,), (1,))).astype(BF16)
                for g in range(nc):
                    gctx[g] = grad[:, g * half:(g + 1) * half]
                swap.start()
                gctx_all[c] = gctx[c]

            def weight_in(mask):
                d = net.flips(mask)
                at = pl.ds(pl.multiple_of(d * (width // nd), 8), width // nd)
                split_rows("i", d, dot(norm_t[at, :], pre_grad[...]), r)

            def weight_out():
                for d in range(nd):
                    at = slice(d * (width // nd), (d + 1) * (width // nd))
                    split_rows("o", d, dot(ctx_t[at, :], st["attn"]), r)

            masks = range(nd - 1, -1, -1)
            acts = [enter, turn]
            acts += [functools.partial(down, m) for m in masks]
            acts += [functools.partial(pre, i, at) for i, at in enumerate(chunks)] + [norm_one]
            return acts + [functools.partial(weight_in, m) for m in masks] + [weight_out]

        n_ffn = 4 + len(chunks) + 2 * nd
        steps = nb * pairs
        n_work = n_ffn + 1 + steps + 4 + len(whole.stages())
        order = []
        for name in names:
            p = piece[name]
            for mask in range(p.nd):
                for e in range(nb):
                    order.append((back_time(nd, nb, name, mask, e), functools.partial(p.reduce, mask, e), None))
        for i in range(n_work):
            order.append((back_time(nd, nb, "work", i, n_work), None, i))
        order.sort(key=lambda q: q[0])
        index = [i for i, q in enumerate(order) if q[2] is not None]
        first, last = index[n_ffn + 1], index[n_ffn + steps]

        def run(entries, acts, base):
            for _, act, i in entries:
                (act if i is None else acts[i - base])()

        def feed_forward_scope(*refs):
            run(order[:index[n_ffn - 1] + 1], feed_forward_steps(*refs), 0)
            for name in "dio":
                piece[name].sent()

        def attention_scope(tok_t, w_v, kaug, v_scr, qaug, do_m, delta_row, dq_scr, dkv, t_part, q_part, q_full):
            held.update(t=t_part, q=q_part, q_full=q_full)
            loads = [(qaug_h, qaug)]
            for k in range(3):
                lanes = pl.ds(pl.multiple_of((k * nc + c) * half, 128), half)
                loads.append((w_h.at[:, lanes], w_v.at[:, pl.ds(k * half, half)]))
            loads.append((tok_t_h, tok_t))
            loads = [pltpu.make_async_copy(src, dst, load_sem.at[8 + i]) for i, (src, dst) in enumerate(loads)]

            def block_loads(blk):
                at = pl.ds(pl.multiple_of(blk * qlen, qlen), qlen)
                return [
                    pltpu.make_async_copy(kaug_h.at[:, at], kaug.at[:, at], load_sem.at[13 + blk]),
                    pltpu.make_async_copy(v_h.at[:, at], v_scr.at[:, at], load_sem.at[13 + nb + blk]),
                ]

            loads[0].start()
            for e in range(nb - 1, -1, -1):
                for copy in block_loads(net.near(e)):
                    copy.start()
            for copy in loads[1:]:
                copy.start()

            def prepare():
                swap.wait()
                lane = lambda p: slice(p * 128, (p + 1) * 128)
                prepare_backward(
                    lambda p: jnp.concatenate([gctx_all[g, :, lane(p)] for g in range(nc)], axis=0), exact, do_m, delta_row
                )
                for copy in loads:
                    copy.wait()

            def token_grad(blk):
                at = pl.ds(pl.multiple_of(blk * qlen, qlen), qlen)
                return dot(dkv[at, :], w_v[:, half:3 * half], ((1,), (1,)))

            def put_tokens(blk, grad):
                for g in range(nc):
                    t_part[blk, g] = grad[g * rows:(g + 1) * rows].astype(BF16)
                piece["t"].send(blk, blk)

            def weights():
                grad_q[...] = jnp.concatenate([join_dq(dq_scr, p) for p in range(pairs)], axis=1)
                mine = pl.ds(pl.multiple_of(net.b * qlen, qlen), qlen)
                for k in range(3):
                    if k:
                        grad = dot(tok_t[...], dkv[:, (k - 1) * half:k * half])
                    else:
                        grad = dot(tok_t[:, mine], grad_q[...])
                    for at in range(owners):
                        for g in range(nc):
                            i = at * nc + g
                            q_part[at, g, :, k * half:(k + 1) * half] = grad[i * r:(i + 1) * r].astype(BF16)

            def own_tokens():
                put_tokens(net.b, token_grad(net.b) + dot(grad_q[...], w_v[:, 0:half], ((1,), (1,))))

            def small_sums():
                lanes = pl.ds(pl.multiple_of(c * half, 128), half)
                value[0, 0:1, lanes] = column_sum(grad_q[...].astype(F32))
                value[0, 1:2, lanes] = column_sum(dkv[:, half:2 * half].astype(F32))

            acts = [prepare] + [None] * steps + [weights, piece["q"].start, own_tokens, small_sums] + whole.stages()
            run(order[index[n_ffn - 1] + 1:first], acts, n_ffn)
            beside = {}
            for _, act, i in order[first:last + 1]:
                if i is not None:
                    at_step = i - n_ffn - 1
                else:
                    beside.setdefault(at_step, []).append(act)

            def attention(i, carry):
                pair = i % pairs
                blk = net.near_at(nb - 1 - i // pairs)
                at = pl.ds(pl.multiple_of(blk * qlen, qlen), qlen)

                @pl.when(pair == 0)
                def _():
                    for copy in block_loads(blk):
                        copy.wait()

                def put(dk, dv):
                    dkv[at, pl.ds(pl.multiple_of(pair * 128, 128), 128)] = dk.astype(BF16)
                    dkv[at, pl.ds(pl.multiple_of(half + pair * 128, 128), 128)] = dv.astype(BF16)

                bwd_pair(pair, qaug, kaug[pair, at, :], v_scr[pair, at, :], do_m, lse_row, delta_row, dq_scr, put, i < pairs)

                @pl.when((pair == pairs - 1) & (i < steps - 1))
                def _():
                    put_tokens(blk, token_grad(blk))

                for g, acts in beside.items():

                    @pl.when(i == g)
                    def _(acts=acts):
                        for act in acts:
                            act()

                return carry

            lax.fori_loop(0, steps, attention, 0)
            run(order[last + 1:], acts, n_ffn)
            for k in range(3):
                for g in range(nc):
                    lanes = slice((k * nc + g) * half, (k * nc + g + 1) * half)
                    g_qkv[:, lanes] = q_out[g, :, k * half:(k + 1) * half]
            me = (net.d * nb + net.b) * nc + c
            feature = lax.broadcasted_iota(jnp.int32, (width, 128), 0)
            lane = lax.broadcasted_iota(jnp.int32, (width, 128), 1)
            pick = jnp.where((feature == me * r + lane) & (lane < r), 1.0, 0.0).astype(F32)
            in_row, in_lane = (me * r_ff) // width, (me * r_ff) % width
            pick_in = jnp.where((feature == in_lane + lane) & (lane < r_ff), 1.0, 0.0).astype(F32)
            exactly = dict(precision=lax.Precision.HIGHEST, preferred_element_type=F32)
            g_small[0:8, :] = jnp.dot(value[0, 0:8, :], pick, **exactly)
            found = jnp.dot(value[0, 8:16, :], pick_in, **exactly)
            row = lax.broadcasted_iota(jnp.int32, found.shape, 0)
            g_small[8:16, :] = jnp.broadcast_to(column_sum(jnp.where(row == in_row, found, 0.0)), (8, 128))
            for name in names:
                piece[name].drain()

        pl.run_scoped(feed_forward_scope, *scopes[0])
        pl.run_scoped(attention_scope, *scopes[1])

    block = {"d": (r_ff, width), "i": (r, ff), "o": (r, width), "t": (rows, width)}
    joined = (nc, r, 3 * half)
    vmem = lambda shape, kind=BF16: pltpu.VMEM(shape, kind)
    held_out = [vmem((owners,) + block[k]) for k in "dio"]
    scopes = (
        [
            vmem((width, width)),
            vmem((width, ff)),
            vmem((ff, width)),
            vmem((rows, ff)),
            vmem((rows, ff), F32),
            vmem((rows, ff)),
            vmem((width, rows)),
            vmem((width, rows)),
        ]
        + held_out,
        [
            vmem((width, total)),
            vmem((width, 3 * half)),
            vmem((pairs, total, 256)),
            vmem((pairs, total, 128)),
            vmem((heads, qlen, 256)),
            vmem((heads, qlen, 128)),
            vmem((heads, 8, qlen), F32),
            vmem((heads, 128, qlen), F32),
            vmem((total, 2 * half)),
            vmem((nb, nc, rows, width)),
            vmem((owners,) + joined),
            vmem((owners,) + joined),
        ],
    )
    scratch = [vmem((owners,) + block[k]) for k in "dio"] + [vmem((owners,) + block[k]) for k in "dio"]
    scratch += [vmem((nb,) + block["t"]), vmem((owners, r, 3 * half))]
    scratch += [vmem(((nd - 1) * nb,) + block[k]) for k in "dio"] + [vmem(((nd - 1) * nb,) + joined)]
    scratch += [vmem((nb + 1,) + block[k]) for k in "diot"] + [vmem((nb + 1,) + joined)]
    scratch += [
        vmem(joined, F32),
        vmem((rows, width), F32),
        vmem((nc, rows, half)),
        vmem((nc, rows, half)),
        vmem((qlen, half)),
        vmem((rows, width), F32),
        vmem((rows, width), F32),
        vmem((pairs, qlen, 128), F32),
        vmem((levels + 2, n_sums, width), F32),
        vmem((levels + nb, n_sums, width), F32),
        pltpu.SemaphoreType.DMA((13 + 2 * nb,)),
        pltpu.SemaphoreType.DMA((2,)),
    ]
    scratch += scatter_sems(5, nd, nb) + [pltpu.SemaphoreType.DMA((levels + nb,))] * 2
    return pl.pallas_call(
        kernel,
        out_shape=[
            jax.ShapeDtypeStruct((rows, width), BF16),
            jax.ShapeDtypeStruct((rows, width), F32),
            jax.ShapeDtypeStruct((r, 3 * width), F32),
            jax.ShapeDtypeStruct((r, width), F32),
            jax.ShapeDtypeStruct((r, ff), F32),
            jax.ShapeDtypeStruct((r_ff, width), F32),
            jax.ShapeDtypeStruct((16, 128), F32),
        ],
        in_specs=[VMEM] * 5 + [HBM] * 13,
        out_specs=[VMEM] * 7,
        scratch_shapes=scratch,
        compiler_params=params(62, 3),
    )(
        ctx, cot, vecs, lse, scale_one, normed, unit_one, exact_in, w_out, w_in, w_down, act_in, slope_in,
        tok_t_in, w_qkv, kaug_in, v_in, qaug_in,
    )


def body(
    tokens,
    segment,
    w_qkv,
    bias_query,
    bias_value,
    w_out,
    bias_out,
    gain_attn,
    shift_attn,
    w_in,
    bias_in,
    w_down,
    bias_down,
    gain_ffn,
    shift_ffn,
    cotangent,
):
    nd, nb, nc = lax.axis_size("dp"), lax.axis_size("blk"), lax.axis_size("head")
    n_dev = nd * nb * nc
    d_idx, b_idx, c_idx = lax.axis_index("dp"), lax.axis_index("blk"), lax.axis_index("head")
    me = (d_idx * nb + b_idx) * nc + c_idx
    seqs, rows, width = tokens.shape
    ff = w_in.shape[1]
    half_w = width // nc
    qlen = nc * rows
    r = w_qkv.shape[0]
    r_ff = w_down.shape[0]
    flat_in = tokens.reshape(rows, width)
    cot = cotangent.reshape(rows, width)
    vectors = [bias_query, bias_value, bias_out, gain_attn, shift_attn, bias_down, gain_ffn, shift_ffn]
    if nb * qlen <= 2048 and r % 8 == 0 and ff // width <= 8:
        few, many = pack_vectors(vectors, bias_in)
        (
            ctx2, vecs, lse, scale_one,
            f_qkv, f_out, f_in, f_down, kaug, v_all, qaug, tok_t, act, slope, exact, normed, unit_one,
        ) = front(few, many, w_qkv, flat_in, w_out, w_in, w_down, segment, nd, nb, nc)
        out, g_tok, o_qkv, o_out, o_in, o_down, g_small = back(
            ctx2, cot, vecs, lse, scale_one, normed, unit_one, exact, f_out, f_in, f_down, act, slope,
            tok_t, f_qkv, kaug, v_all, qaug, nd, nb, nc,
        )
        out, g_tok, o_qkv, o_out, o_in, o_down, g_bq, g_bv, g_bo, g_g1, g_s1, g_bd, g_g2, g_s2, g_bin = hand_out(
            [out, g_tok, o_qkv, o_out, o_in, o_down], g_small, r, r_ff
        )
        return (
            out.reshape(seqs, rows, width), g_tok.reshape(seqs, rows, width),
            o_qkv, g_bq, g_bv, o_out, g_bo, g_g1, g_s1, o_in, g_bin, o_down, g_bd, g_g2, g_s2,
        )
    packed = jnp.concatenate(vectors + [bias_in])
    used = packed.shape[0]
    lanes = -(-used // 128) * 128
    packed = jnp.broadcast_to(jnp.pad(packed, (0, lanes - used))[None], (8, lanes))
    n4 = 4
    parts = [flat_in[i * (rows // n4):(i + 1) * (rows // n4)] for i in range(n4)]
    shards = [packed, w_qkv] + parts + [w_out, w_in, w_down]
    narrow = [False, False] + [True] * n4 + [False] * 3
    keys = [(-1, 3, 3), (0, 3, 3), (7, 9, 0), (10, 9, 0), (13, 9, 0), (16, 9, 0), (2, 4, 4), (9, 6, 5), (22, 6, 5)]
    small, g_qkv, t0, t1, t2, t3, g_out, g_in, g_down = gather_all(shards, narrow, keys, nd, nb, nc)
    full_small = small[:, 0, :used]
    vecs = full_small[:, :8 * r].reshape(n_dev, 8, r).transpose(1, 0, 2).reshape(8, width).astype(F32)
    full_bin = full_small[:, 8 * r:].reshape(ff).astype(F32)
    bq, bv, bout, gain_one, shift_one, bdown, gain_two, shift_two = (vecs[i] for i in range(8))
    full_qkv = g_qkv.reshape(width, 3 * width)
    full_wout = g_out.reshape(width, width)
    full_win = g_in.reshape(width, ff)
    full_wdown = g_down.reshape(ff, width)
    tok_all = jnp.stack([t0, t1, t2, t3], axis=1).reshape(nb * qlen, width)
    my_bias = lax.dynamic_slice(vecs, (0, c_idx * half_w), (2, half_w))
    ctx, kaug, v_scr, qaug, lse, exact = attend_forward(tok_all, full_qkv, my_bias, segment, qlen, half_w)
    context_low = ctx.reshape(seqs, qlen, 1, half_w)
    back_tokens = lax.all_to_all(context_low, "head", split_axis=1, concat_axis=2, tiled=True)
    ctx2 = back_tokens.reshape(rows, nc, half_w).transpose(1, 0, 2)
    out, grad_resid_one, gctx2, dw_down, dw_in, dw_out, sums = feed_forward(
        ctx2, flat_in, cot, vecs, full_bin.reshape(1, ff), full_wout, full_win, full_wdown
    )
    output = out.reshape(seqs, rows, width)
    grad_context = gctx2.transpose(1, 0, 2)
    grad_headed = lax.all_to_all(
        grad_context.reshape(seqs, rows, nc, half_w), "head", split_axis=2, concat_axis=1, tiled=True
    )
    gctx = grad_headed.reshape(qlen, half_w)
    tok_mine = lax.dynamic_slice(tok_all, (b_idx * qlen, 0), (qlen, width))
    dtok, dw, dbias = attend_backward(tok_all, tok_mine, full_qkv, qaug, kaug, v_scr, lse, exact, gctx)
    dw = dw.astype(BF16).reshape(nd * nb, nc, r, 3 * half_w)
    ours = lax.dynamic_index_in_dim(dw, c_idx, 1, keepdims=False)
    theirs = lax.dynamic_index_in_dim(dw, 1 - c_idx, 1, keepdims=False)
    joined_full = jnp.stack([ours, ours], axis=1)
    sums = lax.dynamic_update_slice(sums, dbias, (0, c_idx * half_w))
    o_down, o_in, o_out, o_tok, o_qkv, total = scatter_all(
        [
            dw_down.reshape(n_dev, r_ff, width),
            dw_in.reshape(n_dev, r, ff),
            dw_out.reshape(n_dev, r, width),
            dtok.reshape(nb * nc, rows, width),
            (joined_full, theirs),
        ],
        [False, False, False, True, False],
        [False, False, False, False, True],
        sums,
        nd,
        nb,
        nc,
    )
    grad_tokens = (grad_resid_one + o_tok).reshape(seqs, rows, width)
    o_qkv = o_qkv.reshape(2, r, 3, half_w).transpose(1, 2, 0, 3).reshape(r, 3 * width)
    mine = lax.dynamic_slice(total, (0, me * r), (8, r))
    mine_in = lax.dynamic_slice(total[8:8 + ff // width].reshape(ff), (me * r_ff,), (r_ff,))
    g_bq, g_bv, g_bo, g_g1, g_s1, g_bd, g_g2, g_s2 = (mine[i] for i in range(8))
    return (
        output,
        grad_tokens,
        o_qkv,
        g_bq,
        g_bv,
        o_out,
        g_bo,
        g_g1,
        g_s1,
        o_in,
        mine_in,
        o_down,
        g_bd,
        g_g2,
        g_s2,
    )


def solution(mesh):
    weight, vector = P(("dp", "blk", "head"), None), P(("dp", "blk", "head"))
    token = P("dp", ("blk", "head"), None)
    return jax.shard_map(
        body,
        mesh=mesh,
        in_specs=(
            token,
            P("dp", None),
            weight,
            vector,
            vector,
            weight,
            vector,
            vector,
            vector,
            weight,
            vector,
            weight,
            vector,
            vector,
            vector,
            token,
        ),
        out_specs=(
            token,
            token,
            weight,
            vector,
            vector,
            weight,
            vector,
            vector,
            vector,
            weight,
            vector,
            weight,
            vector,
            vector,
            vector,
        ),
        check_vma=False,
    )
```

```python
import functools

import jax
import jax.numpy as jnp
from jax import lax
from jax.experimental import pallas as pl
from jax.experimental.pallas import tpu as pltpu
from jax.sharding import PartitionSpec as P

MESH = pl.DeviceIdType.MESH
F32, BF16 = jnp.float32, jnp.bfloat16
HD = 64
HEADS = 12
BIG = 2.0**30

class Net:
    def __init__(self, nd, nb, nc):
        self.nd, self.nb, self.nc = nd, nb, nc
        self.levels = nd.bit_length() - 1
        self.d, self.b, self.c = (lax.axis_index(a) for a in ("dp", "blk", "head"))
        top = self.levels - 1
        self.stride = [(1 - self.c) * 2**k + self.c * 2 ** (top - k) for k in range(self.levels)]
        self.sibling = (self.d, self.b, self.nc - 1 - self.c)
        steps = [s * (1 - 2 * ((self.d // s) % 2)) for s in self.stride]
        self.flipped = [self.d]
        for step in steps:
            self.flipped += [d + step for d in self.flipped]
        self.nearest = [self.find_near(e) for e in range(self.nb)]

    def flips(self, mask):
        return self.flipped[mask]

    def across(self, k):
        return (self.flipped[1 << k], self.b, self.c)

    def near(self, e):
        return self.nearest[e]

    def find_near(self, e):
        order = [sorted(range(self.nb), key=lambda j: (abs(j - i), -j)) for i in range(self.nb)]
        got = order[0][e]
        for i in range(1, self.nb):
            got = jnp.where(self.b == i, order[i][e], got)
        return got

    def near_at(self, e):
        got = self.near(0)
        for i in range(1, self.nb):
            got = jnp.where(e == i, self.near(i), got)
        return got

    def slot(self, mask, blk):
        return (self.flips(mask) * self.nb + blk) * self.nc + self.c

    def peers(self):
        out = [(self.d, (self.b + u) % self.nb, self.c) for u in range(1, self.nb)]
        out += [self.across(k) for k in range(self.levels)]
        return out + [self.sibling]

    def barrier(self):
        bar = pltpu.get_barrier_semaphore()
        ps = self.peers()
        for p in ps:
            pl.semaphore_signal(bar, inc=1, device_id=p, device_id_type=MESH)
        pl.semaphore_wait(bar, len(ps))


def remote(src, dst, send, recv, dev):
    return pltpu.make_async_remote_copy(src_ref=src, dst_ref=dst, send_sem=send, recv_sem=recv, device_id=dev, device_id_type=MESH)


def blocks_of(full):
    return (lambda i: full.at[i]), (lambda k: full.at[pl.ds(0, k)])


def rows_of(full, rows, offset=0, stride=None):
    every = rows if stride is None else stride

    def place(i):
        return full.at[pl.ds(pl.multiple_of(i * every + offset, 8), rows)]

    return place, (lambda k: full.at[pl.ds(0, k * rows)])


class Gather:
    def __init__(self, net, mine, place, span, sems, narrow=False, direct=False):
        self.net, self.mine, self.place, self.span, self.narrow, self.direct = net, mine, place, span, narrow, direct
        self.zsend, self.xsend, self.ssend, self.srecv, self.recv = sems

    def at(self, mask, blk):
        n = self.net
        if self.narrow:
            return self.place(blk * n.nc + n.c)
        return self.place(n.slot(mask, blk))

    def rsem(self, mask, blk):
        return self.recv.at[mask * self.net.nb + blk]

    def spread(self, mask, blk, src, dst):
        n = self.net
        if not self.narrow:
            for k in range(n.levels):
                if mask < (1 << k):
                    remote(src, dst, self.xsend, self.rsem(mask + (1 << k), blk), n.across(k)).start()
        arrival = self.srecv.at[blk] if self.narrow else self.srecv
        remote(src, dst, self.ssend, arrival, n.sibling).start()

    def along(self, blk, src, dst):
        n = self.net
        sem = self.rsem(0, blk)

        @pl.when((n.b < n.nb - 1) & (blk <= n.b))
        def _():
            remote(src, dst, self.zsend, sem, (n.d, n.b + 1, n.c)).start()

        @pl.when((n.b > 0) & (blk >= n.b))
        def _():
            remote(src, dst, self.zsend, sem, (n.d, n.b - 1, n.c)).start()

    def own_line(self):
        n = self.net
        dst = self.at(0, n.b)
        if not self.direct:
            self.along(n.b, self.mine, dst)
            return
        for e in range(n.nb - 1, 0, -1):
            remote(self.mine, dst, self.zsend, self.rsem(0, n.b), (n.d, n.near(e), n.c)).start()

    def own_spread(self):
        self.spread(0, self.net.b, self.mine, self.at(0, self.net.b))

    def z(self, e):
        blk = self.net.near(e)
        dst = self.at(0, blk)
        pltpu.make_async_copy(dst, dst, self.rsem(0, blk)).wait()
        if not self.direct:
            self.along(blk, dst, dst)
        self.spread(0, blk, dst, dst)

    def x(self, mask, e):
        n = self.net
        blk = n.near(e)
        dst = self.at(mask, blk)
        pltpu.make_async_copy(dst, dst, self.rsem(mask, blk)).wait()
        self.spread(mask, blk, dst, dst)

    def own(self, sem):
        n = self.net
        return pltpu.make_async_copy(self.mine, self.at(0, n.b), sem)

    def wait_sibling_block(self, blk):
        one = self.span(1)
        pltpu.make_async_copy(one, one, self.srecv.at[blk]).wait()

    def wait_sibling(self):
        n = self.net
        if self.narrow:
            for blk in range(n.nb):
                self.wait_sibling_block(blk)
            return
        half = self.span(n.nd * n.nb)
        pltpu.make_async_copy(half, half, self.srecv).wait()

    def drain(self):
        n = self.net
        half = self.span(n.nb if self.narrow else n.nd * n.nb)
        pltpu.make_async_copy(half, half, self.ssend).wait()
        if not self.narrow:
            part = self.span((n.nd - 1) * n.nb)
            pltpu.make_async_copy(part, part, self.xsend).wait()
        if self.direct:
            sent = self.span(n.nb - 1)
            pltpu.make_async_copy(sent, sent, self.zsend).wait()
            return
        edge = (n.b == 0) | (n.b == n.nb - 1)

        @pl.when(edge)
        def _():
            one = self.span(1)
            pltpu.make_async_copy(one, one, self.zsend).wait()

        @pl.when(jnp.logical_not(edge))
        def _():
            many = self.span(n.nb + 1)
            pltpu.make_async_copy(many, many, self.zsend).wait()


def gather_refs(four, recv, block, p, narrow):
    last = block.at[p] if narrow else four.at[p, 3]
    return [four.at[p, 0], four.at[p, 1], four.at[p, 2], last, recv.at[p]]


def gather_sems(n_pieces, nd, nb):
    return [pltpu.SemaphoreType.DMA((n_pieces, 4)), pltpu.SemaphoreType.DMA((n_pieces, nd * nb)), pltpu.SemaphoreType.DMA]


class Scatter:
    def __init__(self, net, parts, place, theirs, landing, span, xrecv, zrecv, out, sems, narrow=False, extra=(), early=False, direct=False):
        self.net, self.parts, self.place, self.theirs, self.landing = net, parts, place, theirs, landing
        self.span, self.xbuf, self.zbuf, self.out, self.extra = span, xrecv, zrecv, out, extra
        self.sib_send, self.x_send, self.z_send, self.sib_sem, self.x_sem, self.z_sem = sems
        self.narrow, self.seen, self.early, self.direct = narrow, set(), early, direct
        self.nd = 1 if narrow else net.nd
        self.levels = 0 if narrow else net.levels

    def home(self, mask):
        return 0 if self.narrow else self.net.flips(mask)

    def start(self):
        for mask in range(self.nd - 1, -1, -1):
            self.start_home(self.home(mask))

    def start_home(self, d):
        for blk in range(self.net.nb):
            self.send(d * self.net.nb + blk, d)

    def send(self, at, sem):
        remote(self.theirs(at), self.landing(at), self.sib_send, self.sib_sem.at[sem], self.net.sibling).start()

    def arrived(self, sem, count):
        some = self.span(count)
        pltpu.make_async_copy(some, some, self.sib_sem.at[sem]).wait()

    def sent(self):
        some = self.span(self.nd * self.net.nb)
        pltpu.make_async_copy(some, some, self.sib_send).wait()

    def x_at(self, k, mask, blk):
        return ((1 << k) - 1 + mask) * self.net.nb + blk

    def z_at(self, side, blk, owner):
        return blk + side * jnp.where(blk == owner, self.net.nb - blk, 0)

    def add(self, at, more, to, extra=()):
        for pick, places in self.parts(at):
            def chosen(ref):
                return ref if pick is None else ref.at[pick]

            add_up(places + [chosen(m) for m in more] + list(extra), chosen(to))

    def reduce(self, mask, e):
        n = self.net
        blk = n.near(e)
        if self.narrow:
            self.arrived(blk, 1)
        elif mask not in self.seen:
            self.seen.add(mask)
            self.arrived(self.home(mask), n.nb)
        at = self.home(mask) * n.nb + blk
        place = self.place(at)
        more = []
        for k in range(self.levels - 1, -1, -1):
            if mask < (1 << k):
                i = self.x_at(k, mask, blk)
                got = self.xbuf.at[i]
                pltpu.make_async_copy(got, got, self.x_sem.at[i]).wait()
                more.append(got)
        if mask:
            k = mask.bit_length() - 1
            self.add(at, more, place)
            i = self.x_at(k, mask - (1 << k), blk)
            remote(place, self.xbuf.at[i], self.x_send, self.x_sem.at[i], n.across(k)).start()
            return

        if self.direct:
            if e:
                self.add(at, more, place)
                remote(place, self.zbuf.at[n.b], self.z_send, self.z_sem.at[n.b], (n.d, blk, n.c)).start()
                return
            for u in range(1, n.nb):
                got = self.zbuf.at[n.near(u)]
                pltpu.make_async_copy(got, got, self.z_sem.at[n.near(u)]).wait()
                more.append(got)
            self.add(at, more, self.out, self.extra)
            return

        def line(side, there):
            i = self.z_at(side, blk, n.b)
            got = self.zbuf.at[i]

            @pl.when(there)
            def _():
                pltpu.make_async_copy(got, got, self.z_sem.at[i]).wait()

            more.append(got)

        if e == 0:
            line(0, n.b > 0)
            line(1, n.b < n.nb - 1)
            self.add(at, more, self.out, self.extra)
            return
        side = jnp.where(blk > n.b, 0, 1)
        line(side, jnp.where(blk > n.b, n.b, n.nb - 1 - n.b) > 0)
        self.add(at, more, place)
        to = n.b + 1 - 2 * side
        i = self.z_at(side, blk, to)
        remote(place, self.zbuf.at[i], self.z_send, self.z_sem.at[i], (n.d, to, n.c)).start()

    def clear_edges(self):
        n = self.net
        if self.direct:
            return

        def clear(i, carry):
            self.zbuf[i] = jnp.zeros(self.zbuf.shape[1:], self.zbuf.dtype)
            return carry

        @pl.when(n.b == 0)
        def _():
            lax.fori_loop(0, n.nb, clear, 0)

        @pl.when(n.b == n.nb - 1)
        def _():
            lax.fori_loop(0, n.nb - 1, clear, 0)
            clear(n.nb, 0)

    def drain(self):
        n = self.net
        if not self.early:
            self.sent()
        if not self.narrow:
            some = self.xbuf.at[pl.ds(0, (n.nd - 1) * n.nb)]
            pltpu.make_async_copy(some, some, self.x_send).wait()
        some = self.zbuf.at[pl.ds(0, n.nb - 1)]
        pltpu.make_async_copy(some, some, self.z_send).wait()


def add_up(terms, to):
    shape = to.shape
    rows = shape[-2]
    step = rows
    while step % 2 == 0 and step > 32:
        step //= 2
    lead = [()] if len(shape) == 2 else [(g,) for g in range(shape[0])]
    for g in lead:
        for r in range(0, rows, step):
            at = g + (slice(r, r + step),)
            total = terms[0][at].astype(F32)
            for t in terms[1:]:
                total = total + t[at].astype(F32)
            to[at] = total.astype(to.dtype)


class AllSum:
    def __init__(self, net, value, got, send, recv):
        self.net, self.value, self.got, self.send, self.recv = net, value, got, send, recv

    def copy(self, stage, dev, src, slot):
        return remote(self.value.at[src], self.got.at[slot], self.send.at[slot], self.recv.at[slot], dev)

    def stages(self):
        n = self.net
        devs = [n.sibling] + [n.across(k) for k in range(n.levels)]
        steps = []
        for i, dev in enumerate(devs):
            steps.append(functools.partial(self.one, i, dev))
        steps.append(self.line_start)
        steps.append(self.line_end)
        return [lambda: self.copy(0, devs[0], 0, 0).start()] + steps

    def one(self, i, dev):
        n = self.net
        self.copy(i, dev, i, i).wait()
        self.value[i + 1] = self.value[i] + self.got[i]
        if i + 1 <= n.levels:
            self.copy(i + 1, n.across(i), i + 1, i + 1).start()

    def line_copy(self, u):
        n = self.net
        return self.copy(None, (n.d, (n.b + u) % n.nb, n.c), n.levels + 1, n.levels + u)

    def line_start(self):
        for u in range(1, self.net.nb):
            self.line_copy(u).start()

    def line_end(self):
        n = self.net
        for u in range(1, n.nb):
            self.line_copy(u).wait()
        total = self.value[n.levels + 1]
        for u in range(1, n.nb):
            total = total + self.got[n.levels + u]
        self.value[0] = total


def scatter_sems(n_pieces, nd, nb):
    return [
        pltpu.SemaphoreType.DMA((n_pieces, 3)),
        pltpu.SemaphoreType.DMA((n_pieces, max(nd, nb))),
        pltpu.SemaphoreType.DMA((n_pieces, (nd - 1) * nb)),
        pltpu.SemaphoreType.DMA((n_pieces, nb + 1)),
    ]


def dot(a, b, dims=((1,), (0,))):
    return lax.dot_general(a, b, (dims, ((), ())), preferred_element_type=F32)


def mask_lanes(seg_row, count):
    lanes = lax.broadcasted_iota(jnp.int32, (128, count), 0)
    return jnp.transpose(jnp.where(lanes == seg_row, -1.0, 0.0).astype(F32), (1, 0))


def project_keys(i, step, tok, wk, wv, bias_v, seg, kaug, v_scr):
    at = pl.ds(pl.multiple_of(i * step, step), step)
    piece = tok[at, :]
    keys = dot(piece, wk).astype(BF16)
    vals = (dot(piece, wv) + bias_v).astype(BF16)
    lanes = mask_lanes(seg[:, at], step).astype(BF16)
    for p in range(kaug.shape[0]):
        kaug[p, at, 0:128] = keys[:, p * 128:(p + 1) * 128]
        kaug[p, at, 128:256] = lanes
        v_scr[p, at, :] = vals[:, p * 128:(p + 1) * 128]


def project_queries(tok, wq, bias_q, seg, qaug, blk, qlen):
    mine = pl.ds(pl.multiple_of(blk * qlen, qlen), qlen)
    query = (dot(tok[mine, :], wq) + bias_q).astype(BF16)
    lane = lax.broadcasted_iota(jnp.int32, (qlen, 128), 1)
    feat = jnp.where(lane < 8, BIG * (1.0 + mask_lanes(seg[:, mine], qlen)), 0.0).astype(BF16)
    for p in range(qaug.shape[0] // 2):
        q_pair = query[:, p * 128:(p + 1) * 128].astype(F32) * HD**-0.5
        for half in range(2):
            keep = (lane >= 64) if half else (lane < 64)
            qaug[2 * p + half, :, 0:128] = jnp.where(keep, q_pair, 0.0).astype(BF16)
            qaug[2 * p + half, :, 128:256] = feat


def attend_chunk(i, qaug, kaug, v_scr, o_scr, exact_scr, lse_scr, chunk, per_head):
    h = i // per_head
    at = pl.ds(pl.multiple_of((i % per_head) * chunk, chunk), chunk)
    s = dot(qaug[h, at, :], kaug[h // 2], ((1,), (1,)))
    top = jnp.max(s, axis=-1, keepdims=True)
    p = jnp.exp(s - top)
    total = jnp.sum(p, axis=-1, keepdims=True)
    low = p.astype(BF16)
    rest = (p - low.astype(F32)).astype(BF16)
    value = v_scr[h // 2]
    o = dot(low, value)
    inverse = 1.0 / total
    o_scr[h, at, :] = o * inverse
    exact_scr[h, at, :] = (o + dot(rest, value)) * inverse
    lse_scr[h, at, :] = jnp.broadcast_to(top + jnp.log(total), (chunk, 128))


def attend_block(h, at, qaug, kaug, v_scr, top_scr, sum_scr, o_scr, rest_scr):
    s = dot(qaug[h], kaug[h // 2, at, :], ((1,), (1,)))
    before = top_scr[h]
    top = jnp.maximum(before, jnp.broadcast_to(jnp.max(s, axis=-1, keepdims=True), before.shape))
    p = jnp.exp(s - jnp.concatenate([top] * (s.shape[1] // 128), axis=1))
    fade = jnp.exp(before - top)
    low = p.astype(BF16)
    rest = (p - low.astype(F32)).astype(BF16)
    value = v_scr[h // 2, at, :]
    top_scr[h] = top
    sum_scr[h] = sum_scr[h] * fade + jnp.broadcast_to(jnp.sum(p, axis=-1, keepdims=True), before.shape)
    o_scr[h] = o_scr[h] * fade + dot(low, value)
    rest_scr[h] = rest_scr[h] * fade + dot(rest, value)


def close_blocks(top_scr, sum_scr, o_scr, rest_scr):
    for h in range(o_scr.shape[0]):
        total = sum_scr[h]
        inverse = 1.0 / total
        o = o_scr[h]
        rest_scr[h] = (o + rest_scr[h]) * inverse
        o_scr[h] = o * inverse
        top_scr[h] = top_scr[h] + jnp.log(total)


def join_heads(scr, p, at=slice(None)):
    first, second = scr[2 * p, at, :], scr[2 * p + 1, at, :]
    lane = lax.broadcasted_iota(jnp.int32, first.shape, 1)
    return jnp.where(lane < 64, first, second)


def head_columns(w, part, c, width):
    return w[:, pl.ds(pl.multiple_of((part * 2 + c) * width, 128), width)]


def fwd_kernel(tok, w, bias, seg, ctx, kaug, v_scr, qaug, lse_out, exact, lse_scr, o_scr, exact_scr, chunk=256):
    blk, c = lax.axis_index("blk"), lax.axis_index("head")
    qlen, width = ctx.shape
    total = tok.shape[0]
    step = min(512, total)
    wk, wv = head_columns(w, 1, c, width), head_columns(w, 2, c, width)

    def rows(i, carry):
        project_keys(i, step, tok, wk, wv, bias[1:2, :], seg, kaug, v_scr)
        return carry

    lax.fori_loop(0, total // step, rows, 0)
    project_queries(tok, head_columns(w, 0, c, width), bias[0:1, :], seg, qaug, blk, qlen)
    per_head = qlen // chunk

    def go(i, carry):
        attend_chunk(i, qaug, kaug, v_scr, o_scr, exact_scr, lse_scr, chunk, per_head)
        return carry

    lax.fori_loop(0, (width // HD) * per_head, go, 0)
    finish_forward(o_scr, exact_scr, lse_scr, lambda p, v: store_lanes(ctx, p, v), lse_out, exact)


def store_lanes(ref, p, value):
    ref[:, p * 128:(p + 1) * 128] = value


def finish_forward(o_scr, exact_scr, lse_scr, put, lse_out, exact):
    for p in range(o_scr.shape[0] // 2):
        put(p, join_heads(o_scr, p).astype(BF16))
        exact[p] = join_heads(exact_scr, p)
    for h in range(o_scr.shape[0]):
        lse_out[h] = jnp.transpose(lse_scr[h], (1, 0))[0:8, :]


def prepare_backward(gctx_of, exact, do_m, delta_row):
    pairs, qlen, _ = exact.shape
    lane = lax.broadcasted_iota(jnp.int32, (qlen, 128), 1)
    for p in range(pairs):
        grad = gctx_of(p)
        product = grad.astype(F32) * exact[p]
        for half in range(2):
            keep = (lane >= 64) if half else (lane < 64)
            do_m[2 * p + half] = jnp.where(keep, grad, jnp.zeros_like(grad))
            across = jnp.transpose(jnp.where(keep, product, 0.0), (1, 0))
            delta_row[2 * p + half] = jnp.broadcast_to(jnp.sum(across, axis=0, keepdims=True), (8, qlen))


def bwd_pair(pair, qaug, k_part, v_part, do_m, lse_row, delta_row, dq_scr, put, first, qs=slice(None)):
    dk = dv = None
    for half in range(2):
        h = 2 * pair + half
        q_part, do_part = qaug[h, qs, :], do_m[h, qs, :]
        s = dot(k_part, q_part, ((1,), (1,)))
        p = jnp.exp(s - lse_row[h, 0:1, qs])
        dp = dot(v_part, do_part, ((1,), (1,)))
        ds = (p * (dp - delta_row[h, 0:1, qs])).astype(BF16)
        v_term = dot(p.astype(BF16), do_part)
        k_term = dot(ds, q_part[:, 0:128])
        dv = v_term if dv is None else dv + v_term
        dk = k_term if dk is None else dk + k_term
        dq = dot(k_part[:, 0:128], ds, ((0,), (0,)))
        if first is True:
            dq_scr[h, :, qs] = dq
        elif first is None:
            dq_scr[h, :, qs] += dq
        else:
            dq_scr[h, :, qs] = jnp.where(first, dq, dq_scr[h, :, qs] + dq)
    put(dk, dv)


def join_dq(dq_scr, p):
    qlen = dq_scr.shape[2]
    lane = lax.broadcasted_iota(jnp.int32, (qlen, 128), 1)
    first, second = jnp.transpose(dq_scr[2 * p], (1, 0)), jnp.transpose(dq_scr[2 * p + 1], (1, 0))
    return (jnp.where(lane < 64, first, second) * HD**-0.5).astype(BF16)


VMEM = pl.BlockSpec(memory_space=pltpu.VMEM)
HBM = pl.BlockSpec(memory_space=pltpu.HBM)


def params(limit, collective=None):
    more = {} if collective is None else dict(collective_id=collective, has_side_effects=True)
    return pltpu.CompilerParams(vmem_limit_bytes=limit << 20, **more)


def lane_mean(x):
    return jnp.mean(x, axis=-1, keepdims=True)


def norm_parts(hidden):
    centered = hidden - lane_mean(hidden)
    scale = lax.rsqrt(lane_mean(centered * centered) + 1e-12)
    return centered * scale, scale


def norm_back(grad, unit, scale, gain):
    scaled = grad * gain
    return scale * (scaled - lane_mean(scaled) - unit * lane_mean(scaled * unit))


def gelu_and_slope(pre):
    cdf = 0.5 * (1.0 + lax.erf(pre * 0.7071067811865476))
    return pre * cdf, cdf + pre * (0.3989422804014327 * jnp.exp(-0.5 * pre * pre))


def column_sum(x):
    return jnp.sum(x, axis=0, keepdims=True)


def ffn_kernel(
    ctx, tok, cot, vecs, bias_in, w_out_h, w_in_h, w_down_h,
    out, resid_grad, gctx, dw_down_h, dw_in_h, dw_out_h, sums,
    w_out, w_in, w_down, act, slope, dw_a, dw_b, dw_c, in_sem, out_sem,
):
    groups, rows, half = ctx.shape
    width, ff = w_in.shape
    step = width
    loads = [
        pltpu.make_async_copy(src, dst, in_sem.at[i])
        for i, (src, dst) in enumerate([(w_out_h, w_out), (w_in_h, w_in), (w_down_h, w_down)])
    ]
    for load in loads:
        load.start()
    bias_out, gain_one, shift_one = vecs[2:3, :], vecs[3:4, :], vecs[4:5, :]
    bias_down, gain_two, shift_two = vecs[5:6, :], vecs[6:7, :], vecs[7:8, :]
    context = jnp.concatenate([ctx[g] for g in range(groups)], axis=1)
    loads[0].wait()
    resid_one = tok[...].astype(F32) + (dot(context, w_out[...]) + bias_out)
    unit_one, scale_one = norm_parts(resid_one)
    normed = unit_one * gain_one + shift_one
    normed_low = normed.astype(BF16)
    loads[1].wait()
    chunks = [slice(i, i + step) for i in range(0, ff, step)]
    for at in chunks:
        pre = dot(normed_low, w_in[:, at]) + bias_in[0:1, at]
        value, grad = gelu_and_slope(pre)
        act[:, at] = value.astype(BF16)
        slope[:, at] = grad
    loads[2].wait()
    resid_two = normed + (dot(act[...], w_down[...]) + bias_down)
    unit_two, scale_two = norm_parts(resid_two)
    out[...] = (unit_two * gain_two + shift_two).astype(BF16)
    grad_out = cot[...].astype(F32)
    grad_two = norm_back(grad_out, unit_two, scale_two, gain_two)
    grad_ffn = grad_two.astype(BF16)
    sums[0:2, :] = jnp.zeros((2, width), F32)
    sums[5:6, :] = column_sum(grad_ffn.astype(F32))
    sums[6:7, :] = column_sum(grad_out * unit_two)
    sums[7:8, :] = column_sum(grad_out)
    stores = []

    def store(src, dst):
        copy = pltpu.make_async_copy(src, dst, out_sem.at[len(stores)])
        copy.start()
        stores.append(copy)

    for at in chunks:
        dw_a[at, :] = dot(act[:, at], grad_ffn, ((0,), (0,))).astype(BF16)
        store(dw_a.at[at], dw_down_h.at[at])
    grad_normed = grad_two
    for i, at in enumerate(chunks):
        grad_act = dot(grad_ffn, w_down[at, :], ((1,), (1,)))
        grad_pre = (grad_act * slope[:, at]).astype(BF16)
        sums[8 + i:9 + i, :] = column_sum(grad_pre.astype(F32))
        dw_b[:, at] = dot(normed_low, grad_pre, ((0,), (0,))).astype(BF16)
        grad_normed = grad_normed + dot(grad_pre, w_in[:, at], ((1,), (1,)))
    store(dw_b, dw_in_h)
    sums[8 + len(chunks):, :] = jnp.zeros((sums.shape[0] - 8 - len(chunks), width), F32)
    sums[3:4, :] = column_sum(grad_normed * unit_one)
    sums[4:5, :] = column_sum(grad_normed)
    grad_one = norm_back(grad_normed, unit_one, scale_one, gain_one)
    resid_grad[...] = grad_one
    grad_attn = grad_one.astype(BF16)
    sums[2:3, :] = column_sum(grad_attn.astype(F32))
    dw_c[...] = dot(context, grad_attn, ((0,), (0,))).astype(BF16)
    store(dw_c, dw_out_h)
    grad_context = dot(grad_attn, w_out[...], ((1,), (1,))).astype(BF16)
    for g in range(groups):
        gctx[g] = grad_context[:, g * half:(g + 1) * half]
    for copy in stores:
        copy.wait()


def feed_forward(ctx, tok, cot, vecs, bias_in, w_out, w_in, w_down):
    groups, rows, half = ctx.shape
    width, ff = w_in.shape
    n_sums = 8 + -(-(ff // width) // 8) * 8
    return pl.pallas_call(
        ffn_kernel,
        out_shape=[
            jax.ShapeDtypeStruct((rows, width), BF16),
            jax.ShapeDtypeStruct((rows, width), F32),
            jax.ShapeDtypeStruct((groups, rows, half), BF16),
            jax.ShapeDtypeStruct((ff, width), BF16),
            jax.ShapeDtypeStruct((width, ff), BF16),
            jax.ShapeDtypeStruct((width, width), BF16),
            jax.ShapeDtypeStruct((n_sums, width), F32),
        ],
        in_specs=[VMEM] * 5 + [HBM] * 3,
        out_specs=[VMEM] * 3 + [HBM] * 3 + [VMEM],
        scratch_shapes=[
            pltpu.VMEM((width, width), BF16),
            pltpu.VMEM((width, ff), BF16),
            pltpu.VMEM((ff, width), BF16),
            pltpu.VMEM((rows, ff), BF16),
            pltpu.VMEM((rows, ff), F32),
            pltpu.VMEM((ff, width), BF16),
            pltpu.VMEM((width, ff), BF16),
            pltpu.VMEM((width, width), BF16),
            pltpu.SemaphoreType.DMA((3,)),
            pltpu.SemaphoreType.DMA((ff // width + 2,)),
        ],
        compiler_params=params(56),
    )(ctx, tok, cot, vecs, bias_in, w_out, w_in, w_down)


def gather_order(keys, narrow, nd, nb):
    events = []
    for p, (begin, dz, dx) in enumerate(keys):
        for e in range(nb):
            events.append((begin + e * dz, ("z", p, e)))
            if not narrow[p]:
                for mask in range(1, nd):
                    events.append((begin + e * dz + dx * mask.bit_length(), ("x", p, mask, e)))
    events.sort(key=lambda q: q[0])
    return [ev for _, ev in events]


def gather_all(shards, narrow, keys, nd, nb, nc):
    count = len(shards)

    def kernel(*refs):
        mine, full = refs[:count], refs[count:2 * count]
        four, recv, own_sem, block_sem = refs[2 * count:]
        net = Net(nd, nb, nc)
        pieces = [
            Gather(net, mine[p], *blocks_of(full[p]), gather_refs(four, recv, block_sem, p, narrow[p]), narrow[p]) for p in range(count)
        ]
        net.barrier()
        for ev in gather_order(keys, narrow, nd, nb):
            if ev[0] == "z" and ev[2] == 0:
                pieces[ev[1]].own_line()
                pieces[ev[1]].own_spread()
            elif ev[0] == "z":
                pieces[ev[1]].z(ev[2])
            else:
                pieces[ev[1]].x(ev[2], ev[3])
        for piece in pieces:
            own = piece.own(own_sem)
            own.start()
            own.wait()
        for piece in pieces:
            piece.wait_sibling()
        for piece in pieces:
            piece.drain()

    outs = [
        jax.ShapeDtypeStruct(((nb * nc if thin else nd * nb * nc),) + s.shape, s.dtype) for s, thin in zip(shards, narrow)
    ]
    return pl.pallas_call(
        kernel,
        out_shape=outs,
        in_specs=[VMEM] * count,
        out_specs=[HBM] * count,
        scratch_shapes=gather_sems(count, nd, nb) + [pltpu.SemaphoreType.DMA((count, nb))],
        compiler_params=params(56, 0),
    )(*shards)


def attend_forward(tok, w, bias, seg, qlen, width):
    total = tok.shape[0]
    heads = width // HD
    chunk = min(256, qlen)
    while chunk * total > 256 * 4096:
        chunk //= 2
    return pl.pallas_call(
        functools.partial(fwd_kernel, chunk=chunk),
        out_shape=[
            jax.ShapeDtypeStruct((qlen, width), BF16),
            jax.ShapeDtypeStruct((width // 128, total, 256), BF16),
            jax.ShapeDtypeStruct((width // 128, total, 128), BF16),
            jax.ShapeDtypeStruct((heads, qlen, 256), BF16),
            jax.ShapeDtypeStruct((heads, 8, qlen), F32),
            jax.ShapeDtypeStruct((heads // 2, qlen, 128), F32),
        ],
        in_specs=[VMEM] * 4,
        out_specs=[VMEM] * 6,
        scratch_shapes=[pltpu.VMEM((heads, qlen, 128), F32)] * 3,
        compiler_params=params(58),
    )(tok, w, bias, seg)


def pair_bwd_kernel(qaug, kaug, v_scr, lse, exact, gctx, dk, dv, dq, do_m, delta_row, dq_scr):
    step = pl.program_id(1)

    @pl.when(step == 0)
    def _():
        prepare_backward(lambda p: gctx[...], exact, do_m, delta_row)

    def put(k_term, v_term):
        dk[...] = k_term.astype(BF16)
        dv[...] = v_term.astype(BF16)

    bwd_pair(0, qaug, kaug[0], v_scr[0], do_m, lse, delta_row, dq_scr, put, step == 0)

    @pl.when(step == pl.num_programs(1) - 1)
    def _():
        dq[...] = join_dq(dq_scr, 0)


def finish_kernel(tok, dk, dv, tok_mine, dq, w, dtok, dw, dbias, own):
    i, c = pl.program_id(0), lax.axis_index("head")
    blk = lax.axis_index("blk")
    step, width = dk.shape
    qlen = dq.shape[0]

    def cols(part):
        return w[:, pl.ds(pl.multiple_of((part * 2 + c) * width, 128), width)]

    piece, grad_k, grad_v = tok[...], dk[...], dv[...]

    @pl.when(i == 0)
    def _():
        dw[:, 0:width] = dot(tok_mine[...], dq[...], ((0,), (0,)))
        dw[:, width:3 * width] = jnp.zeros((dw.shape[0], 2 * width), F32)
        dbias[0:1, :] = jnp.sum(dq[...].astype(F32), axis=0, keepdims=True)
        dbias[1:2, :] = jnp.zeros((1, width), F32)
        own[...] = dot(dq[...], cols(0), ((1,), (1,)))

    dw[:, width:2 * width] += dot(piece, grad_k, ((0,), (0,)))
    dw[:, 2 * width:3 * width] += dot(piece, grad_v, ((0,), (0,)))
    dbias[1:2, :] += jnp.sum(grad_v.astype(F32), axis=0, keepdims=True)
    grad = dot(grad_k, cols(1), ((1,), (1,))) + dot(grad_v, cols(2), ((1,), (1,)))
    per = qlen // step
    mine = i // per == blk
    at = pl.ds(pl.multiple_of((i % per) * step, step), step)
    dtok[...] = (grad + jnp.where(mine, own[at, :], 0.0)).astype(BF16)


def attend_backward(tok, tok_mine, w, qaug, kaug, v_scr, lse, exact, gctx):
    heads, qlen, _ = qaug.shape
    total, d_model = tok.shape
    width = heads * HD
    kc = min(512, total)
    dk, dv, dq = pl.pallas_call(
        pair_bwd_kernel,
        grid=(heads // 2, total // kc),
        out_shape=[
            jax.ShapeDtypeStruct((total, width), BF16),
            jax.ShapeDtypeStruct((total, width), BF16),
            jax.ShapeDtypeStruct((qlen, width), BF16),
        ],
        in_specs=[
            pl.BlockSpec((2, qlen, 256), lambda p, j: (p, 0, 0)),
            pl.BlockSpec((1, kc, 256), lambda p, j: (p, j, 0)),
            pl.BlockSpec((1, kc, 128), lambda p, j: (p, j, 0)),
            pl.BlockSpec((2, 8, qlen), lambda p, j: (p, 0, 0)),
            pl.BlockSpec((1, qlen, 128), lambda p, j: (p, 0, 0)),
            pl.BlockSpec((qlen, 128), lambda p, j: (0, p)),
        ],
        out_specs=[pl.BlockSpec((kc, 128), lambda p, j: (j, p))] * 2 + [pl.BlockSpec((qlen, 128), lambda p, j: (0, p))],
        scratch_shapes=[
            pltpu.VMEM((2, qlen, 128), BF16),
            pltpu.VMEM((2, 8, qlen), F32),
            pltpu.VMEM((2, 128, qlen), F32),
        ],
        compiler_params=params(56),
    )(qaug, kaug, v_scr, lse, exact, gctx)
    step = min(512, qlen)
    whole = lambda i: (0, 0)
    rows = lambda i: (i, 0)
    return pl.pallas_call(
        finish_kernel,
        grid=(total // step,),
        out_shape=[
            jax.ShapeDtypeStruct((total, d_model), BF16),
            jax.ShapeDtypeStruct((d_model, 3 * width), F32),
            jax.ShapeDtypeStruct((2, width), F32),
        ],
        in_specs=[
            pl.BlockSpec((step, d_model), rows),
            pl.BlockSpec((step, width), rows),
            pl.BlockSpec((step, width), rows),
            pl.BlockSpec((qlen, d_model), whole),
            pl.BlockSpec((qlen, width), whole),
            pl.BlockSpec((d_model, w.shape[1]), whole),
        ],
        out_specs=[
            pl.BlockSpec((step, d_model), rows),
            pl.BlockSpec((d_model, 3 * width), whole),
            pl.BlockSpec((2, width), whole),
        ],
        scratch_shapes=[pltpu.VMEM((qlen, d_model), F32)],
        compiler_params=params(56),
    )(tok, dk, dv, tok_mine, dq, w)


SPACE = (0.25, 1.0, 0.2)


def send_blocks(piece, nb):
    for blk in range(nb):
        piece.send(blk, blk)


def scatter_all(arrays, narrow, joined, small, nd, nb, nc):
    count = len(arrays)
    flat = []
    for a, j in zip(arrays, joined):
        flat += list(a) if j else [a]
    n_in = len(flat) + 1

    def kernel(*refs):
        ins, small_in = list(refs[:n_in - 1]), refs[n_in - 1]
        outs, small_out = refs[n_in:n_in + count], refs[n_in + count]
        rest = list(refs[n_in + count + 1:])
        net = Net(nd, nb, nc)
        s3, sib_sem, x_sem, z_sem, sum_send, sum_recv = rest[-6:]
        value, got = rest[-8:-6]
        bufs = rest[:-8]
        pieces = []
        for p in range(count):
            first = ins.pop(0)
            sib = ins.pop(0) if joined[p] else bufs.pop(0)
            xbuf = None if narrow[p] else bufs.pop(0)
            zbuf = bufs.pop(0)
            sems = [s3.at[p, i] for i in range(3)] + [sib_sem.at[p], x_sem.at[p], z_sem.at[p]]
            if joined[p]:
                parts = lambda at, first=first: [(None, [first.at[at]])]
                place = lambda at, first=first: first.at[at]
                theirs = lambda at, sib=sib: sib.at[at]
                landing = lambda at, first=first: first.at[at, net.c]
            else:
                place = lambda at, first=first: first.at[at * nc + net.c]
                parts = lambda at, place=place, sib=sib: [(None, [place(at), sib.at[at]])]
                theirs = lambda at, first=first: first.at[at * nc + nc - 1 - net.c]
                landing = lambda at, sib=sib: sib.at[at]
            span = lambda k, sib=sib: sib.at[pl.ds(0, k)]
            pieces.append(Scatter(net, parts, place, theirs, landing, span, xbuf, zbuf, outs[p], sems, narrow[p]))
        sums = AllSum(net, value, got, sum_send, sum_recv)
        for piece in pieces:
            piece.clear_edges()
        value[0] = small_in[...]
        net.barrier()
        events = []
        for p, piece in enumerate(pieces):
            t = SPACE[0] * p
            begin = functools.partial(send_blocks, piece, nb) if narrow[p] else piece.start
            events.append((t - 0.4, begin))
            for mask in range(piece.nd - 1, -1, -1):
                for e in range(nb - 1, -1, -1):
                    when = t + SPACE[1] * (piece.levels - mask.bit_length()) + SPACE[2] * (nb - 1 - e)
                    events.append((when, functools.partial(piece.reduce, mask, e)))
        for i, s in enumerate(sums.stages()):
            events.append((0.3 * i, s))
        events.sort(key=lambda q: q[0])
        for _, ev in events:
            ev()
        small_out[...] = value[0]
        for piece in pieces:
            piece.drain()

    outs, scratch = [], []
    for a, thin, j in zip(arrays, narrow, joined):
        full = a[0] if j else a
        block = full.shape[1:]
        outs.append(jax.ShapeDtypeStruct(block, F32))
        n_dp = 1 if thin else nd
        if not j:
            scratch.append(pltpu.VMEM((n_dp * nb,) + block, BF16))
        if not thin:
            scratch.append(pltpu.VMEM(((nd - 1) * nb,) + block, BF16))
        scratch.append(pltpu.VMEM((nb + 1,) + block, BF16))
    levels = nd.bit_length() - 1
    scratch += [pltpu.VMEM((levels + 2,) + small.shape, F32), pltpu.VMEM((levels + nb,) + small.shape, F32)]
    scratch += scatter_sems(count, nd, nb)
    scratch += [pltpu.SemaphoreType.DMA((levels + nb,))] * 2
    outs.append(jax.ShapeDtypeStruct(small.shape, F32))
    return pl.pallas_call(
        kernel,
        out_shape=outs,
        in_specs=[VMEM] * n_in,
        out_specs=[VMEM] * (count + 1),
        scratch_shapes=scratch,
        compiler_params=params(60, 1),
    )(*flat, small)


def hand_out(arrays, small, r, r_ff):
    count = len(arrays)

    def kernel(*refs):
        ins, small_in = refs[:count], refs[count]
        outs, vectors, sems = refs[count + 1:2 * count + 1], refs[2 * count + 1:-1], refs[-1]
        copies = [pltpu.make_async_copy(a, b, sems.at[i]) for i, (a, b) in enumerate(zip(ins, outs))]
        for copy in copies:
            copy.start()
        for i, out in enumerate(vectors):
            out[...] = small_in[i, 0:out.shape[0]]
        for copy in copies:
            copy.wait()

    sizes = [r] * 8 + [r_ff]
    return pl.pallas_call(
        kernel,
        out_shape=[jax.ShapeDtypeStruct(a.shape, a.dtype) for a in arrays] + [jax.ShapeDtypeStruct((s,), F32) for s in sizes],
        in_specs=[VMEM] * (count + 1),
        out_specs=[HBM] * count + [VMEM] * 9,
        scratch_shapes=[pltpu.SemaphoreType.DMA((count,))],
        compiler_params=params(60),
    )(*arrays, small)


def unpack_vectors(small, vecs, bias_in, r, r_ff):
    n = small.shape[0]
    width, ff = vecs.shape[1], bias_in.shape[1]

    def gathered(rows, per, count):
        lane = lax.broadcasted_iota(jnp.int32, (8, 128), 1)
        tiles = [jnp.zeros((8, 128), F32) for _ in range(count // 128)]
        for i in range(n):
            piece = small[i, rows, :].astype(F32)
            shift, tile = per * i % 128, per * i // 128
            if shift:
                piece = pltpu.roll(piece, shift, 1)
            if shift + per <= 128:
                tiles[tile] = tiles[tile] + piece
            else:
                tiles[tile] = tiles[tile] + jnp.where(lane >= shift, piece, 0.0)
                tiles[tile + 1] = tiles[tile + 1] + jnp.where(lane < shift, piece, 0.0)
        return tiles

    for t, tile in enumerate(gathered(slice(0, 8), r, width)):
        vecs[:, t * 128:(t + 1) * 128] = tile
    for t, tile in enumerate(gathered(slice(8, 16), r_ff, ff)):
        bias_in[:, t * 128:(t + 1) * 128] = tile[0:1, :]


FRONT = {
    "small": (2, 22, ((2, 6, 15, 24), (27, 12, 39, 37), (35, 13, 29, 38), (47, 23, 46, 43))),
    "q": (3, 20, ((3, 10, 14, 25), (30, 16, 28, 40), (34, 17, 44, 45), (41, 32, 42, 50))),
    "t0": (26, 36, ((26, 54, 71, 99),)),
    "t1": (4, 8, ((4, 18, 49, 78),)),
    "o": (0, 89, ((0, 5, 21, 48), (102, 60, 51, 72), (105, 11, 33, 61), (110, 73, 82, 86))),
    "i": (31, 55, ((31, 53, 64, 84), (69, 62, 91, 103), (70, 65, 81, 100), (88, 83, 104, 121))),
    "d": (52, 1, ((52, 74, 93, 107), (9, 92, 111, 120), (7, 96, 113, 119), (19, 112, 122, 125))),
    "work": (56, 57, 58, 59, 63, 66, 67, 68, 75, 76, 77, 79, 80, 85, 87, 90, 94, 95, 97, 98, 101, 106, 108, 109, 114, 115, 116, 117, 118, 123, 124, 126, 127, 128),
}


def front_time(nd, nb, kind, what, e=0):
    if (nd, nb) == (4, 4) and (kind != "work" or e == len(FRONT["work"])):
        row = FRONT[kind]
        if kind == "work":
            return row[what]
        if what == "line":
            return row[0]
        if what == "spread":
            return row[1]
        return row[2][what][e]
    first = ["small", "q", "t0", "t1", "o", "i", "d"].index(kind) * 10 if kind != "work" else 0
    if kind == "work":
        return (40 if what == 0 else 200) + what
    if what in ("line", "spread"):
        return first
    return first + 3 * e + (4 * what.bit_length() if what else 0)


DIRECT = ()


def front(vectors, many, w_qkv, tok, w_out, w_in, w_down, seg, nd, nb, nc):
    n = nd * nb * nc
    rows, width = tok.shape
    half, qlen, total = width // nc, nc * rows, nb * nc * rows
    heads = half // HD
    pairs = heads // 2
    r, r_ff, ff = w_qkv.shape[0], w_down.shape[0], w_in.shape[1]
    parts = 2
    part = rows // parts
    steps = nb * heads
    chunks = [slice(i, i + width) for i in range(0, ff, width)]

    def kernel(
        *refs,
    ):
        few_in, many_in = refs[:8], refs[8]
        inside(few_in, many_in, *refs[9:])

    def inside(
        few_in, many_in, q_in, tok_in, o_in, i_in, d_in, seg_in,
        ctx2, vecs, lse_out, scale_one,
        q_h, o_h, i_h, d_h, kaug_h, v_h, qaug_h, tok_t_h, act_h, slope_h, exact_h, normed_h, unit_h,
        small_in, small_all, w_v, tok_v, tok_t, kaug, v_scr, qaug, top_scr, sum_scr, o_scr, rest_scr, ctx_loc,
        w_o, w_i, act, slope, bias_in, exact, normed, unit_one,
        four, recv, block_sem, own_sem, load_sem, save_sem, swap_sem,
    ):
        net = Net(nd, nb, nc)
        c = net.c
        small_in[...] = jnp.zeros((16, 128), BF16)
        few_row = lax.broadcasted_iota(jnp.int32, (16, r), 0)
        few = jnp.zeros((16, r), BF16)
        for i, ref in enumerate(few_in):
            few = jnp.where(few_row == i, jnp.broadcast_to(ref[...], (16, r)), few)
        small_in[:, 0:r] = few
        row = lax.broadcasted_iota(jnp.int32, (16, r_ff), 0)
        small_in[:, 0:r_ff] = jnp.where(row == 8, jnp.broadcast_to(many_in[...], (16, r_ff)), small_in[:, 0:r_ff])
        specs = [("small", small_in, blocks_of(small_all), False), ("q", q_in, rows_of(q_h, r), False)]
        for i in range(parts):
            mine = tok_in.at[pl.ds(i * part, part)]
            specs.append(("t" + str(i), mine, rows_of(tok_v, part, i * part, rows), True))
        specs += [("o", o_in, rows_of(o_h, r), False), ("i", i_in, rows_of(i_h, r), False), ("d", d_in, rows_of(d_h, r_ff), False)]
        piece, own = {}, {}
        for p, (name, mine, (place, span), narrow) in enumerate(specs):
            piece[name] = Gather(net, mine, place, span, gather_refs(four, recv, block_sem, p, narrow), narrow, name in DIRECT)
            own[name] = piece[name].own(own_sem.at[p])
        tokens = ["t" + str(i) for i in range(parts)]
        for name in piece:
            own[name].start()
        net.barrier()
        lanes = pl.ds(pl.multiple_of(c * half, 128), half)

        def whole(name):
            piece[name].wait_sibling()
            own[name].wait()

        def unpack():
            whole("small")
            unpack_vectors(small_all, vecs, bias_in, r, r_ff)

        def load():
            whole("q")
            copies = []
            for k in range(3):
                at = pl.ds(pl.multiple_of((k * nc + c) * half, 128), half)
                copies.append(pltpu.make_async_copy(q_h.at[:, at], w_v.at[:, pl.ds(k * half, half)], load_sem.at[k]))
            for copy in copies:
                copy.start()
            for copy in copies:
                copy.wait()

        def queries():
            for name in tokens:
                own[name].wait()
                piece[name].wait_sibling_block(net.b)
            project_queries(tok_v, w_v[:, 0:half], vecs[0:1, lanes], seg_in, qaug, net.b, qlen)
            for scr, start in ((top_scr, -3e38), (sum_scr, 0.0), (o_scr, 0.0), (rest_scr, 0.0)):
                scr[...] = jnp.full(scr.shape, start, F32)

        saves = [
            pltpu.make_async_copy(src, dst, save_sem.at[i])
            for i, (src, dst) in enumerate(
                [
                    (kaug, kaug_h), (v_scr, v_h), (qaug, qaug_h), (tok_t, tok_t_h),
                    (exact, exact_h), (normed, normed_h), (unit_one, unit_h),
                ]
                + [(a.at[:, at], b.at[:, at]) for a, b in ((act, act_h), (slope, slope_h)) for at in chunks]
            )
        ]

        def turn_tokens():
            tok_t[...] = jnp.transpose(tok_v[...], (1, 0))
            for save in saves[:4]:
                save.start()

        swap = remote(ctx_loc.at[nc - 1 - c], ctx2.at[c], swap_sem.at[0], swap_sem.at[1], net.sibling)
        st = {}

        def finish():
            def put(p, value):
                for g in range(nc):
                    ctx_loc[g, :, p * 128:(p + 1) * 128] = value[g * rows:(g + 1) * rows]

            close_blocks(top_scr, sum_scr, o_scr, rest_scr)
            finish_forward(o_scr, rest_scr, top_scr, put, lse_out, exact)
            swap.start()
            saves[4].start()
            ctx2[c] = ctx_loc[c]

        def fetch(name, src, dst):
            whole(name)
            copy = pltpu.make_async_copy(src, dst, load_sem.at[3])
            copy.start()
            copy.wait()

        def first_norm():
            fetch("o", o_h, w_o)
            swap.wait()
            context = jnp.concatenate([ctx2[g] for g in range(nc)], axis=1)
            resid = tok_in[...].astype(F32) + (dot(context, w_o[...]) + vecs[2:3, :])
            unit, scale = norm_parts(resid)
            value = unit * vecs[3:4, :] + vecs[4:5, :]
            normed[...] = value
            unit_one[...] = unit
            scale_one[...] = jnp.broadcast_to(scale, scale_one.shape)
            saves[5].start()
            saves[6].start()
            st["low"] = value.astype(BF16)

        def expand(i, at):
            if i == 0:
                fetch("i", i_h, w_i)
            pre = dot(st["low"], w_i[:, at]) + bias_in[0:1, at]
            result, grad = gelu_and_slope(pre)
            act[:, at] = result.astype(BF16)
            slope[:, at] = grad
            saves[7 + i].start()
            saves[7 + len(chunks) + i].start()

        order = []
        for name in piece:
            order.append((front_time(nd, nb, name, "line"), piece[name].own_line, None))
            order.append((front_time(nd, nb, name, "spread"), piece[name].own_spread, None))
            for e in range(1, nb):
                order.append((front_time(nd, nb, name, 0, e), functools.partial(piece[name].z, e), None))
            for mask in range(1, 1 if name in tokens else nd):
                for e in range(nb):
                    order.append((front_time(nd, nb, name, mask, e), functools.partial(piece[name].x, mask, e), None))
        work = [unpack, load, queries] + [None] * steps + [turn_tokens, finish, first_norm]
        work += [functools.partial(expand, i, at) for i, at in enumerate(chunks)]
        for i, act_now in enumerate(work):
            order.append((front_time(nd, nb, "work", i, len(work)), act_now, i - 3 if act_now is None else None))
        order.sort(key=lambda q: q[0])
        begin = next(i for i, q in enumerate(order) if q[2] == 0)
        end = next(i for i, q in enumerate(order) if q[2] == steps - 1)
        for _, act_now, _ in order[:begin]:
            act_now()
        beside = {}
        for _, act_now, i in order[begin:end + 1]:
            if act_now is None:
                at_step = i
            else:
                beside.setdefault(at_step, []).append(act_now)

        def attention(e, h, carry):
            blk = net.near(e)
            at = pl.ds(pl.multiple_of(blk * qlen, qlen), qlen)
            attend_block(h, at, qaug, kaug, v_scr, top_scr, sum_scr, o_scr, rest_scr)
            for g in range(heads):
                acts = beside.get(e * heads + g, ())
                if acts:

                    @pl.when(h == g)
                    def _(acts=acts):
                        for act_now in acts:
                            act_now()

            return carry

        for e in range(nb):
            blk = net.near(e)
            if e:
                for name in tokens:
                    piece[name].wait_sibling_block(blk)
            project_keys(blk, qlen, tok_v, w_v[:, half:2 * half], w_v[:, 2 * half:3 * half], vecs[1:2, lanes], seg_in, kaug, v_scr)
            lax.fori_loop(0, heads, functools.partial(attention, e), 0)
        for _, act_now, _ in order[end + 1:]:
            act_now()
        whole("d")
        for name in piece:
            piece[name].drain()
        for save in saves:
            save.wait()

    count = 5 + parts
    vmem = lambda *shape: pltpu.VMEM(shape, BF16)
    wide = pltpu.VMEM((heads, qlen, 128), F32)
    return pl.pallas_call(
        kernel,
        out_shape=[
            jax.ShapeDtypeStruct((nc, rows, half), BF16),
            jax.ShapeDtypeStruct((8, width), F32),
            jax.ShapeDtypeStruct((heads, 8, qlen), F32),
            jax.ShapeDtypeStruct((rows, 128), F32),
            jax.ShapeDtypeStruct((n * r, 3 * width), BF16),
            jax.ShapeDtypeStruct((n * r, width), BF16),
            jax.ShapeDtypeStruct((n * r, ff), BF16),
            jax.ShapeDtypeStruct((n * r_ff, width), BF16),
            jax.ShapeDtypeStruct((pairs, total, 256), BF16),
            jax.ShapeDtypeStruct((pairs, total, 128), BF16),
            jax.ShapeDtypeStruct((heads, qlen, 256), BF16),
            jax.ShapeDtypeStruct((width, total), BF16),
            jax.ShapeDtypeStruct((rows, ff), BF16),
            jax.ShapeDtypeStruct((rows, ff), F32),
            jax.ShapeDtypeStruct((pairs, qlen, 128), F32),
            jax.ShapeDtypeStruct((rows, width), F32),
            jax.ShapeDtypeStruct((rows, width), F32),
        ],
        in_specs=[VMEM] * 15,
        out_specs=[VMEM] * 4 + [HBM] * 13,
        scratch_shapes=[
            vmem(16, 128),
            vmem(n, 16, 128),
            vmem(width, 3 * half),
            vmem(total, width),
            vmem(width, total),
            vmem(pairs, total, 256),
            vmem(pairs, total, 128),
            vmem(heads, qlen, 256),
            wide,
            wide,
            wide,
            wide,
            vmem(nc, rows, half),
            vmem(width, width),
            vmem(width, ff),
            vmem(rows, ff),
            pltpu.VMEM((rows, ff), F32),
            pltpu.VMEM((1, ff), F32),
            pltpu.VMEM((pairs, qlen, 128), F32),
            pltpu.VMEM((rows, width), F32),
            pltpu.VMEM((rows, width), F32),
            pltpu.SemaphoreType.DMA((count, 4)),
            pltpu.SemaphoreType.DMA((count, nd * nb)),
            pltpu.SemaphoreType.DMA((count, nb)),
            pltpu.SemaphoreType.DMA((count,)),
            pltpu.SemaphoreType.DMA((4,)),
            pltpu.SemaphoreType.DMA((7 + 2 * len(chunks),)),
            pltpu.SemaphoreType.DMA((2,)),
        ],
        compiler_params=params(58, 2),
    )(*vectors, many, w_qkv, tok, w_out, w_in, w_down, seg)


BACK = {
    "d": (0, ((64, 49, 47, 42), (50, 25, 21, 18), (26, 15, 14, 13), (27, 11, 8, 7))),
    "i": (0, ((104, 97, 90, 72), (79, 76, 62, 45), (68, 54, 41, 29), (69, 55, 43, 24))),
    "o": (0, ((100, 73, 67, 66), (59, 58, 53, 52), (37, 35, 33, 31), (38, 36, 34, 32))),
    "q": (0, ((103, 99, 95, 94), (98, 93, 88, 85), (91, 86, 82, 81), (92, 87, 83, 80))),
    "t": (0, ((101, 77, 70, 57),)),
    "work": (0, 1, 2, 3, 4, 5, 6, 9, 10, 12, 16, 17, 19, 20, 22, 23, 28, 30, 39, 40, 44, 46, 48, 51, 56, 60, 61, 63, 65, 71, 74, 78, 75, 75.1, 84, 89, 96, 96.1, 102),
}


def back_time(nd, nb, kind, what, e=0):
    if (nd, nb) == (4, 4) and (kind != "work" or e == len(BACK["work"])):
        row = BACK[kind]
        if kind == "work":
            return row[what]
        return row[0] if what == "start" else row[1][what][e]
    if kind == "work":
        return 20 + 10 * what + (100 if what > e - 10 else 0)
    first = {"d": 0, "i": 10, "o": 20, "t": 300, "q": 400}[kind]
    if what == "start":
        return first
    return first + 30 - 5 * what.bit_length() + (nb - 1 - e)


def back(
    ctx, cot, vecs, lse, scale_one, normed, unit_one, exact_in, w_out, w_in, w_down, act_in, slope_in,
    tok_t_in, w_qkv, kaug_in, v_in, qaug_in, nd, nb, nc,
):
    owners = nd * nb
    rows, width = cot.shape
    total = tok_t_in.shape[1]
    ff = w_in.shape[1]
    half, qlen = width // nc, nc * rows
    heads = half // HD
    pairs = heads // 2
    r, r_ff = width // (owners * nc), ff // (owners * nc)
    levels = nd.bit_length() - 1
    names = ["d", "i", "o", "t", "q"]
    chunks = [slice(i, i + width) for i in range(0, ff, width)]
    n_sums = 8 + -(-len(chunks) // 8) * 8

    def kernel(
        ctx_in, cot_in, vecs_in, lse_row, scale_in, normed_h, unit_h, exact_h, wo_h, wi_h, wd_h, act_h, slope_h, tok_t_h, w_h,
        kaug_h, v_h, qaug_h,
        out, g_tok, g_qkv, g_out, g_in, g_down, g_small,
        d_own, i_own, o_own, d_sib, i_sib, o_sib, t_sib, q_sib, d_x, i_x, o_x, q_x, d_z, i_z, o_z, t_z, q_z,
        q_out, resid, gctx, gctx_all, grad_q, normed_in, unit_in, exact, value, got,
        load_sem, swap_sem, s3, sib_sem, x_sem, z_sem, sum_send, sum_recv,
    ):
        net = Net(nd, nb, nc)
        c, other = net.c, nc - 1 - net.c
        piece, held = {}, {}
        for p, (name, own, sib, xbuf, zbuf, result) in enumerate(
            [
                ("d", d_own, d_sib, d_x, d_z, g_down),
                ("i", i_own, i_sib, i_x, i_z, g_in),
                ("o", o_own, o_sib, o_x, o_z, g_out),
                ("t", None, t_sib, None, t_z, g_tok),
                ("q", None, q_sib, q_x, q_z, q_out),
            ]
        ):
            sems = [s3.at[p, i] for i in range(3)] + [sib_sem.at[p], x_sem.at[p], z_sem.at[p]]
            landing = lambda at, sib=sib: sib.at[at]
            span = lambda k, sib=sib: sib.at[pl.ds(0, k)]
            extra = ()
            if name == "t":
                place = lambda at: held["t"].at[at, c]
                parts = lambda at: [(None, [held["t"].at[at, c], t_sib.at[at]])]
                theirs = lambda at: held["t"].at[at, other]
                extra = (resid,)
            elif name == "q":
                place = lambda at: held["q_full"].at[at]
                parts = lambda at: [(c, [held["q"].at[at, c]]), (other, [q_sib.at[at]])]
                theirs = lambda at: held["q"].at[at, other]
            else:
                place = lambda at, own=own: own.at[at]
                parts = lambda at, own=own, sib=sib: [(None, [own.at[at], sib.at[at]])]
                theirs = lambda at, name=name: held[name].at[at]
            piece[name] = Scatter(
                net, parts, place, theirs, landing, span, xbuf, zbuf, result, sems, name == "t", extra, name in "dio", name in "oq"
            )
        whole = AllSum(net, value, got, sum_send, sum_recv)
        swap = remote(gctx.at[other], gctx_all.at[c], swap_sem.at[0], swap_sem.at[1], net.sibling)
        st = {}

        def split(name, at, first, second):
            mine = c == 0
            own = {"d": d_own, "i": i_own, "o": o_own}[name]
            own[at] = jnp.where(mine, first, second).astype(BF16)
            held[name][at] = jnp.where(mine, second, first).astype(BF16)

        def split_rows(name, d, grad, per):
            for a in range(nb):
                at = 2 * a * per
                split(name, d * nb + a, grad[at:at + per], grad[at + per:at + 2 * per])
            piece[name].start_home(d)

        def feed_forward_steps(w_o, w_i, w_d, act, slope, pre_grad, norm_t, ctx_t, d_out, i_out, o_out):
            held.update(d=d_out, i=i_out, o=o_out)
            loads = [
                pltpu.make_async_copy(src, dst, load_sem.at[i])
                for i, (src, dst) in enumerate(
                    [
                        (act_h, act), (wd_h, w_d), (normed_h, normed_in), (slope_h, slope), (wi_h, w_i), (unit_h, unit_in),
                        (wo_h, w_o), (exact_h, exact),
                    ]
                )
            ]
            for load in loads:
                load.start()
            gain_one, bias_down = vecs_in[3:4, :], vecs_in[5:6, :]
            gain_two, shift_two = vecs_in[6:7, :], vecs_in[7:8, :]

            def enter():
                for p in piece.values():
                    p.clear_edges()
                net.barrier()
                ctx_t[...] = jnp.transpose(jnp.concatenate([ctx_in[g] for g in range(nc)], axis=1), (1, 0))
                for load in loads[:3]:
                    load.wait()
                norm_t[...] = jnp.transpose(normed_in[...].astype(BF16), (1, 0))

            def turn():
                unit, scale = norm_parts(normed_in[...] + (dot(act[...], w_d[...]) + bias_down))
                out[...] = (unit * gain_two + shift_two).astype(BF16)
                grad_out = cot_in[...].astype(F32)
                st["two"] = norm_back(grad_out, unit, scale, gain_two)
                st["ffn"] = st["two"].astype(BF16)
                value[0] = jnp.zeros((n_sums, width), F32)
                value[0, 5:6, :] = column_sum(st["ffn"].astype(F32))
                value[0, 6:7, :] = column_sum(grad_out * unit)
                value[0, 7:8, :] = column_sum(grad_out)

            def down(mask):
                d = net.flips(mask)
                lanes = pl.ds(pl.multiple_of(d * (ff // nd), 128), ff // nd)
                split_rows("d", d, dot(act[:, lanes], st["ffn"], ((0,), (0,))), r_ff)

            def pre(i, at):
                if i == 0:
                    loads[3].wait()
                    loads[4].wait()
                grad = (dot(st["ffn"], w_d[at, :], ((1,), (1,))) * slope[:, at]).astype(BF16)
                pre_grad[:, at] = grad
                value[0, 8 + i:9 + i, :] = column_sum(grad.astype(F32))
                st["two"] = st["two"] + dot(grad, w_i[:, at], ((1,), (1,)))

            def norm_one():
                grad = st["two"]
                for load in loads[5:]:
                    load.wait()
                value[0, 3:4, :] = column_sum(grad * unit_in[...])
                value[0, 4:5, :] = column_sum(grad)
                grad = norm_back(grad, unit_in[...], scale_in[:, 0:1], gain_one)
                resid[...] = grad
                st["attn"] = grad.astype(BF16)
                value[0, 2:3, :] = column_sum(st["attn"].astype(F32))
                grad = dot(st["attn"], w_o[...], ((1,), (1,))).astype(BF16)
                for g in range(nc):
                    gctx[g] = grad[:, g * half:(g + 1) * half]
                swap.start()
                gctx_all[c] = gctx[c]

            def weight_in(mask):
                d = net.flips(mask)
                at = pl.ds(pl.multiple_of(d * (width // nd), 8), width // nd)
                split_rows("i", d, dot(norm_t[at, :], pre_grad[...]), r)

            def weight_out():
                for d in range(nd):
                    at = slice(d * (width // nd), (d + 1) * (width // nd))
                    split_rows("o", d, dot(ctx_t[at, :], st["attn"]), r)

            masks = range(nd - 1, -1, -1)
            acts = [enter, turn]
            acts += [functools.partial(down, m) for m in masks]
            acts += [functools.partial(pre, i, at) for i, at in enumerate(chunks)] + [norm_one]
            return acts + [functools.partial(weight_in, m) for m in masks] + [weight_out]

        n_ffn = 4 + len(chunks) + 2 * nd
        steps = nb * pairs
        n_work = n_ffn + 1 + steps + 4 + len(whole.stages())
        order = []
        for name in names:
            p = piece[name]
            for mask in range(p.nd):
                for e in range(nb):
                    order.append((back_time(nd, nb, name, mask, e), functools.partial(p.reduce, mask, e), None))
        for i in range(n_work):
            order.append((back_time(nd, nb, "work", i, n_work), None, i))
        order.sort(key=lambda q: q[0])
        index = [i for i, q in enumerate(order) if q[2] is not None]
        first, last = index[n_ffn + 1], index[n_ffn + steps]

        def run(entries, acts, base):
            for _, act, i in entries:
                (act if i is None else acts[i - base])()

        def feed_forward_scope(*refs):
            run(order[:index[n_ffn - 1] + 1], feed_forward_steps(*refs), 0)
            for name in "dio":
                piece[name].sent()

        def attention_scope(tok_t, w_v, kaug, v_scr, qaug, do_m, delta_row, dq_scr, dkv, t_part, q_part, q_full):
            held.update(t=t_part, q=q_part, q_full=q_full)
            loads = [(qaug_h, qaug)]
            for k in range(3):
                lanes = pl.ds(pl.multiple_of((k * nc + c) * half, 128), half)
                loads.append((w_h.at[:, lanes], w_v.at[:, pl.ds(k * half, half)]))
            loads.append((tok_t_h, tok_t))
            loads = [pltpu.make_async_copy(src, dst, load_sem.at[8 + i]) for i, (src, dst) in enumerate(loads)]

            def block_loads(blk):
                at = pl.ds(pl.multiple_of(blk * qlen, qlen), qlen)
                return [
                    pltpu.make_async_copy(kaug_h.at[:, at], kaug.at[:, at], load_sem.at[13 + blk]),
                    pltpu.make_async_copy(v_h.at[:, at], v_scr.at[:, at], load_sem.at[13 + nb + blk]),
                ]

            loads[0].start()
            for e in range(nb - 1, -1, -1):
                for copy in block_loads(net.near(e)):
                    copy.start()
            for copy in loads[1:]:
                copy.start()

            def prepare():
                swap.wait()
                lane = lambda p: slice(p * 128, (p + 1) * 128)
                prepare_backward(
                    lambda p: jnp.concatenate([gctx_all[g, :, lane(p)] for g in range(nc)], axis=0), exact, do_m, delta_row
                )
                for copy in loads:
                    copy.wait()

            def token_grad(blk):
                at = pl.ds(pl.multiple_of(blk * qlen, qlen), qlen)
                return dot(dkv[at, :], w_v[:, half:3 * half], ((1,), (1,)))

            def put_tokens(blk, grad):
                for g in range(nc):
                    t_part[blk, g] = grad[g * rows:(g + 1) * rows].astype(BF16)
                piece["t"].send(blk, blk)

            def weights():
                grad_q[...] = jnp.concatenate([join_dq(dq_scr, p) for p in range(pairs)], axis=1)
                mine = pl.ds(pl.multiple_of(net.b * qlen, qlen), qlen)
                for k in range(3):
                    if k:
                        grad = dot(tok_t[...], dkv[:, (k - 1) * half:k * half])
                    else:
                        grad = dot(tok_t[:, mine], grad_q[...])
                    for at in range(owners):
                        for g in range(nc):
                            i = at * nc + g
                            q_part[at, g, :, k * half:(k + 1) * half] = grad[i * r:(i + 1) * r].astype(BF16)

            def own_tokens():
                put_tokens(net.b, token_grad(net.b) + dot(grad_q[...], w_v[:, 0:half], ((1,), (1,))))

            def small_sums():
                lanes = pl.ds(pl.multiple_of(c * half, 128), half)
                value[0, 0:1, lanes] = column_sum(grad_q[...].astype(F32))
                value[0, 1:2, lanes] = column_sum(dkv[:, half:2 * half].astype(F32))

            acts = [prepare] + [None] * steps + [weights, piece["q"].start, own_tokens, small_sums] + whole.stages()
            run(order[index[n_ffn - 1] + 1:first], acts, n_ffn)
            beside = {}
            for _, act, i in order[first:last + 1]:
                if i is not None:
                    at_step = i - n_ffn - 1
                else:
                    beside.setdefault(at_step, []).append(act)

            def attention(i, carry):
                pair = i % pairs
                blk = net.near_at(nb - 1 - i // pairs)
                at = pl.ds(pl.multiple_of(blk * qlen, qlen), qlen)

                @pl.when(pair == 0)
                def _():
                    for copy in block_loads(blk):
                        copy.wait()

                def put(dk, dv):
                    dkv[at, pl.ds(pl.multiple_of(pair * 128, 128), 128)] = dk.astype(BF16)
                    dkv[at, pl.ds(pl.multiple_of(half + pair * 128, 128), 128)] = dv.astype(BF16)

                bwd_pair(pair, qaug, kaug[pair, at, :], v_scr[pair, at, :], do_m, lse_row, delta_row, dq_scr, put, i < pairs)

                @pl.when((pair == pairs - 1) & (i < steps - 1))
                def _():
                    put_tokens(blk, token_grad(blk))

                for g, acts in beside.items():

                    @pl.when(i == g)
                    def _(acts=acts):
                        for act in acts:
                            act()

                return carry

            lax.fori_loop(0, steps, attention, 0)
            run(order[last + 1:], acts, n_ffn)
            for k in range(3):
                for g in range(nc):
                    lanes = slice((k * nc + g) * half, (k * nc + g + 1) * half)
                    g_qkv[:, lanes] = q_out[g, :, k * half:(k + 1) * half]
            me = (net.d * nb + net.b) * nc + c
            feature = lax.broadcasted_iota(jnp.int32, (width, 128), 0)
            lane = lax.broadcasted_iota(jnp.int32, (width, 128), 1)
            pick = jnp.where((feature == me * r + lane) & (lane < r), 1.0, 0.0).astype(F32)
            in_row, in_lane = (me * r_ff) // width, (me * r_ff) % width
            pick_in = jnp.where((feature == in_lane + lane) & (lane < r_ff), 1.0, 0.0).astype(F32)
            exactly = dict(precision=lax.Precision.HIGHEST, preferred_element_type=F32)
            g_small[0:8, :] = jnp.dot(value[0, 0:8, :], pick, **exactly)
            found = jnp.dot(value[0, 8:16, :], pick_in, **exactly)
            row = lax.broadcasted_iota(jnp.int32, found.shape, 0)
            g_small[8:16, :] = jnp.broadcast_to(column_sum(jnp.where(row == in_row, found, 0.0)), (8, 128))
            for name in names:
                piece[name].drain()

        pl.run_scoped(feed_forward_scope, *scopes[0])
        pl.run_scoped(attention_scope, *scopes[1])

    block = {"d": (r_ff, width), "i": (r, ff), "o": (r, width), "t": (rows, width)}
    joined = (nc, r, 3 * half)
    vmem = lambda shape, kind=BF16: pltpu.VMEM(shape, kind)
    held_out = [vmem((owners,) + block[k]) for k in "dio"]
    scopes = (
        [
            vmem((width, width)),
            vmem((width, ff)),
            vmem((ff, width)),
            vmem((rows, ff)),
            vmem((rows, ff), F32),
            vmem((rows, ff)),
            vmem((width, rows)),
            vmem((width, rows)),
        ]
        + held_out,
        [
            vmem((width, total)),
            vmem((width, 3 * half)),
            vmem((pairs, total, 256)),
            vmem((pairs, total, 128)),
            vmem((heads, qlen, 256)),
            vmem((heads, qlen, 128)),
            vmem((heads, 8, qlen), F32),
            vmem((heads, 128, qlen), F32),
            vmem((total, 2 * half)),
            vmem((nb, nc, rows, width)),
            vmem((owners,) + joined),
            vmem((owners,) + joined),
        ],
    )
    scratch = [vmem((owners,) + block[k]) for k in "dio"] + [vmem((owners,) + block[k]) for k in "dio"]
    scratch += [vmem((nb,) + block["t"]), vmem((owners, r, 3 * half))]
    scratch += [vmem(((nd - 1) * nb,) + block[k]) for k in "dio"] + [vmem(((nd - 1) * nb,) + joined)]
    scratch += [vmem((nb + 1,) + block[k]) for k in "diot"] + [vmem((nb + 1,) + joined)]
    scratch += [
        vmem(joined, F32),
        vmem((rows, width), F32),
        vmem((nc, rows, half)),
        vmem((nc, rows, half)),
        vmem((qlen, half)),
        vmem((rows, width), F32),
        vmem((rows, width), F32),
        vmem((pairs, qlen, 128), F32),
        vmem((levels + 2, n_sums, width), F32),
        vmem((levels + nb, n_sums, width), F32),
        pltpu.SemaphoreType.DMA((13 + 2 * nb,)),
        pltpu.SemaphoreType.DMA((2,)),
    ]
    scratch += scatter_sems(5, nd, nb) + [pltpu.SemaphoreType.DMA((levels + nb,))] * 2
    return pl.pallas_call(
        kernel,
        out_shape=[
            jax.ShapeDtypeStruct((rows, width), BF16),
            jax.ShapeDtypeStruct((rows, width), F32),
            jax.ShapeDtypeStruct((r, 3 * width), F32),
            jax.ShapeDtypeStruct((r, width), F32),
            jax.ShapeDtypeStruct((r, ff), F32),
            jax.ShapeDtypeStruct((r_ff, width), F32),
            jax.ShapeDtypeStruct((16, 128), F32),
        ],
        in_specs=[VMEM] * 5 + [HBM] * 13,
        out_specs=[VMEM] * 7,
        scratch_shapes=scratch,
        compiler_params=params(62, 3),
    )(
        ctx, cot, vecs, lse, scale_one, normed, unit_one, exact_in, w_out, w_in, w_down, act_in, slope_in,
        tok_t_in, w_qkv, kaug_in, v_in, qaug_in,
    )


def body(
    tokens,
    segment,
    w_qkv,
    bias_query,
    bias_value,
    w_out,
    bias_out,
    gain_attn,
    shift_attn,
    w_in,
    bias_in,
    w_down,
    bias_down,
    gain_ffn,
    shift_ffn,
    cotangent,
):
    nd, nb, nc = lax.axis_size("dp"), lax.axis_size("blk"), lax.axis_size("head")
    n_dev = nd * nb * nc
    d_idx, b_idx, c_idx = lax.axis_index("dp"), lax.axis_index("blk"), lax.axis_index("head")
    me = (d_idx * nb + b_idx) * nc + c_idx
    seqs, rows, width = tokens.shape
    ff = w_in.shape[1]
    half_w = width // nc
    qlen = nc * rows
    r = w_qkv.shape[0]
    r_ff = w_down.shape[0]
    flat_in = tokens.reshape(rows, width)
    cot = cotangent.reshape(rows, width)
    vectors = [bias_query, bias_value, bias_out, gain_attn, shift_attn, bias_down, gain_ffn, shift_ffn]
    if nb * qlen <= 2048 and r % 8 == 0 and ff // width <= 8:
        (
            ctx2, vecs, lse, scale_one,
            f_qkv, f_out, f_in, f_down, kaug, v_all, qaug, tok_t, act, slope, exact, normed, unit_one,
        ) = front([v[None, :] for v in vectors], bias_in[None, :], w_qkv, flat_in, w_out, w_in, w_down, segment, nd, nb, nc)
        out, g_tok, o_qkv, o_out, o_in, o_down, g_small = back(
            ctx2, cot, vecs, lse, scale_one, normed, unit_one, exact, f_out, f_in, f_down, act, slope,
            tok_t, f_qkv, kaug, v_all, qaug, nd, nb, nc,
        )
        out, g_tok, o_qkv, o_out, o_in, o_down, g_bq, g_bv, g_bo, g_g1, g_s1, g_bd, g_g2, g_s2, g_bin = hand_out(
            [out, g_tok, o_qkv, o_out, o_in, o_down], g_small, r, r_ff
        )
        return (
            out.reshape(seqs, rows, width), g_tok.reshape(seqs, rows, width),
            o_qkv, g_bq, g_bv, o_out, g_bo, g_g1, g_s1, o_in, g_bin, o_down, g_bd, g_g2, g_s2,
        )
    packed = jnp.concatenate(vectors + [bias_in])
    used = packed.shape[0]
    lanes = -(-used // 128) * 128
    packed = jnp.broadcast_to(jnp.pad(packed, (0, lanes - used))[None], (8, lanes))
    n4 = 4
    parts = [flat_in[i * (rows // n4):(i + 1) * (rows // n4)] for i in range(n4)]
    shards = [packed, w_qkv] + parts + [w_out, w_in, w_down]
    narrow = [False, False] + [True] * n4 + [False] * 3
    keys = [(-1, 3, 3), (0, 3, 3), (7, 9, 0), (10, 9, 0), (13, 9, 0), (16, 9, 0), (2, 4, 4), (9, 6, 5), (22, 6, 5)]
    small, g_qkv, t0, t1, t2, t3, g_out, g_in, g_down = gather_all(shards, narrow, keys, nd, nb, nc)
    full_small = small[:, 0, :used]
    vecs = full_small[:, :8 * r].reshape(n_dev, 8, r).transpose(1, 0, 2).reshape(8, width).astype(F32)
    full_bin = full_small[:, 8 * r:].reshape(ff).astype(F32)
    bq, bv, bout, gain_one, shift_one, bdown, gain_two, shift_two = (vecs[i] for i in range(8))
    full_qkv = g_qkv.reshape(width, 3 * width)
    full_wout = g_out.reshape(width, width)
    full_win = g_in.reshape(width, ff)
    full_wdown = g_down.reshape(ff, width)
    tok_all = jnp.stack([t0, t1, t2, t3], axis=1).reshape(nb * qlen, width)
    my_bias = lax.dynamic_slice(vecs, (0, c_idx * half_w), (2, half_w))
    ctx, kaug, v_scr, qaug, lse, exact = attend_forward(tok_all, full_qkv, my_bias, segment, qlen, half_w)
    context_low = ctx.reshape(seqs, qlen, 1, half_w)
    back_tokens = lax.all_to_all(context_low, "head", split_axis=1, concat_axis=2, tiled=True)
    ctx2 = back_tokens.reshape(rows, nc, half_w).transpose(1, 0, 2)
    out, grad_resid_one, gctx2, dw_down, dw_in, dw_out, sums = feed_forward(
        ctx2, flat_in, cot, vecs, full_bin.reshape(1, ff), full_wout, full_win, full_wdown
    )
    output = out.reshape(seqs, rows, width)
    grad_context = gctx2.transpose(1, 0, 2)
    grad_headed = lax.all_to_all(
        grad_context.reshape(seqs, rows, nc, half_w), "head", split_axis=2, concat_axis=1, tiled=True
    )
    gctx = grad_headed.reshape(qlen, half_w)
    tok_mine = lax.dynamic_slice(tok_all, (b_idx * qlen, 0), (qlen, width))
    dtok, dw, dbias = attend_backward(tok_all, tok_mine, full_qkv, qaug, kaug, v_scr, lse, exact, gctx)
    dw = dw.astype(BF16).reshape(nd * nb, nc, r, 3 * half_w)
    ours = lax.dynamic_index_in_dim(dw, c_idx, 1, keepdims=False)
    theirs = lax.dynamic_index_in_dim(dw, 1 - c_idx, 1, keepdims=False)
    joined_full = jnp.stack([ours, ours], axis=1)
    sums = lax.dynamic_update_slice(sums, dbias, (0, c_idx * half_w))
    o_down, o_in, o_out, o_tok, o_qkv, total = scatter_all(
        [
            dw_down.reshape(n_dev, r_ff, width),
            dw_in.reshape(n_dev, r, ff),
            dw_out.reshape(n_dev, r, width),
            dtok.reshape(nb * nc, rows, width),
            (joined_full, theirs),
        ],
        [False, False, False, True, False],
        [False, False, False, False, True],
        sums,
        nd,
        nb,
        nc,
    )
    grad_tokens = (grad_resid_one + o_tok).reshape(seqs, rows, width)
    o_qkv = o_qkv.reshape(2, r, 3, half_w).transpose(1, 2, 0, 3).reshape(r, 3 * width)
    mine = lax.dynamic_slice(total, (0, me * r), (8, r))
    mine_in = lax.dynamic_slice(total[8:8 + ff // width].reshape(ff), (me * r_ff,), (r_ff,))
    g_bq, g_bv, g_bo, g_g1, g_s1, g_bd, g_g2, g_s2 = (mine[i] for i in range(8))
    return (
        output,
        grad_tokens,
        o_qkv,
        g_bq,
        g_bv,
        o_out,
        g_bo,
        g_g1,
        g_s1,
        o_in,
        mine_in,
        o_down,
        g_bd,
        g_g2,
        g_s2,
    )


def solution(mesh):
    weight, vector = P(("dp", "blk", "head"), None), P(("dp", "blk", "head"))
    token = P("dp", ("blk", "head"), None)
    return jax.shard_map(
        body,
        mesh=mesh,
        in_specs=(
            token,
            P("dp", None),
            weight,
            vector,
            vector,
            weight,
            vector,
            vector,
            vector,
            weight,
            vector,
            weight,
            vector,
            vector,
            vector,
            token,
        ),
        out_specs=(
            token,
            token,
            weight,
            vector,
            vector,
            weight,
            vector,
            vector,
            vector,
            weight,
            vector,
            weight,
            vector,
            vector,
            vector,
        ),
        check_vma=False,
    )
```

```python
import functools

import jax
import jax.numpy as jnp
from jax import lax
from jax.experimental import pallas as pl
from jax.experimental.pallas import tpu as pltpu
from jax.sharding import PartitionSpec as P

MESH = pl.DeviceIdType.MESH
F32, BF16 = jnp.float32, jnp.bfloat16
HD = 64
HEADS = 12
BIG = 2.0**30

class Net:
    def __init__(self, nd, nb, nc):
        self.nd, self.nb, self.nc = nd, nb, nc
        self.levels = nd.bit_length() - 1
        self.d, self.b, self.c = (lax.axis_index(a) for a in ("dp", "blk", "head"))
        top = self.levels - 1
        self.stride = [(1 - self.c) * 2**k + self.c * 2 ** (top - k) for k in range(self.levels)]
        self.sibling = (self.d, self.b, self.nc - 1 - self.c)
        steps = [s * (1 - 2 * ((self.d // s) % 2)) for s in self.stride]
        self.flipped = [self.d]
        for step in steps:
            self.flipped += [d + step for d in self.flipped]
        self.nearest = [self.find_near(e) for e in range(self.nb)]

    def flips(self, mask):
        return self.flipped[mask]

    def across(self, k):
        return (self.flipped[1 << k], self.b, self.c)

    def near(self, e):
        return self.nearest[e]

    def find_near(self, e):
        order = [sorted(range(self.nb), key=lambda j: (abs(j - i), -j)) for i in range(self.nb)]
        got = order[0][e]
        for i in range(1, self.nb):
            got = jnp.where(self.b == i, order[i][e], got)
        return got

    def near_at(self, e):
        got = self.near(0)
        for i in range(1, self.nb):
            got = jnp.where(e == i, self.near(i), got)
        return got

    def slot(self, mask, blk):
        return (self.flips(mask) * self.nb + blk) * self.nc + self.c

    def peers(self):
        out = [(self.d, (self.b + u) % self.nb, self.c) for u in range(1, self.nb)]
        out += [self.across(k) for k in range(self.levels)]
        return out + [self.sibling]

    def greet(self):
        bar = pltpu.get_barrier_semaphore()
        for p in self.peers():
            pl.semaphore_signal(bar, inc=1, device_id=p, device_id_type=MESH)

    def meet(self):
        pl.semaphore_wait(pltpu.get_barrier_semaphore(), len(self.peers()))

    def barrier(self):
        self.greet()
        self.meet()


def remote(src, dst, send, recv, dev):
    return pltpu.make_async_remote_copy(src_ref=src, dst_ref=dst, send_sem=send, recv_sem=recv, device_id=dev, device_id_type=MESH)


def blocks_of(full):
    return (lambda i: full.at[i]), (lambda k: full.at[pl.ds(0, k)])


def rows_of(full, rows, offset=0, stride=None):
    every = rows if stride is None else stride

    def place(i):
        return full.at[pl.ds(pl.multiple_of(i * every + offset, 8), rows)]

    return place, (lambda k: full.at[pl.ds(0, k * rows)])


class Gather:
    def __init__(self, net, mine, place, span, sems, narrow=False, direct=False):
        self.net, self.mine, self.place, self.span, self.narrow, self.direct = net, mine, place, span, narrow, direct
        self.zsend, self.xsend, self.ssend, self.srecv, self.recv = sems

    def at(self, mask, blk):
        n = self.net
        if self.narrow:
            return self.place(blk * n.nc + n.c)
        return self.place(n.slot(mask, blk))

    def rsem(self, mask, blk):
        return self.recv.at[mask * self.net.nb + blk]

    def spread(self, mask, blk, src, dst):
        n = self.net
        if not self.narrow:
            for k in range(n.levels):
                if mask < (1 << k):
                    remote(src, dst, self.xsend, self.rsem(mask + (1 << k), blk), n.across(k)).start()
        arrival = self.srecv.at[blk] if self.narrow else self.srecv
        remote(src, dst, self.ssend, arrival, n.sibling).start()

    def along(self, blk, src, dst):
        n = self.net
        sem = self.rsem(0, blk)

        @pl.when((n.b < n.nb - 1) & (blk <= n.b))
        def _():
            remote(src, dst, self.zsend, sem, (n.d, n.b + 1, n.c)).start()

        @pl.when((n.b > 0) & (blk >= n.b))
        def _():
            remote(src, dst, self.zsend, sem, (n.d, n.b - 1, n.c)).start()

    def own_line(self):
        n = self.net
        dst = self.at(0, n.b)
        if not self.direct:
            self.along(n.b, self.mine, dst)
            return
        for e in range(n.nb - 1, 0, -1):
            remote(self.mine, dst, self.zsend, self.rsem(0, n.b), (n.d, n.near(e), n.c)).start()

    def own_spread(self):
        self.spread(0, self.net.b, self.mine, self.at(0, self.net.b))

    def z(self, e):
        blk = self.net.near(e)
        dst = self.at(0, blk)
        pltpu.make_async_copy(dst, dst, self.rsem(0, blk)).wait()
        if not self.direct:
            self.along(blk, dst, dst)
        self.spread(0, blk, dst, dst)

    def x(self, mask, e):
        n = self.net
        blk = n.near(e)
        dst = self.at(mask, blk)
        pltpu.make_async_copy(dst, dst, self.rsem(mask, blk)).wait()
        self.spread(mask, blk, dst, dst)

    def own(self, sem):
        n = self.net
        return pltpu.make_async_copy(self.mine, self.at(0, n.b), sem)

    def wait_sibling_block(self, blk):
        one = self.span(1)
        pltpu.make_async_copy(one, one, self.srecv.at[blk]).wait()

    def wait_sibling(self):
        n = self.net
        if self.narrow:
            for blk in range(n.nb):
                self.wait_sibling_block(blk)
            return
        half = self.span(n.nd * n.nb)
        pltpu.make_async_copy(half, half, self.srecv).wait()

    def drain(self):
        n = self.net
        half = self.span(n.nb if self.narrow else n.nd * n.nb)
        pltpu.make_async_copy(half, half, self.ssend).wait()
        if not self.narrow:
            part = self.span((n.nd - 1) * n.nb)
            pltpu.make_async_copy(part, part, self.xsend).wait()
        if self.direct:
            sent = self.span(n.nb - 1)
            pltpu.make_async_copy(sent, sent, self.zsend).wait()
            return
        edge = (n.b == 0) | (n.b == n.nb - 1)

        @pl.when(edge)
        def _():
            one = self.span(1)
            pltpu.make_async_copy(one, one, self.zsend).wait()

        @pl.when(jnp.logical_not(edge))
        def _():
            many = self.span(n.nb + 1)
            pltpu.make_async_copy(many, many, self.zsend).wait()


def gather_refs(four, recv, block, p, narrow):
    last = block.at[p] if narrow else four.at[p, 3]
    return [four.at[p, 0], four.at[p, 1], four.at[p, 2], last, recv.at[p]]


def gather_sems(n_pieces, nd, nb):
    return [pltpu.SemaphoreType.DMA((n_pieces, 4)), pltpu.SemaphoreType.DMA((n_pieces, nd * nb)), pltpu.SemaphoreType.DMA]


class Scatter:
    def __init__(self, net, parts, place, theirs, landing, span, xrecv, zrecv, out, sems, narrow=False, extra=(), early=False, direct=False):
        self.net, self.parts, self.place, self.theirs, self.landing = net, parts, place, theirs, landing
        self.span, self.xbuf, self.zbuf, self.out, self.extra = span, xrecv, zrecv, out, extra
        self.sib_send, self.x_send, self.z_send, self.sib_sem, self.x_sem, self.z_sem = sems
        self.narrow, self.seen, self.early, self.direct = narrow, set(), early, direct
        self.nd = 1 if narrow else net.nd
        self.levels = 0 if narrow else net.levels

    def home(self, mask):
        return 0 if self.narrow else self.net.flips(mask)

    def start(self):
        for mask in range(self.nd - 1, -1, -1):
            self.start_home(self.home(mask))

    def start_home(self, d):
        for blk in range(self.net.nb):
            self.send(d * self.net.nb + blk, d)

    def send(self, at, sem):
        remote(self.theirs(at), self.landing(at), self.sib_send, self.sib_sem.at[sem], self.net.sibling).start()

    def arrived(self, sem, count):
        some = self.span(count)
        pltpu.make_async_copy(some, some, self.sib_sem.at[sem]).wait()

    def sent(self):
        some = self.span(self.nd * self.net.nb)
        pltpu.make_async_copy(some, some, self.sib_send).wait()

    def x_at(self, k, mask, blk):
        return ((1 << k) - 1 + mask) * self.net.nb + blk

    def z_at(self, side, blk, owner):
        return blk + side * jnp.where(blk == owner, self.net.nb - blk, 0)

    def add(self, at, more, to, extra=()):
        for pick, places in self.parts(at):
            def chosen(ref):
                return ref if pick is None else ref.at[pick]

            add_up(places + [chosen(m) for m in more] + list(extra), chosen(to))

    def reduce(self, mask, e):
        n = self.net
        blk = n.near(e)
        if self.narrow:
            self.arrived(blk, 1)
        elif mask not in self.seen:
            self.seen.add(mask)
            self.arrived(self.home(mask), n.nb)
        at = self.home(mask) * n.nb + blk
        place = self.place(at)
        more = []
        for k in range(self.levels - 1, -1, -1):
            if mask < (1 << k):
                i = self.x_at(k, mask, blk)
                got = self.xbuf.at[i]
                pltpu.make_async_copy(got, got, self.x_sem.at[i]).wait()
                more.append(got)
        if mask:
            k = mask.bit_length() - 1
            self.add(at, more, place)
            i = self.x_at(k, mask - (1 << k), blk)
            remote(place, self.xbuf.at[i], self.x_send, self.x_sem.at[i], n.across(k)).start()
            return

        if self.direct:
            if e:
                self.add(at, more, place)
                remote(place, self.zbuf.at[n.b], self.z_send, self.z_sem.at[n.b], (n.d, blk, n.c)).start()
                return
            for u in range(1, n.nb):
                got = self.zbuf.at[n.near(u)]
                pltpu.make_async_copy(got, got, self.z_sem.at[n.near(u)]).wait()
                more.append(got)
            self.add(at, more, self.out, self.extra)
            return

        def line(side, there):
            i = self.z_at(side, blk, n.b)
            got = self.zbuf.at[i]

            @pl.when(there)
            def _():
                pltpu.make_async_copy(got, got, self.z_sem.at[i]).wait()

            more.append(got)

        if e == 0:
            line(0, n.b > 0)
            line(1, n.b < n.nb - 1)
            self.add(at, more, self.out, self.extra)
            return
        side = jnp.where(blk > n.b, 0, 1)
        line(side, jnp.where(blk > n.b, n.b, n.nb - 1 - n.b) > 0)
        self.add(at, more, place)
        to = n.b + 1 - 2 * side
        i = self.z_at(side, blk, to)
        remote(place, self.zbuf.at[i], self.z_send, self.z_sem.at[i], (n.d, to, n.c)).start()

    def clear_edges(self):
        n = self.net
        if self.direct:
            return

        def clear(i, carry):
            self.zbuf[i] = jnp.zeros(self.zbuf.shape[1:], self.zbuf.dtype)
            return carry

        @pl.when(n.b == 0)
        def _():
            lax.fori_loop(0, n.nb, clear, 0)

        @pl.when(n.b == n.nb - 1)
        def _():
            lax.fori_loop(0, n.nb - 1, clear, 0)
            clear(n.nb, 0)

    def drain(self):
        n = self.net
        if not self.early:
            self.sent()
        if not self.narrow:
            some = self.xbuf.at[pl.ds(0, (n.nd - 1) * n.nb)]
            pltpu.make_async_copy(some, some, self.x_send).wait()
        some = self.zbuf.at[pl.ds(0, n.nb - 1)]
        pltpu.make_async_copy(some, some, self.z_send).wait()


def add_up(terms, to):
    shape = to.shape
    rows = shape[-2]
    step = rows
    while step % 2 == 0 and step > 32:
        step //= 2
    lead = [()] if len(shape) == 2 else [(g,) for g in range(shape[0])]
    for g in lead:
        for r in range(0, rows, step):
            at = g + (slice(r, r + step),)
            total = terms[0][at].astype(F32)
            for t in terms[1:]:
                total = total + t[at].astype(F32)
            to[at] = total.astype(to.dtype)


class AllSum:
    def __init__(self, net, value, got, send, recv):
        self.net, self.value, self.got, self.send, self.recv = net, value, got, send, recv

    def copy(self, stage, dev, src, slot):
        return remote(self.value.at[src], self.got.at[slot], self.send.at[slot], self.recv.at[slot], dev)

    def stages(self):
        n = self.net
        devs = [n.sibling] + [n.across(k) for k in range(n.levels)]
        steps = []
        for i, dev in enumerate(devs):
            steps.append(functools.partial(self.one, i, dev))
        steps.append(self.line_start)
        steps.append(self.line_end)
        return [lambda: self.copy(0, devs[0], 0, 0).start()] + steps

    def one(self, i, dev):
        n = self.net
        self.copy(i, dev, i, i).wait()
        self.value[i + 1] = self.value[i] + self.got[i]
        if i + 1 <= n.levels:
            self.copy(i + 1, n.across(i), i + 1, i + 1).start()

    def line_copy(self, u):
        n = self.net
        return self.copy(None, (n.d, (n.b + u) % n.nb, n.c), n.levels + 1, n.levels + u)

    def line_start(self):
        for u in range(1, self.net.nb):
            self.line_copy(u).start()

    def line_end(self):
        n = self.net
        for u in range(1, n.nb):
            self.line_copy(u).wait()
        total = self.value[n.levels + 1]
        for u in range(1, n.nb):
            total = total + self.got[n.levels + u]
        self.value[0] = total


def scatter_sems(n_pieces, nd, nb):
    return [
        pltpu.SemaphoreType.DMA((n_pieces, 3)),
        pltpu.SemaphoreType.DMA((n_pieces, max(nd, nb))),
        pltpu.SemaphoreType.DMA((n_pieces, (nd - 1) * nb)),
        pltpu.SemaphoreType.DMA((n_pieces, nb + 1)),
    ]


def dot(a, b, dims=((1,), (0,))):
    return lax.dot_general(a, b, (dims, ((), ())), preferred_element_type=F32)


def mask_lanes(seg_row, count):
    lanes = lax.broadcasted_iota(jnp.int32, (128, count), 0)
    return jnp.transpose(jnp.where(lanes == seg_row, -1.0, 0.0).astype(F32), (1, 0))


def project_keys(i, step, tok, wk, wv, bias_v, seg, kaug, v_scr):
    at = pl.ds(pl.multiple_of(i * step, step), step)
    piece = tok[at, :]
    keys = dot(piece, wk).astype(BF16)
    vals = (dot(piece, wv) + bias_v).astype(BF16)
    lanes = mask_lanes(seg[:, at], step).astype(BF16)
    for p in range(kaug.shape[0]):
        kaug[p, at, 0:128] = keys[:, p * 128:(p + 1) * 128]
        kaug[p, at, 128:256] = lanes
        v_scr[p, at, :] = vals[:, p * 128:(p + 1) * 128]


def project_queries(tok, wq, bias_q, seg, qaug, blk, qlen):
    mine = pl.ds(pl.multiple_of(blk * qlen, qlen), qlen)
    query = (dot(tok[mine, :], wq) + bias_q).astype(BF16)
    lane = lax.broadcasted_iota(jnp.int32, (qlen, 128), 1)
    feat = jnp.where(lane < 8, BIG * (1.0 + mask_lanes(seg[:, mine], qlen)), 0.0).astype(BF16)
    for p in range(qaug.shape[0] // 2):
        q_pair = query[:, p * 128:(p + 1) * 128].astype(F32) * HD**-0.5
        for half in range(2):
            keep = (lane >= 64) if half else (lane < 64)
            qaug[2 * p + half, :, 0:128] = jnp.where(keep, q_pair, 0.0).astype(BF16)
            qaug[2 * p + half, :, 128:256] = feat


def attend_chunk(i, qaug, kaug, v_scr, o_scr, exact_scr, lse_scr, chunk, per_head):
    h = i // per_head
    at = pl.ds(pl.multiple_of((i % per_head) * chunk, chunk), chunk)
    s = dot(qaug[h, at, :], kaug[h // 2], ((1,), (1,)))
    top = jnp.max(s, axis=-1, keepdims=True)
    p = jnp.exp(s - top)
    total = jnp.sum(p, axis=-1, keepdims=True)
    low = p.astype(BF16)
    rest = (p - low.astype(F32)).astype(BF16)
    value = v_scr[h // 2]
    o = dot(low, value)
    inverse = 1.0 / total
    o_scr[h, at, :] = o * inverse
    exact_scr[h, at, :] = (o + dot(rest, value)) * inverse
    lse_scr[h, at, :] = jnp.broadcast_to(top + jnp.log(total), (chunk, 128))


def attend_block(h, at, qaug, kaug, v_scr, top_scr, sum_scr, o_scr, rest_scr):
    s = dot(qaug[h], kaug[h // 2, at, :], ((1,), (1,)))
    before = top_scr[h]
    top = jnp.maximum(before, jnp.broadcast_to(jnp.max(s, axis=-1, keepdims=True), before.shape))
    p = jnp.exp(s - jnp.concatenate([top] * (s.shape[1] // 128), axis=1))
    fade = jnp.exp(before - top)
    low = p.astype(BF16)
    rest = (p - low.astype(F32)).astype(BF16)
    value = v_scr[h // 2, at, :]
    top_scr[h] = top
    sum_scr[h] = sum_scr[h] * fade + jnp.broadcast_to(jnp.sum(p, axis=-1, keepdims=True), before.shape)
    o_scr[h] = o_scr[h] * fade + dot(low, value)
    rest_scr[h] = rest_scr[h] * fade + dot(rest, value)


def close_blocks(top_scr, sum_scr, o_scr, rest_scr):
    for h in range(o_scr.shape[0]):
        total = sum_scr[h]
        inverse = 1.0 / total
        o = o_scr[h]
        rest_scr[h] = (o + rest_scr[h]) * inverse
        o_scr[h] = o * inverse
        top_scr[h] = top_scr[h] + jnp.log(total)


def join_heads(scr, p, at=slice(None)):
    first, second = scr[2 * p, at, :], scr[2 * p + 1, at, :]
    lane = lax.broadcasted_iota(jnp.int32, first.shape, 1)
    return jnp.where(lane < 64, first, second)


def head_columns(w, part, c, width):
    return w[:, pl.ds(pl.multiple_of((part * 2 + c) * width, 128), width)]


def fwd_kernel(tok, w, bias, seg, ctx, kaug, v_scr, qaug, lse_out, exact, lse_scr, o_scr, exact_scr, chunk=256):
    blk, c = lax.axis_index("blk"), lax.axis_index("head")
    qlen, width = ctx.shape
    total = tok.shape[0]
    step = min(512, total)
    wk, wv = head_columns(w, 1, c, width), head_columns(w, 2, c, width)

    def rows(i, carry):
        project_keys(i, step, tok, wk, wv, bias[1:2, :], seg, kaug, v_scr)
        return carry

    lax.fori_loop(0, total // step, rows, 0)
    project_queries(tok, head_columns(w, 0, c, width), bias[0:1, :], seg, qaug, blk, qlen)
    per_head = qlen // chunk

    def go(i, carry):
        attend_chunk(i, qaug, kaug, v_scr, o_scr, exact_scr, lse_scr, chunk, per_head)
        return carry

    lax.fori_loop(0, (width // HD) * per_head, go, 0)
    finish_forward(o_scr, exact_scr, lse_scr, lambda p, v: store_lanes(ctx, p, v), lse_out, exact)


def store_lanes(ref, p, value):
    ref[:, p * 128:(p + 1) * 128] = value


def finish_forward(o_scr, exact_scr, lse_scr, put, lse_out, exact):
    for p in range(o_scr.shape[0] // 2):
        put(p, join_heads(o_scr, p).astype(BF16))
        exact[p] = join_heads(exact_scr, p)
    for h in range(o_scr.shape[0]):
        lse_out[h] = jnp.transpose(lse_scr[h], (1, 0))[0:8, :]


def prepare_backward(gctx_of, exact, do_m, delta_row):
    pairs, qlen, _ = exact.shape
    lane = lax.broadcasted_iota(jnp.int32, (qlen, 128), 1)
    for p in range(pairs):
        grad = gctx_of(p)
        product = grad.astype(F32) * exact[p]
        for half in range(2):
            keep = (lane >= 64) if half else (lane < 64)
            do_m[2 * p + half] = jnp.where(keep, grad, jnp.zeros_like(grad))
            across = jnp.transpose(jnp.where(keep, product, 0.0), (1, 0))
            delta_row[2 * p + half] = jnp.broadcast_to(jnp.sum(across, axis=0, keepdims=True), (8, qlen))


def bwd_pair(pair, qaug, k_part, v_part, do_m, lse_row, delta_row, dq_scr, put, first, qs=slice(None)):
    dk = dv = None
    for half in range(2):
        h = 2 * pair + half
        q_part, do_part = qaug[h, qs, :], do_m[h, qs, :]
        s = dot(k_part, q_part, ((1,), (1,)))
        p = jnp.exp(s - lse_row[h, 0:1, qs])
        dp = dot(v_part, do_part, ((1,), (1,)))
        ds = (p * (dp - delta_row[h, 0:1, qs])).astype(BF16)
        v_term = dot(p.astype(BF16), do_part)
        k_term = dot(ds, q_part[:, 0:128])
        dv = v_term if dv is None else dv + v_term
        dk = k_term if dk is None else dk + k_term
        dq = dot(k_part[:, 0:128], ds, ((0,), (0,)))
        if first is True:
            dq_scr[h, :, qs] = dq
        elif first is None:
            dq_scr[h, :, qs] += dq
        else:
            dq_scr[h, :, qs] = jnp.where(first, dq, dq_scr[h, :, qs] + dq)
    put(dk, dv)


def join_dq(dq_scr, p):
    qlen = dq_scr.shape[2]
    lane = lax.broadcasted_iota(jnp.int32, (qlen, 128), 1)
    first, second = jnp.transpose(dq_scr[2 * p], (1, 0)), jnp.transpose(dq_scr[2 * p + 1], (1, 0))
    return (jnp.where(lane < 64, first, second) * HD**-0.5).astype(BF16)


VMEM = pl.BlockSpec(memory_space=pltpu.VMEM)
HBM = pl.BlockSpec(memory_space=pltpu.HBM)


def params(limit, collective=None):
    more = {} if collective is None else dict(collective_id=collective, has_side_effects=True)
    return pltpu.CompilerParams(vmem_limit_bytes=limit << 20, **more)


def lane_mean(x):
    return jnp.mean(x, axis=-1, keepdims=True)


def norm_parts(hidden):
    centered = hidden - lane_mean(hidden)
    scale = lax.rsqrt(lane_mean(centered * centered) + 1e-12)
    return centered * scale, scale


def norm_back(grad, unit, scale, gain):
    scaled = grad * gain
    return scale * (scaled - lane_mean(scaled) - unit * lane_mean(scaled * unit))


def gelu_and_slope(pre):
    cdf = 0.5 * (1.0 + lax.erf(pre * 0.7071067811865476))
    return pre * cdf, cdf + pre * (0.3989422804014327 * jnp.exp(-0.5 * pre * pre))


def column_sum(x):
    return jnp.sum(x, axis=0, keepdims=True)


def ffn_kernel(
    ctx, tok, cot, vecs, bias_in, w_out_h, w_in_h, w_down_h,
    out, resid_grad, gctx, dw_down_h, dw_in_h, dw_out_h, sums,
    w_out, w_in, w_down, act, slope, dw_a, dw_b, dw_c, in_sem, out_sem,
):
    groups, rows, half = ctx.shape
    width, ff = w_in.shape
    step = width
    loads = [
        pltpu.make_async_copy(src, dst, in_sem.at[i])
        for i, (src, dst) in enumerate([(w_out_h, w_out), (w_in_h, w_in), (w_down_h, w_down)])
    ]
    for load in loads:
        load.start()
    bias_out, gain_one, shift_one = vecs[2:3, :], vecs[3:4, :], vecs[4:5, :]
    bias_down, gain_two, shift_two = vecs[5:6, :], vecs[6:7, :], vecs[7:8, :]
    context = jnp.concatenate([ctx[g] for g in range(groups)], axis=1)
    loads[0].wait()
    resid_one = tok[...].astype(F32) + (dot(context, w_out[...]) + bias_out)
    unit_one, scale_one = norm_parts(resid_one)
    normed = unit_one * gain_one + shift_one
    normed_low = normed.astype(BF16)
    loads[1].wait()
    chunks = [slice(i, i + step) for i in range(0, ff, step)]
    for at in chunks:
        pre = dot(normed_low, w_in[:, at]) + bias_in[0:1, at]
        value, grad = gelu_and_slope(pre)
        act[:, at] = value.astype(BF16)
        slope[:, at] = grad
    loads[2].wait()
    resid_two = normed + (dot(act[...], w_down[...]) + bias_down)
    unit_two, scale_two = norm_parts(resid_two)
    out[...] = (unit_two * gain_two + shift_two).astype(BF16)
    grad_out = cot[...].astype(F32)
    grad_two = norm_back(grad_out, unit_two, scale_two, gain_two)
    grad_ffn = grad_two.astype(BF16)
    sums[0:2, :] = jnp.zeros((2, width), F32)
    sums[5:6, :] = column_sum(grad_ffn.astype(F32))
    sums[6:7, :] = column_sum(grad_out * unit_two)
    sums[7:8, :] = column_sum(grad_out)
    stores = []

    def store(src, dst):
        copy = pltpu.make_async_copy(src, dst, out_sem.at[len(stores)])
        copy.start()
        stores.append(copy)

    for at in chunks:
        dw_a[at, :] = dot(act[:, at], grad_ffn, ((0,), (0,))).astype(BF16)
        store(dw_a.at[at], dw_down_h.at[at])
    grad_normed = grad_two
    for i, at in enumerate(chunks):
        grad_act = dot(grad_ffn, w_down[at, :], ((1,), (1,)))
        grad_pre = (grad_act * slope[:, at]).astype(BF16)
        sums[8 + i:9 + i, :] = column_sum(grad_pre.astype(F32))
        dw_b[:, at] = dot(normed_low, grad_pre, ((0,), (0,))).astype(BF16)
        grad_normed = grad_normed + dot(grad_pre, w_in[:, at], ((1,), (1,)))
    store(dw_b, dw_in_h)
    sums[8 + len(chunks):, :] = jnp.zeros((sums.shape[0] - 8 - len(chunks), width), F32)
    sums[3:4, :] = column_sum(grad_normed * unit_one)
    sums[4:5, :] = column_sum(grad_normed)
    grad_one = norm_back(grad_normed, unit_one, scale_one, gain_one)
    resid_grad[...] = grad_one
    grad_attn = grad_one.astype(BF16)
    sums[2:3, :] = column_sum(grad_attn.astype(F32))
    dw_c[...] = dot(context, grad_attn, ((0,), (0,))).astype(BF16)
    store(dw_c, dw_out_h)
    grad_context = dot(grad_attn, w_out[...], ((1,), (1,))).astype(BF16)
    for g in range(groups):
        gctx[g] = grad_context[:, g * half:(g + 1) * half]
    for copy in stores:
        copy.wait()


def feed_forward(ctx, tok, cot, vecs, bias_in, w_out, w_in, w_down):
    groups, rows, half = ctx.shape
    width, ff = w_in.shape
    n_sums = 8 + -(-(ff // width) // 8) * 8
    return pl.pallas_call(
        ffn_kernel,
        out_shape=[
            jax.ShapeDtypeStruct((rows, width), BF16),
            jax.ShapeDtypeStruct((rows, width), F32),
            jax.ShapeDtypeStruct((groups, rows, half), BF16),
            jax.ShapeDtypeStruct((ff, width), BF16),
            jax.ShapeDtypeStruct((width, ff), BF16),
            jax.ShapeDtypeStruct((width, width), BF16),
            jax.ShapeDtypeStruct((n_sums, width), F32),
        ],
        in_specs=[VMEM] * 5 + [HBM] * 3,
        out_specs=[VMEM] * 3 + [HBM] * 3 + [VMEM],
        scratch_shapes=[
            pltpu.VMEM((width, width), BF16),
            pltpu.VMEM((width, ff), BF16),
            pltpu.VMEM((ff, width), BF16),
            pltpu.VMEM((rows, ff), BF16),
            pltpu.VMEM((rows, ff), F32),
            pltpu.VMEM((ff, width), BF16),
            pltpu.VMEM((width, ff), BF16),
            pltpu.VMEM((width, width), BF16),
            pltpu.SemaphoreType.DMA((3,)),
            pltpu.SemaphoreType.DMA((ff // width + 2,)),
        ],
        compiler_params=params(56),
    )(ctx, tok, cot, vecs, bias_in, w_out, w_in, w_down)


def gather_order(keys, narrow, nd, nb):
    events = []
    for p, (begin, dz, dx) in enumerate(keys):
        for e in range(nb):
            events.append((begin + e * dz, ("z", p, e)))
            if not narrow[p]:
                for mask in range(1, nd):
                    events.append((begin + e * dz + dx * mask.bit_length(), ("x", p, mask, e)))
    events.sort(key=lambda q: q[0])
    return [ev for _, ev in events]


def gather_all(shards, narrow, keys, nd, nb, nc):
    count = len(shards)

    def kernel(*refs):
        mine, full = refs[:count], refs[count:2 * count]
        four, recv, own_sem, block_sem = refs[2 * count:]
        net = Net(nd, nb, nc)
        pieces = [
            Gather(net, mine[p], *blocks_of(full[p]), gather_refs(four, recv, block_sem, p, narrow[p]), narrow[p]) for p in range(count)
        ]
        net.barrier()
        for ev in gather_order(keys, narrow, nd, nb):
            if ev[0] == "z" and ev[2] == 0:
                pieces[ev[1]].own_line()
                pieces[ev[1]].own_spread()
            elif ev[0] == "z":
                pieces[ev[1]].z(ev[2])
            else:
                pieces[ev[1]].x(ev[2], ev[3])
        for piece in pieces:
            own = piece.own(own_sem)
            own.start()
            own.wait()
        for piece in pieces:
            piece.wait_sibling()
        for piece in pieces:
            piece.drain()

    outs = [
        jax.ShapeDtypeStruct(((nb * nc if thin else nd * nb * nc),) + s.shape, s.dtype) for s, thin in zip(shards, narrow)
    ]
    return pl.pallas_call(
        kernel,
        out_shape=outs,
        in_specs=[VMEM] * count,
        out_specs=[HBM] * count,
        scratch_shapes=gather_sems(count, nd, nb) + [pltpu.SemaphoreType.DMA((count, nb))],
        compiler_params=params(56, 0),
    )(*shards)


def attend_forward(tok, w, bias, seg, qlen, width):
    total = tok.shape[0]
    heads = width // HD
    chunk = min(256, qlen)
    while chunk * total > 256 * 4096:
        chunk //= 2
    return pl.pallas_call(
        functools.partial(fwd_kernel, chunk=chunk),
        out_shape=[
            jax.ShapeDtypeStruct((qlen, width), BF16),
            jax.ShapeDtypeStruct((width // 128, total, 256), BF16),
            jax.ShapeDtypeStruct((width // 128, total, 128), BF16),
            jax.ShapeDtypeStruct((heads, qlen, 256), BF16),
            jax.ShapeDtypeStruct((heads, 8, qlen), F32),
            jax.ShapeDtypeStruct((heads // 2, qlen, 128), F32),
        ],
        in_specs=[VMEM] * 4,
        out_specs=[VMEM] * 6,
        scratch_shapes=[pltpu.VMEM((heads, qlen, 128), F32)] * 3,
        compiler_params=params(58),
    )(tok, w, bias, seg)


def pair_bwd_kernel(qaug, kaug, v_scr, lse, exact, gctx, dk, dv, dq, do_m, delta_row, dq_scr):
    step = pl.program_id(1)

    @pl.when(step == 0)
    def _():
        prepare_backward(lambda p: gctx[...], exact, do_m, delta_row)

    def put(k_term, v_term):
        dk[...] = k_term.astype(BF16)
        dv[...] = v_term.astype(BF16)

    bwd_pair(0, qaug, kaug[0], v_scr[0], do_m, lse, delta_row, dq_scr, put, step == 0)

    @pl.when(step == pl.num_programs(1) - 1)
    def _():
        dq[...] = join_dq(dq_scr, 0)


def finish_kernel(tok, dk, dv, tok_mine, dq, w, dtok, dw, dbias, own):
    i, c = pl.program_id(0), lax.axis_index("head")
    blk = lax.axis_index("blk")
    step, width = dk.shape
    qlen = dq.shape[0]

    def cols(part):
        return w[:, pl.ds(pl.multiple_of((part * 2 + c) * width, 128), width)]

    piece, grad_k, grad_v = tok[...], dk[...], dv[...]

    @pl.when(i == 0)
    def _():
        dw[:, 0:width] = dot(tok_mine[...], dq[...], ((0,), (0,)))
        dw[:, width:3 * width] = jnp.zeros((dw.shape[0], 2 * width), F32)
        dbias[0:1, :] = jnp.sum(dq[...].astype(F32), axis=0, keepdims=True)
        dbias[1:2, :] = jnp.zeros((1, width), F32)
        own[...] = dot(dq[...], cols(0), ((1,), (1,)))

    dw[:, width:2 * width] += dot(piece, grad_k, ((0,), (0,)))
    dw[:, 2 * width:3 * width] += dot(piece, grad_v, ((0,), (0,)))
    dbias[1:2, :] += jnp.sum(grad_v.astype(F32), axis=0, keepdims=True)
    grad = dot(grad_k, cols(1), ((1,), (1,))) + dot(grad_v, cols(2), ((1,), (1,)))
    per = qlen // step
    mine = i // per == blk
    at = pl.ds(pl.multiple_of((i % per) * step, step), step)
    dtok[...] = (grad + jnp.where(mine, own[at, :], 0.0)).astype(BF16)


def attend_backward(tok, tok_mine, w, qaug, kaug, v_scr, lse, exact, gctx):
    heads, qlen, _ = qaug.shape
    total, d_model = tok.shape
    width = heads * HD
    kc = min(512, total)
    dk, dv, dq = pl.pallas_call(
        pair_bwd_kernel,
        grid=(heads // 2, total // kc),
        out_shape=[
            jax.ShapeDtypeStruct((total, width), BF16),
            jax.ShapeDtypeStruct((total, width), BF16),
            jax.ShapeDtypeStruct((qlen, width), BF16),
        ],
        in_specs=[
            pl.BlockSpec((2, qlen, 256), lambda p, j: (p, 0, 0)),
            pl.BlockSpec((1, kc, 256), lambda p, j: (p, j, 0)),
            pl.BlockSpec((1, kc, 128), lambda p, j: (p, j, 0)),
            pl.BlockSpec((2, 8, qlen), lambda p, j: (p, 0, 0)),
            pl.BlockSpec((1, qlen, 128), lambda p, j: (p, 0, 0)),
            pl.BlockSpec((qlen, 128), lambda p, j: (0, p)),
        ],
        out_specs=[pl.BlockSpec((kc, 128), lambda p, j: (j, p))] * 2 + [pl.BlockSpec((qlen, 128), lambda p, j: (0, p))],
        scratch_shapes=[
            pltpu.VMEM((2, qlen, 128), BF16),
            pltpu.VMEM((2, 8, qlen), F32),
            pltpu.VMEM((2, 128, qlen), F32),
        ],
        compiler_params=params(56),
    )(qaug, kaug, v_scr, lse, exact, gctx)
    step = min(512, qlen)
    whole = lambda i: (0, 0)
    rows = lambda i: (i, 0)
    return pl.pallas_call(
        finish_kernel,
        grid=(total // step,),
        out_shape=[
            jax.ShapeDtypeStruct((total, d_model), BF16),
            jax.ShapeDtypeStruct((d_model, 3 * width), F32),
            jax.ShapeDtypeStruct((2, width), F32),
        ],
        in_specs=[
            pl.BlockSpec((step, d_model), rows),
            pl.BlockSpec((step, width), rows),
            pl.BlockSpec((step, width), rows),
            pl.BlockSpec((qlen, d_model), whole),
            pl.BlockSpec((qlen, width), whole),
            pl.BlockSpec((d_model, w.shape[1]), whole),
        ],
        out_specs=[
            pl.BlockSpec((step, d_model), rows),
            pl.BlockSpec((d_model, 3 * width), whole),
            pl.BlockSpec((2, width), whole),
        ],
        scratch_shapes=[pltpu.VMEM((qlen, d_model), F32)],
        compiler_params=params(56),
    )(tok, dk, dv, tok_mine, dq, w)


SPACE = (0.25, 1.0, 0.2)


def send_blocks(piece, nb):
    for blk in range(nb):
        piece.send(blk, blk)


def scatter_all(arrays, narrow, joined, small, nd, nb, nc):
    count = len(arrays)
    flat = []
    for a, j in zip(arrays, joined):
        flat += list(a) if j else [a]
    n_in = len(flat) + 1

    def kernel(*refs):
        ins, small_in = list(refs[:n_in - 1]), refs[n_in - 1]
        outs, small_out = refs[n_in:n_in + count], refs[n_in + count]
        rest = list(refs[n_in + count + 1:])
        net = Net(nd, nb, nc)
        s3, sib_sem, x_sem, z_sem, sum_send, sum_recv = rest[-6:]
        value, got = rest[-8:-6]
        bufs = rest[:-8]
        pieces = []
        for p in range(count):
            first = ins.pop(0)
            sib = ins.pop(0) if joined[p] else bufs.pop(0)
            xbuf = None if narrow[p] else bufs.pop(0)
            zbuf = bufs.pop(0)
            sems = [s3.at[p, i] for i in range(3)] + [sib_sem.at[p], x_sem.at[p], z_sem.at[p]]
            if joined[p]:
                parts = lambda at, first=first: [(None, [first.at[at]])]
                place = lambda at, first=first: first.at[at]
                theirs = lambda at, sib=sib: sib.at[at]
                landing = lambda at, first=first: first.at[at, net.c]
            else:
                place = lambda at, first=first: first.at[at * nc + net.c]
                parts = lambda at, place=place, sib=sib: [(None, [place(at), sib.at[at]])]
                theirs = lambda at, first=first: first.at[at * nc + nc - 1 - net.c]
                landing = lambda at, sib=sib: sib.at[at]
            span = lambda k, sib=sib: sib.at[pl.ds(0, k)]
            pieces.append(Scatter(net, parts, place, theirs, landing, span, xbuf, zbuf, outs[p], sems, narrow[p]))
        sums = AllSum(net, value, got, sum_send, sum_recv)
        for piece in pieces:
            piece.clear_edges()
        value[0] = small_in[...]
        net.barrier()
        events = []
        for p, piece in enumerate(pieces):
            t = SPACE[0] * p
            begin = functools.partial(send_blocks, piece, nb) if narrow[p] else piece.start
            events.append((t - 0.4, begin))
            for mask in range(piece.nd - 1, -1, -1):
                for e in range(nb - 1, -1, -1):
                    when = t + SPACE[1] * (piece.levels - mask.bit_length()) + SPACE[2] * (nb - 1 - e)
                    events.append((when, functools.partial(piece.reduce, mask, e)))
        for i, s in enumerate(sums.stages()):
            events.append((0.3 * i, s))
        events.sort(key=lambda q: q[0])
        for _, ev in events:
            ev()
        small_out[...] = value[0]
        for piece in pieces:
            piece.drain()

    outs, scratch = [], []
    for a, thin, j in zip(arrays, narrow, joined):
        full = a[0] if j else a
        block = full.shape[1:]
        outs.append(jax.ShapeDtypeStruct(block, F32))
        n_dp = 1 if thin else nd
        if not j:
            scratch.append(pltpu.VMEM((n_dp * nb,) + block, BF16))
        if not thin:
            scratch.append(pltpu.VMEM(((nd - 1) * nb,) + block, BF16))
        scratch.append(pltpu.VMEM((nb + 1,) + block, BF16))
    levels = nd.bit_length() - 1
    scratch += [pltpu.VMEM((levels + 2,) + small.shape, F32), pltpu.VMEM((levels + nb,) + small.shape, F32)]
    scratch += scatter_sems(count, nd, nb)
    scratch += [pltpu.SemaphoreType.DMA((levels + nb,))] * 2
    outs.append(jax.ShapeDtypeStruct(small.shape, F32))
    return pl.pallas_call(
        kernel,
        out_shape=outs,
        in_specs=[VMEM] * n_in,
        out_specs=[VMEM] * (count + 1),
        scratch_shapes=scratch,
        compiler_params=params(60, 1),
    )(*flat, small)


def hand_out(arrays, small, r, r_ff):
    count = len(arrays)

    def kernel(*refs):
        ins, small_in = refs[:count], refs[count]
        outs, vectors, sems = refs[count + 1:2 * count + 1], refs[2 * count + 1:-1], refs[-1]
        copies = [pltpu.make_async_copy(a, b, sems.at[i]) for i, (a, b) in enumerate(zip(ins, outs))]
        for copy in copies:
            copy.start()
        for i, out in enumerate(vectors):
            out[...] = small_in[i, 0:out.shape[0]]
        for copy in copies:
            copy.wait()

    sizes = [r] * 8 + [r_ff]
    return pl.pallas_call(
        kernel,
        out_shape=[jax.ShapeDtypeStruct(a.shape, a.dtype) for a in arrays] + [jax.ShapeDtypeStruct((s,), F32) for s in sizes],
        in_specs=[VMEM] * (count + 1),
        out_specs=[HBM] * count + [VMEM] * 9,
        scratch_shapes=[pltpu.SemaphoreType.DMA((count,))],
        compiler_params=params(60),
    )(*arrays, small)


def unpack_vectors(small, vecs, bias_in, r, r_ff):
    n = small.shape[0]
    width, ff = vecs.shape[1], bias_in.shape[1]

    def gathered(rows, per, count):
        lane = lax.broadcasted_iota(jnp.int32, (8, 128), 1)
        tiles = [jnp.zeros((8, 128), F32) for _ in range(count // 128)]
        for i in range(n):
            piece = small[i, rows, :].astype(F32)
            shift, tile = per * i % 128, per * i // 128
            if shift:
                piece = pltpu.roll(piece, shift, 1)
            if shift + per <= 128:
                tiles[tile] = tiles[tile] + piece
            else:
                tiles[tile] = tiles[tile] + jnp.where(lane >= shift, piece, 0.0)
                tiles[tile + 1] = tiles[tile + 1] + jnp.where(lane < shift, piece, 0.0)
        return tiles

    for t, tile in enumerate(gathered(slice(0, 8), r, width)):
        vecs[:, t * 128:(t + 1) * 128] = tile
    for t, tile in enumerate(gathered(slice(8, 16), r_ff, ff)):
        bias_in[:, t * 128:(t + 1) * 128] = tile[0:1, :]


FRONT = {
    "small": (2, 22, ((2, 6, 15, 24), (27, 12, 39, 37), (35, 13, 29, 38), (47, 23, 46, 43))),
    "q": (3, 20, ((3, 10, 14, 25), (30, 16, 28, 40), (34, 17, 44, 45), (41, 32, 42, 50))),
    "t0": (26, 36, ((26, 54, 71, 99),)),
    "t1": (4, 8, ((4, 18, 49, 78),)),
    "o": (0, 89, ((0, 5, 21, 48), (102, 60, 51, 72), (105, 11, 33, 61), (110, 73, 82, 86))),
    "i": (31, 55, ((31, 53, 64, 84), (69, 62, 91, 103), (70, 65, 81, 100), (88, 83, 104, 121))),
    "d": (52, 1, ((52, 74, 93, 107), (9, 92, 111, 120), (7, 96, 113, 119), (19, 112, 122, 125))),
    "work": (56, 57, 58, 59, 63, 66, 67, 68, 75, 76, 77, 79, 80, 85, 87, 90, 94, 95, 97, 98, 101, 106, 108, 109, 114, 115, 116, 117, 118, 123, 124, 126, 127, 128),
}


def front_time(nd, nb, kind, what, e=0):
    if (nd, nb) == (4, 4) and (kind != "work" or e == len(FRONT["work"])):
        row = FRONT[kind]
        if kind == "work":
            return row[what]
        if what == "line":
            return row[0]
        if what == "spread":
            return row[1]
        return row[2][what][e]
    first = ["small", "q", "t0", "t1", "o", "i", "d"].index(kind) * 10 if kind != "work" else 0
    if kind == "work":
        return (40 if what == 0 else 200) + what
    if what in ("line", "spread"):
        return first
    return first + 3 * e + (4 * what.bit_length() if what else 0)


DIRECT = ()


def front(vectors, many, w_qkv, tok, w_out, w_in, w_down, seg, nd, nb, nc):
    n = nd * nb * nc
    rows, width = tok.shape
    half, qlen, total = width // nc, nc * rows, nb * nc * rows
    heads = half // HD
    pairs = heads // 2
    r, r_ff, ff = w_qkv.shape[0], w_down.shape[0], w_in.shape[1]
    parts = 2
    part = rows // parts
    steps = nb * heads
    chunks = [slice(i, i + width) for i in range(0, ff, width)]

    def kernel(
        *refs,
    ):
        few_in, many_in = refs[:8], refs[8]
        inside(few_in, many_in, *refs[9:])

    def inside(
        few_in, many_in, q_in, tok_in, o_in, i_in, d_in, seg_in,
        ctx2, vecs, lse_out, scale_one,
        q_h, o_h, i_h, d_h, kaug_h, v_h, qaug_h, tok_t_h, act_h, slope_h, exact_h, normed_h, unit_h,
        small_in, small_all, w_v, tok_v, tok_t, kaug, v_scr, qaug, top_scr, sum_scr, o_scr, rest_scr, ctx_loc,
        w_o, w_i, act, slope, bias_in, exact, normed, unit_one,
        four, recv, block_sem, own_sem, load_sem, save_sem, swap_sem,
    ):
        net = Net(nd, nb, nc)
        c = net.c
        net.greet()
        small_in[...] = jnp.zeros((16, 128), BF16)
        few_row = lax.broadcasted_iota(jnp.int32, (16, r), 0)
        few = jnp.zeros((16, r), BF16)
        for i, ref in enumerate(few_in):
            few = jnp.where(few_row == i, jnp.broadcast_to(ref[...], (16, r)), few)
        small_in[:, 0:r] = few
        row = lax.broadcasted_iota(jnp.int32, (16, r_ff), 0)
        small_in[:, 0:r_ff] = jnp.where(row == 8, jnp.broadcast_to(many_in[...], (16, r_ff)), small_in[:, 0:r_ff])
        specs = [("small", small_in, blocks_of(small_all), False), ("q", q_in, rows_of(q_h, r), False)]
        for i in range(parts):
            mine = tok_in.at[pl.ds(i * part, part)]
            specs.append(("t" + str(i), mine, rows_of(tok_v, part, i * part, rows), True))
        specs += [("o", o_in, rows_of(o_h, r), False), ("i", i_in, rows_of(i_h, r), False), ("d", d_in, rows_of(d_h, r_ff), False)]
        piece, own = {}, {}
        for p, (name, mine, (place, span), narrow) in enumerate(specs):
            piece[name] = Gather(net, mine, place, span, gather_refs(four, recv, block_sem, p, narrow), narrow, name in DIRECT)
            own[name] = piece[name].own(own_sem.at[p])
        tokens = ["t" + str(i) for i in range(parts)]
        for name in piece:
            own[name].start()
        net.meet()
        lanes = pl.ds(pl.multiple_of(c * half, 128), half)

        def whole(name):
            piece[name].wait_sibling()
            own[name].wait()

        def unpack():
            whole("small")
            unpack_vectors(small_all, vecs, bias_in, r, r_ff)

        def load():
            whole("q")
            copies = []
            for k in range(3):
                at = pl.ds(pl.multiple_of((k * nc + c) * half, 128), half)
                copies.append(pltpu.make_async_copy(q_h.at[:, at], w_v.at[:, pl.ds(k * half, half)], load_sem.at[k]))
            for copy in copies:
                copy.start()
            for copy in copies:
                copy.wait()

        def queries():
            for name in tokens:
                own[name].wait()
                piece[name].wait_sibling_block(net.b)
            project_queries(tok_v, w_v[:, 0:half], vecs[0:1, lanes], seg_in, qaug, net.b, qlen)
            for scr, start in ((top_scr, -3e38), (sum_scr, 0.0), (o_scr, 0.0), (rest_scr, 0.0)):
                scr[...] = jnp.full(scr.shape, start, F32)

        saves = [
            pltpu.make_async_copy(src, dst, save_sem.at[i])
            for i, (src, dst) in enumerate(
                [
                    (kaug, kaug_h), (v_scr, v_h), (qaug, qaug_h), (tok_t, tok_t_h),
                    (exact, exact_h), (normed, normed_h), (unit_one, unit_h),
                ]
                + [(a.at[:, at], b.at[:, at]) for a, b in ((act, act_h), (slope, slope_h)) for at in chunks]
            )
        ]

        def turn_tokens():
            tok_t[...] = jnp.transpose(tok_v[...], (1, 0))
            for save in saves[:4]:
                save.start()

        swap = remote(ctx_loc.at[nc - 1 - c], ctx2.at[c], swap_sem.at[0], swap_sem.at[1], net.sibling)
        st = {}

        def finish():
            def put(p, value):
                for g in range(nc):
                    ctx_loc[g, :, p * 128:(p + 1) * 128] = value[g * rows:(g + 1) * rows]

            close_blocks(top_scr, sum_scr, o_scr, rest_scr)
            finish_forward(o_scr, rest_scr, top_scr, put, lse_out, exact)
            swap.start()
            saves[4].start()
            ctx2[c] = ctx_loc[c]

        def fetch(name, src, dst):
            whole(name)
            copy = pltpu.make_async_copy(src, dst, load_sem.at[3])
            copy.start()
            copy.wait()

        def first_norm():
            fetch("o", o_h, w_o)
            swap.wait()
            context = jnp.concatenate([ctx2[g] for g in range(nc)], axis=1)
            resid = tok_in[...].astype(F32) + (dot(context, w_o[...]) + vecs[2:3, :])
            unit, scale = norm_parts(resid)
            value = unit * vecs[3:4, :] + vecs[4:5, :]
            normed[...] = value
            unit_one[...] = unit
            scale_one[...] = jnp.broadcast_to(scale, scale_one.shape)
            saves[5].start()
            saves[6].start()
            st["low"] = value.astype(BF16)

        def expand(i, at):
            if i == 0:
                fetch("i", i_h, w_i)
            pre = dot(st["low"], w_i[:, at]) + bias_in[0:1, at]
            result, grad = gelu_and_slope(pre)
            act[:, at] = result.astype(BF16)
            slope[:, at] = grad
            saves[7 + i].start()
            saves[7 + len(chunks) + i].start()

        order = []
        for name in piece:
            order.append((front_time(nd, nb, name, "line"), piece[name].own_line, None))
            order.append((front_time(nd, nb, name, "spread"), piece[name].own_spread, None))
            for e in range(1, nb):
                order.append((front_time(nd, nb, name, 0, e), functools.partial(piece[name].z, e), None))
            for mask in range(1, 1 if name in tokens else nd):
                for e in range(nb):
                    order.append((front_time(nd, nb, name, mask, e), functools.partial(piece[name].x, mask, e), None))
        work = [unpack, load, queries] + [None] * steps + [turn_tokens, finish, first_norm]
        work += [functools.partial(expand, i, at) for i, at in enumerate(chunks)]
        for i, act_now in enumerate(work):
            order.append((front_time(nd, nb, "work", i, len(work)), act_now, i - 3 if act_now is None else None))
        order.sort(key=lambda q: q[0])
        begin = next(i for i, q in enumerate(order) if q[2] == 0)
        end = next(i for i, q in enumerate(order) if q[2] == steps - 1)
        for _, act_now, _ in order[:begin]:
            act_now()
        beside = {}
        for _, act_now, i in order[begin:end + 1]:
            if act_now is None:
                at_step = i
            else:
                beside.setdefault(at_step, []).append(act_now)

        def attention(e, h, carry):
            blk = net.near(e)
            at = pl.ds(pl.multiple_of(blk * qlen, qlen), qlen)
            attend_block(h, at, qaug, kaug, v_scr, top_scr, sum_scr, o_scr, rest_scr)
            for g in range(heads):
                acts = beside.get(e * heads + g, ())
                if acts:

                    @pl.when(h == g)
                    def _(acts=acts):
                        for act_now in acts:
                            act_now()

            return carry

        for e in range(nb):
            blk = net.near(e)
            if e:
                for name in tokens:
                    piece[name].wait_sibling_block(blk)
            project_keys(blk, qlen, tok_v, w_v[:, half:2 * half], w_v[:, 2 * half:3 * half], vecs[1:2, lanes], seg_in, kaug, v_scr)
            lax.fori_loop(0, heads, functools.partial(attention, e), 0)
        for _, act_now, _ in order[end + 1:]:
            act_now()
        whole("d")
        for name in piece:
            piece[name].drain()
        for save in saves:
            save.wait()

    count = 5 + parts
    vmem = lambda *shape: pltpu.VMEM(shape, BF16)
    wide = pltpu.VMEM((heads, qlen, 128), F32)
    return pl.pallas_call(
        kernel,
        out_shape=[
            jax.ShapeDtypeStruct((nc, rows, half), BF16),
            jax.ShapeDtypeStruct((8, width), F32),
            jax.ShapeDtypeStruct((heads, 8, qlen), F32),
            jax.ShapeDtypeStruct((rows, 128), F32),
            jax.ShapeDtypeStruct((n * r, 3 * width), BF16),
            jax.ShapeDtypeStruct((n * r, width), BF16),
            jax.ShapeDtypeStruct((n * r, ff), BF16),
            jax.ShapeDtypeStruct((n * r_ff, width), BF16),
            jax.ShapeDtypeStruct((pairs, total, 256), BF16),
            jax.ShapeDtypeStruct((pairs, total, 128), BF16),
            jax.ShapeDtypeStruct((heads, qlen, 256), BF16),
            jax.ShapeDtypeStruct((width, total), BF16),
            jax.ShapeDtypeStruct((rows, ff), BF16),
            jax.ShapeDtypeStruct((rows, ff), F32),
            jax.ShapeDtypeStruct((pairs, qlen, 128), F32),
            jax.ShapeDtypeStruct((rows, width), F32),
            jax.ShapeDtypeStruct((rows, width), F32),
        ],
        in_specs=[VMEM] * 15,
        out_specs=[VMEM] * 4 + [HBM] * 13,
        scratch_shapes=[
            vmem(16, 128),
            vmem(n, 16, 128),
            vmem(width, 3 * half),
            vmem(total, width),
            vmem(width, total),
            vmem(pairs, total, 256),
            vmem(pairs, total, 128),
            vmem(heads, qlen, 256),
            wide,
            wide,
            wide,
            wide,
            vmem(nc, rows, half),
            vmem(width, width),
            vmem(width, ff),
            vmem(rows, ff),
            pltpu.VMEM((rows, ff), F32),
            pltpu.VMEM((1, ff), F32),
            pltpu.VMEM((pairs, qlen, 128), F32),
            pltpu.VMEM((rows, width), F32),
            pltpu.VMEM((rows, width), F32),
            pltpu.SemaphoreType.DMA((count, 4)),
            pltpu.SemaphoreType.DMA((count, nd * nb)),
            pltpu.SemaphoreType.DMA((count, nb)),
            pltpu.SemaphoreType.DMA((count,)),
            pltpu.SemaphoreType.DMA((4,)),
            pltpu.SemaphoreType.DMA((7 + 2 * len(chunks),)),
            pltpu.SemaphoreType.DMA((2,)),
        ],
        compiler_params=params(58, 2),
    )(*vectors, many, w_qkv, tok, w_out, w_in, w_down, seg)


BACK = {
    "d": (0, ((64, 49, 47, 42), (50, 25, 21, 18), (26, 15, 14, 13), (27, 11, 8, 7))),
    "i": (0, ((104, 97, 90, 72), (79, 76, 62, 45), (68, 54, 41, 29), (69, 55, 43, 24))),
    "o": (0, ((100, 73, 67, 66), (59, 58, 53, 52), (37, 35, 33, 31), (38, 36, 34, 32))),
    "q": (0, ((103, 99, 95, 94), (98, 93, 88, 85), (91, 86, 82, 81), (92, 87, 83, 80))),
    "t": (0, ((101, 77, 70, 57),)),
    "work": (0, 1, 2, 3, 4, 5, 6, 9, 10, 12, 16, 17, 19, 20, 22, 23, 28, 30, 39, 40, 44, 46, 48, 51, 56, 60, 61, 63, 65, 71, 74, 78, 75, 75.1, 84, 89, 96, 96.1, 102),
}


def back_time(nd, nb, kind, what, e=0):
    if (nd, nb) == (4, 4) and (kind != "work" or e == len(BACK["work"])):
        row = BACK[kind]
        if kind == "work":
            return row[what]
        return row[0] if what == "start" else row[1][what][e]
    if kind == "work":
        return 20 + 10 * what + (100 if what > e - 10 else 0)
    first = {"d": 0, "i": 10, "o": 20, "t": 300, "q": 400}[kind]
    if what == "start":
        return first
    return first + 30 - 5 * what.bit_length() + (nb - 1 - e)


def back(
    ctx, cot, vecs, lse, scale_one, normed, unit_one, exact_in, w_out, w_in, w_down, act_in, slope_in,
    tok_t_in, w_qkv, kaug_in, v_in, qaug_in, nd, nb, nc,
):
    owners = nd * nb
    rows, width = cot.shape
    total = tok_t_in.shape[1]
    ff = w_in.shape[1]
    half, qlen = width // nc, nc * rows
    heads = half // HD
    pairs = heads // 2
    r, r_ff = width // (owners * nc), ff // (owners * nc)
    levels = nd.bit_length() - 1
    names = ["d", "i", "o", "t", "q"]
    chunks = [slice(i, i + width) for i in range(0, ff, width)]
    n_sums = 8 + -(-len(chunks) // 8) * 8

    def kernel(
        ctx_in, cot_in, vecs_in, lse_row, scale_in, normed_h, unit_h, exact_h, wo_h, wi_h, wd_h, act_h, slope_h, tok_t_h, w_h,
        kaug_h, v_h, qaug_h,
        out, g_tok, g_qkv, g_out, g_in, g_down, g_small,
        d_own, i_own, o_own, d_sib, i_sib, o_sib, t_sib, q_sib, d_x, i_x, o_x, q_x, d_z, i_z, o_z, t_z, q_z,
        q_out, resid, gctx, gctx_all, grad_q, normed_in, unit_in, exact, value, got,
        load_sem, swap_sem, s3, sib_sem, x_sem, z_sem, sum_send, sum_recv,
    ):
        net = Net(nd, nb, nc)
        c, other = net.c, nc - 1 - net.c
        piece, held = {}, {}
        for p, (name, own, sib, xbuf, zbuf, result) in enumerate(
            [
                ("d", d_own, d_sib, d_x, d_z, g_down),
                ("i", i_own, i_sib, i_x, i_z, g_in),
                ("o", o_own, o_sib, o_x, o_z, g_out),
                ("t", None, t_sib, None, t_z, g_tok),
                ("q", None, q_sib, q_x, q_z, q_out),
            ]
        ):
            sems = [s3.at[p, i] for i in range(3)] + [sib_sem.at[p], x_sem.at[p], z_sem.at[p]]
            landing = lambda at, sib=sib: sib.at[at]
            span = lambda k, sib=sib: sib.at[pl.ds(0, k)]
            extra = ()
            if name == "t":
                place = lambda at: held["t"].at[at, c]
                parts = lambda at: [(None, [held["t"].at[at, c], t_sib.at[at]])]
                theirs = lambda at: held["t"].at[at, other]
                extra = (resid,)
            elif name == "q":
                place = lambda at: held["q_full"].at[at]
                parts = lambda at: [(c, [held["q"].at[at, c]]), (other, [q_sib.at[at]])]
                theirs = lambda at: held["q"].at[at, other]
            else:
                place = lambda at, own=own: own.at[at]
                parts = lambda at, own=own, sib=sib: [(None, [own.at[at], sib.at[at]])]
                theirs = lambda at, name=name: held[name].at[at]
            piece[name] = Scatter(
                net, parts, place, theirs, landing, span, xbuf, zbuf, result, sems, name == "t", extra, name in "dio", name in "oq"
            )
        whole = AllSum(net, value, got, sum_send, sum_recv)
        swap = remote(gctx.at[other], gctx_all.at[c], swap_sem.at[0], swap_sem.at[1], net.sibling)
        st = {}

        def split(name, at, first, second):
            mine = c == 0
            own = {"d": d_own, "i": i_own, "o": o_own}[name]
            own[at] = jnp.where(mine, first, second).astype(BF16)
            held[name][at] = jnp.where(mine, second, first).astype(BF16)

        def split_rows(name, d, grad, per):
            for a in range(nb):
                at = 2 * a * per
                split(name, d * nb + a, grad[at:at + per], grad[at + per:at + 2 * per])
            piece[name].start_home(d)

        def feed_forward_steps(w_o, w_i, w_d, act, slope, pre_grad, norm_t, ctx_t, d_out, i_out, o_out):
            held.update(d=d_out, i=i_out, o=o_out)
            loads = [
                pltpu.make_async_copy(src, dst, load_sem.at[i])
                for i, (src, dst) in enumerate(
                    [
                        (act_h, act), (wd_h, w_d), (normed_h, normed_in), (slope_h, slope), (wi_h, w_i), (unit_h, unit_in),
                        (wo_h, w_o), (exact_h, exact),
                    ]
                )
            ]
            for load in loads:
                load.start()
            gain_one, bias_down = vecs_in[3:4, :], vecs_in[5:6, :]
            gain_two, shift_two = vecs_in[6:7, :], vecs_in[7:8, :]

            def enter():
                for p in piece.values():
                    p.clear_edges()
                net.greet()
                ctx_t[...] = jnp.transpose(jnp.concatenate([ctx_in[g] for g in range(nc)], axis=1), (1, 0))
                net.meet()
                for load in loads[:3]:
                    load.wait()
                norm_t[...] = jnp.transpose(normed_in[...].astype(BF16), (1, 0))

            def turn():
                unit, scale = norm_parts(normed_in[...] + (dot(act[...], w_d[...]) + bias_down))
                out[...] = (unit * gain_two + shift_two).astype(BF16)
                grad_out = cot_in[...].astype(F32)
                st["two"] = norm_back(grad_out, unit, scale, gain_two)
                st["ffn"] = st["two"].astype(BF16)
                value[0] = jnp.zeros((n_sums, width), F32)
                value[0, 5:6, :] = column_sum(st["ffn"].astype(F32))
                value[0, 6:7, :] = column_sum(grad_out * unit)
                value[0, 7:8, :] = column_sum(grad_out)

            def down(mask):
                d = net.flips(mask)
                lanes = pl.ds(pl.multiple_of(d * (ff // nd), 128), ff // nd)
                split_rows("d", d, dot(act[:, lanes], st["ffn"], ((0,), (0,))), r_ff)

            def pre(i, at):
                if i == 0:
                    loads[3].wait()
                    loads[4].wait()
                grad = (dot(st["ffn"], w_d[at, :], ((1,), (1,))) * slope[:, at]).astype(BF16)
                pre_grad[:, at] = grad
                value[0, 8 + i:9 + i, :] = column_sum(grad.astype(F32))
                st["two"] = st["two"] + dot(grad, w_i[:, at], ((1,), (1,)))

            def norm_one():
                grad = st["two"]
                for load in loads[5:]:
                    load.wait()
                value[0, 3:4, :] = column_sum(grad * unit_in[...])
                value[0, 4:5, :] = column_sum(grad)
                grad = norm_back(grad, unit_in[...], scale_in[:, 0:1], gain_one)
                resid[...] = grad
                st["attn"] = grad.astype(BF16)
                value[0, 2:3, :] = column_sum(st["attn"].astype(F32))
                grad = dot(st["attn"], w_o[...], ((1,), (1,))).astype(BF16)
                for g in range(nc):
                    gctx[g] = grad[:, g * half:(g + 1) * half]
                swap.start()
                gctx_all[c] = gctx[c]

            def weight_in(mask):
                d = net.flips(mask)
                at = pl.ds(pl.multiple_of(d * (width // nd), 8), width // nd)
                split_rows("i", d, dot(norm_t[at, :], pre_grad[...]), r)

            def weight_out():
                for d in range(nd):
                    at = slice(d * (width // nd), (d + 1) * (width // nd))
                    split_rows("o", d, dot(ctx_t[at, :], st["attn"]), r)

            masks = range(nd - 1, -1, -1)
            acts = [enter, turn]
            acts += [functools.partial(down, m) for m in masks]
            acts += [functools.partial(pre, i, at) for i, at in enumerate(chunks)] + [norm_one]
            return acts + [functools.partial(weight_in, m) for m in masks] + [weight_out]

        n_ffn = 4 + len(chunks) + 2 * nd
        steps = nb * pairs
        n_work = n_ffn + 1 + steps + 4 + len(whole.stages())
        order = []
        for name in names:
            p = piece[name]
            for mask in range(p.nd):
                for e in range(nb):
                    order.append((back_time(nd, nb, name, mask, e), functools.partial(p.reduce, mask, e), None))
        for i in range(n_work):
            order.append((back_time(nd, nb, "work", i, n_work), None, i))
        order.sort(key=lambda q: q[0])
        index = [i for i, q in enumerate(order) if q[2] is not None]
        first, last = index[n_ffn + 1], index[n_ffn + steps]

        def run(entries, acts, base):
            for _, act, i in entries:
                (act if i is None else acts[i - base])()

        def feed_forward_scope(*refs):
            run(order[:index[n_ffn - 1] + 1], feed_forward_steps(*refs), 0)
            for name in "dio":
                piece[name].sent()

        def attention_scope(tok_t, w_v, kaug, v_scr, qaug, do_m, delta_row, dq_scr, dkv, t_part, q_part, q_full):
            held.update(t=t_part, q=q_part, q_full=q_full)
            loads = [(qaug_h, qaug)]
            for k in range(3):
                lanes = pl.ds(pl.multiple_of((k * nc + c) * half, 128), half)
                loads.append((w_h.at[:, lanes], w_v.at[:, pl.ds(k * half, half)]))
            loads.append((tok_t_h, tok_t))
            loads = [pltpu.make_async_copy(src, dst, load_sem.at[8 + i]) for i, (src, dst) in enumerate(loads)]

            def block_loads(blk):
                at = pl.ds(pl.multiple_of(blk * qlen, qlen), qlen)
                return [
                    pltpu.make_async_copy(kaug_h.at[:, at], kaug.at[:, at], load_sem.at[13 + blk]),
                    pltpu.make_async_copy(v_h.at[:, at], v_scr.at[:, at], load_sem.at[13 + nb + blk]),
                ]

            loads[0].start()
            for e in range(nb - 1, -1, -1):
                for copy in block_loads(net.near(e)):
                    copy.start()
            for copy in loads[1:]:
                copy.start()

            def prepare():
                swap.wait()
                lane = lambda p: slice(p * 128, (p + 1) * 128)
                prepare_backward(
                    lambda p: jnp.concatenate([gctx_all[g, :, lane(p)] for g in range(nc)], axis=0), exact, do_m, delta_row
                )
                for copy in loads:
                    copy.wait()

            def token_grad(blk):
                at = pl.ds(pl.multiple_of(blk * qlen, qlen), qlen)
                return dot(dkv[at, :], w_v[:, half:3 * half], ((1,), (1,)))

            def put_tokens(blk, grad):
                for g in range(nc):
                    t_part[blk, g] = grad[g * rows:(g + 1) * rows].astype(BF16)
                piece["t"].send(blk, blk)

            def weights():
                grad_q[...] = jnp.concatenate([join_dq(dq_scr, p) for p in range(pairs)], axis=1)
                mine = pl.ds(pl.multiple_of(net.b * qlen, qlen), qlen)
                for k in range(3):
                    if k:
                        grad = dot(tok_t[...], dkv[:, (k - 1) * half:k * half])
                    else:
                        grad = dot(tok_t[:, mine], grad_q[...])
                    for at in range(owners):
                        for g in range(nc):
                            i = at * nc + g
                            q_part[at, g, :, k * half:(k + 1) * half] = grad[i * r:(i + 1) * r].astype(BF16)

            def own_tokens():
                put_tokens(net.b, token_grad(net.b) + dot(grad_q[...], w_v[:, 0:half], ((1,), (1,))))

            def small_sums():
                lanes = pl.ds(pl.multiple_of(c * half, 128), half)
                value[0, 0:1, lanes] = column_sum(grad_q[...].astype(F32))
                value[0, 1:2, lanes] = column_sum(dkv[:, half:2 * half].astype(F32))

            stages = whole.stages()

            def pick_small():
                stages[-1]()
                me = (net.d * nb + net.b) * nc + c
                feature = lax.broadcasted_iota(jnp.int32, (width, 128), 0)
                lane = lax.broadcasted_iota(jnp.int32, (width, 128), 1)
                pick = jnp.where((feature == me * r + lane) & (lane < r), 1.0, 0.0).astype(F32)
                in_row, in_lane = (me * r_ff) // width, (me * r_ff) % width
                pick_in = jnp.where((feature == in_lane + lane) & (lane < r_ff), 1.0, 0.0).astype(F32)
                exactly = dict(precision=lax.Precision.HIGHEST, preferred_element_type=F32)
                g_small[0:8, :] = jnp.dot(value[0, 0:8, :], pick, **exactly)
                found = jnp.dot(value[0, 8:16, :], pick_in, **exactly)
                row = lax.broadcasted_iota(jnp.int32, found.shape, 0)
                g_small[8:16, :] = jnp.broadcast_to(column_sum(jnp.where(row == in_row, found, 0.0)), (8, 128))

            acts = [prepare] + [None] * steps + [weights, piece["q"].start, own_tokens, small_sums]
            acts += stages[:-1] + [pick_small]
            run(order[index[n_ffn - 1] + 1:first], acts, n_ffn)
            beside = {}
            for _, act, i in order[first:last + 1]:
                if i is not None:
                    at_step = i - n_ffn - 1
                else:
                    beside.setdefault(at_step, []).append(act)

            def attention(i, carry):
                pair = i % pairs
                blk = net.near_at(nb - 1 - i // pairs)
                at = pl.ds(pl.multiple_of(blk * qlen, qlen), qlen)

                @pl.when(pair == 0)
                def _():
                    for copy in block_loads(blk):
                        copy.wait()

                def put(dk, dv):
                    dkv[at, pl.ds(pl.multiple_of(pair * 128, 128), 128)] = dk.astype(BF16)
                    dkv[at, pl.ds(pl.multiple_of(half + pair * 128, 128), 128)] = dv.astype(BF16)

                bwd_pair(pair, qaug, kaug[pair, at, :], v_scr[pair, at, :], do_m, lse_row, delta_row, dq_scr, put, i < pairs)

                @pl.when((pair == pairs - 1) & (i < steps - 1))
                def _():
                    put_tokens(blk, token_grad(blk))

                for g, acts in beside.items():

                    @pl.when(i == g)
                    def _(acts=acts):
                        for act in acts:
                            act()

                return carry

            lax.fori_loop(0, steps, attention, 0)
            run(order[last + 1:], acts, n_ffn)
            for k in range(3):
                for g in range(nc):
                    lanes = slice((k * nc + g) * half, (k * nc + g + 1) * half)
                    g_qkv[:, lanes] = q_out[g, :, k * half:(k + 1) * half]
            for name in names:
                piece[name].drain()

        pl.run_scoped(feed_forward_scope, *scopes[0])
        pl.run_scoped(attention_scope, *scopes[1])

    block = {"d": (r_ff, width), "i": (r, ff), "o": (r, width), "t": (rows, width)}
    joined = (nc, r, 3 * half)
    vmem = lambda shape, kind=BF16: pltpu.VMEM(shape, kind)
    held_out = [vmem((owners,) + block[k]) for k in "dio"]
    scopes = (
        [
            vmem((width, width)),
            vmem((width, ff)),
            vmem((ff, width)),
            vmem((rows, ff)),
            vmem((rows, ff), F32),
            vmem((rows, ff)),
            vmem((width, rows)),
            vmem((width, rows)),
        ]
        + held_out,
        [
            vmem((width, total)),
            vmem((width, 3 * half)),
            vmem((pairs, total, 256)),
            vmem((pairs, total, 128)),
            vmem((heads, qlen, 256)),
            vmem((heads, qlen, 128)),
            vmem((heads, 8, qlen), F32),
            vmem((heads, 128, qlen), F32),
            vmem((total, 2 * half)),
            vmem((nb, nc, rows, width)),
            vmem((owners,) + joined),
            vmem((owners,) + joined),
        ],
    )
    scratch = [vmem((owners,) + block[k]) for k in "dio"] + [vmem((owners,) + block[k]) for k in "dio"]
    scratch += [vmem((nb,) + block["t"]), vmem((owners, r, 3 * half))]
    scratch += [vmem(((nd - 1) * nb,) + block[k]) for k in "dio"] + [vmem(((nd - 1) * nb,) + joined)]
    scratch += [vmem((nb + 1,) + block[k]) for k in "diot"] + [vmem((nb + 1,) + joined)]
    scratch += [
        vmem(joined, F32),
        vmem((rows, width), F32),
        vmem((nc, rows, half)),
        vmem((nc, rows, half)),
        vmem((qlen, half)),
        vmem((rows, width), F32),
        vmem((rows, width), F32),
        vmem((pairs, qlen, 128), F32),
        vmem((levels + 2, n_sums, width), F32),
        vmem((levels + nb, n_sums, width), F32),
        pltpu.SemaphoreType.DMA((13 + 2 * nb,)),
        pltpu.SemaphoreType.DMA((2,)),
    ]
    scratch += scatter_sems(5, nd, nb) + [pltpu.SemaphoreType.DMA((levels + nb,))] * 2
    return pl.pallas_call(
        kernel,
        out_shape=[
            jax.ShapeDtypeStruct((rows, width), BF16),
            jax.ShapeDtypeStruct((rows, width), F32),
            jax.ShapeDtypeStruct((r, 3 * width), F32),
            jax.ShapeDtypeStruct((r, width), F32),
            jax.ShapeDtypeStruct((r, ff), F32),
            jax.ShapeDtypeStruct((r_ff, width), F32),
            jax.ShapeDtypeStruct((16, 128), F32),
        ],
        in_specs=[VMEM] * 5 + [HBM] * 13,
        out_specs=[VMEM] * 7,
        scratch_shapes=scratch,
        compiler_params=params(62, 3),
    )(
        ctx, cot, vecs, lse, scale_one, normed, unit_one, exact_in, w_out, w_in, w_down, act_in, slope_in,
        tok_t_in, w_qkv, kaug_in, v_in, qaug_in,
    )


def body(
    tokens,
    segment,
    w_qkv,
    bias_query,
    bias_value,
    w_out,
    bias_out,
    gain_attn,
    shift_attn,
    w_in,
    bias_in,
    w_down,
    bias_down,
    gain_ffn,
    shift_ffn,
    cotangent,
):
    nd, nb, nc = lax.axis_size("dp"), lax.axis_size("blk"), lax.axis_size("head")
    n_dev = nd * nb * nc
    d_idx, b_idx, c_idx = lax.axis_index("dp"), lax.axis_index("blk"), lax.axis_index("head")
    me = (d_idx * nb + b_idx) * nc + c_idx
    seqs, rows, width = tokens.shape
    ff = w_in.shape[1]
    half_w = width // nc
    qlen = nc * rows
    r = w_qkv.shape[0]
    r_ff = w_down.shape[0]
    flat_in = tokens.reshape(rows, width)
    cot = cotangent.reshape(rows, width)
    vectors = [bias_query, bias_value, bias_out, gain_attn, shift_attn, bias_down, gain_ffn, shift_ffn]
    if nb * qlen <= 2048 and r % 8 == 0 and ff // width <= 8:
        (
            ctx2, vecs, lse, scale_one,
            f_qkv, f_out, f_in, f_down, kaug, v_all, qaug, tok_t, act, slope, exact, normed, unit_one,
        ) = front([v[None, :] for v in vectors], bias_in[None, :], w_qkv, flat_in, w_out, w_in, w_down, segment, nd, nb, nc)
        out, g_tok, o_qkv, o_out, o_in, o_down, g_small = back(
            ctx2, cot, vecs, lse, scale_one, normed, unit_one, exact, f_out, f_in, f_down, act, slope,
            tok_t, f_qkv, kaug, v_all, qaug, nd, nb, nc,
        )
        out, g_tok, o_qkv, o_out, o_in, o_down, g_bq, g_bv, g_bo, g_g1, g_s1, g_bd, g_g2, g_s2, g_bin = hand_out(
            [out, g_tok, o_qkv, o_out, o_in, o_down], g_small, r, r_ff
        )
        return (
            out.reshape(seqs, rows, width), g_tok.reshape(seqs, rows, width),
            o_qkv, g_bq, g_bv, o_out, g_bo, g_g1, g_s1, o_in, g_bin, o_down, g_bd, g_g2, g_s2,
        )
    packed = jnp.concatenate(vectors + [bias_in])
    used = packed.shape[0]
    lanes = -(-used // 128) * 128
    packed = jnp.broadcast_to(jnp.pad(packed, (0, lanes - used))[None], (8, lanes))
    n4 = 4
    parts = [flat_in[i * (rows // n4):(i + 1) * (rows // n4)] for i in range(n4)]
    shards = [packed, w_qkv] + parts + [w_out, w_in, w_down]
    narrow = [False, False] + [True] * n4 + [False] * 3
    keys = [(-1, 3, 3), (0, 3, 3), (7, 9, 0), (10, 9, 0), (13, 9, 0), (16, 9, 0), (2, 4, 4), (9, 6, 5), (22, 6, 5)]
    small, g_qkv, t0, t1, t2, t3, g_out, g_in, g_down = gather_all(shards, narrow, keys, nd, nb, nc)
    full_small = small[:, 0, :used]
    vecs = full_small[:, :8 * r].reshape(n_dev, 8, r).transpose(1, 0, 2).reshape(8, width).astype(F32)
    full_bin = full_small[:, 8 * r:].reshape(ff).astype(F32)
    bq, bv, bout, gain_one, shift_one, bdown, gain_two, shift_two = (vecs[i] for i in range(8))
    full_qkv = g_qkv.reshape(width, 3 * width)
    full_wout = g_out.reshape(width, width)
    full_win = g_in.reshape(width, ff)
    full_wdown = g_down.reshape(ff, width)
    tok_all = jnp.stack([t0, t1, t2, t3], axis=1).reshape(nb * qlen, width)
    my_bias = lax.dynamic_slice(vecs, (0, c_idx * half_w), (2, half_w))
    ctx, kaug, v_scr, qaug, lse, exact = attend_forward(tok_all, full_qkv, my_bias, segment, qlen, half_w)
    context_low = ctx.reshape(seqs, qlen, 1, half_w)
    back_tokens = lax.all_to_all(context_low, "head", split_axis=1, concat_axis=2, tiled=True)
    ctx2 = back_tokens.reshape(rows, nc, half_w).transpose(1, 0, 2)
    out, grad_resid_one, gctx2, dw_down, dw_in, dw_out, sums = feed_forward(
        ctx2, flat_in, cot, vecs, full_bin.reshape(1, ff), full_wout, full_win, full_wdown
    )
    output = out.reshape(seqs, rows, width)
    grad_context = gctx2.transpose(1, 0, 2)
    grad_headed = lax.all_to_all(
        grad_context.reshape(seqs, rows, nc, half_w), "head", split_axis=2, concat_axis=1, tiled=True
    )
    gctx = grad_headed.reshape(qlen, half_w)
    tok_mine = lax.dynamic_slice(tok_all, (b_idx * qlen, 0), (qlen, width))
    dtok, dw, dbias = attend_backward(tok_all, tok_mine, full_qkv, qaug, kaug, v_scr, lse, exact, gctx)
    dw = dw.astype(BF16).reshape(nd * nb, nc, r, 3 * half_w)
    ours = lax.dynamic_index_in_dim(dw, c_idx, 1, keepdims=False)
    theirs = lax.dynamic_index_in_dim(dw, 1 - c_idx, 1, keepdims=False)
    joined_full = jnp.stack([ours, ours], axis=1)
    sums = lax.dynamic_update_slice(sums, dbias, (0, c_idx * half_w))
    o_down, o_in, o_out, o_tok, o_qkv, total = scatter_all(
        [
            dw_down.reshape(n_dev, r_ff, width),
            dw_in.reshape(n_dev, r, ff),
            dw_out.reshape(n_dev, r, width),
            dtok.reshape(nb * nc, rows, width),
            (joined_full, theirs),
        ],
        [False, False, False, True, False],
        [False, False, False, False, True],
        sums,
        nd,
        nb,
        nc,
    )
    grad_tokens = (grad_resid_one + o_tok).reshape(seqs, rows, width)
    o_qkv = o_qkv.reshape(2, r, 3, half_w).transpose(1, 2, 0, 3).reshape(r, 3 * width)
    mine = lax.dynamic_slice(total, (0, me * r), (8, r))
    mine_in = lax.dynamic_slice(total[8:8 + ff // width].reshape(ff), (me * r_ff,), (r_ff,))
    g_bq, g_bv, g_bo, g_g1, g_s1, g_bd, g_g2, g_s2 = (mine[i] for i in range(8))
    return (
        output,
        grad_tokens,
        o_qkv,
        g_bq,
        g_bv,
        o_out,
        g_bo,
        g_g1,
        g_s1,
        o_in,
        mine_in,
        o_down,
        g_bd,
        g_g2,
        g_s2,
    )


def solution(mesh):
    weight, vector = P(("dp", "blk", "head"), None), P(("dp", "blk", "head"))
    token = P("dp", ("blk", "head"), None)
    return jax.shard_map(
        body,
        mesh=mesh,
        in_specs=(
            token,
            P("dp", None),
            weight,
            vector,
            vector,
            weight,
            vector,
            vector,
            vector,
            weight,
            vector,
            weight,
            vector,
            vector,
            vector,
            token,
        ),
        out_specs=(
            token,
            token,
            weight,
            vector,
            vector,
            weight,
            vector,
            vector,
            vector,
            weight,
            vector,
            weight,
            vector,
            vector,
            vector,
        ),
        check_vma=False,
    )
```
